32 devices in a mesh: tok: 4 (over z), row: 2 (over y), col: 4 (over x, core).
Axes of the slice: x: 2, y: 2, z: 4, core: 2. Of those that a mesh axis runs over, the one named last changes fastest.
Arguments:
- activations: bfloat16 [1408, 4096], P(('tok', 'row'), 'col'), may hold values from -512 to 512
- norm_gain: bfloat16 [4096], P('col'), may hold values from 1.5 to 10
- qkv_weight: bfloat16 [4096, 16, 384], P('row', 'col'), may hold values from -0.09375 to 0.09375
- doc_ids: int32 [1408], P(('tok', 'row')), may hold values from 0 to 3, never falling along the last dimension, each value on 1 to 1056 neighbouring positions
Outputs:
- attended: bfloat16 [1408, 2048], P(('tok', 'row'), 'col')
The draws below stay inside these ranges and needn't reach their ends.
Inputs may be any that keep to these rules, and one draw needn't show every extreme that they name: `doc_ids`: never falls along the sequence; each of the 4 documents holds 1 to 1056 tokens and one holds exactly 1056.
All inputs are finite; a program needn't handle non-finite values.
Results may differ from the reference program's by a relative error of at most 0.007.
The reference program's roundings to bfloat16 on the way (of `normed`, `query`, `keys`, `values` and `weights`) count: a program that leaves them out, or rounds other values in their place, can miss the bound.
Values may be sent and summed in bfloat16 or wider, within the bound.
No kernel may reach another device: no remote copies, remote signals or barrier semaphores. Data moves between devices by JAX's collectives and lax.ppermute only.
A program may use at most 128 MiB of HBM per device.

```python
import math
import jax
import jax.numpy as jnp
import numpy as np
from jax import lax

D = 4096
HEADS = 16
HEAD_DIM = 128
DOCS = 4
TOKENS = 1408
DOC_MOST = 1056


def draw_activations(key, part):
    column_key, row_key, base_key = jax.random.split(key, 3)
    column_scale = jnp.exp(jax.random.uniform(column_key, (1, D), jnp.float32, 0.0, math.log(10.0)))
    row_scale = jnp.exp(jax.random.uniform(row_key, (TOKENS, 1), jnp.float32, 0.0, math.log(10.0)))
    values = jax.random.normal(base_key, (TOKENS, D), jnp.float32) * column_scale * row_scale
    return jnp.clip(values, -512.0, 512.0).astype(jnp.bfloat16)


def draw_norm_gain(key, part):
    lowest = 1.5
    highest = 6.0
    drawn = jax.random.uniform(key, (D,), jnp.float32, math.log(lowest), math.log(highest))
    return jnp.exp(drawn).astype(jnp.bfloat16)


def level_of(stream_key, dims, cuts, smallest, largest):
    def one(position, shards_of):
        heights = jax.random.uniform(jax.random.fold_in(jax.random.fold_in(stream_key, 6), position), (shards_of,), jnp.float32, smallest / len(cuts), largest / len(cuts))
        return jnp.repeat(jnp.exp(heights), dims[position] // shards_of).reshape((-1,) + (1,) * (len(dims) - position - 1))

    factor_of = one(*cuts[0])
    for cut in cuts[1:]:
        factor_of = factor_of * one(*cut)
    return factor_of


def length_profile(count, total, bound, skew):
    weights = [(1 << 20) // math.isqrt(standing ** skew) + 1 for standing in range(2, count + 1)]
    rest, counts = total - bound - (count - 1), [1] * (count - 1)
    while rest > 0:
        candidates = [i for i in range(count - 1) if counts[i] < bound]
        mass, remaining = sum([weights[i] for i in candidates]), rest
        for i in candidates:
            addition = min(bound - counts[i], max(1, remaining * weights[i] // mass), rest)
            counts[i] = counts[i] + addition
            rest = rest - addition
    return np.array([bound] + counts)


def ragged(key, count, total, bound, lean):
    if count == 2:
        one = jax.random.randint(key, (), max(1, total - bound), min(bound, total - 1) + 1)
        return jnp.stack([one, total - one])
    sizes = jnp.asarray(length_profile(count, total, bound, lean), jnp.int32)
    twos = (count - 1) // 2
    donor, receiver = sizes[1:1 + 2 * twos:2], sizes[2:2 + 2 * twos:2]
    slack = jnp.minimum(donor - 1, bound - receiver)
    moved = jax.random.randint(jax.random.fold_in(key, 1), (twos,), 0, 1 << 20) % (slack + 1)
    sizes = sizes.at[1:1 + 2 * twos:2].set(donor - moved).at[2:2 + 2 * twos:2].set(receiver + moved)
    return sizes[jax.random.permutation(jax.random.fold_in(key, 2), count)]


def scatter_about(own_key, shape, spread, bound, cuts=(), kind=jnp.bfloat16):
    entries = jax.random.normal(own_key, shape, jnp.float32) * spread
    if len(cuts) > 0:
        entries = level_of(own_key, shape, cuts, -0.22, 0.18) * entries
    return jnp.clip(entries, min=-bound, max=bound).astype(kind)


def setup_inputs(seed: int = 0) -> dict:
    key_of = jax.random.split(jax.random.key(seed), 5)
    return {
        "activations": draw_activations(jax.random.fold_in(key_of[4], 71), 0),
        "norm_gain": draw_norm_gain(jax.random.fold_in(key_of[4], 71), 0),
        "qkv_weight": scatter_about(key_of[2], (D, HEADS, 3 * HEAD_DIM), D ** -0.5, 0.09375, ((0, 2), (1, 4))),
        "doc_ids": jnp.searchsorted(jnp.cumsum(ragged(key_of[3], DOCS, TOKENS, DOC_MOST, 0)), jnp.arange(TOKENS), side="right").astype(jnp.int32),
    }


def rotate(vectors, places):
    half = vectors.shape[-1] // 2
    spacing = jnp.arange(half).astype(jnp.float32) * (2.0 / vectors.shape[-1])
    inverse = jnp.power(10000.0, -spacing)
    angles = places.astype(jnp.float32)[:, None] * inverse[None, :]
    cosine = jnp.cos(angles)[:, None, :]
    sine = jnp.sin(angles)[:, None, :]
    first_half = vectors[..., :half]
    second_half = vectors[..., half:]
    return jnp.concatenate([first_half * cosine - second_half * sine, first_half * sine + second_half * cosine], axis=-1)

def reference(activations, norm_gain, qkv_weight, doc_ids):
    widened = activations.astype(jnp.float32)
    mean_square = lax.optimization_barrier(jnp.mean(widened * widened, axis=1, keepdims=True))
    normed = (widened * lax.rsqrt(mean_square + 1e-05) * norm_gain.astype(jnp.float32)).astype(jnp.bfloat16)
    flat_weight = qkv_weight.reshape(D, HEADS * 3 * HEAD_DIM)
    projected = jnp.dot(normed, flat_weight, preferred_element_type=jnp.float32).reshape(TOKENS, HEADS, 3 * HEAD_DIM)
    places = jnp.arange(TOKENS).astype(jnp.int32)
    query = rotate(projected[..., :HEAD_DIM], places).astype(jnp.bfloat16)
    keys = rotate(projected[..., HEAD_DIM:2 * HEAD_DIM], places).astype(jnp.bfloat16)
    values = projected[..., 2 * HEAD_DIM:].astype(jnp.bfloat16)
    block = math.gcd(TOKENS, 512)
    scale = 1.0 / math.sqrt(HEAD_DIM)

    def one_head(operands):
        head_query, head_keys, head_values = operands

        def one_block(index):
            begin = index * block
            query_rows = lax.dynamic_slice_in_dim(head_query, begin, block, 0)
            query_places = begin + jnp.arange(block).astype(jnp.int32)
            query_docs = lax.dynamic_slice_in_dim(doc_ids, begin, block, 0)
            scores = jnp.dot(query_rows, head_keys.T, preferred_element_type=jnp.float32) * scale
            visible = (places[None, :] <= query_places[:, None]) & (doc_ids[None, :] == query_docs[:, None])
            masked = jnp.where(visible, scores, -jnp.inf)
            row_top = lax.optimization_barrier(jnp.max(masked, axis=1, keepdims=True))
            exponentials = jnp.where(visible, jnp.exp(masked - row_top), 0.0)
            weights = exponentials.astype(jnp.bfloat16)
            numerator = jnp.dot(weights, head_values, preferred_element_type=jnp.float32)
            return (numerator / lax.optimization_barrier(jnp.sum(exponentials, axis=1, keepdims=True))).astype(jnp.bfloat16)
        blocks = lax.map(one_block, jnp.arange(TOKENS // block).astype(jnp.int32))
        return blocks.reshape(TOKENS, HEAD_DIM)
    heads_out = lax.map(one_head, (query.transpose(1, 0, 2), keys.transpose(1, 0, 2), values.transpose(1, 0, 2)))
    return heads_out.transpose(1, 0, 2).reshape(TOKENS, HEADS * HEAD_DIM)
```

```python
import math

import jax
import jax.numpy as jnp
from jax import lax
from jax.experimental import pallas as pl
from jax.experimental.pallas import tpu as pltpu
from jax.sharding import PartitionSpec as P

EPS = 1e-05
MIB = 1 << 20


def rotary_tables(places, head_size):
    half = head_size // 2
    spacing = jnp.arange(half).astype(jnp.float32) * (2.0 / head_size)
    inverse = jnp.power(10000.0, -spacing)
    angles = places.astype(jnp.float32)[:, None] * inverse[None, :]
    cosine, sine = jnp.cos(angles), jnp.sin(angles)
    return (
        jnp.concatenate([cosine, cosine], axis=1),
        jnp.concatenate([-sine, sine], axis=1),
    )


def project_heads(normed, weight_ref, cos_ref, sin_ref, out_ref):
    heads, size = out_ref.shape[0], out_ref.shape[3]
    depth = weight_ref.shape[0] // 2
    cosine, sine = cos_ref[...], sin_ref[...]
    for head in range(heads):
        columns = slice(head * 3 * size, (head + 1) * 3 * size)
        part = jnp.dot(
            normed[0], weight_ref[:depth, columns], preferred_element_type=jnp.float32
        ) + jnp.dot(normed[1], weight_ref[depth:, columns], preferred_element_type=jnp.float32)
        for kind in range(3):
            piece = part[:, kind * size : (kind + 1) * size]
            if kind < 2:
                piece = piece * cosine + pltpu.roll(piece, size // 2, 1) * sine
            out_ref[head, kind] = piece


def normalise_project_kernel(
    place_ref, a_near, a_far, b_near, b_far, squares_ref, gain_ref, weight_ref, cos_ref, sin_ref,
    out_ref, normed_ref,
):
    rows = a_near.shape[0]
    features = 2 * gain_ref.shape[0] * gain_ref.shape[2]
    core, near_row = place_ref[0], place_ref[1]
    for shards, half in (((a_near, a_far), core), ((b_near, b_far), 1 - core)):
        gain = gain_ref[half]
        for shard, row in zip(shards, (near_row, 1 - near_row)):
            at = pl.ds(pl.multiple_of(row * rows, 16), rows)
            factor = lax.rsqrt(squares_ref[at, :] / features + EPS)
            normed_ref[half, at, :] = (shard[...].astype(jnp.float32) * factor * gain).astype(
                jnp.bfloat16
            )
    project_heads(normed_ref, weight_ref, cos_ref, sin_ref, out_ref)


def project_kernel(normed_ref, weight_ref, cos_ref, sin_ref, out_ref):
    project_heads(normed_ref, weight_ref, cos_ref, sin_ref, out_ref)


def attend_kernel(scale, query_ref, *refs):
    key_value_refs, (key_place_ref, place_ref, start_ref, out_ref) = refs[:-4], refs[-4:]
    heads, size = query_ref.shape[0], query_ref.shape[2]
    key_places = key_place_ref[...]
    visible = (key_places <= place_ref[...]) & (key_places >= start_ref[...])
    for head in range(heads):
        keys = jnp.concatenate([ref[head, 0] for ref in key_value_refs], axis=0)
        values = jnp.concatenate([ref[head, 1] for ref in key_value_refs], axis=0)
        scores = (
            lax.dot_general(
                query_ref[head], keys, (((1,), (1,)), ((), ())), preferred_element_type=jnp.float32
            )
            * scale
        )
        masked = jnp.where(visible, scores, -1e30)
        top = jnp.max(masked, axis=1, keepdims=True)
        exponentials = jnp.where(visible, jnp.exp(masked - top), 0.0)
        total = jnp.sum(exponentials, axis=1, keepdims=True)
        summed = jnp.dot(
            exponentials.astype(jnp.bfloat16), values, preferred_element_type=jnp.float32
        )
        out_ref[:, head * size : (head + 1) * size] = (summed / total).astype(jnp.bfloat16)


def attend_gathered(query, keys, values, places, starts, scale):
    heads, count, size = query.shape
    chunk = math.gcd(keys.shape[1], 1024)
    rounds = keys.shape[1] // chunk
    stacked = (
        keys.reshape(heads, rounds, chunk, size).transpose(1, 0, 2, 3),
        values.reshape(heads, rounds, chunk, size).transpose(1, 0, 2, 3),
        jnp.arange(rounds * chunk, dtype=jnp.int32).reshape(rounds, chunk),
    )

    def advance(state, blocks):
        running, totals, summed = state
        block_keys, block_values, key_places = blocks
        scores = (
            jnp.einsum("hqd,hkd->hqk", query, block_keys, preferred_element_type=jnp.float32) * scale
        )
        visible = (key_places[None, None, :] <= places[None, :, None]) & (
            key_places[None, None, :] >= starts[None, :, None]
        )
        masked = jnp.where(visible, scores, -jnp.inf)
        newest = jnp.maximum(running, jnp.max(masked, axis=2))
        factor = jnp.exp(running - newest)
        exponentials = jnp.where(visible, jnp.exp(masked - newest[:, :, None]), 0.0)
        totals = totals * factor + jnp.sum(exponentials, axis=2)
        summed = summed * factor[:, :, None] + jnp.einsum(
            "hqk,hkd->hqd", exponentials.astype(jnp.bfloat16), block_values,
            preferred_element_type=jnp.float32,
        )
        return (newest, totals, summed), None

    initial = (
        jnp.full((heads, count), -1e30, jnp.float32),
        jnp.zeros((heads, count), jnp.float32),
        jnp.zeros((heads, count, size), jnp.float32),
    )
    (running, totals, summed), unused = lax.scan(advance, initial, stacked)
    attended = (summed / totals[:, :, None]).astype(jnp.bfloat16)
    return attended.transpose(1, 0, 2).reshape(count, heads * size)


def in_vmem(count):
    return [pl.BlockSpec(memory_space=pltpu.VMEM)] * count


def per_device(activations, norm_gain, qkv_weight, doc_ids):
    rows, width = activations.shape
    span, local_heads, triple = qkv_weight.shape
    size = triple // 3
    pair = local_heads // 2
    block = 2 * rows
    toks = lax.axis_size("tok")
    tok, row, col = lax.axis_index("tok"), lax.axis_index("row"), lax.axis_index("col")
    chip, core = col // 2, col % 2
    grid = [(r, c) for r in range(2) for c in range(4)]

    def by_col(value, flip):
        return lax.ppermute(value, "col", [(c, c ^ flip) for c in range(4)])

    def by_row(value):
        return lax.ppermute(value, "row", [(0, 1), (1, 0)])

    def ordered(index, own, other):
        first = index == 0
        return jnp.concatenate([jnp.where(first, own, other), jnp.where(first, other, own)])

    near = lax.ppermute(
        activations,
        ("row", "col"),
        [(r * 4 + c, (c // 2) * 4 + 2 * r + c % 2) for r, c in grid],
    )
    far = lax.ppermute(
        activations,
        ("row", "col"),
        [(r * 4 + c, (c // 2) * 4 + 2 * (1 - r) + c % 2) for r, c in grid],
    )
    near_other, far_other = by_col(near, 1), by_col(far, 1)

    widened = activations.astype(jnp.float32)
    squares = jnp.sum(widened * widened, axis=1)
    gain = norm_gain.astype(jnp.float32)
    got = by_col(jnp.concatenate([squares, gain]), 1)
    squares = squares + got[:rows]
    gain = ordered(core, gain, got[rows:])
    got = by_col(jnp.concatenate([squares, gain]), 2)
    squares = squares + got[:rows]
    gain = jnp.where(chip == row, gain, got[rows:]).reshape(2, 1, width)
    docs = doc_ids.astype(jnp.float32)
    got = by_row(jnp.concatenate([squares, docs]))
    squares = ordered(row, squares, got[:rows]).reshape(block, 1)
    block_docs = ordered(row, docs, got[rows:])
    all_docs = block_docs
    if toks == 4:
        for flip in (1, 2):
            got = lax.ppermute(all_docs, "tok", [(t, t ^ flip) for t in range(4)])
            all_docs = ordered((tok // flip) % 2, all_docs, got)
    else:
        all_docs = lax.all_gather(block_docs, "tok", axis=0, tiled=True)
    starts = jnp.sum((all_docs[None, :] < block_docs[:, None]).astype(jnp.int32), axis=1)
    places = tok * block + jnp.arange(block, dtype=jnp.int32)
    cosine, sine = rotary_tables(places, size)

    halves = qkv_weight.reshape(span, 2, pair * triple)
    weight_away = lax.dynamic_index_in_dim(halves, 1 - row, 1, keepdims=False)
    weight_own = lax.dynamic_index_in_dim(halves, row, 1, keepdims=False)

    partial_shape = jax.ShapeDtypeStruct((pair, 3, block, size), jnp.float32)
    flops = 2 * block * span * pair * triple
    away, normed = pl.pallas_call(
        normalise_project_kernel,
        out_shape=(partial_shape, jax.ShapeDtypeStruct((2, block, width), jnp.bfloat16)),
        in_specs=[pl.BlockSpec(memory_space=pltpu.SMEM)] + in_vmem(9),
        out_specs=tuple(in_vmem(2)),
        compiler_params=pltpu.CompilerParams(vmem_limit_bytes=24 * MIB),
        cost_estimate=pl.CostEstimate(flops=flops, bytes_accessed=6 * MIB, transcendentals=0),
    )(
        jnp.stack([core, chip]), near, far, near_other, far_other, squares, gain, weight_away,
        cosine, sine,
    )
    arrived = by_row(away.astype(jnp.float16))
    own = pl.pallas_call(
        project_kernel,
        out_shape=partial_shape,
        in_specs=in_vmem(4),
        out_specs=in_vmem(1)[0],
        compiler_params=pltpu.CompilerParams(vmem_limit_bytes=24 * MIB),
        cost_estimate=pl.CostEstimate(flops=flops, bytes_accessed=6 * MIB, transcendentals=0),
    )(normed, weight_own, cosine, sine)
    projected = (own + arrived.astype(jnp.float32)).astype(jnp.bfloat16)
    query, key_values = projected[:, 0], projected[:, 1:]
    scale = 1.0 / math.sqrt(size)

    if toks == 4:
        steps = range(1, 4)
        received = [
            lax.ppermute(key_values, "tok", [(t, t + s) for t in range(4 - s)]) for s in steps
        ]
        key_places = jnp.concatenate(
            [(tok - s) * block + jnp.arange(block, dtype=jnp.int32) for s in range(4)]
        )
        attended = pl.pallas_call(
            lambda *refs: attend_kernel(scale, *refs),
            out_shape=jax.ShapeDtypeStruct((block, pair * size), jnp.bfloat16),
            in_specs=in_vmem(8),
            out_specs=in_vmem(1)[0],
            compiler_params=pltpu.CompilerParams(vmem_limit_bytes=32 * MIB),
            cost_estimate=pl.CostEstimate(
                flops=4 * pair * block * 4 * block * size,
                bytes_accessed=4 * MIB,
                transcendentals=pair * block * 4 * block,
            ),
        )(
            query, key_values, *received, key_places.reshape(1, 4 * block),
            places.reshape(block, 1), starts.reshape(block, 1),
        )
    else:
        everything = lax.all_gather(key_values, "tok", axis=2, tiled=True)
        attended = attend_gathered(query, everything[:, 0], everything[:, 1], places, starts, scale)

    mine = lax.dynamic_slice_in_dim(attended, row * rows, rows, 0)
    theirs = by_row(lax.dynamic_slice_in_dim(attended, (1 - row) * rows, rows, 0))
    first = row == 0
    return jnp.concatenate(
        [jnp.where(first, mine, theirs), jnp.where(first, theirs, mine)], axis=1
    )


def solution(mesh):
    placed = (P(("tok", "row"), "col"), P("col"), P("row", "col", None), P(("tok", "row")))
    return jax.shard_map(
        per_device, mesh=mesh, in_specs=placed, out_specs=P(("tok", "row"), "col"), check_vma=False
    )
```

```python
import math

import jax
import jax.numpy as jnp
from jax import lax
from jax.experimental import pallas as pl
from jax.experimental.pallas import tpu as pltpu
from jax.sharding import PartitionSpec as P

EPS = 1e-05
MIB = 1 << 20


def rotary_tables(places, head_size):
    half = head_size // 2
    spacing = jnp.arange(half).astype(jnp.float32) * (2.0 / head_size)
    inverse = jnp.power(10000.0, -spacing)
    angles = places.astype(jnp.float32)[:, None] * inverse[None, :]
    cosine, sine = jnp.cos(angles), jnp.sin(angles)
    return (
        jnp.concatenate([cosine, cosine], axis=1),
        jnp.concatenate([-sine, sine], axis=1),
    )


def project_heads(normed, pair_index, weight_ref, cos_ref, sin_ref, out_ref):
    heads, size = out_ref.shape[0], out_ref.shape[3]
    depth = weight_ref.shape[0] // 2
    cosine, sine = cos_ref[...], sin_ref[...]
    for head in range(heads):
        first = pl.multiple_of((pair_index * heads + head) * 3 * size, 128)
        columns = pl.ds(first, 3 * size)
        part = jnp.dot(
            normed[0], weight_ref[:depth, columns], preferred_element_type=jnp.float32
        ) + jnp.dot(normed[1], weight_ref[depth:, columns], preferred_element_type=jnp.float32)
        for kind in range(3):
            piece = part[:, kind * size : (kind + 1) * size]
            if kind < 2:
                piece = piece * cosine + pltpu.roll(piece, size // 2, 1) * sine
            out_ref[head, kind] = piece


def normalise_project_kernel(
    place_ref, a_near, a_far, b_near, b_far, squares_ref, gain_ref, weight_ref, cos_ref, sin_ref,
    out_ref, normed_ref,
):
    rows = a_near.shape[0]
    features = 2 * gain_ref.shape[0] * gain_ref.shape[2]
    core, near_row = place_ref[0], place_ref[1]
    for shards, half in (((a_near, a_far), core), ((b_near, b_far), 1 - core)):
        gain = gain_ref[half]
        for shard, row in zip(shards, (near_row, 1 - near_row)):
            at = pl.ds(pl.multiple_of(row * rows, 16), rows)
            factor = lax.rsqrt(squares_ref[at, :] / features + EPS)
            normed_ref[half, at, :] = (shard[...].astype(jnp.float32) * factor * gain).astype(
                jnp.bfloat16
            )
    project_heads(normed_ref, place_ref[2], weight_ref, cos_ref, sin_ref, out_ref)


def project_kernel(place_ref, normed_ref, weight_ref, cos_ref, sin_ref, out_ref):
    project_heads(normed_ref, place_ref[0], weight_ref, cos_ref, sin_ref, out_ref)


def attend_kernel(scale, query_ref, *refs):
    key_value_refs, (key_place_ref, place_ref, start_ref, out_ref) = refs[:-4], refs[-4:]
    heads, size = query_ref.shape[0], query_ref.shape[2]
    key_places = key_place_ref[...]
    visible = (key_places <= place_ref[...]) & (key_places >= start_ref[...])
    for head in range(heads):
        keys = jnp.concatenate([ref[head, 0] for ref in key_value_refs], axis=0)
        values = jnp.concatenate([ref[head, 1] for ref in key_value_refs], axis=0)
        scores = (
            lax.dot_general(
                query_ref[head], keys, (((1,), (1,)), ((), ())), preferred_element_type=jnp.float32
            )
            * scale
        )
        masked = jnp.where(visible, scores, -1e30)
        top = jnp.max(masked, axis=1, keepdims=True)
        exponentials = jnp.where(visible, jnp.exp(masked - top), 0.0)
        total = jnp.sum(exponentials, axis=1, keepdims=True)
        summed = jnp.dot(
            exponentials.astype(jnp.bfloat16), values, preferred_element_type=jnp.float32
        )
        out_ref[:, head * size : (head + 1) * size] = (summed / total).astype(jnp.bfloat16)


def attend_gathered(query, keys, values, places, starts, scale):
    heads, count, size = query.shape
    chunk = math.gcd(keys.shape[1], 1024)
    rounds = keys.shape[1] // chunk
    stacked = (
        keys.reshape(heads, rounds, chunk, size).transpose(1, 0, 2, 3),
        values.reshape(heads, rounds, chunk, size).transpose(1, 0, 2, 3),
        jnp.arange(rounds * chunk, dtype=jnp.int32).reshape(rounds, chunk),
    )

    def advance(state, blocks):
        running, totals, summed = state
        block_keys, block_values, key_places = blocks
        scores = (
            jnp.einsum("hqd,hkd->hqk", query, block_keys, preferred_element_type=jnp.float32) * scale
        )
        visible = (key_places[None, None, :] <= places[None, :, None]) & (
            key_places[None, None, :] >= starts[None, :, None]
        )
        masked = jnp.where(visible, scores, -jnp.inf)
        newest = jnp.maximum(running, jnp.max(masked, axis=2))
        factor = jnp.exp(running - newest)
        exponentials = jnp.where(visible, jnp.exp(masked - newest[:, :, None]), 0.0)
        totals = totals * factor + jnp.sum(exponentials, axis=2)
        summed = summed * factor[:, :, None] + jnp.einsum(
            "hqk,hkd->hqd", exponentials.astype(jnp.bfloat16), block_values,
            preferred_element_type=jnp.float32,
        )
        return (newest, totals, summed), None

    initial = (
        jnp.full((heads, count), -1e30, jnp.float32),
        jnp.zeros((heads, count), jnp.float32),
        jnp.zeros((heads, count, size), jnp.float32),
    )
    (running, totals, summed), unused = lax.scan(advance, initial, stacked)
    attended = (summed / totals[:, :, None]).astype(jnp.bfloat16)
    return attended.transpose(1, 0, 2).reshape(count, heads * size)


def in_vmem(count):
    return [pl.BlockSpec(memory_space=pltpu.VMEM)] * count


def per_device(activations, norm_gain, qkv_weight, doc_ids):
    rows, width = activations.shape
    span, local_heads, triple = qkv_weight.shape
    size = triple // 3
    pair = local_heads // 2
    block = 2 * rows
    toks = lax.axis_size("tok")
    tok, row, col = lax.axis_index("tok"), lax.axis_index("row"), lax.axis_index("col")
    chip, core = col >> 1, col & 1
    grid = [(r, c) for r in range(2) for c in range(4)]

    def by_col(value, flip):
        return lax.ppermute(value, "col", [(c, c ^ flip) for c in range(4)])

    def by_row(value):
        return lax.ppermute(value, "row", [(0, 1), (1, 0)])

    def ordered(index, own, other):
        first = index == 0
        return jnp.concatenate([jnp.where(first, own, other), jnp.where(first, other, own)])

    near = lax.ppermute(
        activations,
        ("row", "col"),
        [(r * 4 + c, (c // 2) * 4 + 2 * r + c % 2) for r, c in grid],
    )
    far = lax.ppermute(
        activations,
        ("row", "col"),
        [(r * 4 + c, (c // 2) * 4 + 2 * (1 - r) + c % 2) for r, c in grid],
    )
    near_other, far_other = by_col(near, 1), by_col(far, 1)

    widened = activations.astype(jnp.float32)
    squares = jnp.sum(widened * widened, axis=1)
    gain = norm_gain.astype(jnp.float32)
    got = by_col(jnp.concatenate([squares, gain]), 1)
    squares = squares + got[:rows]
    gain = ordered(core, gain, got[rows:])
    got = by_col(jnp.concatenate([squares, gain]), 2)
    squares = squares + got[:rows]
    gain = jnp.where(chip == row, gain, got[rows:]).reshape(2, 1, width)
    docs = doc_ids.astype(jnp.float32)
    got = by_row(jnp.concatenate([squares, docs]))
    squares = ordered(row, squares, got[:rows]).reshape(block, 1)
    block_docs = ordered(row, docs, got[rows:])
    all_docs = block_docs
    if toks == 4:
        for flip in (1, 2):
            got = lax.ppermute(all_docs, "tok", [(t, t ^ flip) for t in range(4)])
            all_docs = ordered(tok & flip, all_docs, got)
    else:
        all_docs = lax.all_gather(block_docs, "tok", axis=0, tiled=True)
    starts = jnp.sum((all_docs[None, :] < block_docs[:, None]).astype(jnp.int32), axis=1)
    places = tok * block + jnp.arange(block, dtype=jnp.int32)
    cosine, sine = rotary_tables(places, size)

    flat_weight = qkv_weight.reshape(span, local_heads * triple)

    partial_shape = jax.ShapeDtypeStruct((pair, 3, block, size), jnp.float32)
    flops = 2 * block * span * pair * triple
    away, normed = pl.pallas_call(
        normalise_project_kernel,
        out_shape=(partial_shape, jax.ShapeDtypeStruct((2, block, width), jnp.bfloat16)),
        in_specs=[pl.BlockSpec(memory_space=pltpu.SMEM)] + in_vmem(9),
        out_specs=tuple(in_vmem(2)),
        compiler_params=pltpu.CompilerParams(vmem_limit_bytes=24 * MIB),
        cost_estimate=pl.CostEstimate(flops=flops, bytes_accessed=6 * MIB, transcendentals=0),
    )(
        jnp.stack([core, chip, 1 - row]), near, far, near_other, far_other, squares, gain,
        flat_weight, cosine, sine,
    )
    arrived = by_row(away.astype(jnp.float16))
    own = pl.pallas_call(
        project_kernel,
        out_shape=partial_shape,
        in_specs=[pl.BlockSpec(memory_space=pltpu.SMEM)] + in_vmem(4),
        out_specs=in_vmem(1)[0],
        compiler_params=pltpu.CompilerParams(vmem_limit_bytes=24 * MIB),
        cost_estimate=pl.CostEstimate(flops=flops, bytes_accessed=6 * MIB, transcendentals=0),
    )(row.reshape(1), normed, flat_weight, cosine, sine)
    projected = (own + arrived.astype(jnp.float32)).astype(jnp.bfloat16)
    query, key_values = projected[:, 0], projected[:, 1:]
    scale = 1.0 / math.sqrt(size)

    if toks == 4:
        steps = range(1, 4)
        received = [
            lax.ppermute(key_values, "tok", [(t, t + s) for t in range(4 - s)]) for s in steps
        ]
        key_places = jnp.concatenate(
            [(tok - s) * block + jnp.arange(block, dtype=jnp.int32) for s in range(4)]
        )
        attended = pl.pallas_call(
            lambda *refs: attend_kernel(scale, *refs),
            out_shape=jax.ShapeDtypeStruct((block, pair * size), jnp.bfloat16),
            in_specs=in_vmem(8),
            out_specs=in_vmem(1)[0],
            compiler_params=pltpu.CompilerParams(vmem_limit_bytes=32 * MIB),
            cost_estimate=pl.CostEstimate(
                flops=4 * pair * block * 4 * block * size,
                bytes_accessed=4 * MIB,
                transcendentals=pair * block * 4 * block,
            ),
        )(
            query, key_values, *received, key_places.reshape(1, 4 * block),
            places.reshape(block, 1), starts.reshape(block, 1),
        )
    else:
        everything = lax.all_gather(key_values, "tok", axis=2, tiled=True)
        attended = attend_gathered(query, everything[:, 0], everything[:, 1], places, starts, scale)

    mine = lax.dynamic_slice_in_dim(attended, row * rows, rows, 0)
    theirs = by_row(lax.dynamic_slice_in_dim(attended, (1 - row) * rows, rows, 0))
    first = row == 0
    return jnp.concatenate(
        [jnp.where(first, mine, theirs), jnp.where(first, theirs, mine)], axis=1
    )


def solution(mesh):
    placed = (P(("tok", "row"), "col"), P("col"), P("row", "col", None), P(("tok", "row")))
    return jax.shard_map(
        per_device, mesh=mesh, in_specs=placed, out_specs=P(("tok", "row"), "col"), check_vma=False
    )
```

```python
import math

import jax
import jax.numpy as jnp
from jax import lax
from jax.experimental import pallas as pl
from jax.experimental.pallas import tpu as pltpu
from jax.sharding import PartitionSpec as P

EPS = 1e-05
MIB = 1 << 20


def rotary_tables(places, head_size):
    half = head_size // 2
    spacing = jnp.arange(half).astype(jnp.float32) * (2.0 / head_size)
    inverse = jnp.power(10000.0, -spacing)
    angles = places.astype(jnp.float32)[:, None] * inverse[None, :]
    cosine, sine = jnp.cos(angles), jnp.sin(angles)
    return (
        jnp.concatenate([cosine, cosine], axis=1),
        jnp.concatenate([-sine, sine], axis=1),
    )


def weight_copies(first_head, triple, weight_hbm, weight_buffer, semaphores):
    depth = weight_buffer.shape[0] // 2
    columns = weight_buffer.shape[1]
    first = pl.multiple_of(first_head * triple, 128)
    return [
        pltpu.make_async_copy(
            weight_hbm.at[pl.ds(half * depth, depth), pl.ds(first, columns)],
            weight_buffer.at[pl.ds(half * depth, depth), :],
            semaphores.at[half],
        )
        for half in range(2)
    ]


def project_heads(normed_ref, copies, weight_buffer, cos_ref, sin_ref, out_ref):
    heads, size = out_ref.shape[0], out_ref.shape[3]
    depth = weight_buffer.shape[0] // 2
    for copy in copies:
        copy.wait()
    for head in range(heads):
        columns = slice(head * 3 * size, (head + 1) * 3 * size)
        part = jnp.dot(
            normed_ref[0], weight_buffer[:depth, columns], preferred_element_type=jnp.float32
        ) + jnp.dot(
            normed_ref[1], weight_buffer[depth:, columns], preferred_element_type=jnp.float32
        )
        for kind in range(3):
            piece = part[:, kind * size : (kind + 1) * size]
            if kind < 2:
                piece = piece * cos_ref[...] + pltpu.roll(piece, size // 2, 1) * sin_ref[...]
            out_ref[head, kind] = piece


def normalise_project_kernel(
    place_ref, a_near, a_far, b_near, b_far, squares_ref, gain_ref, weight_hbm, cos_ref, sin_ref,
    out_ref, normed_ref, weight_buffer, semaphores,
):
    rows = a_near.shape[0]
    features = 2 * gain_ref.shape[0] * gain_ref.shape[2]
    core, near_row, head = place_ref[0], place_ref[1], place_ref[2]
    copies = weight_copies(head, 3 * cos_ref.shape[1], weight_hbm, weight_buffer, semaphores)
    for copy in copies:
        copy.start()
    for shards, half in (((a_near, a_far), core), ((b_near, b_far), 1 - core)):
        gain = gain_ref[half]
        for shard, row in zip(shards, (near_row, 1 - near_row)):
            at = pl.ds(pl.multiple_of(row * rows, 16), rows)
            factor = lax.rsqrt(squares_ref[at, :] / features + EPS)
            normed_ref[half, at, :] = (shard[...].astype(jnp.float32) * factor * gain).astype(
                jnp.bfloat16
            )
    project_heads(normed_ref, copies, weight_buffer, cos_ref, sin_ref, out_ref)


def project_kernel(
    place_ref, normed_ref, weight_hbm, cos_ref, sin_ref, out_ref, weight_buffer, semaphores
):
    copies = weight_copies(
        place_ref[0], 3 * cos_ref.shape[1], weight_hbm, weight_buffer, semaphores
    )
    for copy in copies:
        copy.start()
    project_heads(normed_ref, copies, weight_buffer, cos_ref, sin_ref, out_ref)


def attend_kernel(scale, query_ref, *refs):
    key_value_refs, (key_place_ref, place_ref, start_ref, out_ref) = refs[:-4], refs[-4:]
    key_places = key_place_ref[...]
    visible = (key_places <= place_ref[...]) & (key_places >= start_ref[...])
    keys = jnp.concatenate([ref[0] for ref in key_value_refs], axis=0)
    values = jnp.concatenate([ref[1] for ref in key_value_refs], axis=0)
    scores = (
        lax.dot_general(
            query_ref[...], keys, (((1,), (1,)), ((), ())), preferred_element_type=jnp.float32
        )
        * scale
    )
    masked = jnp.where(visible, scores, -1e30)
    top = jnp.max(masked, axis=1, keepdims=True)
    exponentials = jnp.where(visible, jnp.exp(masked - top), 0.0)
    total = jnp.sum(exponentials, axis=1, keepdims=True)
    summed = jnp.dot(
        exponentials.astype(jnp.bfloat16), values, preferred_element_type=jnp.float32
    )
    out_ref[...] = (summed / total).astype(jnp.bfloat16)


def attend_gathered(query, keys, values, places, starts, scale):
    heads, count, size = query.shape
    chunk = math.gcd(keys.shape[1], 1024)
    rounds = keys.shape[1] // chunk
    stacked = (
        keys.reshape(heads, rounds, chunk, size).transpose(1, 0, 2, 3),
        values.reshape(heads, rounds, chunk, size).transpose(1, 0, 2, 3),
        jnp.arange(rounds * chunk, dtype=jnp.int32).reshape(rounds, chunk),
    )

    def advance(state, blocks):
        running, totals, summed = state
        block_keys, block_values, key_places = blocks
        scores = (
            jnp.einsum("hqd,hkd->hqk", query, block_keys, preferred_element_type=jnp.float32) * scale
        )
        visible = (key_places[None, None, :] <= places[None, :, None]) & (
            key_places[None, None, :] >= starts[None, :, None]
        )
        masked = jnp.where(visible, scores, -jnp.inf)
        newest = jnp.maximum(running, jnp.max(masked, axis=2))
        factor = jnp.exp(running - newest)
        exponentials = jnp.where(visible, jnp.exp(masked - newest[:, :, None]), 0.0)
        totals = totals * factor + jnp.sum(exponentials, axis=2)
        summed = summed * factor[:, :, None] + jnp.einsum(
            "hqk,hkd->hqd", exponentials.astype(jnp.bfloat16), block_values,
            preferred_element_type=jnp.float32,
        )
        return (newest, totals, summed), None

    initial = (
        jnp.full((heads, count), -1e30, jnp.float32),
        jnp.zeros((heads, count), jnp.float32),
        jnp.zeros((heads, count, size), jnp.float32),
    )
    (running, totals, summed), unused = lax.scan(advance, initial, stacked)
    attended = (summed / totals[:, :, None]).astype(jnp.bfloat16)
    return attended.transpose(1, 0, 2).reshape(count, heads * size)


def in_vmem(count):
    return [pl.BlockSpec(memory_space=pltpu.VMEM)] * count


def per_device(activations, norm_gain, qkv_weight, doc_ids):
    rows, width = activations.shape
    span, local_heads, triple = qkv_weight.shape
    size = triple // 3
    pair = local_heads // 2
    block = 2 * rows
    toks = lax.axis_size("tok")
    tok, row, col = lax.axis_index("tok"), lax.axis_index("row"), lax.axis_index("col")
    chip, core = col >> 1, col & 1
    grid = [(r, c) for r in range(2) for c in range(4)]

    def by_col(value, flip):
        return lax.ppermute(value, "col", [(c, c ^ flip) for c in range(4)])

    def by_row(value):
        return lax.ppermute(value, "row", [(0, 1), (1, 0)])

    def ordered(index, own, other):
        first = index == 0
        return jnp.concatenate([jnp.where(first, own, other), jnp.where(first, other, own)])

    near = lax.ppermute(
        activations,
        ("row", "col"),
        [(r * 4 + c, (c // 2) * 4 + 2 * r + c % 2) for r, c in grid],
    )
    far = lax.ppermute(
        activations,
        ("row", "col"),
        [(r * 4 + c, (c // 2) * 4 + 2 * (1 - r) + c % 2) for r, c in grid],
    )
    widened = activations.astype(jnp.float32)
    squares = jnp.sum(widened * widened, axis=1)
    gain = norm_gain.astype(jnp.float32)
    message = jnp.concatenate([squares, gain])
    message, qkv_weight = lax.optimization_barrier((message, qkv_weight))
    flat_weight = qkv_weight.reshape(span, local_heads * triple)
    got = by_col(message, 1)
    squares = squares + got[:rows]
    gain = ordered(core, gain, got[rows:])
    got = by_col(jnp.concatenate([squares, gain]), 2)
    near, far, got, flat_weight = lax.optimization_barrier((near, far, got, flat_weight))
    near_other, far_other = by_col(near, 1), by_col(far, 1)
    squares = squares + got[:rows]
    gain = jnp.where(chip == row, gain, got[rows:]).reshape(2, 1, width)
    docs = doc_ids.astype(jnp.float32)
    got = by_row(jnp.concatenate([squares, docs]))
    squares = ordered(row, squares, got[:rows]).reshape(block, 1)
    block_docs = ordered(row, docs, got[rows:])
    places = tok * block + jnp.arange(block, dtype=jnp.int32)
    cosine, sine = rotary_tables(places, size)

    def projection(kernel, heads, normalising):
        normed_shape = (jax.ShapeDtypeStruct((2, block, width), jnp.bfloat16),)
        return pl.pallas_call(
            kernel,
            out_shape=(jax.ShapeDtypeStruct((heads, 3, block, size), jnp.float32),)
            + (normed_shape if normalising else ()),
            in_specs=[pl.BlockSpec(memory_space=pltpu.SMEM)]
            + in_vmem(6 if normalising else 1)
            + [pl.BlockSpec(memory_space=pl.ANY)]
            + in_vmem(2),
            out_specs=tuple(in_vmem(2 if normalising else 1)),
            scratch_shapes=[
                pltpu.VMEM((span, heads * triple), jnp.bfloat16),
                pltpu.SemaphoreType.DMA((2,)),
            ],
            compiler_params=pltpu.CompilerParams(vmem_limit_bytes=24 * MIB),
            cost_estimate=pl.CostEstimate(
                flops=2 * block * span * heads * triple,
                bytes_accessed=(2 + heads) * MIB,
                transcendentals=0,
            ),
        )

    away_head, own_head = (1 - row) * pair, row * pair
    away, normed = projection(normalise_project_kernel, 1, True)(
        jnp.stack([core, chip, away_head]), near, far, near_other, far_other, squares, gain,
        flat_weight, cosine, sine,
    )
    arrived = []
    for head in range(pair):
        if head > 0:
            (away,) = projection(project_kernel, 1, False)(
                (away_head + head).reshape(1), normed, flat_weight, cosine, sine
            )
        away, normed = lax.optimization_barrier((away.astype(jnp.float16), normed))
        arrived.append(by_row(away[0]))
    (own,) = projection(project_kernel, pair, False)(
        own_head.reshape(1), normed, flat_weight, cosine, sine
    )

    block_docs, own = lax.optimization_barrier((block_docs, own))
    all_docs = block_docs
    if toks == 4:
        for flip in (1, 2):
            got = lax.ppermute(all_docs, "tok", [(t, t ^ flip) for t in range(4)])
            all_docs = ordered(tok & flip, all_docs, got)
    else:
        all_docs = lax.all_gather(block_docs, "tok", axis=0, tiled=True)
    starts = jnp.sum((all_docs[None, :] < block_docs[:, None]).astype(jnp.int32), axis=1)
    scale = 1.0 / math.sqrt(size)

    queries, key_values = [], []
    for head in range(pair):
        query = (own[head, 0] + arrived[head][0].astype(jnp.float32)).astype(jnp.bfloat16)
        both = (own[head, 1:] + arrived[head][1:].astype(jnp.float32)).astype(jnp.bfloat16)
        if head + 1 < pair:
            query, both, arrived[head + 1] = lax.optimization_barrier(
                (query, both, arrived[head + 1])
            )
        queries.append(query)
        key_values.append(both)
    if toks == 4:
        received = [
            [lax.ppermute(key_values[head], "tok", [(t, t + s) for t in range(4 - s)]) for s in (1, 2, 3)]
            for head in range(pair)
        ]
        key_places = jnp.concatenate(
            [(tok - s) * block + jnp.arange(block, dtype=jnp.int32) for s in range(4)]
        )
        attend = pl.pallas_call(
            lambda *refs: attend_kernel(scale, *refs),
            out_shape=jax.ShapeDtypeStruct((block, size), jnp.bfloat16),
            in_specs=in_vmem(8),
            out_specs=in_vmem(1)[0],
            compiler_params=pltpu.CompilerParams(vmem_limit_bytes=24 * MIB),
            cost_estimate=pl.CostEstimate(
                flops=4 * block * 4 * block * size,
                bytes_accessed=2 * MIB,
                transcendentals=block * 4 * block,
            ),
        )
        attended = [
            attend(
                queries[head], key_values[head], *received[head],
                key_places.reshape(1, 4 * block), places.reshape(block, 1), starts.reshape(block, 1),
            )
            for head in range(pair)
        ]
    else:
        everything = lax.all_gather(jnp.stack(key_values), "tok", axis=2, tiled=True)
        together = attend_gathered(
            jnp.stack(queries), everything[:, 0], everything[:, 1], places, starts, scale
        )
        attended = [together[:, head * size : (head + 1) * size] for head in range(pair)]

    mine, theirs = [], []
    for one in attended:
        mine.append(jnp.where(row == 0, one[:rows], one[rows:]))
        theirs.append(by_row(jnp.where(row == 0, one[rows:], one[:rows])))
    return jnp.concatenate(
        [jnp.where(row == 0, a, b) for a, b in zip(mine + theirs, theirs + mine)], axis=1
    )


def solution(mesh):
    placed = (P(("tok", "row"), "col"), P("col"), P("row", "col", None), P(("tok", "row")))
    return jax.shard_map(
        per_device, mesh=mesh, in_specs=placed, out_specs=P(("tok", "row"), "col"), check_vma=False
    )
```

```python
import math

import jax
import jax.numpy as jnp
from jax import lax
from jax.experimental import pallas as pl
from jax.experimental.pallas import tpu as pltpu
from jax.sharding import PartitionSpec as P

EPS = 1e-05
MIB = 1 << 20


def rotary_tables(places, head_size):
    half = head_size // 2
    spacing = jnp.arange(half).astype(jnp.float32) * (2.0 / head_size)
    inverse = jnp.power(10000.0, -spacing)
    angles = places.astype(jnp.float32)[:, None] * inverse[None, :]
    cosine, sine = jnp.cos(angles), jnp.sin(angles)
    return (
        jnp.concatenate([cosine, cosine], axis=1),
        jnp.concatenate([-sine, sine], axis=1),
    )


def weight_copies(first_head, triple, weight_hbm, weight_buffer, semaphores):
    depth = weight_buffer.shape[0] // 2
    columns = weight_buffer.shape[1]
    first = pl.multiple_of(first_head * triple, 128)
    return [
        pltpu.make_async_copy(
            weight_hbm.at[pl.ds(half * depth, depth), pl.ds(first, columns)],
            weight_buffer.at[pl.ds(half * depth, depth), :],
            semaphores.at[half],
        )
        for half in range(2)
    ]


def project_heads(normed_ref, copies, weight_buffer, cos_ref, sin_ref, out_ref):
    heads, size = out_ref.shape[0], out_ref.shape[3]
    depth = weight_buffer.shape[0] // 2
    for copy in copies:
        copy.wait()
    for head in range(heads):
        columns = slice(head * 3 * size, (head + 1) * 3 * size)
        part = jnp.dot(
            normed_ref[0], weight_buffer[:depth, columns], preferred_element_type=jnp.float32
        ) + jnp.dot(
            normed_ref[1], weight_buffer[depth:, columns], preferred_element_type=jnp.float32
        )
        for kind in range(3):
            piece = part[:, kind * size : (kind + 1) * size]
            if kind < 2:
                piece = piece * cos_ref[...] + pltpu.roll(piece, size // 2, 1) * sin_ref[...]
            out_ref[head, kind] = piece


def normalise_project_kernel(
    place_ref, a_near, a_far, b_near, b_far, squares_ref, gain_ref, weight_hbm, cos_ref, sin_ref,
    out_ref, normed_ref, weight_buffer, semaphores,
):
    rows = a_near.shape[0]
    features = 2 * gain_ref.shape[0] * gain_ref.shape[2]
    core, near_row, head = place_ref[0], place_ref[1], place_ref[2]
    copies = weight_copies(head, 3 * cos_ref.shape[1], weight_hbm, weight_buffer, semaphores)
    for copy in copies:
        copy.start()
    for shards, half in (((a_near, a_far), core), ((b_near, b_far), 1 - core)):
        gain = gain_ref[half]
        for shard, row in zip(shards, (near_row, 1 - near_row)):
            at = pl.ds(pl.multiple_of(row * rows, 16), rows)
            factor = lax.rsqrt(squares_ref[at, :] / features + EPS)
            normed_ref[half, at, :] = (shard[...].astype(jnp.float32) * factor * gain).astype(
                jnp.bfloat16
            )
    project_heads(normed_ref, copies, weight_buffer, cos_ref, sin_ref, out_ref)


def project_kernel(
    place_ref, normed_ref, weight_hbm, cos_ref, sin_ref, out_ref, weight_buffer, semaphores
):
    copies = weight_copies(
        place_ref[0], 3 * cos_ref.shape[1], weight_hbm, weight_buffer, semaphores
    )
    for copy in copies:
        copy.start()
    project_heads(normed_ref, copies, weight_buffer, cos_ref, sin_ref, out_ref)


def attend_kernel(scale, query_ref, *refs):
    key_value_refs, (key_place_ref, place_ref, start_ref, out_ref) = refs[:-4], refs[-4:]
    key_places = key_place_ref[...]
    visible = (key_places <= place_ref[...]) & (key_places >= start_ref[...])
    keys = jnp.concatenate([ref[0] for ref in key_value_refs], axis=0)
    values = jnp.concatenate([ref[1] for ref in key_value_refs], axis=0)
    scores = (
        lax.dot_general(
            query_ref[...], keys, (((1,), (1,)), ((), ())), preferred_element_type=jnp.float32
        )
        * scale
    )
    masked = jnp.where(visible, scores, -1e30)
    top = jnp.max(masked, axis=1, keepdims=True)
    exponentials = jnp.where(visible, jnp.exp(masked - top), 0.0)
    total = jnp.sum(exponentials, axis=1, keepdims=True)
    summed = jnp.dot(
        exponentials.astype(jnp.bfloat16), values, preferred_element_type=jnp.float32
    )
    out_ref[...] = (summed / total).astype(jnp.bfloat16)


def attend_gathered(query, keys, values, places, starts, scale):
    heads, count, size = query.shape
    chunk = math.gcd(keys.shape[1], 1024)
    rounds = keys.shape[1] // chunk
    stacked = (
        keys.reshape(heads, rounds, chunk, size).transpose(1, 0, 2, 3),
        values.reshape(heads, rounds, chunk, size).transpose(1, 0, 2, 3),
        jnp.arange(rounds * chunk, dtype=jnp.int32).reshape(rounds, chunk),
    )

    def advance(state, blocks):
        running, totals, summed = state
        block_keys, block_values, key_places = blocks
        scores = (
            jnp.einsum("hqd,hkd->hqk", query, block_keys, preferred_element_type=jnp.float32) * scale
        )
        visible = (key_places[None, None, :] <= places[None, :, None]) & (
            key_places[None, None, :] >= starts[None, :, None]
        )
        masked = jnp.where(visible, scores, -jnp.inf)
        newest = jnp.maximum(running, jnp.max(masked, axis=2))
        factor = jnp.exp(running - newest)
        exponentials = jnp.where(visible, jnp.exp(masked - newest[:, :, None]), 0.0)
        totals = totals * factor + jnp.sum(exponentials, axis=2)
        summed = summed * factor[:, :, None] + jnp.einsum(
            "hqk,hkd->hqd", exponentials.astype(jnp.bfloat16), block_values,
            preferred_element_type=jnp.float32,
        )
        return (newest, totals, summed), None

    initial = (
        jnp.full((heads, count), -1e30, jnp.float32),
        jnp.zeros((heads, count), jnp.float32),
        jnp.zeros((heads, count, size), jnp.float32),
    )
    (running, totals, summed), unused = lax.scan(advance, initial, stacked)
    attended = (summed / totals[:, :, None]).astype(jnp.bfloat16)
    return attended.transpose(1, 0, 2).reshape(count, heads * size)


def in_vmem(count):
    return [pl.BlockSpec(memory_space=pltpu.VMEM)] * count


def per_device(activations, norm_gain, qkv_weight, doc_ids):
    rows, width = activations.shape
    span, local_heads, triple = qkv_weight.shape
    size = triple // 3
    pair = local_heads // 2
    block = 2 * rows
    toks = lax.axis_size("tok")
    tok, row, col = lax.axis_index("tok"), lax.axis_index("row"), lax.axis_index("col")
    chip, core = col >> 1, col & 1
    grid = [(r, c) for r in range(2) for c in range(4)]

    def by_col(value, flip):
        return lax.ppermute(value, "col", [(c, c ^ flip) for c in range(4)])

    def by_row(value):
        return lax.ppermute(value, "row", [(0, 1), (1, 0)])

    def ordered(index, own, other):
        first = index == 0
        return jnp.concatenate([jnp.where(first, own, other), jnp.where(first, other, own)])

    near = lax.ppermute(
        activations,
        ("row", "col"),
        [(r * 4 + c, (c // 2) * 4 + 2 * r + c % 2) for r, c in grid],
    )
    far = lax.ppermute(
        activations,
        ("row", "col"),
        [(r * 4 + c, (c // 2) * 4 + 2 * (1 - r) + c % 2) for r, c in grid],
    )
    widened = activations.astype(jnp.float32)
    squares = jnp.sum(widened * widened, axis=1)
    gain = norm_gain.astype(jnp.float32)
    message = jnp.concatenate([squares, gain])
    message, qkv_weight = lax.optimization_barrier((message, qkv_weight))
    flat_weight = qkv_weight.reshape(span, local_heads * triple)
    got = by_col(message, 1)
    squares = squares + got[:rows]
    gain = ordered(core, gain, got[rows:])
    docs = doc_ids.astype(jnp.float32)
    if toks == 4:
        for flip in (1, 2):
            other = lax.ppermute(docs, "tok", [(t, t ^ flip) for t in range(4)])
            docs = ordered(tok & flip, docs, other)
    got = by_col(jnp.concatenate([squares, gain]), 2)
    near, far, got, docs, flat_weight = lax.optimization_barrier(
        (near, far, got, docs, flat_weight)
    )
    near_other, far_other = by_col(near, 1), by_col(far, 1)
    squares = squares + got[:rows]
    gain = jnp.where(chip == row, gain, got[rows:]).reshape(2, 1, width)
    got = by_row(jnp.concatenate([squares, docs]))
    squares = ordered(row, squares, got[:rows]).reshape(block, 1)
    row_docs = [jnp.where(row == r, docs, got[rows:]).reshape(-1, rows) for r in range(2)]
    all_docs = jnp.stack(row_docs, axis=1).reshape(-1)
    if toks != 4:
        all_docs = lax.all_gather(all_docs, "tok", axis=0, tiled=True)
    block_docs = lax.dynamic_slice_in_dim(all_docs, tok * block, block, 0)
    starts = jnp.sum((all_docs[None, :] < block_docs[:, None]).astype(jnp.int32), axis=1)
    places = tok * block + jnp.arange(block, dtype=jnp.int32)
    cosine, sine = rotary_tables(places, size)

    def projection(kernel, heads, normalising):
        normed_shape = (jax.ShapeDtypeStruct((2, block, width), jnp.bfloat16),)
        return pl.pallas_call(
            kernel,
            out_shape=(jax.ShapeDtypeStruct((heads, 3, block, size), jnp.float32),)
            + (normed_shape if normalising else ()),
            in_specs=[pl.BlockSpec(memory_space=pltpu.SMEM)]
            + in_vmem(6 if normalising else 1)
            + [pl.BlockSpec(memory_space=pltpu.HBM)]
            + in_vmem(2),
            out_specs=tuple(in_vmem(2 if normalising else 1)),
            scratch_shapes=[
                pltpu.VMEM((span, heads * triple), jnp.bfloat16),
                pltpu.SemaphoreType.DMA((2,)),
            ],
            compiler_params=pltpu.CompilerParams(vmem_limit_bytes=24 * MIB),
            cost_estimate=pl.CostEstimate(flops=0, bytes_accessed=0, transcendentals=0),
        )

    away_head, own_head = (1 - row) * pair, row * pair
    away, normed = projection(normalise_project_kernel, 1, True)(
        jnp.stack([core, chip, away_head]), near, far, near_other, far_other, squares, gain,
        flat_weight, cosine, sine,
    )
    arrived = []
    for head in range(pair):
        if head > 0:
            (away,) = projection(project_kernel, 1, False)(
                (away_head + head).reshape(1), normed, flat_weight, cosine, sine
            )
        away, normed = lax.optimization_barrier((away.astype(jnp.float16), normed))
        arrived.append(by_row(away[0]))
    (own,) = projection(project_kernel, pair, False)(
        own_head.reshape(1), normed, flat_weight, cosine, sine
    )

    scale = 1.0 / math.sqrt(size)

    queries, key_values, received = [], [], []
    for head in range(pair):
        sums = arrived[head].astype(jnp.float32)
        if toks == 4 and head > 0:
            sums = jnp.where(tok < toks, sums, received[-1][0][0, 0, 0].astype(jnp.float32))
        queries.append((own[head, 0] + sums[0]).astype(jnp.bfloat16))
        key_values.append((own[head, 1:] + sums[1:]).astype(jnp.bfloat16))
        if toks == 4:
            received.append(
                [
                    lax.ppermute(key_values[head], "tok", [(t, t + s) for t in range(4 - s)])
                    for s in (1, 2, 3)
                ]
            )
    if toks == 4:
        key_places = jnp.concatenate(
            [(tok - s) * block + jnp.arange(block, dtype=jnp.int32) for s in range(4)]
        )
        attend = pl.pallas_call(
            lambda *refs: attend_kernel(scale, *refs),
            out_shape=jax.ShapeDtypeStruct((block, size), jnp.bfloat16),
            in_specs=in_vmem(8),
            out_specs=in_vmem(1)[0],
            compiler_params=pltpu.CompilerParams(vmem_limit_bytes=24 * MIB),
            cost_estimate=pl.CostEstimate(
                flops=4 * block * 4 * block * size,
                bytes_accessed=2 * MIB,
                transcendentals=block * 4 * block,
            ),
        )
        attended = [
            attend(
                queries[head], key_values[head], *received[head],
                key_places.reshape(1, 4 * block), places.reshape(block, 1), starts.reshape(block, 1),
            )
            for head in range(pair)
        ]
    else:
        everything = lax.all_gather(jnp.stack(key_values), "tok", axis=2, tiled=True)
        together = attend_gathered(
            jnp.stack(queries), everything[:, 0], everything[:, 1], places, starts, scale
        )
        attended = [together[:, head * size : (head + 1) * size] for head in range(pair)]

    mine, theirs = [], []
    for one in attended:
        mine.append(jnp.where(row == 0, one[:rows], one[rows:]))
        theirs.append(by_row(jnp.where(row == 0, one[rows:], one[:rows])))
    return jnp.concatenate(
        [jnp.where(row == 0, a, b) for a, b in zip(mine + theirs, theirs + mine)], axis=1
    )


def solution(mesh):
    placed = (P(("tok", "row"), "col"), P("col"), P("row", "col", None), P(("tok", "row")))
    return jax.shard_map(
        per_device, mesh=mesh, in_specs=placed, out_specs=P(("tok", "row"), "col"), check_vma=False
    )
```

```python
import math

import jax
import jax.numpy as jnp
from jax import lax
from jax.experimental import pallas as pl
from jax.experimental.pallas import tpu as pltpu
from jax.sharding import PartitionSpec as P

EPS = 1e-05
LOW = -1e30
EXTRA = 16
MIB = 1 << 20


def rotary_tables(places, head_size):
    half = head_size // 2
    spacing = jnp.arange(half).astype(jnp.float32) * (2.0 / head_size)
    inverse = jnp.power(10000.0, -spacing)
    angles = places.astype(jnp.float32)[:, None] * inverse[None, :]
    cosine, sine = jnp.cos(angles), jnp.sin(angles)
    return (
        jnp.concatenate([cosine, cosine], axis=1),
        jnp.concatenate([-sine, sine], axis=1),
    )


def weight_copies(first_head, triple, weight_hbm, weight_buffer, semaphores):
    depth = weight_buffer.shape[0] // 2
    columns = weight_buffer.shape[1]
    first = pl.multiple_of(first_head * triple, 128)
    return [
        pltpu.make_async_copy(
            weight_hbm.at[pl.ds(half * depth, depth), pl.ds(first, columns)],
            weight_buffer.at[pl.ds(half * depth, depth), :],
            semaphores.at[half],
        )
        for half in range(2)
    ]


def project_heads(normed_ref, copies, weight_buffer, cos_ref, sin_ref, doc_rows, out_ref):
    heads, size = out_ref.shape[0], out_ref.shape[2]
    block, extra = cos_ref.shape[0], doc_rows.shape[0]
    depth = weight_buffer.shape[0] // 2
    for copy in copies:
        copy.wait()
    for head in range(heads):
        columns = slice(head * 3 * size, (head + 1) * 3 * size)
        part = jnp.dot(
            normed_ref[0], weight_buffer[:depth, columns], preferred_element_type=jnp.float32
        ) + jnp.dot(
            normed_ref[1], weight_buffer[depth:, columns], preferred_element_type=jnp.float32
        )
        for kind, at in ((0, 2 * block + extra), (1, 0), (2, block)):
            piece = part[:, kind * size : (kind + 1) * size]
            if kind < 2:
                piece = piece * cos_ref[...] + pltpu.roll(piece, size // 2, 1) * sin_ref[...]
            out_ref[head, at : at + block, :] = piece
        for at in (2 * block, 3 * block + extra):
            out_ref[head, at : at + extra, :] = doc_rows


def normalise_project_kernel(
    place_ref, a_near, a_far, b_near, b_far, squares_ref, gain_ref, weight_hbm, cos_ref, sin_ref,
    out_ref, normed_ref, weight_buffer, semaphores,
):
    rows = a_near.shape[0]
    features = 2 * gain_ref.shape[0] * gain_ref.shape[2]
    core, near_row, head = place_ref[0], place_ref[1], place_ref[2]
    copies = weight_copies(head, 3 * cos_ref.shape[1], weight_hbm, weight_buffer, semaphores)
    for copy in copies:
        copy.start()
    for shards, half in (((a_near, a_far), core), ((b_near, b_far), 1 - core)):
        gain = gain_ref[half]
        for shard, row in zip(shards, (near_row, 1 - near_row)):
            at = pl.ds(pl.multiple_of(row * rows, 16), rows)
            factor = lax.rsqrt(squares_ref[at, :] / features + EPS)
            normed_ref[half, at, :] = (shard[...].astype(jnp.float32) * factor * gain).astype(
                jnp.bfloat16
            )
    nothing = jnp.zeros((EXTRA, out_ref.shape[2]), jnp.float32)
    project_heads(normed_ref, copies, weight_buffer, cos_ref, sin_ref, nothing, out_ref)


def project_kernel(
    place_ref, normed_ref, docs_ref, weight_hbm, cos_ref, sin_ref, out_ref, weight_buffer,
    semaphores,
):
    copies = weight_copies(
        place_ref[0], 3 * cos_ref.shape[1], weight_hbm, weight_buffer, semaphores
    )
    for copy in copies:
        copy.start()
    project_heads(normed_ref, copies, weight_buffer, cos_ref, sin_ref, docs_ref[...], out_ref)


def as_column(rows, count):
    lanes = rows.shape[1]
    pieces = []
    for begin in range(0, count, lanes):
        held = min(lanes, count - begin)
        at = lax.broadcasted_iota(jnp.int32, (held, lanes), 0)
        diagonal = at == lax.broadcasted_iota(jnp.int32, (held, lanes), 1)
        row = rows[begin // lanes : begin // lanes + 1, :]
        pieces.append(jnp.sum(jnp.where(diagonal, row, 0.0), axis=1, keepdims=True))
    return jnp.concatenate(pieces, axis=0)


def as_rows(column, lanes):
    count = column.shape[0]
    rows = []
    for begin in range(0, count, lanes):
        held = min(lanes, count - begin)
        at = lax.broadcasted_iota(jnp.int32, (held, lanes), 0)
        diagonal = at == lax.broadcasted_iota(jnp.int32, (held, lanes), 1)
        rows.append(
            jnp.sum(jnp.where(diagonal, column[begin : begin + held], 0.0), axis=0, keepdims=True)
        )
    return rows


def as_lanes(rows, count):
    lanes = rows.shape[1]
    return jnp.concatenate(
        [
            rows[begin // lanes : begin // lanes + 1, : min(lanes, count - begin)]
            for begin in range(0, count, lanes)
        ],
        axis=1,
    )


def softmax_part(scale, query, query_docs, messages, causal):
    block = (messages[0].shape[0] - EXTRA) // 2
    keys = jnp.concatenate([message[:block] for message in messages], axis=0)
    values = jnp.concatenate([message[block : 2 * block] for message in messages], axis=0)
    key_docs = jnp.concatenate(
        [as_lanes(message[2 * block :].astype(jnp.float32), block) for message in messages], axis=1
    )
    visible = query_docs == key_docs
    if causal:
        shape = (query.shape[0], keys.shape[0])
        query_places = lax.broadcasted_iota(jnp.int32, shape, 0)
        key_places = lax.broadcasted_iota(jnp.int32, shape, 1)
        visible &= (key_places <= query_places) | (key_places >= block)
    scores = (
        lax.dot_general(query, keys, (((1,), (1,)), ((), ())), preferred_element_type=jnp.float32)
        * scale
    )
    top = jnp.max(jnp.where(visible, scores, LOW), axis=1, keepdims=True)
    exponentials = jnp.where(visible, jnp.exp(scores - top), 0.0)
    total = jnp.sum(exponentials, axis=1, keepdims=True)
    summed = jnp.dot(exponentials.astype(jnp.bfloat16), values, preferred_element_type=jnp.float32)
    some = total > 0.0
    safe = jnp.where(some, total, 1.0)
    return summed / safe, jnp.where(some, top + jnp.log(safe), LOW)


def guest_kernel(
    scale, tok_ref, query_one, query_two, up_first, up_second, down_first, down_second, out_ref
):
    block = query_one.shape[0] - EXTRA
    size = query_one.shape[1]
    at_two = tok_ref[0] == 2
    messages = [
        jnp.where(at_two, up_first[...], down_first[...]),
        jnp.where(at_two, up_second[...], down_second[...]),
    ]
    for index, query_ref in enumerate((query_one, query_two)):
        docs = as_column(query_ref[block:, :].astype(jnp.float32), block)
        output, logs = softmax_part(scale, query_ref[:block, :], docs, messages, False)
        out_ref[index, :block, :] = output.astype(jnp.bfloat16)
        high = logs.astype(jnp.bfloat16).astype(jnp.float32)
        middle = (logs - high).astype(jnp.bfloat16).astype(jnp.float32)
        rows = as_rows(high, size) + as_rows(middle, size) + as_rows(logs - high - middle, size)
        rows.append(jnp.zeros((EXTRA - len(rows), size), jnp.float32))
        out_ref[index, block:, :] = jnp.concatenate(rows, axis=0).astype(jnp.bfloat16)


def own_kernel(
    scale, query_a, own_a, one_up_a, two_up_a, query_b, own_b, one_up_b, unused, out_ref, logs_ref
):
    block = query_a.shape[0] - EXTRA
    for index, (query_ref, refs) in enumerate(
        ((query_a, (own_a, one_up_a, two_up_a)), (query_b, (own_b, one_up_b)))
    ):
        docs = as_column(query_ref[block:, :].astype(jnp.float32), block)
        output, logs = softmax_part(
            scale, query_ref[:block, :], docs, [ref[...] for ref in refs], True
        )
        out_ref[index] = output
        logs_ref[index] = logs


def merge_kernel(place_ref, out_ref, logs_ref, one_ref, two_ref, mine_ref, theirs_ref):
    block, size = out_ref.shape[1:]
    groups = pl.cdiv(block, size)
    tok, row = place_ref[0], place_ref[1]
    rows = block // 2
    at_two, at_three = tok == 2, tok == 3

    def joined(index, message, present):
        logs = logs_ref[index]
        tile = message[block:].astype(jnp.float32)
        guest = sum(as_column(tile[k * groups : (k + 1) * groups], block) for k in range(3))
        guest = jnp.where(present, guest, LOW)
        top = jnp.maximum(logs, guest)
        weight, guest_weight = jnp.exp(logs - top), jnp.exp(guest - top)
        output = out_ref[index] * weight + message[:block].astype(jnp.float32) * guest_weight
        return (output / (weight + guest_weight)).astype(jnp.bfloat16)

    first = joined(0, one_ref[...], at_three)
    second = joined(1, jnp.where(at_two, one_ref[...], two_ref[...]), at_two | at_three)
    for index, output in enumerate((first, second)):
        columns = slice(index * size, (index + 1) * size)
        mine_ref[:, columns] = jnp.where(row == 0, output[:rows], output[rows:])
        theirs_ref[:, columns] = jnp.where(row == 0, output[rows:], output[:rows])


def attend_gathered(query, keys, values, places, starts, scale):
    heads, count, size = query.shape
    chunk = math.gcd(keys.shape[1], 1024)
    rounds = keys.shape[1] // chunk
    stacked = (
        keys.reshape(heads, rounds, chunk, size).transpose(1, 0, 2, 3),
        values.reshape(heads, rounds, chunk, size).transpose(1, 0, 2, 3),
        jnp.arange(rounds * chunk, dtype=jnp.int32).reshape(rounds, chunk),
    )

    def advance(state, blocks):
        running, totals, summed = state
        block_keys, block_values, key_places = blocks
        scores = (
            jnp.einsum("hqd,hkd->hqk", query, block_keys, preferred_element_type=jnp.float32) * scale
        )
        visible = (key_places[None, None, :] <= places[None, :, None]) & (
            key_places[None, None, :] >= starts[None, :, None]
        )
        masked = jnp.where(visible, scores, -jnp.inf)
        newest = jnp.maximum(running, jnp.max(masked, axis=2))
        factor = jnp.exp(running - newest)
        exponentials = jnp.where(visible, jnp.exp(masked - newest[:, :, None]), 0.0)
        totals = totals * factor + jnp.sum(exponentials, axis=2)
        summed = summed * factor[:, :, None] + jnp.einsum(
            "hqk,hkd->hqd", exponentials.astype(jnp.bfloat16), block_values,
            preferred_element_type=jnp.float32,
        )
        return (newest, totals, summed), None

    initial = (
        jnp.full((heads, count), -1e30, jnp.float32),
        jnp.zeros((heads, count), jnp.float32),
        jnp.zeros((heads, count, size), jnp.float32),
    )
    (running, totals, summed), unused = lax.scan(advance, initial, stacked)
    attended = (summed / totals[:, :, None]).astype(jnp.bfloat16)
    return attended.transpose(1, 0, 2).reshape(count, heads * size)


def in_vmem(count):
    return [pl.BlockSpec(memory_space=pltpu.VMEM)] * count


def per_device(activations, norm_gain, qkv_weight, doc_ids):
    rows, width = activations.shape
    span, local_heads, triple = qkv_weight.shape
    size = triple // 3
    pair = local_heads // 2
    block = 2 * rows
    toks = lax.axis_size("tok")
    tok, row, col = lax.axis_index("tok"), lax.axis_index("row"), lax.axis_index("col")
    chip, core = col >> 1, col & 1
    grid = [(r, c) for r in range(2) for c in range(4)]

    def by_col(value, flip):
        return lax.ppermute(value, "col", [(c, c ^ flip) for c in range(4)])

    def by_row(value):
        return lax.ppermute(value, "row", [(0, 1), (1, 0)])

    def ordered(index, own, other):
        first = index == 0
        return jnp.concatenate([jnp.where(first, own, other), jnp.where(first, other, own)])

    near = lax.ppermute(
        activations,
        ("row", "col"),
        [(r * 4 + c, (c // 2) * 4 + 2 * r + c % 2) for r, c in grid],
    )
    far = lax.ppermute(
        activations,
        ("row", "col"),
        [(r * 4 + c, (c // 2) * 4 + 2 * (1 - r) + c % 2) for r, c in grid],
    )
    widened = activations.astype(jnp.float32)
    squares = jnp.sum(widened * widened, axis=1)
    gain = norm_gain.astype(jnp.float32)
    message = jnp.concatenate([squares, gain])
    message, qkv_weight = lax.optimization_barrier((message, qkv_weight))
    flat_weight = qkv_weight.reshape(span, local_heads * triple)
    got = by_col(message, 1)
    squares = squares + got[:rows]
    gain = ordered(core, gain, got[rows:])
    got = by_col(jnp.concatenate([squares, gain]), 2)
    near, far, got, flat_weight = lax.optimization_barrier((near, far, got, flat_weight))
    near_other, far_other = by_col(near, 1), by_col(far, 1)
    squares = squares + got[:rows]
    gain = jnp.where(chip == row, gain, got[rows:]).reshape(2, 1, width)
    codes = doc_ids.astype(jnp.float32) + 1.0
    got = by_row(jnp.concatenate([squares, codes]))
    squares = ordered(row, squares, got[:rows]).reshape(block, 1)
    codes = ordered(row, codes, got[rows:])
    doc_rows = jnp.pad(codes, (0, EXTRA * size - block)).reshape(EXTRA, size)
    places = tok * block + jnp.arange(block, dtype=jnp.int32)
    cosine, sine = rotary_tables(places, size)

    taller = 3 * block + 2 * EXTRA
    break_at = 2 * block + EXTRA

    def projection(kernel, heads, normalising):
        normed_shape = (jax.ShapeDtypeStruct((2, block, width), jnp.bfloat16),)
        return pl.pallas_call(
            kernel,
            out_shape=(jax.ShapeDtypeStruct((heads, taller, size), jnp.float32),)
            + (normed_shape if normalising else ()),
            in_specs=[pl.BlockSpec(memory_space=pltpu.SMEM)]
            + in_vmem(6 if normalising else 2)
            + [pl.BlockSpec(memory_space=pltpu.HBM)]
            + in_vmem(2),
            out_specs=tuple(in_vmem(2 if normalising else 1)),
            scratch_shapes=[
                pltpu.VMEM((span, heads * triple), jnp.bfloat16),
                pltpu.SemaphoreType.DMA((2,)),
            ],
            compiler_params=pltpu.CompilerParams(vmem_limit_bytes=12 * MIB),
            cost_estimate=pl.CostEstimate(flops=0, bytes_accessed=0, transcendentals=0),
        )

    away_head, own_head = (1 - row) * pair, row * pair
    away, normed = projection(normalise_project_kernel, 1, True)(
        jnp.stack([core, chip, away_head]), near, far, near_other, far_other, squares, gain,
        flat_weight, cosine, sine,
    )
    arrived = []
    for head in range(pair):
        if head > 0:
            (away,) = projection(project_kernel, 1, False)(
                (away_head + head).reshape(1), normed, jnp.zeros_like(doc_rows), flat_weight,
                cosine, sine,
            )
        away, normed = lax.optimization_barrier((away.astype(jnp.float16), normed))
        arrived.append(by_row(away[0]))
    (own,) = projection(project_kernel, pair, False)(
        own_head.reshape(1), normed, doc_rows, flat_weight, cosine, sine
    )
    scale = 1.0 / math.sqrt(size)

    def along_tok(value, pairs):
        return lax.ppermute(value, "tok", pairs)

    def summed(head, begin, end):
        return own[head, begin:end] + arrived[head][begin:end].astype(jnp.float32)

    if toks == 4 and pair == 2:
        keys_a = summed(0, 0, break_at).astype(jnp.bfloat16)
        query_a = summed(0, break_at, taller).astype(jnp.bfloat16)
        one_up_a = along_tok(keys_a, [(0, 1), (1, 2), (2, 3)])
        two_up_a = along_tok(keys_a, [(0, 2)])
        keys_b = jnp.where(
            tok < toks, summed(1, 0, break_at), one_up_a.astype(jnp.float32)
        ).astype(jnp.bfloat16)
        query_b = summed(1, break_at, taller).astype(jnp.bfloat16)
        guest_one = along_tok(jnp.where(tok == 3, query_a, query_b), [(2, 1), (3, 2)])
        guest_two = along_tok(query_b, [(3, 1)])
        one_up_b = along_tok(keys_b, [(0, 1), (2, 3)])
        guests = pl.pallas_call(
            lambda *refs: guest_kernel(scale, *refs),
            out_shape=jax.ShapeDtypeStruct((2, block + EXTRA, size), jnp.bfloat16),
            in_specs=[pl.BlockSpec(memory_space=pltpu.SMEM)] + in_vmem(6),
            out_specs=in_vmem(1)[0],
            compiler_params=pltpu.CompilerParams(vmem_limit_bytes=16 * MIB),
        )(tok.reshape(1), guest_one, guest_two, two_up_a, one_up_a, one_up_b, keys_b)
        from_one = along_tok(guests[0], [(1, 2), (2, 3)])
        from_two = along_tok(guests[1], [(1, 3)])
        output, logs = pl.pallas_call(
            lambda *refs: own_kernel(scale, *refs),
            out_shape=(
                jax.ShapeDtypeStruct((2, block, size), jnp.float32),
                jax.ShapeDtypeStruct((2, block, 1), jnp.float32),
            ),
            in_specs=in_vmem(7) + [pl.BlockSpec(memory_space=pl.ANY)],
            out_specs=tuple(in_vmem(2)),
            compiler_params=pltpu.CompilerParams(vmem_limit_bytes=16 * MIB),
            cost_estimate=pl.CostEstimate(flops=0, bytes_accessed=0, transcendentals=0),
        )(query_a, keys_a, one_up_a, two_up_a, query_b, keys_b, one_up_b, guests)
        half_shape = jax.ShapeDtypeStruct((rows, 2 * size), jnp.bfloat16)
        mine, theirs = pl.pallas_call(
            merge_kernel,
            out_shape=(half_shape, half_shape),
            in_specs=[pl.BlockSpec(memory_space=pltpu.SMEM)] + in_vmem(4),
            out_specs=tuple(in_vmem(2)),
            compiler_params=pltpu.CompilerParams(vmem_limit_bytes=16 * MIB),
        )(jnp.stack([tok, row]), output, logs, from_one, from_two)
    else:
        sums = jnp.stack([summed(head, 0, taller) for head in range(pair)]).astype(jnp.bfloat16)
        everything = lax.all_gather(sums[:, : 2 * block], "tok", axis=0, tiled=False)
        everything = everything.transpose(1, 0, 2, 3)
        all_codes = lax.all_gather(codes, "tok", axis=0, tiled=True)
        starts = jnp.sum((all_codes[None, :] < codes[:, None]).astype(jnp.int32), axis=1)
        together = attend_gathered(
            sums[:, break_at : break_at + block],
            everything[:, :, :block].reshape(pair, toks * block, size),
            everything[:, :, block:].reshape(pair, toks * block, size),
            places, starts, scale,
        )
        mine = jnp.where(row == 0, together[:rows], together[rows:])
        theirs = jnp.where(row == 0, together[rows:], together[:rows])

    theirs = by_row(theirs)
    return jnp.concatenate(
        [jnp.where(row == 0, mine, theirs), jnp.where(row == 0, theirs, mine)], axis=1
    )


def solution(mesh):
    placed = (P(("tok", "row"), "col"), P("col"), P("row", "col", None), P(("tok", "row")))
    return jax.shard_map(
        per_device, mesh=mesh, in_specs=placed, out_specs=P(("tok", "row"), "col"), check_vma=False
    )
```

```python
import math

import jax
import jax.numpy as jnp
from jax import lax
from jax.experimental import pallas as pl
from jax.experimental.pallas import tpu as pltpu
from jax.sharding import PartitionSpec as P

EPS = 1e-05
LOW = -1e30
EXTRA = 16
MIB = 1 << 20


def rotary_tables(places, head_size):
    half = head_size // 2
    spacing = jnp.arange(half).astype(jnp.float32) * (2.0 / head_size)
    inverse = jnp.power(10000.0, -spacing)
    angles = places.astype(jnp.float32)[:, None] * inverse[None, :]
    cosine, sine = jnp.cos(angles), jnp.sin(angles)
    return (
        jnp.concatenate([cosine, cosine], axis=1),
        jnp.concatenate([-sine, sine], axis=1),
    )


def weight_copies(first_head, triple, weight_hbm, weight_buffer, semaphores):
    depth = weight_buffer.shape[0] // 2
    columns = weight_buffer.shape[1]
    first = pl.multiple_of(first_head * triple, 128)
    return [
        pltpu.make_async_copy(
            weight_hbm.at[pl.ds(half * depth, depth), pl.ds(first, columns)],
            weight_buffer.at[pl.ds(half * depth, depth), :],
            semaphores.at[half],
        )
        for half in range(2)
    ]


def project_heads(normed_ref, copies, weight_buffer, cos_ref, sin_ref, doc_rows, out_ref):
    heads, size = out_ref.shape[0], out_ref.shape[2]
    block, extra = cos_ref.shape[0], doc_rows.shape[0]
    depth = weight_buffer.shape[0] // 2
    for copy in copies:
        copy.wait()
    for head in range(heads):
        columns = slice(head * 3 * size, (head + 1) * 3 * size)
        part = jnp.dot(
            normed_ref[0], weight_buffer[:depth, columns], preferred_element_type=jnp.float32
        ) + jnp.dot(
            normed_ref[1], weight_buffer[depth:, columns], preferred_element_type=jnp.float32
        )
        for kind, at in ((0, 2 * block + extra), (1, 0), (2, block)):
            piece = part[:, kind * size : (kind + 1) * size]
            if kind < 2:
                piece = piece * cos_ref[...] + pltpu.roll(piece, size // 2, 1) * sin_ref[...]
            out_ref[head, at : at + block, :] = piece
        for at in (2 * block, 3 * block + extra):
            out_ref[head, at : at + extra, :] = doc_rows


def normalise_project_kernel(
    place_ref, a_near, a_far, b_near, b_far, squares_ref, gain_ref, weight_hbm, cos_ref, sin_ref,
    out_ref, normed_ref, weight_buffer, semaphores,
):
    rows = a_near.shape[0]
    features = 2 * gain_ref.shape[0] * gain_ref.shape[2]
    core, near_row, head = place_ref[0], place_ref[1], place_ref[2]
    copies = weight_copies(head, 3 * cos_ref.shape[1], weight_hbm, weight_buffer, semaphores)
    for copy in copies:
        copy.start()
    for shards, half in (((a_near, a_far), core), ((b_near, b_far), 1 - core)):
        gain = gain_ref[half]
        for shard, row in zip(shards, (near_row, 1 - near_row)):
            at = pl.ds(pl.multiple_of(row * rows, 16), rows)
            factor = lax.rsqrt(squares_ref[at, :] / features + EPS)
            normed_ref[half, at, :] = (shard[...].astype(jnp.float32) * factor * gain).astype(
                jnp.bfloat16
            )
    nothing = jnp.zeros((EXTRA, out_ref.shape[2]), jnp.float32)
    project_heads(normed_ref, copies, weight_buffer, cos_ref, sin_ref, nothing, out_ref)


def project_kernel(
    place_ref, normed_ref, docs_ref, weight_hbm, cos_ref, sin_ref, out_ref, weight_buffer,
    semaphores,
):
    copies = weight_copies(
        place_ref[0], 3 * cos_ref.shape[1], weight_hbm, weight_buffer, semaphores
    )
    for copy in copies:
        copy.start()
    project_heads(normed_ref, copies, weight_buffer, cos_ref, sin_ref, docs_ref[...], out_ref)


def as_column(rows, count):
    lanes = rows.shape[1]
    pieces = []
    for begin in range(0, count, lanes):
        held = min(lanes, count - begin)
        at = lax.broadcasted_iota(jnp.int32, (held, lanes), 0)
        diagonal = at == lax.broadcasted_iota(jnp.int32, (held, lanes), 1)
        row = rows[begin // lanes : begin // lanes + 1, :]
        pieces.append(jnp.sum(jnp.where(diagonal, row, 0.0), axis=1, keepdims=True))
    return jnp.concatenate(pieces, axis=0)


def as_rows(column, lanes):
    count = column.shape[0]
    rows = []
    for begin in range(0, count, lanes):
        held = min(lanes, count - begin)
        at = lax.broadcasted_iota(jnp.int32, (held, lanes), 0)
        diagonal = at == lax.broadcasted_iota(jnp.int32, (held, lanes), 1)
        rows.append(
            jnp.sum(jnp.where(diagonal, column[begin : begin + held], 0.0), axis=0, keepdims=True)
        )
    return rows


def as_lanes(rows, count):
    lanes = rows.shape[1]
    return jnp.concatenate(
        [
            rows[begin // lanes : begin // lanes + 1, : min(lanes, count - begin)]
            for begin in range(0, count, lanes)
        ],
        axis=1,
    )


def softmax_part(scale, query, query_docs, messages, causal):
    block = (messages[0].shape[0] - EXTRA) // 2
    keys = jnp.concatenate([message[:block] for message in messages], axis=0)
    values = jnp.concatenate([message[block : 2 * block] for message in messages], axis=0)
    key_docs = jnp.concatenate(
        [as_lanes(message[2 * block :].astype(jnp.float32), block) for message in messages], axis=1
    )
    visible = query_docs == key_docs
    if causal:
        shape = (query.shape[0], keys.shape[0])
        query_places = lax.broadcasted_iota(jnp.int32, shape, 0)
        key_places = lax.broadcasted_iota(jnp.int32, shape, 1)
        visible &= (key_places <= query_places) | (key_places >= block)
    scores = (
        lax.dot_general(query, keys, (((1,), (1,)), ((), ())), preferred_element_type=jnp.float32)
        * scale
    )
    top = jnp.max(jnp.where(visible, scores, LOW), axis=1, keepdims=True)
    exponentials = jnp.where(visible, jnp.exp(scores - top), 0.0)
    total = jnp.sum(exponentials, axis=1, keepdims=True)
    summed = jnp.dot(exponentials.astype(jnp.bfloat16), values, preferred_element_type=jnp.float32)
    some = total > 0.0
    safe = jnp.where(some, total, 1.0)
    return summed / safe, jnp.where(some, top + jnp.log(safe), LOW)


def as_message(output, logs, size):
    high = logs.astype(jnp.bfloat16).astype(jnp.float32)
    middle = (logs - high).astype(jnp.bfloat16).astype(jnp.float32)
    rows = as_rows(high, size) + as_rows(middle, size) + as_rows(logs - high - middle, size)
    rows.append(jnp.zeros((EXTRA - len(rows), size), jnp.float32))
    return jnp.concatenate([output] + rows, axis=0).astype(jnp.bfloat16)


def parted(row, value):
    rows = value.shape[0] // 2
    first = row == 0
    return (
        jnp.where(first, value[:rows], value[rows:]),
        jnp.where(first, value[rows:], value[:rows]),
    )


def guest_kernel(scale, here, place_ref, *refs):
    count = len(refs) - 3
    query_refs, message_refs, out_ref = refs[:count], refs[count:-1], refs[-1]

    @pl.when(place_ref[0] == here)
    def attend():
        messages = [ref[...] for ref in message_refs]
        for index, query_ref in enumerate(query_refs):
            block, size = query_ref.shape[0] - EXTRA, query_ref.shape[1]
            docs = as_column(query_ref[block:, :].astype(jnp.float32), block)
            output, logs = softmax_part(scale, query_ref[:block, :], docs, messages, False)
            for owner, (a, b) in enumerate(
                zip(parted(place_ref[1], output), parted(place_ref[1], logs))
            ):
                out_ref[index, owner] = as_message(a, b, size)


def own_kernel(
    scale, place_ref, query_down, own_down, one_down, query_up, own_up, one_up, two_up, unused_ref,
    mine_ref, logs_ref, theirs_ref,
):
    block, size = query_down.shape[0] - EXTRA, query_down.shape[1]
    for index, (query_ref, refs) in enumerate(
        ((query_down, (own_down, one_down)), (query_up, (own_up, one_up, two_up)))
    ):
        docs = as_column(query_ref[block:, :].astype(jnp.float32), block)
        output, logs = softmax_part(
            scale, query_ref[:block, :], docs, [ref[...] for ref in refs], True
        )
        mine, theirs = parted(place_ref[1], output)
        my_logs, their_logs = parted(place_ref[1], logs)
        mine_ref[index] = mine
        logs_ref[index] = my_logs
        theirs_ref[index] = as_message(theirs, their_logs, size)


def merge_kernel(
    place_ref, mine_ref, logs_ref, partner_ref, two_same, two_cross, three_same, three_cross,
    up_same, up_cross, out_ref,
):
    rows, size = mine_ref.shape[1:]
    groups = pl.cdiv(rows, size)
    tok, row = place_ref[0], place_ref[1]

    def logs_of(message):
        tile = message[rows:].astype(jnp.float32)
        return sum(as_column(tile[k * groups : (k + 1) * groups], rows) for k in range(3))

    def joined(output, logs, message, present):
        guest = jnp.where(present, logs_of(message), LOW)
        top = jnp.maximum(logs, guest)
        weight, guest_weight = jnp.exp(logs - top), jnp.exp(guest - top)
        total = output * weight + message[:rows].astype(jnp.float32) * guest_weight
        return (total / (weight + guest_weight)).astype(jnp.bfloat16)

    at_two, at_three = tok == 2, tok == 3
    for mine, two, three, up in (
        (True, two_same, three_same, up_same),
        (False, two_cross, three_cross, up_cross),
    ):
        begin = jnp.where(row == 0, 0, 1) if mine else jnp.where(row == 0, 1, 0)
        down = jnp.where(at_two, two[...], three[...])
        for index, (message, present) in enumerate(
            ((down, at_two | at_three), (up[...], at_three))
        ):
            if mine:
                output, logs = mine_ref[index], logs_ref[index]
            else:
                partner = partner_ref[index]
                output, logs = partner[:rows].astype(jnp.float32), logs_of(partner)
            at = pl.ds(pl.multiple_of((2 * begin + index) * size, size), size)
            out_ref[:, at] = joined(output, logs, message, present)


def attend_gathered(query, keys, values, places, starts, scale):
    heads, count, size = query.shape
    chunk = math.gcd(keys.shape[1], 1024)
    rounds = keys.shape[1] // chunk
    stacked = (
        keys.reshape(heads, rounds, chunk, size).transpose(1, 0, 2, 3),
        values.reshape(heads, rounds, chunk, size).transpose(1, 0, 2, 3),
        jnp.arange(rounds * chunk, dtype=jnp.int32).reshape(rounds, chunk),
    )

    def advance(state, blocks):
        running, totals, summed = state
        block_keys, block_values, key_places = blocks
        scores = (
            jnp.einsum("hqd,hkd->hqk", query, block_keys, preferred_element_type=jnp.float32) * scale
        )
        visible = (key_places[None, None, :] <= places[None, :, None]) & (
            key_places[None, None, :] >= starts[None, :, None]
        )
        masked = jnp.where(visible, scores, -jnp.inf)
        newest = jnp.maximum(running, jnp.max(masked, axis=2))
        factor = jnp.exp(running - newest)
        exponentials = jnp.where(visible, jnp.exp(masked - newest[:, :, None]), 0.0)
        totals = totals * factor + jnp.sum(exponentials, axis=2)
        summed = summed * factor[:, :, None] + jnp.einsum(
            "hqk,hkd->hqd", exponentials.astype(jnp.bfloat16), block_values,
            preferred_element_type=jnp.float32,
        )
        return (newest, totals, summed), None

    initial = (
        jnp.full((heads, count), -1e30, jnp.float32),
        jnp.zeros((heads, count), jnp.float32),
        jnp.zeros((heads, count, size), jnp.float32),
    )
    (running, totals, summed), unused = lax.scan(advance, initial, stacked)
    attended = (summed / totals[:, :, None]).astype(jnp.bfloat16)
    return attended.transpose(1, 0, 2).reshape(count, heads * size)


def in_vmem(count):
    return [pl.BlockSpec(memory_space=pltpu.VMEM)] * count


def per_device(activations, norm_gain, qkv_weight, doc_ids):
    rows, width = activations.shape
    span, local_heads, triple = qkv_weight.shape
    size = triple // 3
    pair = local_heads // 2
    block = 2 * rows
    toks = lax.axis_size("tok")
    tok, row, col = lax.axis_index("tok"), lax.axis_index("row"), lax.axis_index("col")
    chip, core = col >> 1, col & 1
    grid = [(r, c) for r in range(2) for c in range(4)]

    def by_col(value, flip):
        return lax.ppermute(value, "col", [(c, c ^ flip) for c in range(4)])

    def by_row(value):
        return lax.ppermute(value, "row", [(0, 1), (1, 0)])

    def ordered(index, own, other):
        first = index == 0
        return jnp.concatenate([jnp.where(first, own, other), jnp.where(first, other, own)])

    near = lax.ppermute(
        activations,
        ("row", "col"),
        [(r * 4 + c, (c // 2) * 4 + 2 * r + c % 2) for r, c in grid],
    )
    far = lax.ppermute(
        activations,
        ("row", "col"),
        [(r * 4 + c, (c // 2) * 4 + 2 * (1 - r) + c % 2) for r, c in grid],
    )
    widened = activations.astype(jnp.float32)
    squares = jnp.sum(widened * widened, axis=1)
    gain = norm_gain.astype(jnp.float32)
    message = jnp.concatenate([squares, gain])
    message, qkv_weight = lax.optimization_barrier((message, qkv_weight))
    flat_weight = qkv_weight.reshape(span, local_heads * triple)
    got = by_col(message, 1)
    squares = squares + got[:rows]
    gain = ordered(core, gain, got[rows:])
    got = by_col(jnp.concatenate([squares, gain]), 2)
    near, far, got, flat_weight = lax.optimization_barrier((near, far, got, flat_weight))
    near_other, far_other = by_col(near, 1), by_col(far, 1)
    squares = squares + got[:rows]
    gain = jnp.where(chip == row, gain, got[rows:]).reshape(2, 1, width)
    codes = doc_ids.astype(jnp.float32) + 1.0
    got = by_row(jnp.concatenate([squares, codes]))
    squares = ordered(row, squares, got[:rows]).reshape(block, 1)
    codes = ordered(row, codes, got[rows:])
    doc_rows = jnp.pad(codes, (0, EXTRA * size - block)).reshape(EXTRA, size)
    places = tok * block + jnp.arange(block, dtype=jnp.int32)
    cosine, sine = rotary_tables(places, size)

    taller = 3 * block + 2 * EXTRA
    break_at = 2 * block + EXTRA

    def projection(kernel, heads, normalising):
        normed_shape = (jax.ShapeDtypeStruct((2, block, width), jnp.bfloat16),)
        return pl.pallas_call(
            kernel,
            out_shape=(jax.ShapeDtypeStruct((heads, taller, size), jnp.float32),)
            + (normed_shape if normalising else ()),
            in_specs=[pl.BlockSpec(memory_space=pltpu.SMEM)]
            + in_vmem(6 if normalising else 2)
            + [pl.BlockSpec(memory_space=pltpu.HBM)]
            + in_vmem(2),
            out_specs=tuple(in_vmem(2 if normalising else 1)),
            scratch_shapes=[
                pltpu.VMEM((span, heads * triple), jnp.bfloat16),
                pltpu.SemaphoreType.DMA((2,)),
            ],
            compiler_params=pltpu.CompilerParams(vmem_limit_bytes=12 * MIB),
            cost_estimate=pl.CostEstimate(flops=0, bytes_accessed=0, transcendentals=0),
        )

    away_head, own_head = (1 - row) * pair, row * pair
    away, normed = projection(normalise_project_kernel, 1, True)(
        jnp.stack([core, chip, away_head]), near, far, near_other, far_other, squares, gain,
        flat_weight, cosine, sine,
    )
    arrived = []
    for head in range(pair):
        if head > 0:
            (away,) = projection(project_kernel, 1, False)(
                (away_head + head).reshape(1), normed, jnp.zeros_like(doc_rows), flat_weight,
                cosine, sine,
            )
        away, normed = lax.optimization_barrier((away.astype(jnp.float16), normed))
        arrived.append(by_row(away[0]))
    (own,) = projection(project_kernel, pair, False)(
        own_head.reshape(1), normed, doc_rows, flat_weight, cosine, sine
    )
    scale = 1.0 / math.sqrt(size)

    def along_tok(value, pairs):
        return lax.ppermute(value, "tok", pairs)

    def summed(head, begin, end):
        return own[head, begin:end] + arrived[head][begin:end].astype(jnp.float32)

    if toks == 4 and pair == 2:
        places = jnp.stack([tok, row])

        def returned(value, pairs):
            across = [(2 * a + r, 2 * b + 1 - r) for a, b in pairs for r in range(2)]
            return along_tok(value[0], pairs), lax.ppermute(value[1], ("tok", "row"), across)

        def guests(here, queries, messages):
            shape = (len(queries), 2, rows + EXTRA, size)
            return pl.pallas_call(
                lambda *refs: guest_kernel(scale, here, *refs),
                out_shape=jax.ShapeDtypeStruct(shape, jnp.bfloat16),
                in_specs=[pl.BlockSpec(memory_space=pltpu.SMEM)] + in_vmem(len(queries) + 2),
                out_specs=in_vmem(1)[0],
                compiler_params=pltpu.CompilerParams(vmem_limit_bytes=16 * MIB),
            )(places, *queries, *messages)

        query_down = summed(0, break_at, taller).astype(jnp.bfloat16)
        keys_down = summed(0, 0, break_at).astype(jnp.bfloat16)
        from_three = along_tok(query_down, [(3, 1)])
        from_two = along_tok(query_down, [(2, 1)])
        one_down = along_tok(keys_down, [(0, 1), (2, 3)])

        arrived[1] = jnp.where(
            tok < toks,
            arrived[1].astype(jnp.float32),
            jnp.broadcast_to(from_two[:1].astype(jnp.float32), arrived[1].shape),
        )
        keys_up = summed(1, 0, break_at).astype(jnp.bfloat16)
        query_up = summed(1, break_at, taller).astype(jnp.bfloat16)
        two_up = along_tok(keys_up, [(0, 2)])
        three_up = along_tok(query_up, [(3, 2)])
        one_up = along_tok(keys_up, [(0, 1), (1, 2), (2, 3)])

        down = guests(1, [from_two, from_three], [one_down, keys_down])
        three_same, three_cross = returned(down[1], [(1, 3)])
        two_same, two_cross = returned(down[0], [(1, 2)])
        up = guests(2, [three_up], [two_up, one_up])
        up_same, up_cross = returned(up[0], [(2, 3)])

        mine, logs, theirs = pl.pallas_call(
            lambda *refs: own_kernel(scale, *refs),
            out_shape=(
                jax.ShapeDtypeStruct((2, rows, size), jnp.float32),
                jax.ShapeDtypeStruct((2, rows, 1), jnp.float32),
                jax.ShapeDtypeStruct((2, rows + EXTRA, size), jnp.bfloat16),
            ),
            in_specs=[pl.BlockSpec(memory_space=pltpu.SMEM)]
            + in_vmem(7)
            + [pl.BlockSpec(memory_space=pl.ANY)],
            out_specs=tuple(in_vmem(3)),
            compiler_params=pltpu.CompilerParams(vmem_limit_bytes=16 * MIB),
            cost_estimate=pl.CostEstimate(flops=0, bytes_accessed=0, transcendentals=0),
        )(places, query_down, keys_down, one_down, query_up, keys_up, one_up, two_up, up)
        partner = by_row(theirs)
        return pl.pallas_call(
            merge_kernel,
            out_shape=jax.ShapeDtypeStruct((rows, local_heads * size), jnp.bfloat16),
            in_specs=[pl.BlockSpec(memory_space=pltpu.SMEM)] + in_vmem(9),
            out_specs=in_vmem(1)[0],
            compiler_params=pltpu.CompilerParams(vmem_limit_bytes=16 * MIB),
        )(
            places, mine, logs, partner, two_same, two_cross, three_same, three_cross, up_same,
            up_cross,
        )

    sums = jnp.stack([summed(head, 0, taller) for head in range(pair)]).astype(jnp.bfloat16)
    everything = lax.all_gather(sums[:, : 2 * block], "tok", axis=0, tiled=False)
    everything = everything.transpose(1, 0, 2, 3)
    all_codes = lax.all_gather(codes, "tok", axis=0, tiled=True)
    starts = jnp.sum((all_codes[None, :] < codes[:, None]).astype(jnp.int32), axis=1)
    together = attend_gathered(
        sums[:, break_at : break_at + block],
        everything[:, :, :block].reshape(pair, toks * block, size),
        everything[:, :, block:].reshape(pair, toks * block, size),
        places, starts, scale,
    )
    mine = jnp.where(row == 0, together[:rows], together[rows:])
    theirs = jnp.where(row == 0, together[rows:], together[:rows])

    theirs = by_row(theirs)
    return jnp.concatenate(
        [jnp.where(row == 0, mine, theirs), jnp.where(row == 0, theirs, mine)], axis=1
    )


def solution(mesh):
    placed = (P(("tok", "row"), "col"), P("col"), P("row", "col", None), P(("tok", "row")))
    return jax.shard_map(
        per_device, mesh=mesh, in_specs=placed, out_specs=P(("tok", "row"), "col"), check_vma=False
    )
```

```python
import math

import jax
import jax.numpy as jnp
from jax import lax
from jax.experimental import pallas as pl
from jax.experimental.pallas import tpu as pltpu
from jax.sharding import PartitionSpec as P

EPS = 1e-05
LOW = -1e30
EXTRA = 16
MIB = 1 << 20


def rotary_tables(places, head_size):
    half = head_size // 2
    spacing = jnp.arange(half).astype(jnp.float32) * (2.0 / head_size)
    inverse = jnp.power(10000.0, -spacing)
    angles = places.astype(jnp.float32)[:, None] * inverse[None, :]
    cosine, sine = jnp.cos(angles), jnp.sin(angles)
    return (
        jnp.concatenate([cosine, cosine], axis=1),
        jnp.concatenate([-sine, sine], axis=1),
    )


def weight_copies(first_head, triple, weight_hbm, weight_buffer, semaphores):
    depth = weight_buffer.shape[0] // 2
    columns = weight_buffer.shape[1]
    first = pl.multiple_of(first_head * triple, 128)
    return [
        pltpu.make_async_copy(
            weight_hbm.at[pl.ds(half * depth, depth), pl.ds(first, columns)],
            weight_buffer.at[pl.ds(half * depth, depth), :],
            semaphores.at[half],
        )
        for half in range(2)
    ]


def project_heads(normed_ref, copies, weight_buffer, cos_ref, sin_ref, doc_rows, out_refs):
    heads, size = len(out_refs), cos_ref.shape[1]
    block, extra = cos_ref.shape[0], doc_rows.shape[0]
    depth = weight_buffer.shape[0] // 2
    for copy in copies:
        copy.wait()
    for head in range(heads):
        columns = slice(head * 3 * size, (head + 1) * 3 * size)
        part = jnp.dot(
            normed_ref[0], weight_buffer[:depth, columns], preferred_element_type=jnp.float32
        ) + jnp.dot(
            normed_ref[1], weight_buffer[depth:, columns], preferred_element_type=jnp.float32
        )
        for kind, at in ((0, 2 * block + extra), (1, 0), (2, block)):
            piece = part[:, kind * size : (kind + 1) * size]
            if kind < 2:
                piece = piece * cos_ref[...] + pltpu.roll(piece, size // 2, 1) * sin_ref[...]
            out_refs[head][at : at + block, :] = piece
        for at in (2 * block, 3 * block + extra):
            out_refs[head][at : at + extra, :] = doc_rows


def normalise_project_kernel(
    place_ref, a_near, a_far, b_near, b_far, squares_ref, gain_ref, weight_hbm, cos_ref, sin_ref,
    out_ref, normed_ref, weight_buffer, semaphores,
):
    rows = a_near.shape[0]
    features = 2 * gain_ref.shape[0] * gain_ref.shape[2]
    core, near_row, head = place_ref[0], place_ref[1], place_ref[2]
    copies = weight_copies(head, 3 * cos_ref.shape[1], weight_hbm, weight_buffer, semaphores)
    for copy in copies:
        copy.start()
    for shards, half in (((a_near, a_far), core), ((b_near, b_far), 1 - core)):
        gain = gain_ref[half]
        for shard, row in zip(shards, (near_row, 1 - near_row)):
            at = pl.ds(pl.multiple_of(row * rows, 16), rows)
            factor = lax.rsqrt(squares_ref[at, :] / features + EPS)
            normed_ref[half, at, :] = (shard[...].astype(jnp.float32) * factor * gain).astype(
                jnp.bfloat16
            )
    nothing = jnp.zeros((EXTRA, out_ref.shape[1]), jnp.float32)
    project_heads(normed_ref, copies, weight_buffer, cos_ref, sin_ref, nothing, [out_ref])


def project_kernel(place_ref, normed_ref, docs_ref, weight_hbm, cos_ref, sin_ref, *refs):
    out_refs, (weight_buffer, semaphores) = refs[:-2], refs[-2:]
    copies = weight_copies(
        place_ref[0], 3 * cos_ref.shape[1], weight_hbm, weight_buffer, semaphores
    )
    for copy in copies:
        copy.start()
    project_heads(
        normed_ref, copies, weight_buffer, cos_ref, sin_ref, docs_ref[...], out_refs
    )


def as_column(rows, count):
    lanes = rows.shape[1]
    pieces = []
    for begin in range(0, count, lanes):
        held = min(lanes, count - begin)
        at = lax.broadcasted_iota(jnp.int32, (held, lanes), 0)
        diagonal = at == lax.broadcasted_iota(jnp.int32, (held, lanes), 1)
        row = rows[begin // lanes : begin // lanes + 1, :]
        pieces.append(jnp.sum(jnp.where(diagonal, row, 0.0), axis=1, keepdims=True))
    return jnp.concatenate(pieces, axis=0)


def as_rows(column, lanes):
    count = column.shape[0]
    rows = []
    for begin in range(0, count, lanes):
        held = min(lanes, count - begin)
        at = lax.broadcasted_iota(jnp.int32, (held, lanes), 0)
        diagonal = at == lax.broadcasted_iota(jnp.int32, (held, lanes), 1)
        rows.append(
            jnp.sum(jnp.where(diagonal, column[begin : begin + held], 0.0), axis=0, keepdims=True)
        )
    return rows


def as_lanes(rows, count):
    lanes = rows.shape[1]
    return jnp.concatenate(
        [
            rows[begin // lanes : begin // lanes + 1, : min(lanes, count - begin)]
            for begin in range(0, count, lanes)
        ],
        axis=1,
    )


def softmax_part(scale, query, query_docs, messages, causal):
    block = (messages[0].shape[0] - EXTRA) // 2
    keys = jnp.concatenate([message[:block] for message in messages], axis=0)
    values = jnp.concatenate([message[block : 2 * block] for message in messages], axis=0)
    key_docs = jnp.concatenate(
        [as_lanes(message[2 * block :].astype(jnp.float32), block) for message in messages], axis=1
    )
    visible = query_docs == key_docs
    if causal:
        shape = (query.shape[0], keys.shape[0])
        query_places = lax.broadcasted_iota(jnp.int32, shape, 0)
        key_places = lax.broadcasted_iota(jnp.int32, shape, 1)
        visible &= (key_places <= query_places) | (key_places >= block)
    scores = (
        lax.dot_general(query, keys, (((1,), (1,)), ((), ())), preferred_element_type=jnp.float32)
        * scale
    )
    top = jnp.max(jnp.where(visible, scores, LOW), axis=1, keepdims=True)
    exponentials = jnp.where(visible, jnp.exp(scores - top), 0.0)
    total = jnp.sum(exponentials, axis=1, keepdims=True)
    summed = jnp.dot(exponentials.astype(jnp.bfloat16), values, preferred_element_type=jnp.float32)
    some = total > 0.0
    safe = jnp.where(some, total, 1.0)
    return summed / safe, jnp.where(some, top + jnp.log(safe), LOW)


def as_message(output, logs, size):
    along = jnp.concatenate(as_rows(logs, size), axis=0)
    high = along.astype(jnp.bfloat16).astype(jnp.float32)
    middle = (along - high).astype(jnp.bfloat16).astype(jnp.float32)
    pieces = [output, high, middle, along - high - middle]
    pieces.append(jnp.zeros((EXTRA - 3 * along.shape[0], size), jnp.float32))
    return jnp.concatenate(pieces, axis=0).astype(jnp.bfloat16)


def logs_of(message, rows):
    tile = message[rows:].astype(jnp.float32)
    groups = pl.cdiv(rows, tile.shape[1])
    return as_column(sum(tile[k * groups : (k + 1) * groups] for k in range(3)), rows)


def parted(row, value):
    rows = value.shape[0] // 2
    first = row == 0
    return (
        jnp.where(first, value[:rows], value[rows:]),
        jnp.where(first, value[rows:], value[:rows]),
    )


def guests_into(scale, row, query_refs, messages, out_ref):
    for index, query_ref in enumerate(query_refs):
        block, size = query_ref.shape[0] - EXTRA, query_ref.shape[1]
        docs = as_column(query_ref[block:, :].astype(jnp.float32), block)
        output, logs = softmax_part(scale, query_ref[:block, :], docs, messages, False)
        for owner, (a, b) in enumerate(zip(parted(row, output), parted(row, logs))):
            out_ref[index, owner] = as_message(a, b, size)


def guests_down_kernel(
    scale, place_ref, query_two, query_three, first, second, out_ref
):
    @pl.when(place_ref[0] == 1)
    def attend():
        guests_into(scale, place_ref[1], (query_two, query_three), [first[...], second[...]], out_ref)


def guests_up_kernel(
    scale, place_ref, query_three, first, second, down_ref, unused_ref, out_ref
):
    @pl.when(place_ref[0] == 1)
    def forward():
        out_ref[...] = down_ref[...]

    @pl.when(place_ref[0] == 2)
    def attend():
        guests_into(scale, place_ref[1], (query_three,), [first[...], second[...]], out_ref)


def own_kernel(scale, place_ref, query_ref, *refs):
    message_refs, (mine_ref, logs_ref, theirs_ref) = refs[:-3], refs[-3:]
    block, size = query_ref.shape[0] - EXTRA, query_ref.shape[1]
    docs = as_column(query_ref[block:, :].astype(jnp.float32), block)
    output, logs = softmax_part(
        scale, query_ref[:block, :], docs, [ref[...] for ref in message_refs], True
    )
    mine_ref[...], theirs = parted(place_ref[1], output)
    logs_ref[...], their_logs = parted(place_ref[1], logs)
    theirs_ref[...] = as_message(theirs, their_logs, size)


def own_up_kernel(scale, place_ref, query_ref, own, one, two, before_ref, mine, logs, theirs_ref):
    theirs_ref[0] = before_ref[...]
    own_kernel(scale, place_ref, query_ref, own, one, two, mine, logs, theirs_ref.at[1])


def merge_kernel(
    place_ref, mine_down, logs_down, mine_up, logs_up, partner_ref, three_same, three_cross,
    next_same, next_cross, out_ref,
):
    rows, size = mine_down.shape
    tok, row = place_ref[0], place_ref[1]
    at_two, at_three = tok == 2, tok == 3

    def joined(output, logs, message, present):
        guest = jnp.where(present, logs_of(message, rows), LOW)
        top = jnp.maximum(logs, guest)
        weight, guest_weight = jnp.exp(logs - top), jnp.exp(guest - top)
        total = output * weight + message[:rows].astype(jnp.float32) * guest_weight
        return (total / (weight + guest_weight)).astype(jnp.bfloat16)

    for mine, three, following in (
        (True, three_same, next_same),
        (False, three_cross, next_cross),
    ):
        begin = jnp.where(row == 0, 0, 1) if mine else jnp.where(row == 0, 1, 0)
        down = jnp.where(at_two, following[...], three[...])
        for index, (message, present, output_ref, logs_ref) in enumerate(
            (
                (down, at_two | at_three, mine_down, logs_down),
                (following[...], at_three, mine_up, logs_up),
            )
        ):
            if mine:
                output, logs = output_ref[...], logs_ref[...]
            else:
                partner = partner_ref[index]
                output, logs = partner[:rows].astype(jnp.float32), logs_of(partner, rows)
            at = pl.ds(pl.multiple_of((2 * begin + index) * size, size), size)
            out_ref[:, at] = joined(output, logs, message, present)


def attend_gathered(query, keys, values, places, starts, scale):
    heads, count, size = query.shape
    chunk = math.gcd(keys.shape[1], 1024)
    rounds = keys.shape[1] // chunk
    stacked = (
        keys.reshape(heads, rounds, chunk, size).transpose(1, 0, 2, 3),
        values.reshape(heads, rounds, chunk, size).transpose(1, 0, 2, 3),
        jnp.arange(rounds * chunk, dtype=jnp.int32).reshape(rounds, chunk),
    )

    def advance(state, blocks):
        running, totals, summed = state
        block_keys, block_values, key_places = blocks
        scores = (
            jnp.einsum("hqd,hkd->hqk", query, block_keys, preferred_element_type=jnp.float32) * scale
        )
        visible = (key_places[None, None, :] <= places[None, :, None]) & (
            key_places[None, None, :] >= starts[None, :, None]
        )
        masked = jnp.where(visible, scores, -jnp.inf)
        newest = jnp.maximum(running, jnp.max(masked, axis=2))
        factor = jnp.exp(running - newest)
        exponentials = jnp.where(visible, jnp.exp(masked - newest[:, :, None]), 0.0)
        totals = totals * factor + jnp.sum(exponentials, axis=2)
        summed = summed * factor[:, :, None] + jnp.einsum(
            "hqk,hkd->hqd", exponentials.astype(jnp.bfloat16), block_values,
            preferred_element_type=jnp.float32,
        )
        return (newest, totals, summed), None

    initial = (
        jnp.full((heads, count), -1e30, jnp.float32),
        jnp.zeros((heads, count), jnp.float32),
        jnp.zeros((heads, count, size), jnp.float32),
    )
    (running, totals, summed), unused = lax.scan(advance, initial, stacked)
    attended = (summed / totals[:, :, None]).astype(jnp.bfloat16)
    return attended.transpose(1, 0, 2).reshape(count, heads * size)


def in_vmem(count):
    return [pl.BlockSpec(memory_space=pltpu.VMEM)] * count


def per_device(activations, norm_gain, qkv_weight, doc_ids):
    rows, width = activations.shape
    span, local_heads, triple = qkv_weight.shape
    size = triple // 3
    pair = local_heads // 2
    block = 2 * rows
    toks = lax.axis_size("tok")
    tok, row, col = lax.axis_index("tok"), lax.axis_index("row"), lax.axis_index("col")
    chip, core = col >> 1, col & 1
    grid = [(r, c) for r in range(2) for c in range(4)]

    def by_col(value, flip):
        return lax.ppermute(value, "col", [(c, c ^ flip) for c in range(4)])

    def by_row(value):
        return lax.ppermute(value, "row", [(0, 1), (1, 0)])

    def ordered(index, own, other):
        first = index == 0
        return jnp.concatenate([jnp.where(first, own, other), jnp.where(first, other, own)])

    near = lax.ppermute(
        activations,
        ("row", "col"),
        [(r * 4 + c, (c // 2) * 4 + 2 * r + c % 2) for r, c in grid],
    )
    far = lax.ppermute(
        activations,
        ("row", "col"),
        [(r * 4 + c, (c // 2) * 4 + 2 * (1 - r) + c % 2) for r, c in grid],
    )
    widened = activations.astype(jnp.float32)
    squares = jnp.sum(widened * widened, axis=1)
    gain = norm_gain.astype(jnp.float32)
    message = jnp.concatenate([squares, gain])
    message, qkv_weight = lax.optimization_barrier((message, qkv_weight))
    flat_weight = qkv_weight.reshape(span, local_heads * triple)
    got = by_col(message, 1)
    squares = squares + got[:rows]
    gain = ordered(core, gain, got[rows:])
    codes = doc_ids.astype(jnp.float32) + 1.0
    message = jnp.concatenate([squares, gain])
    by_chip = by_col(message, 2)
    by_row_only = by_row(jnp.concatenate([squares, codes]))
    by_both = lax.ppermute(
        squares, ("row", "col"), [(r * 4 + c, (1 - r) * 4 + (c ^ 2)) for r, c in grid]
    )
    near, far, by_chip, flat_weight = lax.optimization_barrier((near, far, by_chip, flat_weight))
    near_other, far_other = by_col(near, 1), by_col(far, 1)
    gain = jnp.where(chip == row, gain, by_chip[rows:]).reshape(2, 1, width)
    squares = ordered(row, squares + by_chip[:rows], by_row_only[:rows] + by_both)
    squares = squares.reshape(block, 1)
    codes = ordered(row, codes, by_row_only[rows:])
    doc_rows = jnp.pad(codes, (0, EXTRA * size - block)).reshape(EXTRA, size)
    places = tok * block + jnp.arange(block, dtype=jnp.int32)
    cosine, sine = rotary_tables(places, size)

    taller = 3 * block + 2 * EXTRA
    break_at = 2 * block + EXTRA

    def projection(kernel, heads, normalising):
        normed_shape = (jax.ShapeDtypeStruct((2, block, width), jnp.bfloat16),)
        return pl.pallas_call(
            kernel,
            out_shape=(jax.ShapeDtypeStruct((taller, size), jnp.float32),) * heads
            + (normed_shape if normalising else ()),
            in_specs=[pl.BlockSpec(memory_space=pltpu.SMEM)]
            + in_vmem(6 if normalising else 2)
            + [pl.BlockSpec(memory_space=pltpu.HBM)]
            + in_vmem(2),
            out_specs=tuple(in_vmem(heads + 1 if normalising else heads)),
            scratch_shapes=[
                pltpu.VMEM((span, heads * triple), jnp.bfloat16),
                pltpu.SemaphoreType.DMA((2,)),
            ],
            compiler_params=pltpu.CompilerParams(vmem_limit_bytes=12 * MIB),
            cost_estimate=pl.CostEstimate(flops=0, bytes_accessed=0, transcendentals=0),
        )

    away_head, own_head = (1 - row) * pair, row * pair
    away, normed = projection(normalise_project_kernel, 1, True)(
        jnp.stack([core, chip, away_head]), near, far, near_other, far_other, squares, gain,
        flat_weight, cosine, sine,
    )
    arrived = []
    for head in range(pair):
        if head > 0:
            (away,) = projection(project_kernel, 1, False)(
                (away_head + head).reshape(1), normed, jnp.zeros_like(doc_rows), flat_weight,
                cosine, sine,
            )
        away, normed = lax.optimization_barrier((away.astype(jnp.float16), normed))
        arrived.append(by_row(away))
    own = projection(project_kernel, pair, False)(
        own_head.reshape(1), normed, doc_rows, flat_weight, cosine, sine
    )
    scale = 1.0 / math.sqrt(size)

    def along_tok(value, pairs):
        return lax.ppermute(value, "tok", pairs)

    def summed(head, begin, end):
        return own[head][begin:end] + arrived[head][begin:end].astype(jnp.float32)

    if toks == 4 and pair == 2:
        places = jnp.stack([tok, row])

        def returned(value, pairs):
            across = [(2 * a + r, 2 * b + 1 - r) for a, b in pairs for r in range(2)]
            return along_tok(value[0], pairs), lax.ppermute(value[1], ("tok", "row"), across)

        def on_place(kernel, out_shape, ins, unused=0):
            return pl.pallas_call(
                kernel,
                out_shape=out_shape,
                in_specs=[pl.BlockSpec(memory_space=pltpu.SMEM)]
                + in_vmem(ins - unused)
                + [pl.BlockSpec(memory_space=pl.ANY)] * unused,
                out_specs=jax.tree.map(lambda unused: in_vmem(1)[0], out_shape),
                compiler_params=pltpu.CompilerParams(vmem_limit_bytes=16 * MIB),
                cost_estimate=pl.CostEstimate(flops=0, bytes_accessed=0, transcendentals=0),
            )

        half_message = (rows + EXTRA, size)
        own_shapes = (
            jax.ShapeDtypeStruct((rows, size), jnp.float32),
            jax.ShapeDtypeStruct((rows, 1), jnp.float32),
        )

        query_down = summed(0, break_at, taller).astype(jnp.bfloat16)
        keys_down = summed(0, 0, break_at).astype(jnp.bfloat16)
        from_three = along_tok(query_down, [(3, 1)])
        from_two = along_tok(query_down, [(2, 1)])
        one_down = along_tok(keys_down, [(0, 1), (2, 3)])

        arrived[1] = jnp.where(
            tok < toks,
            arrived[1].astype(jnp.float32),
            jnp.broadcast_to(from_two[:1].astype(jnp.float32), arrived[1].shape),
        )
        keys_up = summed(1, 0, break_at).astype(jnp.bfloat16)
        query_up = summed(1, break_at, taller).astype(jnp.bfloat16)
        two_up = along_tok(keys_up, [(0, 2)])
        three_up = along_tok(query_up, [(3, 2)])
        one_up = along_tok(keys_up, [(0, 1), (1, 2), (2, 3)])

        down = on_place(
            lambda *refs: guests_down_kernel(scale, *refs),
            jax.ShapeDtypeStruct((2, 2) + half_message, jnp.bfloat16),
            4,
        )(places, from_two, from_three, one_down, keys_down)
        three_same, three_cross = returned(down[1], [(1, 3)])
        mine_down, logs_down, theirs = on_place(
            lambda *refs: own_kernel(scale, *refs),
            own_shapes + (jax.ShapeDtypeStruct(half_message, jnp.bfloat16),),
            3,
        )(places, query_down, keys_down, one_down)
        mine_up, logs_up, theirs = on_place(
            lambda *refs: own_up_kernel(scale, *refs),
            own_shapes + (jax.ShapeDtypeStruct((2,) + half_message, jnp.bfloat16),),
            5,
        )(places, query_up, keys_up, one_up, two_up, theirs)
        partner = by_row(theirs)
        up = on_place(
            lambda *refs: guests_up_kernel(scale, *refs),
            jax.ShapeDtypeStruct((1, 2) + half_message, jnp.bfloat16),
            5,
            1,
        )(places, three_up, two_up, one_up, down[:1], mine_up)
        next_same, next_cross = returned(up[0], [(1, 2), (2, 3)])
        return on_place(
            merge_kernel, jax.ShapeDtypeStruct((rows, local_heads * size), jnp.bfloat16), 9
        )(
            places, mine_down, logs_down, mine_up, logs_up, partner, three_same, three_cross,
            next_same, next_cross,
        )

    sums = jnp.stack([summed(head, 0, taller) for head in range(pair)]).astype(jnp.bfloat16)
    everything = lax.all_gather(sums[:, : 2 * block], "tok", axis=0, tiled=False)
    everything = everything.transpose(1, 0, 2, 3)
    all_codes = lax.all_gather(codes, "tok", axis=0, tiled=True)
    starts = jnp.sum((all_codes[None, :] < codes[:, None]).astype(jnp.int32), axis=1)
    together = attend_gathered(
        sums[:, break_at : break_at + block],
        everything[:, :, :block].reshape(pair, toks * block, size),
        everything[:, :, block:].reshape(pair, toks * block, size),
        places, starts, scale,
    )
    mine = jnp.where(row == 0, together[:rows], together[rows:])
    theirs = jnp.where(row == 0, together[rows:], together[:rows])

    theirs = by_row(theirs)
    return jnp.concatenate(
        [jnp.where(row == 0, mine, theirs), jnp.where(row == 0, theirs, mine)], axis=1
    )


def solution(mesh):
    placed = (P(("tok", "row"), "col"), P("col"), P("row", "col", None), P(("tok", "row")))
    return jax.shard_map(
        per_device, mesh=mesh, in_specs=placed, out_specs=P(("tok", "row"), "col"), check_vma=False
    )
```

```python
import math

import jax
import jax.numpy as jnp
from jax import lax
from jax.experimental import pallas as pl
from jax.experimental.pallas import tpu as pltpu
from jax.sharding import PartitionSpec as P

EPS = 1e-05
LOW = -1e30
EXTRA = 16
MIB = 1 << 20


def rotary_tables(places, head_size):
    half = head_size // 2
    spacing = jnp.arange(half).astype(jnp.float32) * (2.0 / head_size)
    inverse = jnp.power(10000.0, -spacing)
    angles = places.astype(jnp.float32)[:, None] * inverse[None, :]
    cosine, sine = jnp.cos(angles), jnp.sin(angles)
    return (
        jnp.concatenate([cosine, cosine], axis=1),
        jnp.concatenate([-sine, sine], axis=1),
    )


def project_chunks(normed_ref, first_column, weight_ref, cos_ref, sin_ref, doc_rows, out_refs):
    block, size = cos_ref.shape
    extra = doc_rows.shape[0]
    depth = weight_ref.shape[0] // 2

    def product(column, width):
        at = pl.ds(pl.multiple_of(first_column + column * size, size), width * size)
        return jnp.dot(
            normed_ref[0], weight_ref[:depth, at], preferred_element_type=jnp.float32
        ) + jnp.dot(normed_ref[1], weight_ref[depth:, at], preferred_element_type=jnp.float32)

    def rotated(piece):
        return piece * cos_ref[...] + pltpu.roll(piece, size // 2, 1) * sin_ref[...]

    for chunk, out_ref in out_refs:
        both = product(4 if chunk == 0 else 1, 2)
        out_ref[:block, :] = rotated(both[:, :size])
        out_ref[block : 2 * block, :] = both[:, size:]
        out_ref[2 * block : 2 * block + extra, :] = doc_rows
        out_ref[2 * block + extra : 3 * block + extra, :] = rotated(product(0 if chunk == 0 else 3, 1))
        out_ref[3 * block + extra :, :] = doc_rows


def normalise_project_kernel(
    place_ref, a_near, a_far, b_near, b_far, squares_ref, gain_ref, weight_ref, cos_ref, sin_ref,
    out_ref, normed_ref,
):
    rows = a_near.shape[0]
    features = 2 * gain_ref.shape[0] * gain_ref.shape[2]
    core, near_row = place_ref[0], place_ref[1]
    for shards, half in (((a_near, a_far), core), ((b_near, b_far), 1 - core)):
        gain = gain_ref[half]
        for shard, row in zip(shards, (near_row, 1 - near_row)):
            at = pl.ds(pl.multiple_of(row * rows, 16), rows)
            factor = lax.rsqrt(squares_ref[at, :] / features + EPS)
            normed_ref[half, at, :] = (shard[...].astype(jnp.float32) * factor * gain).astype(
                jnp.bfloat16
            )
    nothing = jnp.zeros((EXTRA, out_ref.shape[1]), jnp.float32)
    project_chunks(
        normed_ref, place_ref[2], weight_ref, cos_ref, sin_ref, nothing, [(0, out_ref)]
    )


def project_kernel(
    chunks, place_ref, normed_ref, docs_ref, weight_ref, cos_ref, sin_ref, *out_refs
):
    project_chunks(
        normed_ref, place_ref[0], weight_ref, cos_ref, sin_ref, docs_ref[...], list(zip(chunks, out_refs))
    )


def as_column(rows, count):
    lanes = rows.shape[1]
    pieces = []
    for begin in range(0, count, lanes):
        held = min(lanes, count - begin)
        at = lax.broadcasted_iota(jnp.int32, (held, lanes), 0)
        diagonal = at == lax.broadcasted_iota(jnp.int32, (held, lanes), 1)
        row = rows[begin // lanes : begin // lanes + 1, :]
        pieces.append(jnp.sum(jnp.where(diagonal, row, 0.0), axis=1, keepdims=True))
    return jnp.concatenate(pieces, axis=0)


def as_rows(column, lanes):
    count = column.shape[0]
    rows = []
    for begin in range(0, count, lanes):
        held = min(lanes, count - begin)
        at = lax.broadcasted_iota(jnp.int32, (held, lanes), 0)
        diagonal = at == lax.broadcasted_iota(jnp.int32, (held, lanes), 1)
        rows.append(
            jnp.sum(jnp.where(diagonal, column[begin : begin + held], 0.0), axis=0, keepdims=True)
        )
    return rows


def as_lanes(rows, count):
    lanes = rows.shape[1]
    return jnp.concatenate(
        [
            rows[begin // lanes : begin // lanes + 1, : min(lanes, count - begin)]
            for begin in range(0, count, lanes)
        ],
        axis=1,
    )


def softmax_part(scale, query_message, messages, causal):
    valid = [present for message, present in messages]
    messages = [message for message, present in messages]
    query = query_message[:-EXTRA]
    query_docs = as_column(query_message[-EXTRA:].astype(jnp.float32), query.shape[0])
    block = (messages[0].shape[0] - EXTRA) // 2
    keys = jnp.concatenate([message[:block] for message in messages], axis=0)
    values = jnp.concatenate([message[block : 2 * block] for message in messages], axis=0)
    key_docs = jnp.concatenate(
        [
            jnp.where(present, as_lanes(message[2 * block :].astype(jnp.float32), block), 0.0)
            for message, present in zip(messages, valid)
        ],
        axis=1,
    )
    visible = query_docs == key_docs
    if causal:
        shape = (query.shape[0], keys.shape[0])
        query_places = lax.broadcasted_iota(jnp.int32, shape, 0)
        key_places = lax.broadcasted_iota(jnp.int32, shape, 1)
        visible &= (key_places <= query_places) | (key_places >= block)
    scores = (
        lax.dot_general(query, keys, (((1,), (1,)), ((), ())), preferred_element_type=jnp.float32)
        * scale
    )
    top = jnp.max(jnp.where(visible, scores, LOW), axis=1, keepdims=True)
    exponentials = jnp.where(visible, jnp.exp(scores - top), 0.0)
    total = jnp.sum(exponentials, axis=1, keepdims=True)
    summed = jnp.dot(exponentials.astype(jnp.bfloat16), values, preferred_element_type=jnp.float32)
    some = total > 0.0
    safe = jnp.where(some, total, 1.0)
    return summed / safe, jnp.where(some, top + jnp.log(safe), LOW)


def as_message(output, logs, size):
    along = jnp.concatenate(as_rows(logs, size), axis=0)
    high = along.astype(jnp.bfloat16).astype(jnp.float32)
    middle = (along - high).astype(jnp.bfloat16).astype(jnp.float32)
    pieces = [output, high, middle, along - high - middle]
    pieces.append(jnp.zeros((EXTRA - 3 * along.shape[0], size), jnp.float32))
    return jnp.concatenate(pieces, axis=0).astype(jnp.bfloat16)


def logs_of(message, rows):
    tile = message[rows:].astype(jnp.float32)
    groups = pl.cdiv(rows, tile.shape[1])
    return as_column(sum(tile[k * groups : (k + 1) * groups] for k in range(3)), rows)


def parted(row, value):
    rows = value.shape[0] // 2
    first = row == 0
    return (
        jnp.where(first, value[:rows], value[rows:]),
        jnp.where(first, value[rows:], value[:rows]),
    )


def guests_into(scale, row, queries, messages, out_ref):
    for index, query in enumerate(queries):
        output, logs = softmax_part(scale, query, [(m, True) for m in messages], False)
        for owner, (a, b) in enumerate(zip(parted(row, output), parted(row, logs))):
            out_ref[index, owner] = as_message(a, b, query.shape[1])


def guests_down_kernel(scale, place_ref, one_ref, two_ref, first_ref, own_ref, unused_ref, out_ref):
    @pl.when(place_ref[0] == 1)
    def attend():
        height = first_ref.shape[0]
        queries = [ref[(height - EXTRA) // 2 :, :] for ref in (one_ref, two_ref)]
        guests_into(
            scale, place_ref[1], queries, [first_ref[...], own_ref[:height, :]], out_ref
        )


def guests_up_kernel(scale, place_ref, query_ref, first_ref, second_ref, down_ref, out_ref):
    @pl.when(place_ref[0] == 1)
    def forward():
        out_ref[...] = down_ref[:1]

    @pl.when(place_ref[0] == 2)
    def attend():
        query = query_ref[(query_ref.shape[0] - EXTRA) // 2 :, :]
        guests_into(scale, place_ref[1], [query], [first_ref[...], second_ref[...]], out_ref)


def own_part(scale, row, query, messages, mine_ref, logs_ref):
    output, logs = softmax_part(scale, query, messages, True)
    mine_ref[...], theirs = parted(row, output)
    logs_ref[...], their_logs = parted(row, logs)
    return as_message(theirs, their_logs, query.shape[1])


def own_up_kernel(
    scale, place_ref, query_chunk, own_chunk, one_up, from_one, from_zero, mine, logs, theirs_ref
):
    tok = place_ref[0]
    height = from_one.shape[0]
    previous = jnp.where(tok == 1, one_up[...], from_one[...])
    messages = [
        (own_chunk[:height, :], True), (previous, tok > 0), (from_zero[...], tok == 2)
    ]
    theirs_ref[...] = own_part(
        scale, place_ref[1], query_chunk[height:, :], messages, mine, logs
    )


def own_down_kernel(
    scale, place_ref, query_chunk, own_chunk, previous, before_ref, unused_ref, mine, logs, theirs_ref
):
    tok = place_ref[0]
    height = previous.shape[0]
    messages = [(own_chunk[:height, :], True), (previous[...], (tok == 1) | (tok == 3))]
    theirs_ref[0] = own_part(scale, place_ref[1], query_chunk[height:, :], messages, mine, logs)
    theirs_ref[1] = before_ref[...]


def merge_kernel(
    place_ref, mine_down, logs_down, mine_up, logs_up, partner_ref, three_same, three_cross,
    next_same, next_cross, out_ref,
):
    rows, size = mine_down.shape
    tok, row = place_ref[0], place_ref[1]
    at_two, at_three = tok == 2, tok == 3

    def joined(output, logs, message, present):
        guest = jnp.where(present, logs_of(message, rows), LOW)
        top = jnp.maximum(logs, guest)
        weight, guest_weight = jnp.exp(logs - top), jnp.exp(guest - top)
        guest_output = jnp.where(present, message[:rows].astype(jnp.float32), 0.0)
        total = output * weight + guest_output * guest_weight
        return (total / (weight + guest_weight)).astype(jnp.bfloat16)

    for mine, three, following in (
        (True, three_same, next_same),
        (False, three_cross, next_cross),
    ):
        begin = jnp.where(row == 0, 0, 1) if mine else jnp.where(row == 0, 1, 0)
        down = jnp.where(at_two, following[...], three[...])
        for index, (message, present, output_ref, logs_ref) in enumerate(
            (
                (down, at_two | at_three, mine_down, logs_down),
                (following[...], at_three, mine_up, logs_up),
            )
        ):
            if mine:
                output, logs = output_ref[...], logs_ref[...]
            else:
                partner = partner_ref[index]
                output, logs = partner[:rows].astype(jnp.float32), logs_of(partner, rows)
            at = pl.ds(pl.multiple_of((2 * begin + index) * size, size), size)
            out_ref[:, at] = joined(output, logs, message, present)


def attend_gathered(query, keys, values, places, starts, scale):
    heads, count, size = query.shape
    chunk = math.gcd(keys.shape[1], 1024)
    rounds = keys.shape[1] // chunk
    stacked = (
        keys.reshape(heads, rounds, chunk, size).transpose(1, 0, 2, 3),
        values.reshape(heads, rounds, chunk, size).transpose(1, 0, 2, 3),
        jnp.arange(rounds * chunk, dtype=jnp.int32).reshape(rounds, chunk),
    )

    def advance(state, blocks):
        running, totals, summed = state
        block_keys, block_values, key_places = blocks
        scores = (
            jnp.einsum("hqd,hkd->hqk", query, block_keys, preferred_element_type=jnp.float32) * scale
        )
        visible = (key_places[None, None, :] <= places[None, :, None]) & (
            key_places[None, None, :] >= starts[None, :, None]
        )
        masked = jnp.where(visible, scores, -jnp.inf)
        newest = jnp.maximum(running, jnp.max(masked, axis=2))
        factor = jnp.exp(running - newest)
        exponentials = jnp.where(visible, jnp.exp(masked - newest[:, :, None]), 0.0)
        totals = totals * factor + jnp.sum(exponentials, axis=2)
        summed = summed * factor[:, :, None] + jnp.einsum(
            "hqk,hkd->hqd", exponentials.astype(jnp.bfloat16), block_values,
            preferred_element_type=jnp.float32,
        )
        return (newest, totals, summed), None

    initial = (
        jnp.full((heads, count), -1e30, jnp.float32),
        jnp.zeros((heads, count), jnp.float32),
        jnp.zeros((heads, count, size), jnp.float32),
    )
    (running, totals, summed), unused = lax.scan(advance, initial, stacked)
    attended = (summed / totals[:, :, None]).astype(jnp.bfloat16)
    return attended.transpose(1, 0, 2).reshape(count, heads * size)


def in_vmem(count):
    return [pl.BlockSpec(memory_space=pltpu.VMEM)] * count


def per_device(activations, norm_gain, qkv_weight, doc_ids):
    rows, width = activations.shape
    span, local_heads, triple = qkv_weight.shape
    size = triple // 3
    pair = local_heads // 2
    block = 2 * rows
    toks = lax.axis_size("tok")
    tok, row, col = lax.axis_index("tok"), lax.axis_index("row"), lax.axis_index("col")
    chip, core = col >> 1, col & 1
    grid = [(r, c) for r in range(2) for c in range(4)]

    def by_col(value, flip):
        return lax.ppermute(value, "col", [(c, c ^ flip) for c in range(4)])

    def by_row(value):
        return lax.ppermute(value, "row", [(0, 1), (1, 0)])

    def ordered(index, own, other):
        first = index == 0
        return jnp.concatenate([jnp.where(first, own, other), jnp.where(first, other, own)])

    near = lax.ppermute(
        activations,
        ("row", "col"),
        [(r * 4 + c, (c // 2) * 4 + 2 * r + c % 2) for r, c in grid],
    )
    far = lax.ppermute(
        activations,
        ("row", "col"),
        [(r * 4 + c, (c // 2) * 4 + 2 * (1 - r) + c % 2) for r, c in grid],
    )
    widened = activations.astype(jnp.float32)
    squares = jnp.sum(widened * widened, axis=1)
    gain = norm_gain.astype(jnp.float32)
    message = jnp.concatenate([squares, gain])
    message, qkv_weight = lax.optimization_barrier((message, qkv_weight))
    flat_weight = qkv_weight.reshape(span, local_heads * triple)
    got = by_col(message, 1)
    squares = squares + got[:rows]
    gain = ordered(core, gain, got[rows:])
    codes = doc_ids.astype(jnp.float32) + 1.0
    got = by_row(jnp.concatenate([squares, codes]))
    got, flat_weight = lax.optimization_barrier((got, flat_weight))
    squares = ordered(row, squares, got[:rows])
    codes = ordered(row, codes, got[rows:])
    got = by_col(jnp.concatenate([squares, gain]), 2)
    near_other, far_other = by_col(near, 1), by_col(far, 1)
    squares = (squares + got[:block]).reshape(block, 1)
    gain = jnp.where(chip == row, gain, got[block:]).reshape(2, 1, width)
    doc_rows = jnp.pad(codes, (0, EXTRA * size - block)).reshape(EXTRA, size)
    places = tok * block + jnp.arange(block, dtype=jnp.int32)
    cosine, sine = rotary_tables(places, size)

    taller = 3 * block + 2 * EXTRA
    break_at = 2 * block + EXTRA

    flat_weight = pltpu.with_memory_space_constraint(flat_weight, pltpu.VMEM)

    def projection(kernel, chunks, normalising):
        normed_shape = (jax.ShapeDtypeStruct((2, block, width), jnp.bfloat16),)
        return pl.pallas_call(
            kernel,
            out_shape=(jax.ShapeDtypeStruct((taller, size), jnp.float32),) * chunks
            + (normed_shape if normalising else ()),
            in_specs=[pl.BlockSpec(memory_space=pltpu.SMEM)] + in_vmem(9 if normalising else 5),
            out_specs=tuple(in_vmem(chunks + 1 if normalising else chunks)),
            compiler_params=pltpu.CompilerParams(vmem_limit_bytes=12 * MIB),
            cost_estimate=pl.CostEstimate(flops=0, bytes_accessed=0, transcendentals=0),
        )

    away_column, own_column = (1 - row) * (pair * triple), row * (pair * triple)
    away, normed = projection(normalise_project_kernel, 1, True)(
        jnp.stack([core, chip, away_column]), near, far, near_other, far_other, squares, gain,
        flat_weight, cosine, sine,
    )
    arrived = [by_row(away.astype(jnp.float16))]
    (away,) = projection(lambda *refs: project_kernel((1,), *refs), 1, False)(
        away_column.reshape(1), normed, jnp.zeros_like(doc_rows), flat_weight, cosine, sine
    )
    arrived.append(by_row(away.astype(jnp.float16)))
    own = projection(lambda *refs: project_kernel((0, 1), *refs), 2, False)(
        own_column.reshape(1), normed, doc_rows, flat_weight, cosine, sine
    )
    scale = 1.0 / math.sqrt(size)

    def summed(chunk):
        return (own[chunk] + arrived[chunk].astype(jnp.float32)).astype(jnp.bfloat16)

    if toks == 4:
        places = jnp.stack([tok, row])

        def along_tok(value, targets):
            return lax.ppermute(value, "tok", list(enumerate(targets)))

        def returned(value, targets):
            across = [(2 * t + r, 2 * to + 1 - r) for t, to in enumerate(targets) for r in range(2)]
            return along_tok(value[0], targets), lax.ppermute(value[1], ("tok", "row"), across)

        def keys_or_query(chunk, query_from):
            begin = jnp.where(tok == query_from, taller - break_at, 0)
            return lax.dynamic_slice_in_dim(chunk, begin.astype(jnp.uint32), break_at, 0)

        def on_place(kernel, out_shape, ins, unused=0):
            return pl.pallas_call(
                kernel,
                out_shape=out_shape,
                in_specs=[pl.BlockSpec(memory_space=pltpu.SMEM)]
                + in_vmem(ins - unused)
                + [pl.BlockSpec(memory_space=pl.ANY)] * unused,
                out_specs=jax.tree.map(lambda unused: in_vmem(1)[0], out_shape),
                compiler_params=pltpu.CompilerParams(vmem_limit_bytes=16 * MIB),
                cost_estimate=pl.CostEstimate(flops=0, bytes_accessed=0, transcendentals=0),
            )

        half_message = (rows + EXTRA, size)
        own_shapes = (
            jax.ShapeDtypeStruct((rows, size), jnp.float32),
            jax.ShapeDtypeStruct((rows, 1), jnp.float32),
        )

        chunk_one = summed(0)
        from_zero = along_tok(keys_or_query(chunk_one, 2), (2, 0, 1, 3))
        from_one = along_tok(keys_or_query(chunk_one, 3), (0, 2, 3, 1))
        one_up = along_tok(chunk_one[:break_at], (1, 0, 3, 2))
        across = by_col(chunk_one[:EXTRA], 1)
        arrived[1] = jnp.where(
            tok < toks,
            arrived[1].astype(jnp.float32),
            jnp.broadcast_to(across[:1].astype(jnp.float32), arrived[1].shape),
        )
        chunk_two = summed(1)
        neighbour = along_tok(keys_or_query(chunk_two, 3), (1, 0, 3, 2))

        mine_up, logs_up, theirs = on_place(
            lambda *refs: own_up_kernel(scale, *refs),
            own_shapes + (jax.ShapeDtypeStruct(half_message, jnp.bfloat16),),
            5,
        )(places, chunk_two, chunk_one, one_up, from_one, from_zero)
        down = on_place(
            lambda *refs: guests_down_kernel(scale, *refs),
            jax.ShapeDtypeStruct((2, 2) + half_message, jnp.bfloat16),
            5,
            1,
        )(places, from_zero, from_one, neighbour, chunk_two, mine_up)
        up = on_place(
            lambda *refs: guests_up_kernel(scale, *refs),
            jax.ShapeDtypeStruct((1, 2) + half_message, jnp.bfloat16),
            4,
        )(places, neighbour, from_zero, from_one, down)
        three_same, three_cross = returned(down[1], (2, 3, 0, 1))
        next_same, next_cross = returned(up[0], (1, 2, 3, 0))
        mine_down, logs_down, theirs = on_place(
            lambda *refs: own_down_kernel(scale, *refs),
            own_shapes + (jax.ShapeDtypeStruct((2,) + half_message, jnp.bfloat16),),
            5,
            1,
        )(places, chunk_one, chunk_two, neighbour, theirs, up)
        partner = by_row(theirs)
        return on_place(
            merge_kernel, jax.ShapeDtypeStruct((rows, local_heads * size), jnp.bfloat16), 9
        )(
            places, mine_down, logs_down, mine_up, logs_up, partner, three_same, three_cross,
            next_same, next_cross,
        )

    chunks = [summed(0), summed(1)]
    keys = jnp.stack([chunks[1][: 2 * block], chunks[0][: 2 * block]])
    everything = lax.all_gather(keys, "tok", axis=0, tiled=False).transpose(1, 0, 2, 3)
    all_codes = lax.all_gather(codes, "tok", axis=0, tiled=True)
    starts = jnp.sum((all_codes[None, :] < codes[:, None]).astype(jnp.int32), axis=1)
    together = attend_gathered(
        jnp.stack([chunk[break_at : break_at + block] for chunk in chunks]),
        everything[:, :, :block].reshape(pair, toks * block, size),
        everything[:, :, block:].reshape(pair, toks * block, size),
        places, starts, scale,
    )
    mine = jnp.where(row == 0, together[:rows], together[rows:])
    theirs = jnp.where(row == 0, together[rows:], together[:rows])

    theirs = by_row(theirs)
    return jnp.concatenate(
        [jnp.where(row == 0, mine, theirs), jnp.where(row == 0, theirs, mine)], axis=1
    )


def solution(mesh):
    placed = (P(("tok", "row"), "col"), P("col"), P("row", "col", None), P(("tok", "row")))
    return jax.shard_map(
        per_device, mesh=mesh, in_specs=placed, out_specs=P(("tok", "row"), "col"), check_vma=False
    )
```

```python
import math

import jax
import jax.numpy as jnp
from jax import lax
from jax.experimental import pallas as pl
from jax.experimental.pallas import tpu as pltpu
from jax.sharding import PartitionSpec as P

EPS = 1e-05
LOW = -1e30
EXTRA = 16
MIB = 1 << 20
KEY_COLUMNS = ((4, 2), (1, 2))
QUERY_COLUMNS = ((0, 1), (3, 1))


def rotary_tables(places, head_size):
    half = head_size // 2
    spacing = jnp.arange(half).astype(jnp.float32) * (2.0 / head_size)
    inverse = jnp.power(10000.0, -spacing)
    angles = places.astype(jnp.float32)[:, None] * inverse[None, :]
    cosine, sine = jnp.cos(angles), jnp.sin(angles)
    return (
        jnp.concatenate([cosine, cosine], axis=1),
        jnp.concatenate([-sine, sine], axis=1),
    )


def weight_copies(first_column, chunks, size, weight_hbm, weight_buffer, semaphores):
    copies = []
    for index, chunk in enumerate(chunks):
        for part, (column, width) in enumerate((KEY_COLUMNS[chunk], QUERY_COLUMNS[chunk])):
            source = pl.ds(pl.multiple_of(first_column + column * size, size), width * size)
            target = pl.ds((3 * index + 2 * part) * size, width * size)
            copies.append(
                pltpu.make_async_copy(
                    weight_hbm.at[:, source], weight_buffer.at[:, target], semaphores.at[2 * index + part]
                )
            )
    return copies


def project_chunks(normed_ref, copies, weight_buffer, cos_ref, sin_ref, doc_rows, out_refs):
    block, size = cos_ref.shape
    extra = doc_rows.shape[0]
    depth = weight_buffer.shape[0] // 2

    def product(begin, width):
        at = slice(begin * size, (begin + width) * size)
        return jnp.dot(
            normed_ref[0], weight_buffer[:depth, at], preferred_element_type=jnp.float32
        ) + jnp.dot(normed_ref[1], weight_buffer[depth:, at], preferred_element_type=jnp.float32)

    def rotated(piece):
        return piece * cos_ref[...] + pltpu.roll(piece, size // 2, 1) * sin_ref[...]

    for index, out_ref in enumerate(out_refs):
        copies[2 * index].wait()
        both = product(3 * index, 2)
        out_ref[:block, :] = rotated(both[:, :size])
        out_ref[block : 2 * block, :] = both[:, size:]
        out_ref[2 * block : 2 * block + extra, :] = doc_rows
        copies[2 * index + 1].wait()
        out_ref[2 * block + extra : 3 * block + extra, :] = rotated(product(3 * index + 2, 1))
        out_ref[3 * block + extra :, :] = doc_rows


def normalise_project_kernel(
    place_ref, a_near, a_far, b_near, b_far, squares_ref, gain_ref, cos_ref, sin_ref, weight_hbm,
    out_ref, normed_ref, weight_buffer, semaphores,
):
    rows = a_near.shape[0]
    features = 2 * gain_ref.shape[0] * gain_ref.shape[2]
    core, near_row = place_ref[0], place_ref[1]
    copies = weight_copies(
        place_ref[2], (0,), cos_ref.shape[1], weight_hbm, weight_buffer, semaphores
    )
    for copy in copies:
        copy.start()
    for shards, half in (((a_near, a_far), core), ((b_near, b_far), 1 - core)):
        gain = gain_ref[half]
        for shard, row in zip(shards, (near_row, 1 - near_row)):
            at = pl.ds(pl.multiple_of(row * rows, 16), rows)
            factor = lax.rsqrt(squares_ref[at, :] / features + EPS)
            normed_ref[half, at, :] = (shard[...].astype(jnp.float32) * factor * gain).astype(
                jnp.bfloat16
            )
    nothing = jnp.zeros((EXTRA, out_ref.shape[1]), jnp.float32)
    project_chunks(normed_ref, copies, weight_buffer, cos_ref, sin_ref, nothing, [out_ref])


def project_kernel(chunks, place_ref, normed_ref, docs_ref, cos_ref, sin_ref, weight_hbm, *refs):
    out_refs, (weight_buffer, semaphores) = refs[:-2], refs[-2:]
    copies = weight_copies(
        place_ref[0], chunks, cos_ref.shape[1], weight_hbm, weight_buffer, semaphores
    )
    for copy in copies:
        copy.start()
    project_chunks(
        normed_ref, copies, weight_buffer, cos_ref, sin_ref, docs_ref[...], out_refs
    )


def as_column(rows, count):
    lanes = rows.shape[1]
    pieces = []
    for begin in range(0, count, lanes):
        held = min(lanes, count - begin)
        at = lax.broadcasted_iota(jnp.int32, (held, lanes), 0)
        diagonal = at == lax.broadcasted_iota(jnp.int32, (held, lanes), 1)
        row = rows[begin // lanes : begin // lanes + 1, :]
        pieces.append(jnp.sum(jnp.where(diagonal, row, 0.0), axis=1, keepdims=True))
    return jnp.concatenate(pieces, axis=0)


def as_rows(column, lanes):
    count = column.shape[0]
    rows = []
    for begin in range(0, count, lanes):
        held = min(lanes, count - begin)
        at = lax.broadcasted_iota(jnp.int32, (held, lanes), 0)
        diagonal = at == lax.broadcasted_iota(jnp.int32, (held, lanes), 1)
        rows.append(
            jnp.sum(jnp.where(diagonal, column[begin : begin + held], 0.0), axis=0, keepdims=True)
        )
    return rows


def as_lanes(rows, count):
    lanes = rows.shape[1]
    return jnp.concatenate(
        [
            rows[begin // lanes : begin // lanes + 1, : min(lanes, count - begin)]
            for begin in range(0, count, lanes)
        ],
        axis=1,
    )


def softmax_part(scale, query_message, messages, causal):
    valid = [present for message, present in messages]
    messages = [message for message, present in messages]
    query = query_message[:-EXTRA]
    query_docs = as_column(query_message[-EXTRA:].astype(jnp.float32), query.shape[0])
    block = (messages[0].shape[0] - EXTRA) // 2
    keys = jnp.concatenate([message[:block] for message in messages], axis=0)
    values = jnp.concatenate([message[block : 2 * block] for message in messages], axis=0)
    key_docs = jnp.concatenate(
        [
            jnp.where(present, as_lanes(message[2 * block :].astype(jnp.float32), block), 0.0)
            for message, present in zip(messages, valid)
        ],
        axis=1,
    )
    visible = query_docs == key_docs
    if causal:
        shape = (query.shape[0], keys.shape[0])
        query_places = lax.broadcasted_iota(jnp.int32, shape, 0)
        key_places = lax.broadcasted_iota(jnp.int32, shape, 1)
        visible &= (key_places <= query_places) | (key_places >= block)
    scores = (
        lax.dot_general(query, keys, (((1,), (1,)), ((), ())), preferred_element_type=jnp.float32)
        * scale
    )
    top = jnp.max(jnp.where(visible, scores, LOW), axis=1, keepdims=True)
    exponentials = jnp.where(visible, jnp.exp(scores - top), 0.0)
    total = jnp.sum(exponentials, axis=1, keepdims=True)
    summed = jnp.dot(exponentials.astype(jnp.bfloat16), values, preferred_element_type=jnp.float32)
    some = total > 0.0
    safe = jnp.where(some, total, 1.0)
    return summed / safe, jnp.where(some, top + jnp.log(safe), LOW)


def as_message(output, logs, size):
    along = jnp.concatenate(as_rows(logs, size), axis=0)
    high = along.astype(jnp.bfloat16).astype(jnp.float32)
    middle = (along - high).astype(jnp.bfloat16).astype(jnp.float32)
    pieces = [output, high, middle, along - high - middle]
    pieces.append(jnp.zeros((EXTRA - 3 * along.shape[0], size), jnp.float32))
    return jnp.concatenate(pieces, axis=0).astype(jnp.bfloat16)


def logs_of(message, rows):
    tile = message[rows:].astype(jnp.float32)
    groups = pl.cdiv(rows, tile.shape[1])
    return as_column(sum(tile[k * groups : (k + 1) * groups] for k in range(3)), rows)


def parted(row, value):
    rows = value.shape[0] // 2
    first = row == 0
    return (
        jnp.where(first, value[:rows], value[rows:]),
        jnp.where(first, value[rows:], value[:rows]),
    )


def guest_kernel(
    scale, place_ref, one_ref, two_ref, first_ref, own_chunk, out_ref
):
    height = first_ref.shape[0]
    size = first_ref.shape[1]
    begin = (height - EXTRA) // 2

    def attend(index, query, messages):
        output, logs = softmax_part(scale, query, [(m, True) for m in messages], False)
        out_ref[index] = as_message(output, logs, size)

    @pl.when(place_ref[0] == 1)
    def down():
        keys = [first_ref[...], own_chunk[:height, :]]
        attend(0, two_ref[begin:, :], keys)
        attend(1, one_ref[begin:, :], keys)

    @pl.when(place_ref[0] == 2)
    def up():
        attend(0, first_ref[begin:, :], [one_ref[...], two_ref[...]])


def own_kernel(
    scale, place_ref, chunk_one, chunk_two, from_two_away, swapped, neighbour, one_up, unused_ref,
    out_ref, logs_ref,
):
    tok = place_ref[0]
    height = neighbour.shape[0]
    odd = (tok == 1) | (tok == 3)
    down = [(chunk_two[:height, :], True), (neighbour[...], odd)]
    up = [
        (chunk_one[:height, :], True),
        (jnp.where(tok == 2, swapped[...], one_up[...]), tok > 0),
        (from_two_away[...], tok == 2),
    ]
    for index, (query, messages) in enumerate(
        ((chunk_one[height:, :], down), (chunk_two[height:, :], up))
    ):
        out_ref[index], logs_ref[index] = softmax_part(scale, query, messages, True)


def merge_kernel(place_ref, out_ref, logs_ref, next_ref, three_ref, mine_ref, theirs_ref):
    block, size = out_ref.shape[1:]
    tok, row = place_ref[0], place_ref[1]
    at_two, at_three = tok == 2, tok == 3

    def joined(index, message, present):
        logs = logs_ref[index]
        guest = jnp.where(present, logs_of(message, block), LOW)
        top = jnp.maximum(logs, guest)
        weight, guest_weight = jnp.exp(logs - top), jnp.exp(guest - top)
        guest_output = jnp.where(present, message[:block].astype(jnp.float32), 0.0)
        output = out_ref[index] * weight + guest_output * guest_weight
        return (output / (weight + guest_weight)).astype(jnp.bfloat16)

    down = joined(0, jnp.where(at_two, next_ref[...], three_ref[...]), at_two | at_three)
    up = joined(1, next_ref[...], at_three)
    for index, output in enumerate((down, up)):
        columns = slice(index * size, (index + 1) * size)
        mine_ref[:, columns], theirs_ref[:, columns] = parted(row, output)


def attend_gathered(query, keys, values, places, starts, scale):
    heads, count, size = query.shape
    chunk = math.gcd(keys.shape[1], 1024)
    rounds = keys.shape[1] // chunk
    stacked = (
        keys.reshape(heads, rounds, chunk, size).transpose(1, 0, 2, 3),
        values.reshape(heads, rounds, chunk, size).transpose(1, 0, 2, 3),
        jnp.arange(rounds * chunk, dtype=jnp.int32).reshape(rounds, chunk),
    )

    def advance(state, blocks):
        running, totals, summed = state
        block_keys, block_values, key_places = blocks
        scores = (
            jnp.einsum("hqd,hkd->hqk", query, block_keys, preferred_element_type=jnp.float32) * scale
        )
        visible = (key_places[None, None, :] <= places[None, :, None]) & (
            key_places[None, None, :] >= starts[None, :, None]
        )
        masked = jnp.where(visible, scores, -jnp.inf)
        newest = jnp.maximum(running, jnp.max(masked, axis=2))
        factor = jnp.exp(running - newest)
        exponentials = jnp.where(visible, jnp.exp(masked - newest[:, :, None]), 0.0)
        totals = totals * factor + jnp.sum(exponentials, axis=2)
        summed = summed * factor[:, :, None] + jnp.einsum(
            "hqk,hkd->hqd", exponentials.astype(jnp.bfloat16), block_values,
            preferred_element_type=jnp.float32,
        )
        return (newest, totals, summed), None

    initial = (
        jnp.full((heads, count), -1e30, jnp.float32),
        jnp.zeros((heads, count), jnp.float32),
        jnp.zeros((heads, count, size), jnp.float32),
    )
    (running, totals, summed), unused = lax.scan(advance, initial, stacked)
    attended = (summed / totals[:, :, None]).astype(jnp.bfloat16)
    return attended.transpose(1, 0, 2).reshape(count, heads * size)


def in_vmem(count):
    return [pl.BlockSpec(memory_space=pltpu.VMEM)] * count


def per_device(activations, norm_gain, qkv_weight, doc_ids):
    rows, width = activations.shape
    span, local_heads, triple = qkv_weight.shape
    size = triple // 3
    pair = local_heads // 2
    block = 2 * rows
    toks = lax.axis_size("tok")
    tok, row, col = lax.axis_index("tok"), lax.axis_index("row"), lax.axis_index("col")
    chip, core = col >> 1, col & 1
    grid = [(r, c) for r in range(2) for c in range(4)]

    def by_col(value, flip):
        return lax.ppermute(value, "col", [(c, c ^ flip) for c in range(4)])

    def by_row(value):
        return lax.ppermute(value, "row", [(0, 1), (1, 0)])

    def ordered(index, own, other):
        first = index == 0
        return jnp.concatenate([jnp.where(first, own, other), jnp.where(first, other, own)])

    near = lax.ppermute(
        activations,
        ("row", "col"),
        [(r * 4 + c, (c // 2) * 4 + 2 * r + c % 2) for r, c in grid],
    )
    far = lax.ppermute(
        activations,
        ("row", "col"),
        [(r * 4 + c, (c // 2) * 4 + 2 * (1 - r) + c % 2) for r, c in grid],
    )
    widened = activations.astype(jnp.float32)
    squares = jnp.sum(widened * widened, axis=1)
    gain = norm_gain.astype(jnp.float32)
    message = jnp.concatenate([squares, gain])
    message, qkv_weight = lax.optimization_barrier((message, qkv_weight))
    flat_weight = qkv_weight.reshape(span, local_heads * triple)
    got = by_col(message, 1)
    squares = squares + got[:rows]
    gain = ordered(core, gain, got[rows:])
    got = by_col(jnp.concatenate([squares, gain]), 2)
    near, far, got, flat_weight = lax.optimization_barrier((near, far, got, flat_weight))
    near_other, far_other = by_col(near, 1), by_col(far, 1)
    squares = squares + got[:rows]
    gain = jnp.where(chip == row, gain, got[rows:]).reshape(2, 1, width)
    codes = doc_ids.astype(jnp.float32) + 1.0
    got = by_row(jnp.concatenate([squares, codes]))
    squares = ordered(row, squares, got[:rows]).reshape(block, 1)
    codes = ordered(row, codes, got[rows:])
    doc_rows = jnp.pad(codes, (0, EXTRA * size - block)).reshape(EXTRA, size)
    places = tok * block + jnp.arange(block, dtype=jnp.int32)
    cosine, sine = rotary_tables(places, size)

    taller = 3 * block + 2 * EXTRA
    break_at = 2 * block + EXTRA

    def projection(kernel, chunks, normalising):
        normed_shape = (jax.ShapeDtypeStruct((2, block, width), jnp.bfloat16),)
        return pl.pallas_call(
            kernel,
            out_shape=(jax.ShapeDtypeStruct((taller, size), jnp.float32),) * chunks
            + (normed_shape if normalising else ()),
            in_specs=[pl.BlockSpec(memory_space=pltpu.SMEM)]
            + in_vmem(8 if normalising else 4)
            + [pl.BlockSpec(memory_space=pltpu.HBM)],
            out_specs=tuple(in_vmem(chunks + 1 if normalising else chunks)),
            scratch_shapes=[
                pltpu.VMEM((span, chunks * triple), jnp.bfloat16),
                pltpu.SemaphoreType.DMA((2 * chunks,)),
            ],
            compiler_params=pltpu.CompilerParams(vmem_limit_bytes=6 * MIB),
            cost_estimate=pl.CostEstimate(flops=0, bytes_accessed=0, transcendentals=0),
        )

    away_column, own_column = (1 - row) * (pair * triple), row * (pair * triple)
    away, normed = projection(normalise_project_kernel, 1, True)(
        jnp.stack([core, chip, away_column]), near, far, near_other, far_other, squares, gain,
        cosine, sine, flat_weight,
    )
    arrived = [by_row(away.astype(jnp.float16))]
    (away,) = projection(lambda *refs: project_kernel((1,), *refs), 1, False)(
        away_column.reshape(1), normed, jnp.zeros_like(doc_rows), cosine, sine, flat_weight
    )
    arrived.append(by_row(away.astype(jnp.float16)))
    own = projection(lambda *refs: project_kernel((0, 1), *refs), 2, False)(
        own_column.reshape(1), normed, doc_rows, cosine, sine, flat_weight
    )
    scale = 1.0 / math.sqrt(size)

    def summed(chunk):
        return (own[chunk] + arrived[chunk].astype(jnp.float32)).astype(jnp.bfloat16)

    def gathered_attention():
        chunks = [summed(0), summed(1)]
        keys = jnp.stack([chunks[1][: 2 * block], chunks[0][: 2 * block]])
        everything = lax.all_gather(keys, "tok", axis=0, tiled=False).transpose(1, 0, 2, 3)
        all_codes = lax.all_gather(codes, "tok", axis=0, tiled=True)
        starts = jnp.sum((all_codes[None, :] < codes[:, None]).astype(jnp.int32), axis=1)
        together = attend_gathered(
            jnp.stack([chunk[break_at : break_at + block] for chunk in chunks]),
            everything[:, :, :block].reshape(pair, toks * block, size),
            everything[:, :, block:].reshape(pair, toks * block, size),
            places, starts, scale,
        )
        return parted(row, together)

    if toks == 4:
        places = jnp.stack([tok, row])

        def along_tok(value, pairs):
            return lax.ppermute(value, "tok", pairs)

        def keys_or_query(chunk, query_from):
            begin = jnp.where(tok == query_from, taller - break_at, 0)
            return lax.dynamic_slice_in_dim(chunk, begin.astype(jnp.uint32), break_at, 0)

        def on_place(kernel, out_shape, ins, unused=0):
            return pl.pallas_call(
                kernel,
                out_shape=out_shape,
                in_specs=[pl.BlockSpec(memory_space=pltpu.SMEM)]
                + in_vmem(ins - unused)
                + [pl.BlockSpec(memory_space=pl.ANY)] * unused,
                out_specs=jax.tree.map(lambda unused: in_vmem(1)[0], out_shape),
                compiler_params=pltpu.CompilerParams(vmem_limit_bytes=16 * MIB),
                cost_estimate=pl.CostEstimate(flops=0, bytes_accessed=0, transcendentals=0),
            )

        chunk_one = summed(0)
        two_away = along_tok(keys_or_query(chunk_one, 3), [(3, 1), (0, 2)])
        swapped = along_tok(keys_or_query(chunk_one, 2), [(2, 1), (1, 2)])
        across = by_col(chunk_one[:EXTRA], 1)
        arrived[1] = jnp.where(
            tok < toks,
            arrived[1].astype(jnp.float32),
            jnp.broadcast_to(across[:1].astype(jnp.float32), arrived[1].shape),
        )
        chunk_two = summed(1)
        neighbour = along_tok(keys_or_query(chunk_two, 3), [(0, 1), (2, 3), (3, 2)])
        one_up = along_tok(chunk_one[:break_at], [(0, 1), (2, 3)])

        guests = on_place(
            lambda *refs: guest_kernel(scale, *refs),
            jax.ShapeDtypeStruct((2, block + EXTRA, size), jnp.bfloat16),
            4,
        )(places, two_away, swapped, neighbour, chunk_two)
        from_next = along_tok(guests[0], [(1, 2), (2, 3)])
        from_three = along_tok(guests[1], [(1, 3)])
        output, logs = on_place(
            lambda *refs: own_kernel(scale, *refs),
            (
                jax.ShapeDtypeStruct((2, block, size), jnp.float32),
                jax.ShapeDtypeStruct((2, block, 1), jnp.float32),
            ),
            7,
            1,
        )(places, chunk_one, chunk_two, two_away, swapped, neighbour, one_up, guests)
        half = jax.ShapeDtypeStruct((rows, pair * size), jnp.bfloat16)
        mine, theirs = on_place(merge_kernel, (half, half), 4)(
            places, output, logs, from_next, from_three
        )
    else:
        mine, theirs = gathered_attention()

    theirs = by_row(theirs)
    return jnp.concatenate(
        [jnp.where(row == 0, mine, theirs), jnp.where(row == 0, theirs, mine)], axis=1
    )


def solution(mesh):
    placed = (P(("tok", "row"), "col"), P("col"), P("row", "col", None), P(("tok", "row")))
    return jax.shard_map(
        per_device, mesh=mesh, in_specs=placed, out_specs=P(("tok", "row"), "col"), check_vma=False
    )
```

```python
import math

import jax
import jax.numpy as jnp
from jax import lax
from jax.experimental import pallas as pl
from jax.experimental.pallas import tpu as pltpu
from jax.sharding import PartitionSpec as P

EPS = 1e-05
LOW = -1e30
EXTRA = 16
MIB = 1 << 20


def rotary_tables(places, head_size):
    half = head_size // 2
    spacing = jnp.arange(half).astype(jnp.float32) * (2.0 / head_size)
    inverse = jnp.power(10000.0, -spacing)
    angles = places.astype(jnp.float32)[:, None] * inverse[None, :]
    cosine, sine = jnp.cos(angles), jnp.sin(angles)
    return (
        jnp.concatenate([cosine, cosine], axis=1),
        jnp.concatenate([-sine, sine], axis=1),
    )


def project_chunk(normed_ref, weight_ref, key_column, query_column, cos_ref, sin_ref, doc_rows, out_ref):
    block, size = cos_ref.shape
    extra = doc_rows.shape[0]
    depth = weight_ref.shape[0] // 2

    def product(column, width):
        at = pl.ds(column if isinstance(column, int) else pl.multiple_of(column, size), width)
        return jnp.dot(
            normed_ref[0], weight_ref[:depth, at], preferred_element_type=jnp.float32
        ) + jnp.dot(normed_ref[1], weight_ref[depth:, at], preferred_element_type=jnp.float32)

    def rotated(piece):
        return piece * cos_ref[...] + pltpu.roll(piece, size // 2, 1) * sin_ref[...]

    both = product(key_column, 2 * size)
    out_ref[:block, :] = rotated(both[:, :size])
    out_ref[block : 2 * block, :] = both[:, size:]
    out_ref[2 * block : 2 * block + extra, :] = doc_rows
    out_ref[2 * block + extra : 3 * block + extra, :] = rotated(product(query_column, size))
    out_ref[3 * block + extra :, :] = doc_rows


def normalise_project_kernel(
    place_ref, a_near, a_far, b_near, b_far, squares_ref, gain_ref, cos_ref, sin_ref, weight_ref,
    out_ref, normed_ref, rest_hbm, semaphores,
):
    rows, size = a_near.shape[0], cos_ref.shape[1]
    features = 2 * gain_ref.shape[0] * gain_ref.shape[2]
    core, near_row, away, own = place_ref[0], place_ref[1], place_ref[2], place_ref[3]
    copies = [
        pltpu.make_async_copy(
            weight_ref.at[:, pl.ds(pl.multiple_of(source, size), width)],
            rest_hbm.at[:, pl.ds(target, width)],
            semaphores.at[index],
        )
        for index, (source, target, width) in enumerate(
            ((away + size, 0, 3 * size), (own, 3 * size, 6 * size))
        )
    ]
    for copy in copies:
        copy.start()
    for shards, half in (((a_near, a_far), core), ((b_near, b_far), 1 - core)):
        gain = gain_ref[half]
        for shard, row in zip(shards, (near_row, 1 - near_row)):
            at = pl.ds(pl.multiple_of(row * rows, 16), rows)
            factor = lax.rsqrt(squares_ref[at, :] / features + EPS)
            normed_ref[half, at, :] = (shard[...].astype(jnp.float32) * factor * gain).astype(
                jnp.bfloat16
            )
    nothing = jnp.zeros((EXTRA, size), jnp.float32)
    project_chunk(
        normed_ref, weight_ref, away + 4 * size, away, cos_ref, sin_ref, nothing, out_ref
    )
    for copy in copies:
        copy.wait()


def project_kernel(first, columns, normed_ref, docs_ref, cos_ref, sin_ref, rest_hbm, *refs):
    out_refs, (weight_buffer, semaphore) = refs[:-2], refs[-2:]
    copy = pltpu.make_async_copy(
        rest_hbm.at[:, pl.ds(first, weight_buffer.shape[1])], weight_buffer, semaphore
    )
    copy.start()
    copy.wait()
    for (key_column, query_column), out_ref in zip(columns, out_refs):
        project_chunk(
            normed_ref, weight_buffer, key_column, query_column, cos_ref, sin_ref, docs_ref[...],
            out_ref,
        )


def as_column(rows, count):
    lanes = rows.shape[1]
    pieces = []
    for begin in range(0, count, lanes):
        held = min(lanes, count - begin)
        at = lax.broadcasted_iota(jnp.int32, (held, lanes), 0)
        diagonal = at == lax.broadcasted_iota(jnp.int32, (held, lanes), 1)
        row = rows[begin // lanes : begin // lanes + 1, :]
        pieces.append(jnp.sum(jnp.where(diagonal, row, 0.0), axis=1, keepdims=True))
    return jnp.concatenate(pieces, axis=0)


def as_rows(column, lanes):
    count = column.shape[0]
    rows = []
    for begin in range(0, count, lanes):
        held = min(lanes, count - begin)
        at = lax.broadcasted_iota(jnp.int32, (held, lanes), 0)
        diagonal = at == lax.broadcasted_iota(jnp.int32, (held, lanes), 1)
        rows.append(
            jnp.sum(jnp.where(diagonal, column[begin : begin + held], 0.0), axis=0, keepdims=True)
        )
    return rows


def as_lanes(rows, count):
    lanes = rows.shape[1]
    return jnp.concatenate(
        [
            rows[begin // lanes : begin // lanes + 1, : min(lanes, count - begin)]
            for begin in range(0, count, lanes)
        ],
        axis=1,
    )


def softmax_part(scale, query_message, messages, causal):
    valid = [present for message, present in messages]
    messages = [message for message, present in messages]
    query = query_message[:-EXTRA]
    query_docs = as_column(query_message[-EXTRA:].astype(jnp.float32), query.shape[0])
    block = (messages[0].shape[0] - EXTRA) // 2
    keys = jnp.concatenate([message[:block] for message in messages], axis=0)
    values = jnp.concatenate([message[block : 2 * block] for message in messages], axis=0)
    key_docs = jnp.concatenate(
        [
            jnp.where(present, as_lanes(message[2 * block :].astype(jnp.float32), block), 0.0)
            for message, present in zip(messages, valid)
        ],
        axis=1,
    )
    visible = query_docs == key_docs
    if causal:
        shape = (query.shape[0], keys.shape[0])
        query_places = lax.broadcasted_iota(jnp.int32, shape, 0)
        key_places = lax.broadcasted_iota(jnp.int32, shape, 1)
        visible &= (key_places <= query_places) | (key_places >= block)
    scores = (
        lax.dot_general(query, keys, (((1,), (1,)), ((), ())), preferred_element_type=jnp.float32)
        * scale
    )
    top = jnp.max(jnp.where(visible, scores, LOW), axis=1, keepdims=True)
    exponentials = jnp.where(visible, jnp.exp(scores - top), 0.0)
    total = jnp.sum(exponentials, axis=1, keepdims=True)
    summed = jnp.dot(exponentials.astype(jnp.bfloat16), values, preferred_element_type=jnp.float32)
    some = total > 0.0
    safe = jnp.where(some, total, 1.0)
    return summed / safe, jnp.where(some, top + jnp.log(safe), LOW)


def as_message(output, logs, size):
    along = jnp.concatenate(as_rows(logs, size), axis=0)
    high = along.astype(jnp.bfloat16).astype(jnp.float32)
    middle = (along - high).astype(jnp.bfloat16).astype(jnp.float32)
    pieces = [output, high, middle, along - high - middle]
    pieces.append(jnp.zeros((EXTRA - 3 * along.shape[0], size), jnp.float32))
    return jnp.concatenate(pieces, axis=0).astype(jnp.bfloat16)


def logs_of(message, rows):
    tile = message[rows:].astype(jnp.float32)
    groups = pl.cdiv(rows, tile.shape[1])
    return as_column(sum(tile[k * groups : (k + 1) * groups] for k in range(3)), rows)


def parted(row, value):
    rows = value.shape[0] // 2
    first = row == 0
    return (
        jnp.where(first, value[:rows], value[rows:]),
        jnp.where(first, value[rows:], value[:rows]),
    )


def guest_kernel(
    scale, place_ref, two_away, swapped, neighbour, chunk_one, chunk_two, out_ref
):
    height, size = neighbour.shape
    begin = (height - EXTRA) // 2

    def attend(index, query, messages):
        output, logs = softmax_part(scale, query, [(m, True) for m in messages], False)
        out_ref[index] = as_message(output, logs, size)

    @pl.when(place_ref[0] == 0)
    def one_up():
        attend(0, neighbour[begin:, :], [chunk_one[:height, :]])

    @pl.when(place_ref[0] == 1)
    def down():
        keys = [neighbour[...], chunk_two[:height, :]]
        attend(1, two_away[begin:, :], keys)
        attend(0, swapped[begin:, :], keys)

    @pl.when(place_ref[0] == 2)
    def three_up():
        attend(0, neighbour[begin:, :], [two_away[...], swapped[...], chunk_one[:height, :]])


def own_kernel(
    scale, place_ref, chunk_one, chunk_two, two_away, swapped, neighbour, unused_ref, out_ref,
    logs_ref,
):
    tok = place_ref[0]
    height = neighbour.shape[0]
    down = [(chunk_two[:height, :], True), (neighbour[...], (tok == 1) | (tok == 3))]
    up = [(chunk_one[:height, :], True), (swapped[...], tok == 2), (two_away[...], tok == 2)]
    for index, (query, messages) in enumerate(
        ((chunk_one[height:, :], down), (chunk_two[height:, :], up))
    ):
        out_ref[index], logs_ref[index] = softmax_part(scale, query, messages, True)


def merge_kernel(place_ref, out_ref, logs_ref, next_ref, three_ref, mine_ref, theirs_ref):
    block, size = out_ref.shape[1:]
    tok, row = place_ref[0], place_ref[1]
    at_two, at_three = tok == 2, tok == 3

    def joined(index, message, present):
        logs = logs_ref[index]
        guest = jnp.where(present, logs_of(message, block), LOW)
        top = jnp.maximum(logs, guest)
        weight, guest_weight = jnp.exp(logs - top), jnp.exp(guest - top)
        guest_output = jnp.where(present, message[:block].astype(jnp.float32), 0.0)
        output = out_ref[index] * weight + guest_output * guest_weight
        return (output / (weight + guest_weight)).astype(jnp.bfloat16)

    down = joined(0, jnp.where(at_two, next_ref[...], three_ref[...]), at_two | at_three)
    up = joined(1, next_ref[...], (tok == 1) | at_three)
    for index, output in enumerate((down, up)):
        columns = slice(index * size, (index + 1) * size)
        mine_ref[:, columns], theirs_ref[:, columns] = parted(row, output)


def attend_gathered(query, keys, values, places, starts, scale):
    heads, count, size = query.shape
    chunk = math.gcd(keys.shape[1], 1024)
    rounds = keys.shape[1] // chunk
    stacked = (
        keys.reshape(heads, rounds, chunk, size).transpose(1, 0, 2, 3),
        values.reshape(heads, rounds, chunk, size).transpose(1, 0, 2, 3),
        jnp.arange(rounds * chunk, dtype=jnp.int32).reshape(rounds, chunk),
    )

    def advance(state, blocks):
        running, totals, summed = state
        block_keys, block_values, key_places = blocks
        scores = (
            jnp.einsum("hqd,hkd->hqk", query, block_keys, preferred_element_type=jnp.float32) * scale
        )
        visible = (key_places[None, None, :] <= places[None, :, None]) & (
            key_places[None, None, :] >= starts[None, :, None]
        )
        masked = jnp.where(visible, scores, -jnp.inf)
        newest = jnp.maximum(running, jnp.max(masked, axis=2))
        factor = jnp.exp(running - newest)
        exponentials = jnp.where(visible, jnp.exp(masked - newest[:, :, None]), 0.0)
        totals = totals * factor + jnp.sum(exponentials, axis=2)
        summed = summed * factor[:, :, None] + jnp.einsum(
            "hqk,hkd->hqd", exponentials.astype(jnp.bfloat16), block_values,
            preferred_element_type=jnp.float32,
        )
        return (newest, totals, summed), None

    initial = (
        jnp.full((heads, count), -1e30, jnp.float32),
        jnp.zeros((heads, count), jnp.float32),
        jnp.zeros((heads, count, size), jnp.float32),
    )
    (running, totals, summed), unused = lax.scan(advance, initial, stacked)
    attended = (summed / totals[:, :, None]).astype(jnp.bfloat16)
    return attended.transpose(1, 0, 2).reshape(count, heads * size)


def in_vmem(count):
    return [pl.BlockSpec(memory_space=pltpu.VMEM)] * count


def per_device(activations, norm_gain, qkv_weight, doc_ids):
    rows, width = activations.shape
    span, local_heads, triple = qkv_weight.shape
    size = triple // 3
    pair = local_heads // 2
    block = 2 * rows
    toks = lax.axis_size("tok")
    tok, row, col = lax.axis_index("tok"), lax.axis_index("row"), lax.axis_index("col")
    chip, core = col >> 1, col & 1
    grid = [(r, c) for r in range(2) for c in range(4)]

    def by_col(value, flip):
        return lax.ppermute(value, "col", [(c, c ^ flip) for c in range(4)])

    def by_row(value):
        return lax.ppermute(value, "row", [(0, 1), (1, 0)])

    def ordered(index, own, other):
        first = index == 0
        return jnp.concatenate([jnp.where(first, own, other), jnp.where(first, other, own)])

    near = lax.ppermute(
        activations,
        ("row", "col"),
        [(r * 4 + c, (c // 2) * 4 + 2 * r + c % 2) for r, c in grid],
    )
    far = lax.ppermute(
        activations,
        ("row", "col"),
        [(r * 4 + c, (c // 2) * 4 + 2 * (1 - r) + c % 2) for r, c in grid],
    )
    widened = activations.astype(jnp.float32)
    squares = jnp.sum(widened * widened, axis=1)
    gain = norm_gain.astype(jnp.float32)
    message = jnp.concatenate([squares, gain])
    message, qkv_weight = lax.optimization_barrier((message, qkv_weight))
    flat_weight = qkv_weight.reshape(span, local_heads * triple)
    got = by_col(message, 1)
    squares = squares + got[:rows]
    gain = ordered(core, gain, got[rows:])
    got = by_col(jnp.concatenate([squares, gain]), 2)
    near, far, got, flat_weight = lax.optimization_barrier((near, far, got, flat_weight))
    near_other, far_other = by_col(near, 1), by_col(far, 1)
    squares = squares + got[:rows]
    gain = jnp.where(chip == row, gain, got[rows:]).reshape(2, 1, width)
    codes = doc_ids.astype(jnp.float32) + 1.0
    got = by_row(jnp.concatenate([squares, codes]))
    squares = ordered(row, squares, got[:rows]).reshape(block, 1)
    codes = ordered(row, codes, got[rows:])
    doc_rows = jnp.pad(codes, (0, EXTRA * size - block)).reshape(EXTRA, size)
    places = tok * block + jnp.arange(block, dtype=jnp.int32)
    cosine, sine = rotary_tables(places, size)

    taller = 3 * block + 2 * EXTRA
    break_at = 2 * block + EXTRA

    partial_sums = jax.ShapeDtypeStruct((taller, size), jnp.float32)
    no_cost = pl.CostEstimate(flops=0, bytes_accessed=0, transcendentals=0)
    away, normed, rest = pl.pallas_call(
        normalise_project_kernel,
        out_shape=(
            partial_sums,
            jax.ShapeDtypeStruct((2, block, width), jnp.bfloat16),
            pltpu.HBM((span, 3 * triple), jnp.bfloat16),
        ),
        in_specs=[pl.BlockSpec(memory_space=pltpu.SMEM)] + in_vmem(9),
        out_specs=tuple(in_vmem(2)) + (pl.BlockSpec(memory_space=pltpu.HBM),),
        scratch_shapes=[pltpu.SemaphoreType.DMA((2,))],
        compiler_params=pltpu.CompilerParams(vmem_limit_bytes=12 * MIB),
        cost_estimate=no_cost,
    )(
        jnp.stack([core, chip, (1 - row) * (pair * triple), row * (pair * triple)]),
        near, far, near_other, far_other, squares, gain, cosine, sine, flat_weight,
    )

    def projection(first, columns, doc_rows):
        chunks = len(columns)
        return pl.pallas_call(
            lambda *refs: project_kernel(first, columns, *refs),
            out_shape=(partial_sums,) * chunks,
            in_specs=in_vmem(4) + [pl.BlockSpec(memory_space=pltpu.HBM)],
            out_specs=tuple(in_vmem(chunks)),
            scratch_shapes=[
                pltpu.VMEM((span, chunks * triple), jnp.bfloat16),
                pltpu.SemaphoreType.DMA(()),
            ],
            compiler_params=pltpu.CompilerParams(vmem_limit_bytes=8 * MIB),
            cost_estimate=no_cost,
        )(
            normed, doc_rows, cosine, sine, pltpu.with_memory_space_constraint(rest, pltpu.HBM)
        )

    arrived = [by_row(away.astype(jnp.float16))]
    (away,) = projection(0, [(0, 2 * size)], jnp.zeros_like(doc_rows))
    arrived.append(by_row(away.astype(jnp.float16)))
    own = projection(triple, [(4 * size, 0), (size, 3 * size)], doc_rows)
    scale = 1.0 / math.sqrt(size)

    def summed(chunk):
        return (own[chunk] + arrived[chunk].astype(jnp.float32)).astype(jnp.bfloat16)

    def gathered_attention():
        chunks = [summed(0), summed(1)]
        keys = jnp.stack([chunks[1][: 2 * block], chunks[0][: 2 * block]])
        everything = lax.all_gather(keys, "tok", axis=0, tiled=False).transpose(1, 0, 2, 3)
        all_codes = lax.all_gather(codes, "tok", axis=0, tiled=True)
        starts = jnp.sum((all_codes[None, :] < codes[:, None]).astype(jnp.int32), axis=1)
        together = attend_gathered(
            jnp.stack([chunk[break_at : break_at + block] for chunk in chunks]),
            everything[:, :, :block].reshape(pair, toks * block, size),
            everything[:, :, block:].reshape(pair, toks * block, size),
            places, starts, scale,
        )
        return parted(row, together)

    if toks == 4:
        places = jnp.stack([tok, row])

        def along_tok(value, pairs):
            return lax.ppermute(value, "tok", pairs)

        def keys_or_query(chunk, is_query):
            begin = jnp.where(is_query, taller - break_at, 0)
            return lax.dynamic_slice_in_dim(chunk, begin.astype(jnp.uint32), break_at, 0)

        def on_place(kernel, out_shape, ins, unused=0):
            return pl.pallas_call(
                kernel,
                out_shape=out_shape,
                in_specs=[pl.BlockSpec(memory_space=pltpu.SMEM)]
                + in_vmem(ins - unused)
                + [pl.BlockSpec(memory_space=pl.ANY)] * unused,
                out_specs=jax.tree.map(lambda unused: in_vmem(1)[0], out_shape),
                compiler_params=pltpu.CompilerParams(vmem_limit_bytes=16 * MIB),
                cost_estimate=pl.CostEstimate(flops=0, bytes_accessed=0, transcendentals=0),
            )

        chunk_one = summed(0)
        two_away = along_tok(keys_or_query(chunk_one, tok == 3), [(3, 1), (0, 2)])
        swapped = along_tok(keys_or_query(chunk_one, tok == 2), [(2, 1), (1, 2)])
        across = by_col(chunk_one[:EXTRA], 1)
        arrived[1] = jnp.where(
            tok < toks,
            arrived[1].astype(jnp.float32),
            jnp.broadcast_to(across[:1].astype(jnp.float32), arrived[1].shape),
        )
        chunk_two = summed(1)
        neighbour = along_tok(
            keys_or_query(chunk_two, (tok & 1) == 1), [(0, 1), (1, 0), (2, 3), (3, 2)]
        )
        guests = on_place(
            lambda *refs: guest_kernel(scale, *refs),
            jax.ShapeDtypeStruct((2, block + EXTRA, size), jnp.bfloat16),
            5,
        )(places, two_away, swapped, neighbour, chunk_one, chunk_two)
        from_three = along_tok(guests[1], [(1, 3)])
        from_next = along_tok(guests[0], [(0, 1), (1, 2), (2, 3)])
        output, logs = on_place(
            lambda *refs: own_kernel(scale, *refs),
            (
                jax.ShapeDtypeStruct((2, block, size), jnp.float32),
                jax.ShapeDtypeStruct((2, block, 1), jnp.float32),
            ),
            6,
            1,
        )(places, chunk_one, chunk_two, two_away, swapped, neighbour, guests)
        half = jax.ShapeDtypeStruct((rows, pair * size), jnp.bfloat16)
        mine, theirs = on_place(merge_kernel, (half, half), 4)(
            places, output, logs, from_next, from_three
        )
    else:
        mine, theirs = gathered_attention()

    theirs = by_row(theirs)
    return jnp.concatenate(
        [jnp.where(row == 0, mine, theirs), jnp.where(row == 0, theirs, mine)], axis=1
    )


def solution(mesh):
    placed = (P(("tok", "row"), "col"), P("col"), P("row", "col", None), P(("tok", "row")))
    return jax.shard_map(
        per_device, mesh=mesh, in_specs=placed, out_specs=P(("tok", "row"), "col"), check_vma=False
    )
```

```python
import math

import jax
import jax.numpy as jnp
from jax import lax
from jax.experimental import pallas as pl
from jax.experimental.pallas import tpu as pltpu
from jax.sharding import PartitionSpec as P

EPS = 1e-05
LOG2_E = math.log2(math.e)
LOW = -1e30
EXTRA = 16
MIB = 1 << 20
CHUNKS = ((4, 0), (1, 3))


def rotary_tables(places, head_size):
    half = head_size // 2
    spacing = jnp.arange(half).astype(jnp.float32) * (2.0 / head_size)
    inverse = jnp.power(10000.0, -spacing)
    angles = places.astype(jnp.float32)[:, None] * inverse[None, :]
    cosine, sine = jnp.cos(angles), jnp.sin(angles)
    return (
        jnp.concatenate([cosine, cosine], axis=1),
        jnp.concatenate([-sine, sine], axis=1),
    )


def project_chunk(normed_ref, weight_ref, key_column, query_column, cos_ref, sin_ref, doc_rows, out_ref):
    block, size = cos_ref.shape
    extra = doc_rows.shape[0]
    depth = weight_ref.shape[0] // 2

    def product(column, width):
        at = pl.ds(column if isinstance(column, int) else pl.multiple_of(column, size), width)
        return jnp.dot(
            normed_ref[0], weight_ref[:depth, at], preferred_element_type=jnp.float32
        ) + jnp.dot(normed_ref[1], weight_ref[depth:, at], preferred_element_type=jnp.float32)

    def rotated(piece):
        return piece * cos_ref[...] + pltpu.roll(piece, size // 2, 1) * sin_ref[...]

    both = product(key_column, 2 * size)
    out_ref[:block, :] = rotated(both[:, :size])
    out_ref[block : 2 * block, :] = both[:, size:]
    out_ref[2 * block : 2 * block + extra, :] = doc_rows
    out_ref[2 * block + extra : 3 * block + extra, :] = rotated(product(query_column, size))
    out_ref[3 * block + extra :, :] = doc_rows


def normalise_project_kernel(
    place_ref, a_near, a_far, b_near, b_far, squares_ref, gain_ref, cos_ref, sin_ref, weight_ref,
    one_ref, two_ref, normed_ref, own_hbm, semaphore,
):
    rows, size = a_near.shape[0], cos_ref.shape[1]
    features = 2 * gain_ref.shape[0] * gain_ref.shape[2]
    core, near_row, away, own = place_ref[0], place_ref[1], place_ref[2], place_ref[3]
    copy = pltpu.make_async_copy(
        weight_ref.at[:, pl.ds(pl.multiple_of(own, size), 6 * size)], own_hbm, semaphore
    )
    copy.start()
    for shards, half in (((a_near, a_far), core), ((b_near, b_far), 1 - core)):
        gain = gain_ref[half]
        for shard, row in zip(shards, (near_row, 1 - near_row)):
            at = pl.ds(pl.multiple_of(row * rows, 16), rows)
            factor = lax.rsqrt(squares_ref[at, :] / features + EPS)
            normed_ref[half, at, :] = (shard[...].astype(jnp.float32) * factor * gain).astype(
                jnp.bfloat16
            )
    nothing = jnp.zeros((EXTRA, size), jnp.float32)
    for chunk, (keys, query) in enumerate(CHUNKS):
        project_chunk(
            normed_ref, weight_ref, away + keys * size, away + query * size, cos_ref, sin_ref, nothing,
            (one_ref, two_ref)[chunk],
        )
    copy.wait()


def project_kernel(
    normed_ref, docs_ref, cos_ref, sin_ref, own_hbm, one_ref, two_ref, weight_buffer, semaphore
):
    copy = pltpu.make_async_copy(own_hbm, weight_buffer, semaphore)
    copy.start()
    copy.wait()
    size = cos_ref.shape[1]
    for chunk, (keys, query) in enumerate(CHUNKS):
        project_chunk(
            normed_ref, weight_buffer, keys * size, query * size, cos_ref, sin_ref, docs_ref[...],
            (one_ref, two_ref)[chunk],
        )


def as_column(rows, count):
    lanes = rows.shape[1]
    pieces = []
    for begin in range(0, count, lanes):
        held = min(lanes, count - begin)
        at = lax.broadcasted_iota(jnp.int32, (held, lanes), 0)
        diagonal = at == lax.broadcasted_iota(jnp.int32, (held, lanes), 1)
        row = rows[begin // lanes : begin // lanes + 1, :]
        pieces.append(jnp.sum(jnp.where(diagonal, row, 0.0), axis=1, keepdims=True))
    return jnp.concatenate(pieces, axis=0)


def as_rows(column, lanes):
    count = column.shape[0]
    rows = []
    for begin in range(0, count, lanes):
        held = min(lanes, count - begin)
        at = lax.broadcasted_iota(jnp.int32, (held, lanes), 0)
        diagonal = at == lax.broadcasted_iota(jnp.int32, (held, lanes), 1)
        rows.append(
            jnp.sum(jnp.where(diagonal, column[begin : begin + held], 0.0), axis=0, keepdims=True)
        )
    return rows


def as_lanes(rows, count):
    lanes = rows.shape[1]
    return jnp.concatenate(
        [
            rows[begin // lanes : begin // lanes + 1, : min(lanes, count - begin)]
            for begin in range(0, count, lanes)
        ],
        axis=1,
    )


def softmax_part(scale, query_message, messages, causal):
    valid = [present for message, present in messages]
    messages = [message for message, present in messages]
    query = query_message[:-EXTRA]
    query_docs = as_column(query_message[-EXTRA:].astype(jnp.float32), query.shape[0])
    block = (messages[0].shape[0] - EXTRA) // 2
    keys = jnp.concatenate([message[:block] for message in messages], axis=0)
    values = jnp.concatenate([message[block : 2 * block] for message in messages], axis=0)
    key_docs = jnp.concatenate(
        [
            jnp.where(present, as_lanes(message[2 * block :].astype(jnp.float32), block), 0.0)
            for message, present in zip(messages, valid)
        ],
        axis=1,
    )
    visible = query_docs == key_docs
    if causal:
        shape = (query.shape[0], keys.shape[0])
        query_places = lax.broadcasted_iota(jnp.int32, shape, 0)
        key_places = lax.broadcasted_iota(jnp.int32, shape, 1)
        visible &= (key_places <= query_places) | (key_places >= block)
    scores = lax.dot_general(
        query, keys, (((1,), (1,)), ((), ())), preferred_element_type=jnp.float32
    )
    top = jnp.max(jnp.where(visible, scores, LOW), axis=1, keepdims=True)
    exponentials = jnp.where(visible, jnp.exp2((scores - top) * (scale * LOG2_E)), 0.0)
    total = jnp.sum(exponentials, axis=1, keepdims=True)
    summed = jnp.dot(exponentials.astype(jnp.bfloat16), values, preferred_element_type=jnp.float32)
    some = total > 0.0
    safe = jnp.where(some, total, 1.0)
    return summed / safe, jnp.where(some, top * scale + jnp.log(safe), LOW)


def as_message(output, logs, size):
    along = jnp.concatenate(as_rows(logs, size), axis=0)
    high = along.astype(jnp.bfloat16).astype(jnp.float32)
    middle = (along - high).astype(jnp.bfloat16).astype(jnp.float32)
    pieces = [output, high, middle, along - high - middle]
    pieces.append(jnp.zeros((EXTRA - 3 * along.shape[0], size), jnp.float32))
    return jnp.concatenate(pieces, axis=0).astype(jnp.bfloat16)


def logs_of(message, rows):
    tile = message[rows:].astype(jnp.float32)
    groups = pl.cdiv(rows, tile.shape[1])
    return as_column(sum(tile[k * groups : (k + 1) * groups] for k in range(3)), rows)


def parted(row, value):
    rows = value.shape[0] // 2
    first = row == 0
    return (
        jnp.where(first, value[:rows], value[rows:]),
        jnp.where(first, value[rows:], value[:rows]),
    )


def guest_kernel(
    scale, place_ref, two_away, swapped, neighbour, chunk_one, chunk_two, out_ref
):
    height, size = neighbour.shape
    begin = (height - EXTRA) // 2

    def attend(index, query, messages):
        output, logs = softmax_part(scale, query, [(m, True) for m in messages], False)
        out_ref[index] = as_message(output, logs, size)

    @pl.when(place_ref[0] == 0)
    def one_up():
        attend(0, neighbour[begin:, :], [chunk_one[:height, :]])

    @pl.when(place_ref[0] == 1)
    def down():
        keys = [neighbour[...], chunk_two[:height, :]]
        attend(1, two_away[begin:, :], keys)
        attend(0, swapped[begin:, :], keys)

    @pl.when(place_ref[0] == 2)
    def three_up():
        attend(0, neighbour[begin:, :], [two_away[...], swapped[...], chunk_one[:height, :]])


def own_kernel(
    scale, place_ref, chunk_one, chunk_two, two_away, swapped, neighbour, unused_ref, out_ref,
    logs_ref,
):
    tok = place_ref[0]
    height = neighbour.shape[0]
    down = [(chunk_two[:height, :], True), (neighbour[...], (tok == 1) | (tok == 3))]
    up = [(chunk_one[:height, :], True), (swapped[...], tok == 2), (two_away[...], tok == 2)]
    for index, (query, messages) in enumerate(
        ((chunk_one[height:, :], down), (chunk_two[height:, :], up))
    ):
        out_ref[index], logs_ref[index] = softmax_part(scale, query, messages, True)


def merge_kernel(
    place_ref, out_ref, logs_ref, two_below_ref, one_ref, below_ref, mine_ref, theirs_ref
):
    block, size = out_ref.shape[1:]
    tok, row = place_ref[0], place_ref[1]
    at_two, at_three = tok == 2, tok == 3

    def joined(index, message, present):
        logs = logs_ref[index]
        guest = jnp.where(present, logs_of(message, block), LOW)
        top = jnp.maximum(logs, guest)
        weight, guest_weight = jnp.exp(logs - top), jnp.exp(guest - top)
        guest_output = jnp.where(present, message[:block].astype(jnp.float32), 0.0)
        output = out_ref[index] * weight + guest_output * guest_weight
        return (output / (weight + guest_weight)).astype(jnp.bfloat16)

    down = joined(0, jnp.where(at_two, one_ref[...], two_below_ref[...]), at_two | at_three)
    up = joined(1, below_ref[...], (tok == 1) | at_three)
    for index, output in enumerate((down, up)):
        columns = slice(index * size, (index + 1) * size)
        mine_ref[:, columns], theirs_ref[:, columns] = parted(row, output)


def attend_gathered(query, keys, values, places, starts, scale):
    heads, count, size = query.shape
    chunk = math.gcd(keys.shape[1], 1024)
    rounds = keys.shape[1] // chunk
    stacked = (
        keys.reshape(heads, rounds, chunk, size).transpose(1, 0, 2, 3),
        values.reshape(heads, rounds, chunk, size).transpose(1, 0, 2, 3),
        jnp.arange(rounds * chunk, dtype=jnp.int32).reshape(rounds, chunk),
    )

    def advance(state, blocks):
        running, totals, summed = state
        block_keys, block_values, key_places = blocks
        scores = (
            jnp.einsum("hqd,hkd->hqk", query, block_keys, preferred_element_type=jnp.float32) * scale
        )
        visible = (key_places[None, None, :] <= places[None, :, None]) & (
            key_places[None, None, :] >= starts[None, :, None]
        )
        masked = jnp.where(visible, scores, -jnp.inf)
        newest = jnp.maximum(running, jnp.max(masked, axis=2))
        factor = jnp.exp(running - newest)
        exponentials = jnp.where(visible, jnp.exp(masked - newest[:, :, None]), 0.0)
        totals = totals * factor + jnp.sum(exponentials, axis=2)
        summed = summed * factor[:, :, None] + jnp.einsum(
            "hqk,hkd->hqd", exponentials.astype(jnp.bfloat16), block_values,
            preferred_element_type=jnp.float32,
        )
        return (newest, totals, summed), None

    initial = (
        jnp.full((heads, count), -1e30, jnp.float32),
        jnp.zeros((heads, count), jnp.float32),
        jnp.zeros((heads, count, size), jnp.float32),
    )
    (running, totals, summed), unused = lax.scan(advance, initial, stacked)
    attended = (summed / totals[:, :, None]).astype(jnp.bfloat16)
    return attended.transpose(1, 0, 2).reshape(count, heads * size)


def in_vmem(count):
    return [pl.BlockSpec(memory_space=pltpu.VMEM)] * count


def per_device(activations, norm_gain, qkv_weight, doc_ids):
    rows, width = activations.shape
    span, local_heads, triple = qkv_weight.shape
    size = triple // 3
    pair = local_heads // 2
    block = 2 * rows
    toks = lax.axis_size("tok")
    tok, row, col = lax.axis_index("tok"), lax.axis_index("row"), lax.axis_index("col")
    chip, core = col >> 1, col & 1
    grid = [(r, c) for r in range(2) for c in range(4)]

    def by_col(value, flip):
        return lax.ppermute(value, "col", [(c, c ^ flip) for c in range(4)])

    def by_row(value):
        return lax.ppermute(value, "row", [(0, 1), (1, 0)])

    def ordered(index, own, other):
        first = index == 0
        return jnp.concatenate([jnp.where(first, own, other), jnp.where(first, other, own)])

    near = lax.ppermute(
        activations,
        ("row", "col"),
        [(r * 4 + c, (c // 2) * 4 + 2 * r + c % 2) for r, c in grid],
    )
    far = lax.ppermute(
        activations,
        ("row", "col"),
        [(r * 4 + c, (c // 2) * 4 + 2 * (1 - r) + c % 2) for r, c in grid],
    )
    widened = activations.astype(jnp.float32)
    squares = jnp.sum(widened * widened, axis=1)
    gain = norm_gain.astype(jnp.float32)
    message = jnp.concatenate([squares, gain])
    message, qkv_weight = lax.optimization_barrier((message, qkv_weight))
    flat_weight = qkv_weight.reshape(span, local_heads * triple)
    got = by_col(message, 1)
    squares = squares + got[:rows]
    gain = ordered(core, gain, got[rows:])
    got = by_col(jnp.concatenate([squares, gain]), 2)
    near, far, got, flat_weight = lax.optimization_barrier((near, far, got, flat_weight))
    near_other, far_other = by_col(near, 1), by_col(far, 1)
    squares = squares + got[:rows]
    gain = jnp.where(chip == row, gain, got[rows:]).reshape(2, 1, width)
    codes = doc_ids.astype(jnp.float32) + 1.0
    got = by_row(jnp.concatenate([squares, codes]))
    squares = ordered(row, squares, got[:rows]).reshape(block, 1)
    codes = ordered(row, codes, got[rows:])
    doc_rows = jnp.pad(codes, (0, EXTRA * size - block)).reshape(EXTRA, size)
    places = tok * block + jnp.arange(block, dtype=jnp.int32)
    cosine, sine = rotary_tables(places, size)

    taller = 3 * block + 2 * EXTRA
    break_at = 2 * block + EXTRA

    partial_sums = jax.ShapeDtypeStruct((taller, size), jnp.float32)
    no_cost = pl.CostEstimate(flops=0, bytes_accessed=0, transcendentals=0)
    *away, normed, own_weight = pl.pallas_call(
        normalise_project_kernel,
        out_shape=(
            partial_sums,
            partial_sums,
            jax.ShapeDtypeStruct((2, block, width), jnp.bfloat16),
            pltpu.HBM((span, pair * triple), jnp.bfloat16),
        ),
        in_specs=[pl.BlockSpec(memory_space=pltpu.SMEM)] + in_vmem(9),
        out_specs=tuple(in_vmem(3)) + (pl.BlockSpec(memory_space=pltpu.HBM),),
        scratch_shapes=[pltpu.SemaphoreType.DMA(())],
        compiler_params=pltpu.CompilerParams(vmem_limit_bytes=12 * MIB),
        cost_estimate=no_cost,
    )(
        jnp.stack([core, chip, (1 - row) * (pair * triple), row * (pair * triple)]),
        near, far, near_other, far_other, squares, gain, cosine, sine, flat_weight,
    )
    arrived = [by_row(chunk.astype(jnp.float16)) for chunk in away]
    own = pl.pallas_call(
        project_kernel,
        out_shape=(partial_sums, partial_sums),
        in_specs=in_vmem(4) + [pl.BlockSpec(memory_space=pltpu.HBM)],
        out_specs=tuple(in_vmem(2)),
        scratch_shapes=[
            pltpu.VMEM((span, pair * triple), jnp.bfloat16),
            pltpu.SemaphoreType.DMA(()),
        ],
        compiler_params=pltpu.CompilerParams(vmem_limit_bytes=8 * MIB),
        cost_estimate=no_cost,
    )(
        normed, doc_rows, cosine, sine, pltpu.with_memory_space_constraint(own_weight, pltpu.HBM)
    )
    scale = 1.0 / math.sqrt(size)

    def summed(chunk):
        return (own[chunk] + arrived[chunk].astype(jnp.float32)).astype(jnp.bfloat16)

    def gathered_attention():
        chunks = [summed(0), summed(1)]
        keys = jnp.stack([chunks[1][: 2 * block], chunks[0][: 2 * block]])
        everything = lax.all_gather(keys, "tok", axis=0, tiled=False).transpose(1, 0, 2, 3)
        all_codes = lax.all_gather(codes, "tok", axis=0, tiled=True)
        starts = jnp.sum((all_codes[None, :] < codes[:, None]).astype(jnp.int32), axis=1)
        together = attend_gathered(
            jnp.stack([chunk[break_at : break_at + block] for chunk in chunks]),
            everything[:, :, :block].reshape(pair, toks * block, size),
            everything[:, :, block:].reshape(pair, toks * block, size),
            places, starts, scale,
        )
        return parted(row, together)

    if toks == 4:
        places = jnp.stack([tok, row])

        def along_tok(value, pairs):
            return lax.ppermute(value, "tok", pairs)

        def keys_or_query(chunk, is_query):
            begin = jnp.where(is_query, taller - break_at, 0)
            return lax.dynamic_slice_in_dim(chunk, begin.astype(jnp.uint32), break_at, 0)

        def on_place(kernel, out_shape, ins, unused=0):
            return pl.pallas_call(
                kernel,
                out_shape=out_shape,
                in_specs=[pl.BlockSpec(memory_space=pltpu.SMEM)]
                + in_vmem(ins - unused)
                + [pl.BlockSpec(memory_space=pl.ANY)] * unused,
                out_specs=jax.tree.map(lambda unused: in_vmem(1)[0], out_shape),
                compiler_params=pltpu.CompilerParams(vmem_limit_bytes=16 * MIB),
                cost_estimate=pl.CostEstimate(flops=0, bytes_accessed=0, transcendentals=0),
            )

        chunk_one = summed(0)
        two_away = along_tok(keys_or_query(chunk_one, tok == 3), [(0, 2), (3, 1), (1, 0), (2, 3)])
        swapped = along_tok(keys_or_query(chunk_one, tok == 2), [(1, 2), (2, 1), (0, 0), (3, 3)])
        across = by_col(chunk_one[:EXTRA], 1)
        arrived[1] = jnp.where(
            tok < toks,
            arrived[1].astype(jnp.float32),
            jnp.broadcast_to(across[:1].astype(jnp.float32), arrived[1].shape),
        )
        chunk_two = summed(1)
        neighbour = along_tok(
            keys_or_query(chunk_two, (tok & 1) == 1), [(0, 1), (1, 0), (2, 3), (3, 2)]
        )
        guests = on_place(
            lambda *refs: guest_kernel(scale, *refs),
            jax.ShapeDtypeStruct((2, block + EXTRA, size), jnp.bfloat16),
            5,
        )(places, two_away, swapped, neighbour, chunk_one, chunk_two)
        from_two_below = along_tok(guests[1], [(t, t ^ 2) for t in range(4)])
        from_one = along_tok(guests[0], [(t, t ^ 3) for t in range(4)])
        from_below = along_tok(guests[0], [(t, t ^ 1) for t in range(4)])
        output, logs = on_place(
            lambda *refs: own_kernel(scale, *refs),
            (
                jax.ShapeDtypeStruct((2, block, size), jnp.float32),
                jax.ShapeDtypeStruct((2, block, 1), jnp.float32),
            ),
            6,
            1,
        )(places, chunk_one, chunk_two, two_away, swapped, neighbour, guests)
        half = jax.ShapeDtypeStruct((rows, pair * size), jnp.bfloat16)
        mine, theirs = on_place(merge_kernel, (half, half), 5)(
            places, output, logs, from_two_below, from_one, from_below
        )
    else:
        mine, theirs = gathered_attention()

    theirs = by_row(theirs)
    return jnp.concatenate(
        [jnp.where(row == 0, mine, theirs), jnp.where(row == 0, theirs, mine)], axis=1
    )


def solution(mesh):
    placed = (P(("tok", "row"), "col"), P("col"), P("row", "col", None), P(("tok", "row")))
    return jax.shard_map(
        per_device, mesh=mesh, in_specs=placed, out_specs=P(("tok", "row"), "col"), check_vma=False
    )
```

```python
import math

import jax
import jax.numpy as jnp
from jax import lax
from jax.experimental import pallas as pl
from jax.experimental.pallas import tpu as pltpu
from jax.sharding import PartitionSpec as P

EPS = 1e-05
LOG2_E = math.log2(math.e)
LOW = -1e30
EXTRA = 16
MIB = 1 << 20
CHUNKS = ((4, 0), (1, 3))


def rotary_tables(places, head_size):
    half = head_size // 2
    spacing = jnp.arange(half).astype(jnp.float32) * (2.0 / head_size)
    inverse = jnp.power(10000.0, -spacing)
    angles = places.astype(jnp.float32)[:, None] * inverse[None, :]
    cosine, sine = jnp.cos(angles), jnp.sin(angles)
    return (
        jnp.concatenate([cosine, cosine], axis=1),
        jnp.concatenate([-sine, sine], axis=1),
    )


def project_chunk(normed_ref, weight_ref, key_column, query_column, cos_ref, sin_ref, doc_rows, out_ref):
    block, size = cos_ref.shape
    extra = doc_rows.shape[0]
    depth = weight_ref.shape[0] // 2

    def product(column, width):
        at = pl.ds(column if isinstance(column, int) else pl.multiple_of(column, size), width)
        return jnp.dot(
            normed_ref[0], weight_ref[:depth, at], preferred_element_type=jnp.float32
        ) + jnp.dot(normed_ref[1], weight_ref[depth:, at], preferred_element_type=jnp.float32)

    def rotated(piece):
        return piece * cos_ref[...] + pltpu.roll(piece, size // 2, 1) * sin_ref[...]

    both = product(key_column, 2 * size)
    out_ref[:block, :] = rotated(both[:, :size])
    out_ref[block : 2 * block, :] = both[:, size:]
    out_ref[2 * block : 2 * block + extra, :] = doc_rows
    out_ref[2 * block + extra : 3 * block + extra, :] = rotated(product(query_column, size))
    out_ref[3 * block + extra :, :] = doc_rows


def normalise_project_kernel(
    place_ref, a_near, a_far, b_near, b_far, squares_ref, gain_ref, cos_ref, sin_ref, weight_ref,
    one_ref, two_ref, normed_ref, own_hbm, semaphore,
):
    rows, size = a_near.shape[0], cos_ref.shape[1]
    features = 2 * gain_ref.shape[0] * gain_ref.shape[2]
    core, near_row, away, own = place_ref[0], place_ref[1], place_ref[2], place_ref[3]
    copy = pltpu.make_async_copy(
        weight_ref.at[:, pl.ds(pl.multiple_of(own, size), 6 * size)], own_hbm, semaphore
    )
    copy.start()
    for shards, half in (((a_near, a_far), core), ((b_near, b_far), 1 - core)):
        gain = gain_ref[half]
        for shard, row in zip(shards, (near_row, 1 - near_row)):
            at = pl.ds(pl.multiple_of(row * rows, 16), rows)
            factor = lax.rsqrt(squares_ref[at, :] / features + EPS)
            normed_ref[half, at, :] = (shard[...].astype(jnp.float32) * factor * gain).astype(
                jnp.bfloat16
            )
    nothing = jnp.zeros((EXTRA, size), jnp.float32)
    for chunk, (keys, query) in enumerate(CHUNKS):
        project_chunk(
            normed_ref, weight_ref, away + keys * size, away + query * size, cos_ref, sin_ref, nothing,
            (one_ref, two_ref)[chunk],
        )
    copy.wait()


def project_kernel(
    normed_ref, docs_ref, cos_ref, sin_ref, own_hbm, one_ref, two_ref, weight_buffer, semaphore
):
    copy = pltpu.make_async_copy(own_hbm, weight_buffer, semaphore)
    copy.start()
    copy.wait()
    size = cos_ref.shape[1]
    for chunk, (keys, query) in enumerate(CHUNKS):
        project_chunk(
            normed_ref, weight_buffer, keys * size, query * size, cos_ref, sin_ref, docs_ref[...],
            (one_ref, two_ref)[chunk],
        )


def as_column(rows, count):
    lanes = rows.shape[1]
    pieces = []
    for begin in range(0, count, lanes):
        held = min(lanes, count - begin)
        at = lax.broadcasted_iota(jnp.int32, (held, lanes), 0)
        diagonal = at == lax.broadcasted_iota(jnp.int32, (held, lanes), 1)
        row = rows[begin // lanes : begin // lanes + 1, :]
        pieces.append(jnp.sum(jnp.where(diagonal, row, 0.0), axis=1, keepdims=True))
    return jnp.concatenate(pieces, axis=0)


def as_rows(column, lanes):
    count = column.shape[0]
    rows = []
    for begin in range(0, count, lanes):
        held = min(lanes, count - begin)
        at = lax.broadcasted_iota(jnp.int32, (held, lanes), 0)
        diagonal = at == lax.broadcasted_iota(jnp.int32, (held, lanes), 1)
        rows.append(
            jnp.sum(jnp.where(diagonal, column[begin : begin + held], 0.0), axis=0, keepdims=True)
        )
    return rows


def as_lanes(rows, count):
    lanes = rows.shape[1]
    return jnp.concatenate(
        [
            rows[begin // lanes : begin // lanes + 1, : min(lanes, count - begin)]
            for begin in range(0, count, lanes)
        ],
        axis=1,
    )


def softmax_part(scale, query_message, messages, causal):
    valid = [present for message, present in messages]
    messages = [message for message, present in messages]
    query = query_message[:-EXTRA]
    query_docs = as_column(query_message[-EXTRA:].astype(jnp.float32), query.shape[0])
    block = (messages[0].shape[0] - EXTRA) // 2
    keys = jnp.concatenate([message[:block] for message in messages], axis=0)
    values = jnp.concatenate([message[block : 2 * block] for message in messages], axis=0)
    key_docs = jnp.concatenate(
        [
            jnp.where(present, as_lanes(message[2 * block :].astype(jnp.float32), block), 0.0)
            for message, present in zip(messages, valid)
        ],
        axis=1,
    )
    visible = query_docs == key_docs
    if causal:
        shape = (query.shape[0], keys.shape[0])
        query_places = lax.broadcasted_iota(jnp.int32, shape, 0)
        key_places = lax.broadcasted_iota(jnp.int32, shape, 1)
        visible &= (key_places <= query_places) | (key_places >= block)
    scores = lax.dot_general(
        query, keys, (((1,), (1,)), ((), ())), preferred_element_type=jnp.float32
    )
    top = jnp.max(jnp.where(visible, scores, LOW), axis=1, keepdims=True)
    exponentials = jnp.where(visible, jnp.exp2((scores - top) * (scale * LOG2_E)), 0.0)
    total = jnp.sum(exponentials, axis=1, keepdims=True)
    summed = jnp.dot(exponentials.astype(jnp.bfloat16), values, preferred_element_type=jnp.float32)
    some = total > 0.0
    safe = jnp.where(some, total, 1.0)
    return summed / safe, jnp.where(some, top * scale + jnp.log(safe), LOW)


def as_message(output, logs, size):
    along = jnp.concatenate(as_rows(logs, size), axis=0)
    high = along.astype(jnp.bfloat16).astype(jnp.float32)
    middle = (along - high).astype(jnp.bfloat16).astype(jnp.float32)
    pieces = [output, high, middle, along - high - middle]
    pieces.append(jnp.zeros((EXTRA - 3 * along.shape[0], size), jnp.float32))
    return jnp.concatenate(pieces, axis=0).astype(jnp.bfloat16)


def logs_of(message, rows):
    tile = message[rows:].astype(jnp.float32)
    groups = pl.cdiv(rows, tile.shape[1])
    return as_column(sum(tile[k * groups : (k + 1) * groups] for k in range(3)), rows)


def parted(row, value):
    rows = value.shape[0] // 2
    first = row == 0
    return (
        jnp.where(first, value[:rows], value[rows:]),
        jnp.where(first, value[rows:], value[:rows]),
    )


def joined(first, second):
    (output, logs), (other, other_logs) = first, second
    top = jnp.maximum(logs, other_logs)
    weight, other_weight = jnp.exp(logs - top), jnp.exp(other_logs - top)
    total = weight + other_weight
    return (output * weight + other * other_weight) / total, top + jnp.log(total)


def own_block_kernel(scale, place_ref, chunk_one, chunk_two, out_ref, logs_ref):
    for index, (queries, keys) in enumerate(((chunk_one, chunk_two), (chunk_two, chunk_one))):
        height = keys.shape[0] - out_ref.shape[1] - EXTRA
        out_ref[index], logs_ref[index] = softmax_part(
            scale, queries[height:, :], [(keys[:height, :], True)], True
        )


def guest_kernel(
    scale, place_ref, swapped, two_away, neighbour, chunk_one, chunk_two, unused_ref, out_ref
):
    height, size = neighbour.shape
    begin = (height - EXTRA) // 2

    def attend(index, query, messages):
        output, logs = softmax_part(scale, query, [(m, True) for m in messages], False)
        for owner, (a, b) in enumerate(
            zip(parted(place_ref[1], output), parted(place_ref[1], logs))
        ):
            out_ref[index, owner] = as_message(a, b, size)

    @pl.when(place_ref[0] == 0)
    def one_up():
        attend(0, neighbour[begin:, :], [chunk_one[:height, :]])

    @pl.when(place_ref[0] == 1)
    def down():
        keys = [neighbour[...], chunk_two[:height, :]]
        attend(1, two_away[begin:, :], keys)
        attend(0, swapped[begin:, :], keys)

    @pl.when(place_ref[0] == 2)
    def three_up():
        attend(0, neighbour[begin:, :], [two_away[...], swapped[...], chunk_one[:height, :]])


def own_rest_kernel(
    scale, place_ref, own_out, own_logs, chunk_one, chunk_two, swapped, two_away, neighbour,
    unused_ref, mine_ref, logs_ref, theirs_ref, out_buffer, logs_buffer,
):
    tok, row = place_ref[0], place_ref[1]
    height, size = neighbour.shape
    out_buffer[...] = own_out[...]
    logs_buffer[...] = own_logs[...]

    def add(index, query, messages):
        part = softmax_part(scale, query, [(m, True) for m in messages], False)
        out_buffer[index], logs_buffer[index] = joined(
            (own_out[index], own_logs[index]), part
        )

    @pl.when((tok == 1) | (tok == 3))
    def down():
        add(0, chunk_one[height:, :], [neighbour[...]])

    @pl.when(tok == 2)
    def up():
        add(1, chunk_two[height:, :], [swapped[...], two_away[...]])

    for index in range(2):
        mine_ref[index], theirs = parted(row, out_buffer[index])
        logs_ref[index], their_logs = parted(row, logs_buffer[index])
        theirs_ref[index] = as_message(theirs, their_logs, size)


def merge_kernel(
    place_ref, mine_ref, logs_ref, partner_ref, three_same, three_cross, below_same, below_cross,
    out_ref,
):
    rows, size = mine_ref.shape[1:]
    tok, row = place_ref[0], place_ref[1]

    def from_message(message):
        return message[:rows].astype(jnp.float32), logs_of(message, rows)

    def present(message, condition):
        output, logs = from_message(message)
        return jnp.where(condition, output, 0.0), jnp.where(condition, logs, LOW)

    for mine, three, below in ((True, three_same, below_same), (False, three_cross, below_cross)):
        begin = jnp.where(row == 0, 0, 2) if mine else jnp.where(row == 0, 2, 0)
        guests = (
            present(jnp.where(tok == 2, below[...], three[...]), tok >= 2),
            present(below[...], (tok == 1) | (tok == 3)),
        )
        for index, guest in enumerate(guests):
            own = (mine_ref[index], logs_ref[index]) if mine else from_message(partner_ref[index])
            at = pl.ds(pl.multiple_of((begin + index) * size, size), size)
            out_ref[:, at] = joined(own, guest)[0].astype(jnp.bfloat16)


def attend_gathered(query, keys, values, places, starts, scale):
    heads, count, size = query.shape
    chunk = math.gcd(keys.shape[1], 1024)
    rounds = keys.shape[1] // chunk
    stacked = (
        keys.reshape(heads, rounds, chunk, size).transpose(1, 0, 2, 3),
        values.reshape(heads, rounds, chunk, size).transpose(1, 0, 2, 3),
        jnp.arange(rounds * chunk, dtype=jnp.int32).reshape(rounds, chunk),
    )

    def advance(state, blocks):
        running, totals, summed = state
        block_keys, block_values, key_places = blocks
        scores = (
            jnp.einsum("hqd,hkd->hqk", query, block_keys, preferred_element_type=jnp.float32) * scale
        )
        visible = (key_places[None, None, :] <= places[None, :, None]) & (
            key_places[None, None, :] >= starts[None, :, None]
        )
        masked = jnp.where(visible, scores, -jnp.inf)
        newest = jnp.maximum(running, jnp.max(masked, axis=2))
        factor = jnp.exp(running - newest)
        exponentials = jnp.where(visible, jnp.exp(masked - newest[:, :, None]), 0.0)
        totals = totals * factor + jnp.sum(exponentials, axis=2)
        summed = summed * factor[:, :, None] + jnp.einsum(
            "hqk,hkd->hqd", exponentials.astype(jnp.bfloat16), block_values,
            preferred_element_type=jnp.float32,
        )
        return (newest, totals, summed), None

    initial = (
        jnp.full((heads, count), -1e30, jnp.float32),
        jnp.zeros((heads, count), jnp.float32),
        jnp.zeros((heads, count, size), jnp.float32),
    )
    (running, totals, summed), unused = lax.scan(advance, initial, stacked)
    attended = (summed / totals[:, :, None]).astype(jnp.bfloat16)
    return attended.transpose(1, 0, 2).reshape(count, heads * size)


def in_vmem(count):
    return [pl.BlockSpec(memory_space=pltpu.VMEM)] * count


def per_device(activations, norm_gain, qkv_weight, doc_ids):
    rows, width = activations.shape
    span, local_heads, triple = qkv_weight.shape
    size = triple // 3
    pair = local_heads // 2
    block = 2 * rows
    toks = lax.axis_size("tok")
    tok, row, col = lax.axis_index("tok"), lax.axis_index("row"), lax.axis_index("col")
    chip, core = col >> 1, col & 1
    grid = [(r, c) for r in range(2) for c in range(4)]

    def by_col(value, flip):
        return lax.ppermute(value, "col", [(c, c ^ flip) for c in range(4)])

    def by_row(value):
        return lax.ppermute(value, "row", [(0, 1), (1, 0)])

    def ordered(index, own, other):
        first = index == 0
        return jnp.concatenate([jnp.where(first, own, other), jnp.where(first, other, own)])

    near = lax.ppermute(
        activations,
        ("row", "col"),
        [(r * 4 + c, (c // 2) * 4 + 2 * r + c % 2) for r, c in grid],
    )
    far = lax.ppermute(
        activations,
        ("row", "col"),
        [(r * 4 + c, (c // 2) * 4 + 2 * (1 - r) + c % 2) for r, c in grid],
    )
    widened = activations.astype(jnp.float32)
    squares = jnp.sum(widened * widened, axis=1)
    gain = norm_gain.astype(jnp.float32)
    message = jnp.concatenate([squares, gain])
    message, qkv_weight = lax.optimization_barrier((message, qkv_weight))
    flat_weight = qkv_weight.reshape(span, local_heads * triple)
    got = by_col(message, 1)
    squares = squares + got[:rows]
    gain = ordered(core, gain, got[rows:])
    got = by_col(jnp.concatenate([squares, gain]), 2)
    near, far, got, flat_weight = lax.optimization_barrier((near, far, got, flat_weight))
    near_other, far_other = by_col(near, 1), by_col(far, 1)
    squares = squares + got[:rows]
    gain = jnp.where(chip == row, gain, got[rows:]).reshape(2, 1, width)
    codes = doc_ids.astype(jnp.float32) + 1.0
    got = by_row(jnp.concatenate([squares, codes]))
    squares = ordered(row, squares, got[:rows]).reshape(block, 1)
    codes = ordered(row, codes, got[rows:])
    doc_rows = jnp.pad(codes, (0, EXTRA * size - block)).reshape(EXTRA, size)
    places = tok * block + jnp.arange(block, dtype=jnp.int32)
    cosine, sine = rotary_tables(places, size)

    taller = 3 * block + 2 * EXTRA
    break_at = 2 * block + EXTRA

    partial_sums = jax.ShapeDtypeStruct((taller, size), jnp.float32)
    no_cost = pl.CostEstimate(flops=0, bytes_accessed=0, transcendentals=0)
    *away, normed, own_weight = pl.pallas_call(
        normalise_project_kernel,
        out_shape=(
            partial_sums,
            partial_sums,
            jax.ShapeDtypeStruct((2, block, width), jnp.bfloat16),
            pltpu.HBM((span, pair * triple), jnp.bfloat16),
        ),
        in_specs=[pl.BlockSpec(memory_space=pltpu.SMEM)] + in_vmem(9),
        out_specs=tuple(in_vmem(3)) + (pl.BlockSpec(memory_space=pltpu.HBM),),
        scratch_shapes=[pltpu.SemaphoreType.DMA(())],
        compiler_params=pltpu.CompilerParams(vmem_limit_bytes=12 * MIB),
        cost_estimate=no_cost,
    )(
        jnp.stack([core, chip, (1 - row) * (pair * triple), row * (pair * triple)]),
        near, far, near_other, far_other, squares, gain, cosine, sine, flat_weight,
    )
    arrived = [by_row(chunk.astype(jnp.float16)) for chunk in away]
    own = pl.pallas_call(
        project_kernel,
        out_shape=(partial_sums, partial_sums),
        in_specs=in_vmem(4) + [pl.BlockSpec(memory_space=pltpu.HBM)],
        out_specs=tuple(in_vmem(2)),
        scratch_shapes=[
            pltpu.VMEM((span, pair * triple), jnp.bfloat16),
            pltpu.SemaphoreType.DMA(()),
        ],
        compiler_params=pltpu.CompilerParams(vmem_limit_bytes=8 * MIB),
        cost_estimate=no_cost,
    )(
        normed, doc_rows, cosine, sine, pltpu.with_memory_space_constraint(own_weight, pltpu.HBM)
    )
    scale = 1.0 / math.sqrt(size)

    def summed(chunk):
        return (own[chunk] + arrived[chunk].astype(jnp.float32)).astype(jnp.bfloat16)

    def gathered_attention():
        chunks = [summed(0), summed(1)]
        keys = jnp.stack([chunks[1][: 2 * block], chunks[0][: 2 * block]])
        everything = lax.all_gather(keys, "tok", axis=0, tiled=False).transpose(1, 0, 2, 3)
        all_codes = lax.all_gather(codes, "tok", axis=0, tiled=True)
        starts = jnp.sum((all_codes[None, :] < codes[:, None]).astype(jnp.int32), axis=1)
        together = attend_gathered(
            jnp.stack([chunk[break_at : break_at + block] for chunk in chunks]),
            everything[:, :, :block].reshape(pair, toks * block, size),
            everything[:, :, block:].reshape(pair, toks * block, size),
            places, starts, scale,
        )
        return parted(row, together)

    if toks == 4:
        places = jnp.stack([tok, row])

        def along_tok(value, pairs):
            return lax.ppermute(value, "tok", pairs)

        def keys_or_query(chunk, is_query):
            begin = jnp.where(is_query, taller - break_at, 0)
            return lax.dynamic_slice_in_dim(chunk, begin.astype(jnp.uint32), break_at, 0)

        def on_place(kernel, out_shape, ins, unused=0, scratch=()):
            return pl.pallas_call(
                kernel,
                out_shape=out_shape,
                in_specs=[pl.BlockSpec(memory_space=pltpu.SMEM)]
                + in_vmem(ins - unused)
                + [pl.BlockSpec(memory_space=pl.ANY)] * unused,
                out_specs=jax.tree.map(lambda unused: in_vmem(1)[0], out_shape),
                scratch_shapes=scratch,
                compiler_params=pltpu.CompilerParams(vmem_limit_bytes=16 * MIB),
                cost_estimate=pl.CostEstimate(flops=0, bytes_accessed=0, transcendentals=0),
            )

        chunk_one = summed(0)
        two_away = along_tok(keys_or_query(chunk_one, tok == 3), [(0, 2), (3, 1), (1, 0), (2, 3)])
        swapped = along_tok(keys_or_query(chunk_one, tok == 2), [(1, 2), (2, 1), (0, 0), (3, 3)])
        across = by_col(chunk_one[:EXTRA], 1)
        arrived[1] = jnp.where(
            tok < toks,
            arrived[1].astype(jnp.float32),
            jnp.broadcast_to(across[:1].astype(jnp.float32), arrived[1].shape),
        )
        chunk_two = summed(1)
        neighbour = along_tok(
            keys_or_query(chunk_two, (tok & 1) == 1), [(0, 1), (1, 0), (2, 3), (3, 2)]
        )
        part_shapes = (
            jax.ShapeDtypeStruct((2, block, size), jnp.float32),
            jax.ShapeDtypeStruct((2, block, 1), jnp.float32),
        )
        own_out, own_logs = on_place(
            lambda *refs: own_block_kernel(scale, *refs), part_shapes, 2
        )(places, chunk_one, chunk_two)
        half_message = (rows + EXTRA, size)
        guests = on_place(
            lambda *refs: guest_kernel(scale, *refs),
            jax.ShapeDtypeStruct((2, 2) + half_message, jnp.bfloat16),
            6,
            1,
        )(places, swapped, two_away, neighbour, chunk_one, chunk_two, own_logs)

        def returned(value, targets):
            across = [
                (2 * t + r, 2 * to + (1 - r if t != to else r))
                for t, to in enumerate(targets)
                for r in range(2)
            ]
            return [
                along_tok(value[0], list(enumerate(targets))),
                lax.ppermute(value[1], ("tok", "row"), across),
            ]

        from_three = returned(guests[1], (0, 3, 2, 1))
        from_below = returned(guests[0], (1, 2, 3, 0))
        mine, logs, theirs = on_place(
            lambda *refs: own_rest_kernel(scale, *refs),
            (
                jax.ShapeDtypeStruct((2, rows, size), jnp.float32),
                jax.ShapeDtypeStruct((2, rows, 1), jnp.float32),
                jax.ShapeDtypeStruct((2,) + half_message, jnp.bfloat16),
            ),
            8,
            1,
            [pltpu.VMEM(shape.shape, shape.dtype) for shape in part_shapes],
        )(places, own_out, own_logs, chunk_one, chunk_two, swapped, two_away, neighbour, guests)
        return on_place(
            merge_kernel, jax.ShapeDtypeStruct((rows, local_heads * size), jnp.bfloat16), 7
        )(places, mine, logs, by_row(theirs), *from_three, *from_below)

    mine, theirs = gathered_attention()
    theirs = by_row(theirs)
    return jnp.concatenate(
        [jnp.where(row == 0, mine, theirs), jnp.where(row == 0, theirs, mine)], axis=1
    )


def solution(mesh):
    placed = (P(("tok", "row"), "col"), P("col"), P("row", "col", None), P(("tok", "row")))
    return jax.shard_map(
        per_device, mesh=mesh, in_specs=placed, out_specs=P(("tok", "row"), "col"), check_vma=False
    )
```

```python
import math

import jax
import jax.numpy as jnp
from jax import lax
from jax.experimental import pallas as pl
from jax.experimental.pallas import tpu as pltpu
from jax.sharding import PartitionSpec as P

EPS = 1e-05
LOG2_E = math.log2(math.e)
LOW = -1e30
EXTRA = 16
MIB = 1 << 20
CHUNKS = ((4, 0), (1, 3))


def rotary_tables(places, head_size):
    half = head_size // 2
    spacing = jnp.arange(half).astype(jnp.float32) * (2.0 / head_size)
    inverse = jnp.power(10000.0, -spacing)
    angles = places.astype(jnp.float32)[:, None] * inverse[None, :]
    cosine, sine = jnp.cos(angles), jnp.sin(angles)
    return (
        jnp.concatenate([cosine, cosine], axis=1),
        jnp.concatenate([-sine, sine], axis=1),
    )


def project_chunk(normed_ref, weight_ref, key_column, query_column, cos_ref, sin_ref, doc_rows, out_ref):
    block, size = cos_ref.shape
    extra = doc_rows.shape[0]
    depth = weight_ref.shape[0] // 2

    def product(column, width):
        at = pl.ds(column if isinstance(column, int) else pl.multiple_of(column, size), width)
        return jnp.dot(
            normed_ref[0], weight_ref[:depth, at], preferred_element_type=jnp.float32
        ) + jnp.dot(normed_ref[1], weight_ref[depth:, at], preferred_element_type=jnp.float32)

    def rotated(piece):
        return piece * cos_ref[...] + pltpu.roll(piece, size // 2, 1) * sin_ref[...]

    both = product(key_column, 2 * size)
    out_ref[:block, :] = rotated(both[:, :size])
    out_ref[block : 2 * block, :] = both[:, size:]
    out_ref[2 * block : 2 * block + extra, :] = doc_rows
    out_ref[2 * block + extra : 3 * block + extra, :] = rotated(product(query_column, size))
    out_ref[3 * block + extra :, :] = doc_rows


def normalise_project_kernel(
    place_ref, a_near, a_far, b_near, b_far, squares_ref, gain_ref, cos_ref, sin_ref, weight_ref,
    one_ref, two_ref, normed_ref, own_hbm, semaphore,
):
    rows, size = a_near.shape[0], cos_ref.shape[1]
    features = 2 * gain_ref.shape[0] * gain_ref.shape[2]
    core, near_row, away, own = place_ref[0], place_ref[1], place_ref[2], place_ref[3]
    copy = pltpu.make_async_copy(
        weight_ref.at[:, pl.ds(pl.multiple_of(own, size), 6 * size)], own_hbm, semaphore
    )
    copy.start()
    for shards, half in (((a_near, a_far), core), ((b_near, b_far), 1 - core)):
        gain = gain_ref[half]
        for shard, row in zip(shards, (near_row, 1 - near_row)):
            at = pl.ds(pl.multiple_of(row * rows, 16), rows)
            factor = lax.rsqrt(squares_ref[at, :] / features + EPS)
            normed_ref[half, at, :] = (shard[...].astype(jnp.float32) * factor * gain).astype(
                jnp.bfloat16
            )
    nothing = jnp.zeros((EXTRA, size), jnp.float32)
    for chunk, (keys, query) in enumerate(CHUNKS):
        project_chunk(
            normed_ref, weight_ref, away + keys * size, away + query * size, cos_ref, sin_ref, nothing,
            (one_ref, two_ref)[chunk],
        )
    copy.wait()


def project_kernel(
    normed_ref, docs_ref, cos_ref, sin_ref, own_hbm, one_ref, two_ref, weight_buffer, semaphore
):
    copy = pltpu.make_async_copy(own_hbm, weight_buffer, semaphore)
    copy.start()
    copy.wait()
    size = cos_ref.shape[1]
    for chunk, (keys, query) in enumerate(CHUNKS):
        project_chunk(
            normed_ref, weight_buffer, keys * size, query * size, cos_ref, sin_ref, docs_ref[...],
            (one_ref, two_ref)[chunk],
        )


def as_column(rows, count):
    lanes = rows.shape[1]
    pieces = []
    for begin in range(0, count, lanes):
        held = min(lanes, count - begin)
        at = lax.broadcasted_iota(jnp.int32, (held, lanes), 0)
        diagonal = at == lax.broadcasted_iota(jnp.int32, (held, lanes), 1)
        row = rows[begin // lanes : begin // lanes + 1, :]
        pieces.append(jnp.sum(jnp.where(diagonal, row, 0.0), axis=1, keepdims=True))
    return jnp.concatenate(pieces, axis=0)


def as_rows(column, lanes):
    count = column.shape[0]
    rows = []
    for begin in range(0, count, lanes):
        held = min(lanes, count - begin)
        at = lax.broadcasted_iota(jnp.int32, (held, lanes), 0)
        diagonal = at == lax.broadcasted_iota(jnp.int32, (held, lanes), 1)
        rows.append(
            jnp.sum(jnp.where(diagonal, column[begin : begin + held], 0.0), axis=0, keepdims=True)
        )
    return rows


def as_lanes(rows, count):
    lanes = rows.shape[1]
    return jnp.concatenate(
        [
            rows[begin // lanes : begin // lanes + 1, : min(lanes, count - begin)]
            for begin in range(0, count, lanes)
        ],
        axis=1,
    )


def softmax_part(scale, query_message, messages, causal):
    valid = [present for message, present in messages]
    messages = [message for message, present in messages]
    query = query_message[:-EXTRA]
    query_docs = as_column(query_message[-EXTRA:].astype(jnp.float32), query.shape[0])
    block = (messages[0].shape[0] - EXTRA) // 2
    keys = jnp.concatenate([message[:block] for message in messages], axis=0)
    values = jnp.concatenate([message[block : 2 * block] for message in messages], axis=0)
    key_docs = jnp.concatenate(
        [
            jnp.where(present, as_lanes(message[2 * block :].astype(jnp.float32), block), 0.0)
            for message, present in zip(messages, valid)
        ],
        axis=1,
    )
    visible = query_docs == key_docs
    if causal:
        shape = (query.shape[0], keys.shape[0])
        query_places = lax.broadcasted_iota(jnp.int32, shape, 0)
        key_places = lax.broadcasted_iota(jnp.int32, shape, 1)
        visible &= (key_places <= query_places) | (key_places >= block)
    scores = lax.dot_general(
        query, keys, (((1,), (1,)), ((), ())), preferred_element_type=jnp.float32
    )
    top = jnp.max(jnp.where(visible, scores, LOW), axis=1, keepdims=True)
    exponentials = jnp.where(visible, jnp.exp2((scores - top) * (scale * LOG2_E)), 0.0)
    total = jnp.sum(exponentials, axis=1, keepdims=True)
    summed = jnp.dot(exponentials.astype(jnp.bfloat16), values, preferred_element_type=jnp.float32)
    some = total > 0.0
    safe = jnp.where(some, total, 1.0)
    return summed / safe, jnp.where(some, top * scale + jnp.log(safe), LOW)


def as_message(output, logs, size):
    along = jnp.concatenate(as_rows(logs, size), axis=0)
    high = along.astype(jnp.bfloat16).astype(jnp.float32)
    middle = (along - high).astype(jnp.bfloat16).astype(jnp.float32)
    pieces = [output, high, middle, along - high - middle]
    pieces.append(jnp.zeros((EXTRA - 3 * along.shape[0], size), jnp.float32))
    return jnp.concatenate(pieces, axis=0).astype(jnp.bfloat16)


def logs_of(message, rows):
    tile = message[rows:].astype(jnp.float32)
    groups = pl.cdiv(rows, tile.shape[1])
    return as_column(sum(tile[k * groups : (k + 1) * groups] for k in range(3)), rows)


def parted(row, value):
    rows = value.shape[0] // 2
    first = row == 0
    return (
        jnp.where(first, value[:rows], value[rows:]),
        jnp.where(first, value[rows:], value[:rows]),
    )


def joined(first, second):
    (output, logs), (other, other_logs) = first, second
    top = jnp.maximum(logs, other_logs)
    weight, other_weight = jnp.exp(logs - top), jnp.exp(other_logs - top)
    total = weight + other_weight
    return (output * weight + other * other_weight) / total, top + jnp.log(total)


def own_block_kernel(scale, place_ref, chunk_one, chunk_two, out_ref, logs_ref):
    for index, (queries, keys) in enumerate(((chunk_one, chunk_two), (chunk_two, chunk_one))):
        height = keys.shape[0] - out_ref.shape[1] - EXTRA
        out_ref[index], logs_ref[index] = softmax_part(
            scale, queries[height:, :], [(keys[:height, :], True)], True
        )


def guest_kernel(
    scale, place_ref, two_away, swapped, neighbour, chunk_one, chunk_two, unused_ref, out_ref
):
    height, size = neighbour.shape
    begin = (height - EXTRA) // 2

    def attend(index, query, messages):
        output, logs = softmax_part(scale, query, [(m, True) for m in messages], False)
        out_ref[index] = as_message(output, logs, size)

    @pl.when(place_ref[0] == 0)
    def one_up():
        attend(0, neighbour[begin:, :], [chunk_one[:height, :]])

    @pl.when(place_ref[0] == 1)
    def down():
        keys = [neighbour[...], chunk_two[:height, :]]
        attend(1, two_away[begin:, :], keys)
        attend(0, swapped[begin:, :], keys)

    @pl.when(place_ref[0] == 2)
    def three_up():
        attend(0, neighbour[begin:, :], [two_away[...], swapped[...], chunk_one[:height, :]])


def own_rest_kernel(
    scale, place_ref, own_out, own_logs, chunk_one, chunk_two, two_away, swapped, neighbour,
    unused_ref, out_ref, logs_ref,
):
    tok = place_ref[0]
    height = neighbour.shape[0]
    out_ref[...] = own_out[...]
    logs_ref[...] = own_logs[...]

    def add(index, query, messages):
        part = softmax_part(scale, query, [(m, True) for m in messages], False)
        out_ref[index], logs_ref[index] = joined((own_out[index], own_logs[index]), part)

    @pl.when((tok == 1) | (tok == 3))
    def down():
        add(0, chunk_one[height:, :], [neighbour[...]])

    @pl.when(tok == 2)
    def up():
        add(1, chunk_two[height:, :], [swapped[...], two_away[...]])


def merge_kernel(
    place_ref, out_ref, logs_ref, two_below_ref, below_ref, mine_ref, theirs_ref
):
    block, size = out_ref.shape[1:]
    tok, row = place_ref[0], place_ref[1]

    def with_guest(index, message, present):
        guest = jnp.where(present, message[:block].astype(jnp.float32), 0.0)
        guest_logs = jnp.where(present, logs_of(message, block), LOW)
        output, logs = joined((out_ref[index], logs_ref[index]), (guest, guest_logs))
        return output.astype(jnp.bfloat16)

    down = with_guest(0, jnp.where(tok == 2, below_ref[...], two_below_ref[...]), tok >= 2)
    up = with_guest(1, below_ref[...], (tok == 1) | (tok == 3))
    for index, output in enumerate((down, up)):
        columns = slice(index * size, (index + 1) * size)
        mine_ref[:, columns], theirs_ref[:, columns] = parted(row, output)


def attend_gathered(query, keys, values, places, starts, scale):
    heads, count, size = query.shape
    chunk = math.gcd(keys.shape[1], 1024)
    rounds = keys.shape[1] // chunk
    stacked = (
        keys.reshape(heads, rounds, chunk, size).transpose(1, 0, 2, 3),
        values.reshape(heads, rounds, chunk, size).transpose(1, 0, 2, 3),
        jnp.arange(rounds * chunk, dtype=jnp.int32).reshape(rounds, chunk),
    )

    def advance(state, blocks):
        running, totals, summed = state
        block_keys, block_values, key_places = blocks
        scores = (
            jnp.einsum("hqd,hkd->hqk", query, block_keys, preferred_element_type=jnp.float32) * scale
        )
        visible = (key_places[None, None, :] <= places[None, :, None]) & (
            key_places[None, None, :] >= starts[None, :, None]
        )
        masked = jnp.where(visible, scores, -jnp.inf)
        newest = jnp.maximum(running, jnp.max(masked, axis=2))
        factor = jnp.exp(running - newest)
        exponentials = jnp.where(visible, jnp.exp(masked - newest[:, :, None]), 0.0)
        totals = totals * factor + jnp.sum(exponentials, axis=2)
        summed = summed * factor[:, :, None] + jnp.einsum(
            "hqk,hkd->hqd", exponentials.astype(jnp.bfloat16), block_values,
            preferred_element_type=jnp.float32,
        )
        return (newest, totals, summed), None

    initial = (
        jnp.full((heads, count), -1e30, jnp.float32),
        jnp.zeros((heads, count), jnp.float32),
        jnp.zeros((heads, count, size), jnp.float32),
    )
    (running, totals, summed), unused = lax.scan(advance, initial, stacked)
    attended = (summed / totals[:, :, None]).astype(jnp.bfloat16)
    return attended.transpose(1, 0, 2).reshape(count, heads * size)


def in_vmem(count):
    return [pl.BlockSpec(memory_space=pltpu.VMEM)] * count


def per_device(activations, norm_gain, qkv_weight, doc_ids):
    rows, width = activations.shape
    span, local_heads, triple = qkv_weight.shape
    size = triple // 3
    pair = local_heads // 2
    block = 2 * rows
    toks = lax.axis_size("tok")
    tok, row, col = lax.axis_index("tok"), lax.axis_index("row"), lax.axis_index("col")
    chip, core = col >> 1, col & 1
    grid = [(r, c) for r in range(2) for c in range(4)]

    def by_col(value, flip):
        return lax.ppermute(value, "col", [(c, c ^ flip) for c in range(4)])

    def by_row(value):
        return lax.ppermute(value, "row", [(0, 1), (1, 0)])

    def ordered(index, own, other):
        first = index == 0
        return jnp.concatenate([jnp.where(first, own, other), jnp.where(first, other, own)])

    near = lax.ppermute(
        activations,
        ("row", "col"),
        [(r * 4 + c, (c // 2) * 4 + 2 * r + c % 2) for r, c in grid],
    )
    far = lax.ppermute(
        activations,
        ("row", "col"),
        [(r * 4 + c, (c // 2) * 4 + 2 * (1 - r) + c % 2) for r, c in grid],
    )
    widened = activations.astype(jnp.float32)
    squares = jnp.sum(widened * widened, axis=1)
    gain = norm_gain.astype(jnp.float32)
    message = jnp.concatenate([squares, gain])
    message, qkv_weight = lax.optimization_barrier((message, qkv_weight))
    flat_weight = qkv_weight.reshape(span, local_heads * triple)
    got = by_col(message, 1)
    squares = squares + got[:rows]
    gain = ordered(core, gain, got[rows:])
    got = by_col(jnp.concatenate([squares, gain]), 2)
    near, far, got, flat_weight = lax.optimization_barrier((near, far, got, flat_weight))
    near_other, far_other = by_col(near, 1), by_col(far, 1)
    squares = squares + got[:rows]
    gain = jnp.where(chip == row, gain, got[rows:]).reshape(2, 1, width)
    codes = doc_ids.astype(jnp.float32) + 1.0
    got = by_row(jnp.concatenate([squares, codes]))
    squares = ordered(row, squares, got[:rows]).reshape(block, 1)
    codes = ordered(row, codes, got[rows:])
    doc_rows = jnp.pad(codes, (0, EXTRA * size - block)).reshape(EXTRA, size)
    places = tok * block + jnp.arange(block, dtype=jnp.int32)
    cosine, sine = rotary_tables(places, size)

    taller = 3 * block + 2 * EXTRA
    break_at = 2 * block + EXTRA

    partial_sums = jax.ShapeDtypeStruct((taller, size), jnp.float32)
    no_cost = pl.CostEstimate(flops=0, bytes_accessed=0, transcendentals=0)
    *away, normed, own_weight = pl.pallas_call(
        normalise_project_kernel,
        out_shape=(
            partial_sums,
            partial_sums,
            jax.ShapeDtypeStruct((2, block, width), jnp.bfloat16),
            pltpu.HBM((span, pair * triple), jnp.bfloat16),
        ),
        in_specs=[pl.BlockSpec(memory_space=pltpu.SMEM)] + in_vmem(9),
        out_specs=tuple(in_vmem(3)) + (pl.BlockSpec(memory_space=pltpu.HBM),),
        scratch_shapes=[pltpu.SemaphoreType.DMA(())],
        compiler_params=pltpu.CompilerParams(vmem_limit_bytes=12 * MIB),
        cost_estimate=no_cost,
    )(
        jnp.stack([core, chip, (1 - row) * (pair * triple), row * (pair * triple)]),
        near, far, near_other, far_other, squares, gain, cosine, sine, flat_weight,
    )
    arrived = [by_row(chunk.astype(jnp.float16)) for chunk in away]
    own = pl.pallas_call(
        project_kernel,
        out_shape=(partial_sums, partial_sums),
        in_specs=in_vmem(4) + [pl.BlockSpec(memory_space=pltpu.HBM)],
        out_specs=tuple(in_vmem(2)),
        scratch_shapes=[
            pltpu.VMEM((span, pair * triple), jnp.bfloat16),
            pltpu.SemaphoreType.DMA(()),
        ],
        compiler_params=pltpu.CompilerParams(vmem_limit_bytes=8 * MIB),
        cost_estimate=no_cost,
    )(
        normed, doc_rows, cosine, sine, pltpu.with_memory_space_constraint(own_weight, pltpu.HBM)
    )
    scale = 1.0 / math.sqrt(size)

    def summed(chunk):
        return (own[chunk] + arrived[chunk].astype(jnp.float32)).astype(jnp.bfloat16)

    def gathered_attention():
        chunks = [summed(0), summed(1)]
        keys = jnp.stack([chunks[1][: 2 * block], chunks[0][: 2 * block]])
        everything = lax.all_gather(keys, "tok", axis=0, tiled=False).transpose(1, 0, 2, 3)
        all_codes = lax.all_gather(codes, "tok", axis=0, tiled=True)
        starts = jnp.sum((all_codes[None, :] < codes[:, None]).astype(jnp.int32), axis=1)
        together = attend_gathered(
            jnp.stack([chunk[break_at : break_at + block] for chunk in chunks]),
            everything[:, :, :block].reshape(pair, toks * block, size),
            everything[:, :, block:].reshape(pair, toks * block, size),
            places, starts, scale,
        )
        return parted(row, together)

    if toks == 4:
        places = jnp.stack([tok, row])

        def along_tok(value, pairs):
            return lax.ppermute(value, "tok", pairs)

        def keys_or_query(chunk, is_query):
            begin = jnp.where(is_query, taller - break_at, 0)
            return lax.dynamic_slice_in_dim(chunk, begin.astype(jnp.uint32), break_at, 0)

        def on_place(kernel, out_shape, ins, unused=0):
            return pl.pallas_call(
                kernel,
                out_shape=out_shape,
                in_specs=[pl.BlockSpec(memory_space=pltpu.SMEM)]
                + in_vmem(ins - unused)
                + [pl.BlockSpec(memory_space=pl.ANY)] * unused,
                out_specs=jax.tree.map(lambda unused: in_vmem(1)[0], out_shape),
                compiler_params=pltpu.CompilerParams(vmem_limit_bytes=16 * MIB),
                cost_estimate=pl.CostEstimate(flops=0, bytes_accessed=0, transcendentals=0),
            )

        chunk_one = summed(0)
        two_away = along_tok(keys_or_query(chunk_one, tok == 3), [(0, 2), (3, 1), (1, 0), (2, 3)])
        swapped = along_tok(keys_or_query(chunk_one, tok == 2), [(1, 2), (2, 1), (0, 0), (3, 3)])
        across = by_col(chunk_one[:EXTRA], 1)
        arrived[1] = jnp.where(
            tok < toks,
            arrived[1].astype(jnp.float32),
            jnp.broadcast_to(across[:1].astype(jnp.float32), arrived[1].shape),
        )
        chunk_two = summed(1)
        neighbour = along_tok(
            keys_or_query(chunk_two, (tok & 1) == 1), [(0, 1), (1, 0), (2, 3), (3, 2)]
        )
        part_shapes = (
            jax.ShapeDtypeStruct((2, block, size), jnp.float32),
            jax.ShapeDtypeStruct((2, block, 1), jnp.float32),
        )
        own_out, own_logs = on_place(
            lambda *refs: own_block_kernel(scale, *refs), part_shapes, 2
        )(places, chunk_one, chunk_two)
        guests = on_place(
            lambda *refs: guest_kernel(scale, *refs),
            jax.ShapeDtypeStruct((2, block + EXTRA, size), jnp.bfloat16),
            6,
            1,
        )(places, two_away, swapped, neighbour, chunk_one, chunk_two, own_logs)
        from_two_below = along_tok(guests[1], [(1, 3), (0, 1), (2, 0), (3, 2)])
        from_below = along_tok(guests[0], [(0, 1), (1, 2), (2, 3), (3, 0)])
        output, logs = on_place(
            lambda *refs: own_rest_kernel(scale, *refs), part_shapes, 8, 1
        )(places, own_out, own_logs, chunk_one, chunk_two, two_away, swapped, neighbour, guests)
        half = jax.ShapeDtypeStruct((rows, pair * size), jnp.bfloat16)
        mine, theirs = on_place(merge_kernel, (half, half), 4)(
            places, output, logs, from_two_below, from_below
        )
    else:
        mine, theirs = gathered_attention()
    theirs = by_row(theirs)
    return jnp.concatenate(
        [jnp.where(row == 0, mine, theirs), jnp.where(row == 0, theirs, mine)], axis=1
    )


def solution(mesh):
    placed = (P(("tok", "row"), "col"), P("col"), P("row", "col", None), P(("tok", "row")))
    return jax.shard_map(
        per_device, mesh=mesh, in_specs=placed, out_specs=P(("tok", "row"), "col"), check_vma=False
    )
```

```python
import math

import jax
import jax.numpy as jnp
from jax import lax
from jax.experimental import pallas as pl
from jax.experimental.pallas import tpu as pltpu
from jax.sharding import PartitionSpec as P

EPS = 1e-05
LOG2_E = math.log2(math.e)
LOW = -1e30
EXTRA = 16
MIB = 1 << 20
CHUNKS = ((4, 0), (1, 3))


def rotary_tables(places, head_size, always):
    half = head_size // 2
    spacing = jnp.arange(half).astype(jnp.float32) * (2.0 / head_size)
    inverse = jnp.where(always, jnp.power(10000.0, -spacing), 0.0)
    angles = places.astype(jnp.float32)[:, None] * inverse[None, :]
    cosine, sine = jnp.cos(angles), jnp.sin(angles)
    return (
        jnp.concatenate([cosine, cosine], axis=1),
        jnp.concatenate([-sine, sine], axis=1),
    )


def project_chunk(normed_ref, weight_ref, key_column, query_column, cos_ref, sin_ref, doc_rows, out_ref):
    block, size = cos_ref.shape
    extra = doc_rows.shape[0]
    depth = weight_ref.shape[0] // 2

    def product(column, width):
        at = pl.ds(column if isinstance(column, int) else pl.multiple_of(column, size), width)
        return jnp.dot(
            normed_ref[0], weight_ref[:depth, at], preferred_element_type=jnp.float32
        ) + jnp.dot(normed_ref[1], weight_ref[depth:, at], preferred_element_type=jnp.float32)

    def rotated(piece):
        return piece * cos_ref[...] + pltpu.roll(piece, size // 2, 1) * sin_ref[...]

    both = product(key_column, 2 * size)
    out_ref[:block, :] = rotated(both[:, :size])
    out_ref[block : 2 * block, :] = both[:, size:]
    out_ref[2 * block : 2 * block + extra, :] = doc_rows
    out_ref[2 * block + extra : 3 * block + extra, :] = rotated(product(query_column, size))
    out_ref[3 * block + extra :, :] = doc_rows


def normalise_project_kernel(
    place_ref, a_near, a_far, b_near, b_far, squares_ref, gain_ref, cos_ref, sin_ref, weight_ref,
    one_ref, two_ref, normed_ref, own_hbm, semaphore,
):
    rows, size = a_near.shape[0], cos_ref.shape[1]
    features = 2 * gain_ref.shape[0] * gain_ref.shape[2]
    core, near_row, away, own = place_ref[0], place_ref[1], place_ref[2], place_ref[3]
    copy = pltpu.make_async_copy(
        weight_ref.at[:, pl.ds(pl.multiple_of(own, size), 6 * size)], own_hbm, semaphore
    )
    copy.start()
    for shards, half in (((a_near, a_far), core), ((b_near, b_far), 1 - core)):
        gain = gain_ref[half]
        for shard, row in zip(shards, (near_row, 1 - near_row)):
            at = pl.ds(pl.multiple_of(row * rows, 16), rows)
            factor = lax.rsqrt(squares_ref[at, :] / features + EPS)
            normed_ref[half, at, :] = (shard[...].astype(jnp.float32) * factor * gain).astype(
                jnp.bfloat16
            )
    nothing = jnp.zeros((EXTRA, size), jnp.float32)
    for chunk, (keys, query) in enumerate(CHUNKS):
        project_chunk(
            normed_ref, weight_ref, away + keys * size, away + query * size, cos_ref, sin_ref, nothing,
            (one_ref, two_ref)[chunk],
        )
    copy.wait()


def project_kernel(
    normed_ref, docs_ref, cos_ref, sin_ref, own_hbm, one_ref, two_ref, weight_buffer, semaphore
):
    copy = pltpu.make_async_copy(own_hbm, weight_buffer, semaphore)
    copy.start()
    copy.wait()
    size = cos_ref.shape[1]
    for chunk, (keys, query) in enumerate(CHUNKS):
        project_chunk(
            normed_ref, weight_buffer, keys * size, query * size, cos_ref, sin_ref, docs_ref[...],
            (one_ref, two_ref)[chunk],
        )


def as_column(rows, count):
    lanes = rows.shape[1]
    pieces = []
    for begin in range(0, count, lanes):
        held = min(lanes, count - begin)
        at = lax.broadcasted_iota(jnp.int32, (held, lanes), 0)
        diagonal = at == lax.broadcasted_iota(jnp.int32, (held, lanes), 1)
        row = rows[begin // lanes : begin // lanes + 1, :]
        pieces.append(jnp.sum(jnp.where(diagonal, row, 0.0), axis=1, keepdims=True))
    return jnp.concatenate(pieces, axis=0)


def as_rows(column, lanes):
    count = column.shape[0]
    rows = []
    for begin in range(0, count, lanes):
        held = min(lanes, count - begin)
        at = lax.broadcasted_iota(jnp.int32, (held, lanes), 0)
        diagonal = at == lax.broadcasted_iota(jnp.int32, (held, lanes), 1)
        rows.append(
            jnp.sum(jnp.where(diagonal, column[begin : begin + held], 0.0), axis=0, keepdims=True)
        )
    return rows


def as_lanes(rows, count):
    lanes = rows.shape[1]
    return jnp.concatenate(
        [
            rows[begin // lanes : begin // lanes + 1, : min(lanes, count - begin)]
            for begin in range(0, count, lanes)
        ],
        axis=1,
    )


def softmax_part(scale, query_message, messages, causal):
    valid = [present for message, present in messages]
    messages = [message for message, present in messages]
    query = query_message[:-EXTRA]
    query_docs = as_column(query_message[-EXTRA:].astype(jnp.float32), query.shape[0])
    block = (messages[0].shape[0] - EXTRA) // 2
    keys = jnp.concatenate([message[:block] for message in messages], axis=0)
    values = jnp.concatenate([message[block : 2 * block] for message in messages], axis=0)
    key_docs = jnp.concatenate(
        [
            jnp.where(present, as_lanes(message[2 * block :].astype(jnp.float32), block), 0.0)
            for message, present in zip(messages, valid)
        ],
        axis=1,
    )
    visible = query_docs == key_docs
    if causal:
        shape = (query.shape[0], keys.shape[0])
        query_places = lax.broadcasted_iota(jnp.int32, shape, 0)
        key_places = lax.broadcasted_iota(jnp.int32, shape, 1)
        visible &= (key_places <= query_places) | (key_places >= block)
    scores = lax.dot_general(
        query, keys, (((1,), (1,)), ((), ())), preferred_element_type=jnp.float32
    )
    top = jnp.max(jnp.where(visible, scores, LOW), axis=1, keepdims=True)
    exponentials = jnp.where(visible, jnp.exp2((scores - top) * (scale * LOG2_E)), 0.0)
    total = jnp.sum(exponentials, axis=1, keepdims=True)
    summed = jnp.dot(exponentials.astype(jnp.bfloat16), values, preferred_element_type=jnp.float32)
    some = total > 0.0
    safe = jnp.where(some, total, 1.0)
    return summed / safe, jnp.where(some, top * scale + jnp.log(safe), LOW)


def as_message(output, logs, size):
    along = jnp.concatenate(as_rows(logs, size), axis=0)
    high = along.astype(jnp.bfloat16).astype(jnp.float32)
    middle = (along - high).astype(jnp.bfloat16).astype(jnp.float32)
    pieces = [output, high, middle, along - high - middle]
    pieces.append(jnp.zeros((EXTRA - 3 * along.shape[0], size), jnp.float32))
    return jnp.concatenate(pieces, axis=0).astype(jnp.bfloat16)


def logs_of(message, rows):
    tile = message[rows:].astype(jnp.float32)
    groups = pl.cdiv(rows, tile.shape[1])
    return as_column(sum(tile[k * groups : (k + 1) * groups] for k in range(3)), rows)


def parted(row, value):
    rows = value.shape[0] // 2
    first = row == 0
    return (
        jnp.where(first, value[:rows], value[rows:]),
        jnp.where(first, value[rows:], value[:rows]),
    )


def joined(first, second):
    (output, logs), (other, other_logs) = first, second
    top = jnp.maximum(logs, other_logs)
    weight, other_weight = jnp.exp(logs - top), jnp.exp(other_logs - top)
    total = weight + other_weight
    return (output * weight + other * other_weight) / total, top + jnp.log(total)


def own_block_kernel(scale, place_ref, chunk_one, chunk_two, out_ref, logs_ref):
    for index, (queries, keys) in enumerate(((chunk_one, chunk_two), (chunk_two, chunk_one))):
        height = keys.shape[0] - out_ref.shape[1] - EXTRA
        out_ref[index], logs_ref[index] = softmax_part(
            scale, queries[height:, :], [(keys[:height, :], True)], True
        )


def guest_kernel(
    scale, place_ref, two_away, swapped, neighbour, chunk_one, chunk_two, unused_ref, out_ref
):
    height, size = neighbour.shape
    begin = (height - EXTRA) // 2

    def attend(index, query, messages):
        output, logs = softmax_part(scale, query, [(m, True) for m in messages], False)
        out_ref[index] = as_message(output, logs, size)

    @pl.when(place_ref[0] == 0)
    def one_up():
        attend(1, neighbour[begin:, :], [chunk_one[:height, :]])

    @pl.when(place_ref[0] == 1)
    def down():
        keys = [neighbour[...], chunk_two[:height, :]]
        attend(1, two_away[begin:, :], keys)
        attend(0, swapped[begin:, :], keys)

    @pl.when(place_ref[0] == 2)
    def three_up():
        attend(0, neighbour[begin:, :], [two_away[...], swapped[...], chunk_one[:height, :]])


def own_rest_kernel(
    scale, place_ref, own_out, own_logs, chunk_one, chunk_two, two_away, swapped, neighbour,
    unused_ref, out_ref, logs_ref,
):
    tok = place_ref[0]
    height = neighbour.shape[0]
    out_ref[...] = own_out[...]
    logs_ref[...] = own_logs[...]

    def add(index, query, messages):
        part = softmax_part(scale, query, [(m, True) for m in messages], False)
        out_ref[index], logs_ref[index] = joined((own_out[index], own_logs[index]), part)

    @pl.when((tok == 1) | (tok == 3))
    def down():
        add(0, chunk_one[height:, :], [neighbour[...]])

    @pl.when(tok == 2)
    def up():
        add(1, chunk_two[height:, :], [swapped[...], two_away[...]])


def merge_kernel(
    place_ref, out_ref, logs_ref, first_ref, below_ref, mine_ref, theirs_ref
):
    block, size = out_ref.shape[1:]
    tok, row = place_ref[0], place_ref[1]

    def with_guest(index, message, present):
        guest = jnp.where(present, message[:block].astype(jnp.float32), 0.0)
        guest_logs = jnp.where(present, logs_of(message, block), LOW)
        output, logs = joined((out_ref[index], logs_ref[index]), (guest, guest_logs))
        return output.astype(jnp.bfloat16)

    down = with_guest(0, jnp.where(tok == 2, below_ref[...], first_ref[...]), tok >= 2)
    up = with_guest(1, jnp.where(tok == 1, first_ref[...], below_ref[...]), (tok == 1) | (tok == 3))
    for index, output in enumerate((down, up)):
        columns = slice(index * size, (index + 1) * size)
        mine_ref[:, columns], theirs_ref[:, columns] = parted(row, output)


def attend_gathered(query, keys, values, places, starts, scale):
    heads, count, size = query.shape
    chunk = math.gcd(keys.shape[1], 1024)
    rounds = keys.shape[1] // chunk
    stacked = (
        keys.reshape(heads, rounds, chunk, size).transpose(1, 0, 2, 3),
        values.reshape(heads, rounds, chunk, size).transpose(1, 0, 2, 3),
        jnp.arange(rounds * chunk, dtype=jnp.int32).reshape(rounds, chunk),
    )

    def advance(state, blocks):
        running, totals, summed = state
        block_keys, block_values, key_places = blocks
        scores = (
            jnp.einsum("hqd,hkd->hqk", query, block_keys, preferred_element_type=jnp.float32) * scale
        )
        visible = (key_places[None, None, :] <= places[None, :, None]) & (
            key_places[None, None, :] >= starts[None, :, None]
        )
        masked = jnp.where(visible, scores, -jnp.inf)
        newest = jnp.maximum(running, jnp.max(masked, axis=2))
        factor = jnp.exp(running - newest)
        exponentials = jnp.where(visible, jnp.exp(masked - newest[:, :, None]), 0.0)
        totals = totals * factor + jnp.sum(exponentials, axis=2)
        summed = summed * factor[:, :, None] + jnp.einsum(
            "hqk,hkd->hqd", exponentials.astype(jnp.bfloat16), block_values,
            preferred_element_type=jnp.float32,
        )
        return (newest, totals, summed), None

    initial = (
        jnp.full((heads, count), -1e30, jnp.float32),
        jnp.zeros((heads, count), jnp.float32),
        jnp.zeros((heads, count, size), jnp.float32),
    )
    (running, totals, summed), unused = lax.scan(advance, initial, stacked)
    attended = (summed / totals[:, :, None]).astype(jnp.bfloat16)
    return attended.transpose(1, 0, 2).reshape(count, heads * size)


def in_vmem(count):
    return [pl.BlockSpec(memory_space=pltpu.VMEM)] * count


def per_device(activations, norm_gain, qkv_weight, doc_ids):
    rows, width = activations.shape
    span, local_heads, triple = qkv_weight.shape
    size = triple // 3
    pair = local_heads // 2
    block = 2 * rows
    toks = lax.axis_size("tok")
    tok, row, col = lax.axis_index("tok"), lax.axis_index("row"), lax.axis_index("col")
    chip, core = col >> 1, col & 1
    grid = [(r, c) for r in range(2) for c in range(4)]

    def by_col(value, flip):
        return lax.ppermute(value, "col", [(c, c ^ flip) for c in range(4)])

    def by_row(value):
        return lax.ppermute(value, "row", [(0, 1), (1, 0)])

    def ordered(index, own, other):
        first = index == 0
        return jnp.concatenate([jnp.where(first, own, other), jnp.where(first, other, own)])

    near = lax.ppermute(
        activations,
        ("row", "col"),
        [(r * 4 + c, (c // 2) * 4 + 2 * r + c % 2) for r, c in grid],
    )
    far = lax.ppermute(
        activations,
        ("row", "col"),
        [(r * 4 + c, (c // 2) * 4 + 2 * (1 - r) + c % 2) for r, c in grid],
    )
    widened = activations.astype(jnp.float32)
    squares = jnp.sum(widened * widened, axis=1)
    gain = norm_gain.astype(jnp.float32)
    message = jnp.concatenate([squares, gain])
    message, qkv_weight = lax.optimization_barrier((message, qkv_weight))
    flat_weight = qkv_weight.reshape(span, local_heads * triple)
    got = by_col(message, 1)
    squares = squares + got[:rows]
    gain = ordered(core, gain, got[rows:])
    by_chip = by_col(jnp.concatenate([squares, gain]), 2)
    near, far, by_chip, flat_weight = lax.optimization_barrier((near, far, by_chip, flat_weight))
    near_other, far_other = by_col(near, 1), by_col(far, 1)
    squares = squares + by_chip[:rows]
    gain = jnp.where(chip == row, gain, by_chip[rows:]).reshape(2, 1, width)
    codes = doc_ids.astype(jnp.float32) + 1.0
    got = by_row(jnp.concatenate([squares, codes]))
    squares = ordered(row, squares, got[:rows]).reshape(block, 1)
    codes = ordered(row, codes, got[rows:])
    doc_rows = jnp.pad(codes, (0, EXTRA * size - block)).reshape(EXTRA, size)
    places = tok * block + jnp.arange(block, dtype=jnp.int32)
    cosine, sine = rotary_tables(places, size, near[0, : size // 2].astype(jnp.float32) < 1e30)

    taller = 3 * block + 2 * EXTRA
    break_at = 2 * block + EXTRA

    partial_sums = jax.ShapeDtypeStruct((taller, size), jnp.float32)
    no_cost = pl.CostEstimate(flops=0, bytes_accessed=0, transcendentals=0)
    *away, normed, own_weight = pl.pallas_call(
        normalise_project_kernel,
        out_shape=(
            partial_sums,
            partial_sums,
            jax.ShapeDtypeStruct((2, block, width), jnp.bfloat16),
            pltpu.HBM((span, pair * triple), jnp.bfloat16),
        ),
        in_specs=[pl.BlockSpec(memory_space=pltpu.SMEM)] + in_vmem(9),
        out_specs=tuple(in_vmem(3)) + (pl.BlockSpec(memory_space=pltpu.HBM),),
        scratch_shapes=[pltpu.SemaphoreType.DMA(())],
        compiler_params=pltpu.CompilerParams(vmem_limit_bytes=12 * MIB),
        cost_estimate=no_cost,
    )(
        jnp.stack([core, chip, (1 - row) * (pair * triple), row * (pair * triple)]),
        near, far, near_other, far_other, squares, gain, cosine, sine, flat_weight,
    )
    arrived = [by_row(chunk.astype(jnp.float16)) for chunk in away]
    own = pl.pallas_call(
        project_kernel,
        out_shape=(partial_sums, partial_sums),
        in_specs=in_vmem(4) + [pl.BlockSpec(memory_space=pltpu.HBM)],
        out_specs=tuple(in_vmem(2)),
        scratch_shapes=[
            pltpu.VMEM((span, pair * triple), jnp.bfloat16),
            pltpu.SemaphoreType.DMA(()),
        ],
        compiler_params=pltpu.CompilerParams(vmem_limit_bytes=8 * MIB),
        cost_estimate=no_cost,
    )(
        normed, doc_rows, cosine, sine, pltpu.with_memory_space_constraint(own_weight, pltpu.HBM)
    )
    scale = 1.0 / math.sqrt(size)

    def summed(chunk):
        return (own[chunk] + arrived[chunk].astype(jnp.float32)).astype(jnp.bfloat16)

    def gathered_attention():
        chunks = [summed(0), summed(1)]
        keys = jnp.stack([chunks[1][: 2 * block], chunks[0][: 2 * block]])
        everything = lax.all_gather(keys, "tok", axis=0, tiled=False).transpose(1, 0, 2, 3)
        all_codes = lax.all_gather(codes, "tok", axis=0, tiled=True)
        starts = jnp.sum((all_codes[None, :] < codes[:, None]).astype(jnp.int32), axis=1)
        together = attend_gathered(
            jnp.stack([chunk[break_at : break_at + block] for chunk in chunks]),
            everything[:, :, :block].reshape(pair, toks * block, size),
            everything[:, :, block:].reshape(pair, toks * block, size),
            places, starts, scale,
        )
        return parted(row, together)

    if toks == 4:
        places = jnp.stack([tok, row])

        def along_tok(value, pairs):
            return lax.ppermute(value, "tok", pairs)

        def keys_or_query(chunk, is_query):
            begin = jnp.where(is_query, taller - break_at, 0)
            return lax.dynamic_slice_in_dim(chunk, begin.astype(jnp.uint32), break_at, 0)

        def on_place(kernel, out_shape, ins, unused=0):
            return pl.pallas_call(
                kernel,
                out_shape=out_shape,
                in_specs=[pl.BlockSpec(memory_space=pltpu.SMEM)]
                + in_vmem(ins - unused)
                + [pl.BlockSpec(memory_space=pl.ANY)] * unused,
                out_specs=jax.tree.map(lambda unused: in_vmem(1)[0], out_shape),
                compiler_params=pltpu.CompilerParams(vmem_limit_bytes=16 * MIB),
                cost_estimate=pl.CostEstimate(flops=0, bytes_accessed=0, transcendentals=0),
            )

        chunk_one = summed(0)
        two_away = along_tok(keys_or_query(chunk_one, tok == 3), [(0, 2), (3, 1), (1, 0), (2, 3)])
        swapped = along_tok(keys_or_query(chunk_one, tok == 2), [(1, 2), (2, 1), (0, 0), (3, 3)])
        across = by_col(chunk_one[:EXTRA], 1)
        arrived[1] = jnp.where(
            tok < toks,
            arrived[1].astype(jnp.float32),
            jnp.broadcast_to(across[:1].astype(jnp.float32), arrived[1].shape),
        )
        chunk_two = summed(1)
        neighbour = along_tok(
            keys_or_query(chunk_two, (tok & 1) == 1), [(0, 1), (1, 0), (2, 3), (3, 2)]
        )
        part_shapes = (
            jax.ShapeDtypeStruct((2, block, size), jnp.float32),
            jax.ShapeDtypeStruct((2, block, 1), jnp.float32),
        )
        own_out, own_logs = on_place(
            lambda *refs: own_block_kernel(scale, *refs), part_shapes, 2
        )(places, chunk_one, chunk_two)
        guests = on_place(
            lambda *refs: guest_kernel(scale, *refs),
            jax.ShapeDtypeStruct((2, block + EXTRA, size), jnp.bfloat16),
            6,
            1,
        )(places, two_away, swapped, neighbour, chunk_one, chunk_two, own_logs)
        from_first = along_tok(guests[1], [(0, 1), (1, 3), (2, 0), (3, 2)])
        from_below = along_tok(guests[0], [(1, 2), (2, 3)])
        output, logs = on_place(
            lambda *refs: own_rest_kernel(scale, *refs), part_shapes, 8, 1
        )(places, own_out, own_logs, chunk_one, chunk_two, two_away, swapped, neighbour, guests)
        half = jax.ShapeDtypeStruct((rows, pair * size), jnp.bfloat16)
        mine, theirs = on_place(merge_kernel, (half, half), 4)(
            places, output, logs, from_first, from_below
        )
    else:
        mine, theirs = gathered_attention()
    theirs = by_row(theirs)
    return jnp.concatenate(
        [jnp.where(row == 0, mine, theirs), jnp.where(row == 0, theirs, mine)], axis=1
    )


def solution(mesh):
    placed = (P(("tok", "row"), "col"), P("col"), P("row", "col", None), P(("tok", "row")))
    return jax.shard_map(
        per_device, mesh=mesh, in_specs=placed, out_specs=P(("tok", "row"), "col"), check_vma=False
    )
```

```python
import math

import jax
import jax.numpy as jnp
from jax import lax
from jax.experimental import pallas as pl
from jax.experimental.pallas import tpu as pltpu
from jax.sharding import PartitionSpec as P

EPS = 1e-05
LOG2_E = math.log2(math.e)
LOW = -1e30
EXTRA = 16
MIB = 1 << 20
CHUNKS = ((4, 0), (1, 3))


def rotary_tables(places, head_size, always):
    half = head_size // 2
    spacing = jnp.arange(half).astype(jnp.float32) * (2.0 / head_size)
    inverse = jnp.where(always, jnp.power(10000.0, -spacing), 0.0)
    angles = places.astype(jnp.float32)[:, None] * inverse[None, :]
    cosine, sine = jnp.cos(angles), jnp.sin(angles)
    return (
        jnp.concatenate([cosine, cosine], axis=1),
        jnp.concatenate([-sine, sine], axis=1),
    )


def project_chunk(normed_ref, weight_ref, key_column, query_column, cos_ref, sin_ref, doc_rows, out_ref):
    block, size = cos_ref.shape
    extra = doc_rows.shape[0]
    depth = weight_ref.shape[0] // 2

    def product(column, width):
        at = pl.ds(column if isinstance(column, int) else pl.multiple_of(column, size), width)
        return jnp.dot(
            normed_ref[0], weight_ref[:depth, at], preferred_element_type=jnp.float32
        ) + jnp.dot(normed_ref[1], weight_ref[depth:, at], preferred_element_type=jnp.float32)

    def rotated(piece):
        return piece * cos_ref[...] + pltpu.roll(piece, size // 2, 1) * sin_ref[...]

    both = product(key_column, 2 * size)
    out_ref[:block, :] = rotated(both[:, :size])
    out_ref[block : 2 * block, :] = both[:, size:]
    out_ref[2 * block : 2 * block + extra, :] = doc_rows
    out_ref[2 * block + extra : 3 * block + extra, :] = rotated(product(query_column, size))
    out_ref[3 * block + extra :, :] = doc_rows


def normalise_project_kernel(
    place_ref, a_near, a_far, b_near, b_far, squares_ref, gain_ref, cos_ref, sin_ref, weight_ref,
    one_ref, two_ref, normed_ref, own_hbm, semaphore,
):
    rows, size = a_near.shape[0], cos_ref.shape[1]
    features = 2 * gain_ref.shape[0] * gain_ref.shape[2]
    core, near_row, away, own = place_ref[0], place_ref[1], place_ref[2], place_ref[3]
    copy = pltpu.make_async_copy(
        weight_ref.at[:, pl.ds(pl.multiple_of(own, size), 6 * size)], own_hbm, semaphore
    )
    copy.start()
    for shards, half in (((a_near, a_far), core), ((b_near, b_far), 1 - core)):
        gain = gain_ref[half]
        for shard, row in zip(shards, (near_row, 1 - near_row)):
            at = pl.ds(pl.multiple_of(row * rows, 16), rows)
            factor = lax.rsqrt(squares_ref[at, :] / features + EPS)
            normed_ref[half, at, :] = (shard[...].astype(jnp.float32) * factor * gain).astype(
                jnp.bfloat16
            )
    nothing = jnp.zeros((EXTRA, size), jnp.float32)
    for chunk, (keys, query) in enumerate(CHUNKS):
        project_chunk(
            normed_ref, weight_ref, away + keys * size, away + query * size, cos_ref, sin_ref, nothing,
            (one_ref, two_ref)[chunk],
        )
    copy.wait()


def project_kernel(
    normed_ref, docs_ref, cos_ref, sin_ref, own_hbm, one_ref, two_ref, weight_buffer, semaphore
):
    copy = pltpu.make_async_copy(own_hbm, weight_buffer, semaphore)
    copy.start()
    copy.wait()
    size = cos_ref.shape[1]
    for chunk, (keys, query) in enumerate(CHUNKS):
        project_chunk(
            normed_ref, weight_buffer, keys * size, query * size, cos_ref, sin_ref, docs_ref[...],
            (one_ref, two_ref)[chunk],
        )


def as_column(rows, count):
    lanes = rows.shape[1]
    pieces = []
    for begin in range(0, count, lanes):
        held = min(lanes, count - begin)
        at = lax.broadcasted_iota(jnp.int32, (held, lanes), 0)
        diagonal = at == lax.broadcasted_iota(jnp.int32, (held, lanes), 1)
        row = rows[begin // lanes : begin // lanes + 1, :]
        pieces.append(jnp.sum(jnp.where(diagonal, row, 0.0), axis=1, keepdims=True))
    return jnp.concatenate(pieces, axis=0)


def as_rows(column, lanes):
    count = column.shape[0]
    rows = []
    for begin in range(0, count, lanes):
        held = min(lanes, count - begin)
        at = lax.broadcasted_iota(jnp.int32, (held, lanes), 0)
        diagonal = at == lax.broadcasted_iota(jnp.int32, (held, lanes), 1)
        rows.append(
            jnp.sum(jnp.where(diagonal, column[begin : begin + held], 0.0), axis=0, keepdims=True)
        )
    return rows


def as_lanes(rows, count):
    lanes = rows.shape[1]
    return jnp.concatenate(
        [
            rows[begin // lanes : begin // lanes + 1, : min(lanes, count - begin)]
            for begin in range(0, count, lanes)
        ],
        axis=1,
    )


def softmax_part(scale, query_message, messages, causal):
    valid = [present for message, present in messages]
    messages = [message for message, present in messages]
    query = query_message[:-EXTRA]
    query_docs = as_column(query_message[-EXTRA:].astype(jnp.float32), query.shape[0])
    block = (messages[0].shape[0] - EXTRA) // 2
    keys = jnp.concatenate([message[:block] for message in messages], axis=0)
    values = jnp.concatenate([message[block : 2 * block] for message in messages], axis=0)
    key_docs = jnp.concatenate(
        [
            jnp.where(present, as_lanes(message[2 * block :].astype(jnp.float32), block), 0.0)
            for message, present in zip(messages, valid)
        ],
        axis=1,
    )
    visible = query_docs == key_docs
    if causal:
        shape = (query.shape[0], keys.shape[0])
        query_places = lax.broadcasted_iota(jnp.int32, shape, 0)
        key_places = lax.broadcasted_iota(jnp.int32, shape, 1)
        visible &= (key_places <= query_places) | (key_places >= block)
    scores = lax.dot_general(
        query, keys, (((1,), (1,)), ((), ())), preferred_element_type=jnp.float32
    )
    masked = jnp.where(visible, scores, LOW)
    top = jnp.max(masked, axis=1, keepdims=True)
    exponentials = jnp.exp2((masked - top) * (scale * LOG2_E))
    total = jnp.sum(exponentials, axis=1, keepdims=True)
    summed = jnp.dot(exponentials.astype(jnp.bfloat16), values, preferred_element_type=jnp.float32)
    return summed / total, jnp.where(top > LOW / 2, top * scale + jnp.log(total), LOW)


def as_message(output, logs, size):
    along = jnp.concatenate(as_rows(logs, size), axis=0)
    high = along.astype(jnp.bfloat16).astype(jnp.float32)
    middle = (along - high).astype(jnp.bfloat16).astype(jnp.float32)
    pieces = [output, high, middle, along - high - middle]
    pieces.append(jnp.zeros((EXTRA - 3 * along.shape[0], size), jnp.float32))
    return jnp.concatenate(pieces, axis=0).astype(jnp.bfloat16)


def logs_of(message, rows):
    tile = message[rows:].astype(jnp.float32)
    groups = pl.cdiv(rows, tile.shape[1])
    return as_column(sum(tile[k * groups : (k + 1) * groups] for k in range(3)), rows)


def parted(row, value):
    rows = value.shape[0] // 2
    first = row == 0
    return (
        jnp.where(first, value[:rows], value[rows:]),
        jnp.where(first, value[rows:], value[:rows]),
    )


def joined(first, second):
    (output, logs), (other, other_logs) = first, second
    top = jnp.maximum(logs, other_logs)
    weight, other_weight = jnp.exp(logs - top), jnp.exp(other_logs - top)
    total = weight + other_weight
    return (output * weight + other * other_weight) / total, top + jnp.log(total)


def own_block_kernel(scale, place_ref, chunk_one, chunk_two, out_ref, logs_ref):
    for index, (queries, keys) in enumerate(((chunk_one, chunk_two), (chunk_two, chunk_one))):
        height = keys.shape[0] - out_ref.shape[1] - EXTRA
        out_ref[index], logs_ref[index] = softmax_part(
            scale, queries[height:, :], [(keys[:height, :], True)], True
        )


def guest_kernel(
    scale, place_ref, two_away, swapped, neighbour, chunk_one, chunk_two, unused_ref, out_ref
):
    height, size = neighbour.shape
    begin = (height - EXTRA) // 2

    def attend(index, query, messages):
        output, logs = softmax_part(scale, query, [(m, True) for m in messages], False)
        out_ref[index] = as_message(output, logs, size)

    @pl.when(place_ref[0] == 0)
    def one_up():
        attend(1, neighbour[begin:, :], [chunk_one[:height, :]])

    @pl.when(place_ref[0] == 1)
    def down():
        keys = [neighbour[...], chunk_two[:height, :]]
        attend(1, two_away[begin:, :], keys)
        attend(0, swapped[begin:, :], keys)

    @pl.when(place_ref[0] == 2)
    def three_up():
        attend(0, neighbour[begin:, :], [two_away[...], swapped[...], chunk_one[:height, :]])


def own_rest_kernel(
    scale, place_ref, own_out, own_logs, chunk_one, chunk_two, two_away, swapped, neighbour,
    unused_ref, out_ref, logs_ref,
):
    tok = place_ref[0]
    height = neighbour.shape[0]
    out_ref[...] = own_out[...]
    logs_ref[...] = own_logs[...]

    def add(index, query, messages):
        part = softmax_part(scale, query, [(m, True) for m in messages], False)
        out_ref[index], logs_ref[index] = joined((own_out[index], own_logs[index]), part)

    @pl.when((tok == 1) | (tok == 3))
    def down():
        add(0, chunk_one[height:, :], [neighbour[...]])

    @pl.when(tok == 2)
    def up():
        add(1, chunk_two[height:, :], [swapped[...], two_away[...]])


def merge_kernel(
    place_ref, out_ref, logs_ref, first_ref, below_ref, mine_ref, theirs_ref
):
    block, size = out_ref.shape[1:]
    tok, row = place_ref[0], place_ref[1]

    def with_guest(index, message, present):
        guest = jnp.where(present, message[:block].astype(jnp.float32), 0.0)
        guest_logs = jnp.where(present, logs_of(message, block), LOW)
        output, logs = joined((out_ref[index], logs_ref[index]), (guest, guest_logs))
        return output.astype(jnp.bfloat16)

    down = with_guest(0, jnp.where(tok == 2, below_ref[...], first_ref[...]), tok >= 2)
    up = with_guest(1, jnp.where(tok == 1, first_ref[...], below_ref[...]), (tok == 1) | (tok == 3))
    for index, output in enumerate((down, up)):
        columns = slice(index * size, (index + 1) * size)
        mine_ref[:, columns], theirs_ref[:, columns] = parted(row, output)


def attend_gathered(query, keys, values, places, starts, scale):
    heads, count, size = query.shape
    chunk = math.gcd(keys.shape[1], 1024)
    rounds = keys.shape[1] // chunk
    stacked = (
        keys.reshape(heads, rounds, chunk, size).transpose(1, 0, 2, 3),
        values.reshape(heads, rounds, chunk, size).transpose(1, 0, 2, 3),
        jnp.arange(rounds * chunk, dtype=jnp.int32).reshape(rounds, chunk),
    )

    def advance(state, blocks):
        running, totals, summed = state
        block_keys, block_values, key_places = blocks
        scores = (
            jnp.einsum("hqd,hkd->hqk", query, block_keys, preferred_element_type=jnp.float32) * scale
        )
        visible = (key_places[None, None, :] <= places[None, :, None]) & (
            key_places[None, None, :] >= starts[None, :, None]
        )
        masked = jnp.where(visible, scores, -jnp.inf)
        newest = jnp.maximum(running, jnp.max(masked, axis=2))
        factor = jnp.exp(running - newest)
        exponentials = jnp.where(visible, jnp.exp(masked - newest[:, :, None]), 0.0)
        totals = totals * factor + jnp.sum(exponentials, axis=2)
        summed = summed * factor[:, :, None] + jnp.einsum(
            "hqk,hkd->hqd", exponentials.astype(jnp.bfloat16), block_values,
            preferred_element_type=jnp.float32,
        )
        return (newest, totals, summed), None

    initial = (
        jnp.full((heads, count), -1e30, jnp.float32),
        jnp.zeros((heads, count), jnp.float32),
        jnp.zeros((heads, count, size), jnp.float32),
    )
    (running, totals, summed), unused = lax.scan(advance, initial, stacked)
    attended = (summed / totals[:, :, None]).astype(jnp.bfloat16)
    return attended.transpose(1, 0, 2).reshape(count, heads * size)


def in_vmem(count):
    return [pl.BlockSpec(memory_space=pltpu.VMEM)] * count


def per_device(activations, norm_gain, qkv_weight, doc_ids):
    rows, width = activations.shape
    span, local_heads, triple = qkv_weight.shape
    size = triple // 3
    pair = local_heads // 2
    block = 2 * rows
    toks = lax.axis_size("tok")
    tok, row, col = lax.axis_index("tok"), lax.axis_index("row"), lax.axis_index("col")
    chip, core = col >> 1, col & 1
    grid = [(r, c) for r in range(2) for c in range(4)]

    def by_col(value, flip):
        return lax.ppermute(value, "col", [(c, c ^ flip) for c in range(4)])

    def by_row(value):
        return lax.ppermute(value, "row", [(0, 1), (1, 0)])

    def ordered(index, own, other):
        first = index == 0
        return jnp.concatenate([jnp.where(first, own, other), jnp.where(first, other, own)])

    near = lax.ppermute(
        activations,
        ("row", "col"),
        [(r * 4 + c, (c // 2) * 4 + 2 * r + c % 2) for r, c in grid],
    )
    far = lax.ppermute(
        activations,
        ("row", "col"),
        [(r * 4 + c, (c // 2) * 4 + 2 * (1 - r) + c % 2) for r, c in grid],
    )
    widened = activations.astype(jnp.float32)
    squares = jnp.sum(widened * widened, axis=1)
    gain = norm_gain.astype(jnp.float32)
    message = jnp.concatenate([squares, gain])
    got = by_col(message, 1)
    squares = squares + got[:rows]
    gain = ordered(core, gain, got[rows:])
    codes = doc_ids.astype(jnp.float32) + 1.0
    message = jnp.concatenate([squares, codes])
    message, qkv_weight = lax.optimization_barrier((message, qkv_weight))
    flat_weight = qkv_weight.reshape(span, local_heads * triple)
    got = by_row(message)
    got, flat_weight, near, far = lax.optimization_barrier((got, flat_weight, near, far))
    squares = ordered(row, squares, got[:rows])
    codes = ordered(row, codes, got[rows:])
    by_chip = by_col(jnp.concatenate([squares, gain]), 2)
    near_other, far_other = by_col(near, 1), by_col(far, 1)
    squares = (squares + by_chip[:block]).reshape(block, 1)
    gain = jnp.where(chip == row, gain, by_chip[block:]).reshape(2, 1, width)
    doc_rows = jnp.pad(codes, (0, EXTRA * size - block)).reshape(EXTRA, size)
    places = tok * block + jnp.arange(block, dtype=jnp.int32)
    cosine, sine = rotary_tables(places, size, near[0, : size // 2].astype(jnp.float32) < 1e30)

    taller = 3 * block + 2 * EXTRA
    break_at = 2 * block + EXTRA

    partial_sums = jax.ShapeDtypeStruct((taller, size), jnp.float32)
    no_cost = pl.CostEstimate(flops=0, bytes_accessed=0, transcendentals=0)
    *away, normed, own_weight = pl.pallas_call(
        normalise_project_kernel,
        out_shape=(
            partial_sums,
            partial_sums,
            jax.ShapeDtypeStruct((2, block, width), jnp.bfloat16),
            pltpu.HBM((span, pair * triple), jnp.bfloat16),
        ),
        in_specs=[pl.BlockSpec(memory_space=pltpu.SMEM)] + in_vmem(9),
        out_specs=tuple(in_vmem(3)) + (pl.BlockSpec(memory_space=pltpu.HBM),),
        scratch_shapes=[pltpu.SemaphoreType.DMA(())],
        compiler_params=pltpu.CompilerParams(vmem_limit_bytes=12 * MIB),
        cost_estimate=no_cost,
    )(
        jnp.stack([core, chip, (1 - row) * (pair * triple), row * (pair * triple)]),
        near, far, near_other, far_other, squares, gain, cosine, sine, flat_weight,
    )
    arrived = [by_row(chunk.astype(jnp.float16)) for chunk in away]
    own = pl.pallas_call(
        project_kernel,
        out_shape=(partial_sums, partial_sums),
        in_specs=in_vmem(4) + [pl.BlockSpec(memory_space=pltpu.HBM)],
        out_specs=tuple(in_vmem(2)),
        scratch_shapes=[
            pltpu.VMEM((span, pair * triple), jnp.bfloat16),
            pltpu.SemaphoreType.DMA(()),
        ],
        compiler_params=pltpu.CompilerParams(vmem_limit_bytes=8 * MIB),
        cost_estimate=no_cost,
    )(
        normed, doc_rows, cosine, sine, pltpu.with_memory_space_constraint(own_weight, pltpu.HBM)
    )
    scale = 1.0 / math.sqrt(size)

    def summed(chunk):
        return (own[chunk] + arrived[chunk].astype(jnp.float32)).astype(jnp.bfloat16)

    def gathered_attention():
        chunks = [summed(0), summed(1)]
        keys = jnp.stack([chunks[1][: 2 * block], chunks[0][: 2 * block]])
        everything = lax.all_gather(keys, "tok", axis=0, tiled=False).transpose(1, 0, 2, 3)
        all_codes = lax.all_gather(codes, "tok", axis=0, tiled=True)
        starts = jnp.sum((all_codes[None, :] < codes[:, None]).astype(jnp.int32), axis=1)
        together = attend_gathered(
            jnp.stack([chunk[break_at : break_at + block] for chunk in chunks]),
            everything[:, :, :block].reshape(pair, toks * block, size),
            everything[:, :, block:].reshape(pair, toks * block, size),
            places, starts, scale,
        )
        return parted(row, together)

    if toks == 4:
        places = jnp.stack([tok, row])

        def along_tok(value, pairs):
            return lax.ppermute(value, "tok", pairs)

        def keys_or_query(chunk, is_query):
            begin = jnp.where(is_query, taller - break_at, 0)
            return lax.dynamic_slice_in_dim(chunk, begin.astype(jnp.uint32), break_at, 0)

        def on_place(kernel, out_shape, ins, unused=0):
            return pl.pallas_call(
                kernel,
                out_shape=out_shape,
                in_specs=[pl.BlockSpec(memory_space=pltpu.SMEM)]
                + in_vmem(ins - unused)
                + [pl.BlockSpec(memory_space=pl.ANY)] * unused,
                out_specs=jax.tree.map(lambda unused: in_vmem(1)[0], out_shape),
                compiler_params=pltpu.CompilerParams(vmem_limit_bytes=16 * MIB),
                cost_estimate=pl.CostEstimate(flops=0, bytes_accessed=0, transcendentals=0),
            )

        chunk_one = summed(0)
        two_away = along_tok(keys_or_query(chunk_one, tok == 3), [(0, 2), (3, 1), (1, 0), (2, 3)])
        swapped = along_tok(keys_or_query(chunk_one, tok == 2), [(1, 2), (2, 1), (0, 0), (3, 3)])
        across = by_col(chunk_one[:EXTRA], 1)
        arrived[1] = jnp.where(
            tok < toks,
            arrived[1].astype(jnp.float32),
            jnp.broadcast_to(across[:1].astype(jnp.float32), arrived[1].shape),
        )
        chunk_two = summed(1)
        neighbour = along_tok(
            keys_or_query(chunk_two, (tok & 1) == 1), [(0, 1), (1, 0), (2, 3), (3, 2)]
        )
        part_shapes = (
            jax.ShapeDtypeStruct((2, block, size), jnp.float32),
            jax.ShapeDtypeStruct((2, block, 1), jnp.float32),
        )
        own_out, own_logs = on_place(
            lambda *refs: own_block_kernel(scale, *refs), part_shapes, 2
        )(places, chunk_one, chunk_two)
        guests = on_place(
            lambda *refs: guest_kernel(scale, *refs),
            jax.ShapeDtypeStruct((2, block + EXTRA, size), jnp.bfloat16),
            6,
            1,
        )(places, two_away, swapped, neighbour, chunk_one, chunk_two, own_logs)
        from_first = along_tok(guests[1], [(0, 1), (1, 3), (2, 0), (3, 2)])
        from_below = along_tok(guests[0], [(1, 2), (2, 3)])
        output, logs = on_place(
            lambda *refs: own_rest_kernel(scale, *refs), part_shapes, 8, 1
        )(places, own_out, own_logs, chunk_one, chunk_two, two_away, swapped, neighbour, guests)
        half = jax.ShapeDtypeStruct((rows, pair * size), jnp.bfloat16)
        mine, theirs = on_place(merge_kernel, (half, half), 4)(
            places, output, logs, from_first, from_below
        )
    else:
        mine, theirs = gathered_attention()
    theirs = by_row(theirs)
    return jnp.concatenate(
        [jnp.where(row == 0, mine, theirs), jnp.where(row == 0, theirs, mine)], axis=1
    )


def solution(mesh):
    placed = (P(("tok", "row"), "col"), P("col"), P("row", "col", None), P(("tok", "row")))
    return jax.shard_map(
        per_device, mesh=mesh, in_specs=placed, out_specs=P(("tok", "row"), "col"), check_vma=False
    )
```

```python
import math

import jax
import jax.numpy as jnp
from jax import lax
from jax.experimental import pallas as pl
from jax.experimental.pallas import tpu as pltpu
from jax.sharding import PartitionSpec as P

EPS = 1e-05
LOG2_E = math.log2(math.e)
LOW = -1e30
EXTRA = 16
MIB = 1 << 20
CHUNKS = ((4, 0), (1, 3))


def rotary_tables(places, head_size, always):
    half = head_size // 2
    spacing = jnp.arange(half).astype(jnp.float32) * (2.0 / head_size)
    inverse = jnp.where(always, jnp.power(10000.0, -spacing), 0.0)
    angles = places.astype(jnp.float32)[:, None] * inverse[None, :]
    cosine, sine = jnp.cos(angles), jnp.sin(angles)
    return (
        jnp.concatenate([cosine, cosine], axis=1),
        jnp.concatenate([-sine, sine], axis=1),
    )


def project_chunk(normed_ref, weight_ref, key_column, query_column, cos_ref, sin_ref, doc_rows, out_ref):
    block, size = cos_ref.shape
    extra = doc_rows.shape[0]
    depth = weight_ref.shape[0] // 2

    def product(column, width):
        at = pl.ds(column if isinstance(column, int) else pl.multiple_of(column, size), width)
        return jnp.dot(
            normed_ref[0], weight_ref[:depth, at], preferred_element_type=jnp.float32
        ) + jnp.dot(normed_ref[1], weight_ref[depth:, at], preferred_element_type=jnp.float32)

    def rotated(piece):
        return piece * cos_ref[...] + pltpu.roll(piece, size // 2, 1) * sin_ref[...]

    both = product(key_column, 2 * size)
    out_ref[:block, :] = rotated(both[:, :size])
    out_ref[block : 2 * block, :] = both[:, size:]
    out_ref[2 * block : 2 * block + extra, :] = doc_rows
    out_ref[2 * block + extra : 3 * block + extra, :] = rotated(product(query_column, size))
    out_ref[3 * block + extra :, :] = doc_rows


def normalise_project_kernel(
    place_ref, a_near, a_far, b_near, b_far, squares_ref, gain_ref, cos_ref, sin_ref, weight_ref,
    one_ref, two_ref, normed_ref, own_hbm, semaphore,
):
    rows, size = a_near.shape[0], cos_ref.shape[1]
    features = 2 * gain_ref.shape[0] * gain_ref.shape[2]
    core, near_row, away, own = place_ref[0], place_ref[1], place_ref[2], place_ref[3]
    copy = pltpu.make_async_copy(
        weight_ref.at[:, pl.ds(pl.multiple_of(own, size), 6 * size)], own_hbm, semaphore
    )
    copy.start()
    for shards, half in (((a_near, a_far), core), ((b_near, b_far), 1 - core)):
        gain = gain_ref[half]
        for shard, row in zip(shards, (near_row, 1 - near_row)):
            at = pl.ds(pl.multiple_of(row * rows, 16), rows)
            factor = lax.rsqrt(squares_ref[at, :] / features + EPS)
            normed_ref[half, at, :] = (shard[...].astype(jnp.float32) * factor * gain).astype(
                jnp.bfloat16
            )
    nothing = jnp.zeros((EXTRA, size), jnp.float32)
    for chunk, (keys, query) in enumerate(CHUNKS):
        project_chunk(
            normed_ref, weight_ref, away + keys * size, away + query * size, cos_ref, sin_ref, nothing,
            (one_ref, two_ref)[chunk],
        )
    copy.wait()


def project_kernel(
    normed_ref, docs_ref, cos_ref, sin_ref, own_hbm, one_ref, two_ref, weight_buffer, semaphore
):
    copy = pltpu.make_async_copy(own_hbm, weight_buffer, semaphore)
    copy.start()
    copy.wait()
    size = cos_ref.shape[1]
    for chunk, (keys, query) in enumerate(CHUNKS):
        project_chunk(
            normed_ref, weight_buffer, keys * size, query * size, cos_ref, sin_ref, docs_ref[...],
            (one_ref, two_ref)[chunk],
        )


def as_column(rows, count):
    lanes = rows.shape[1]
    pieces = []
    for begin in range(0, count, lanes):
        held = min(lanes, count - begin)
        at = lax.broadcasted_iota(jnp.int32, (held, lanes), 0)
        diagonal = at == lax.broadcasted_iota(jnp.int32, (held, lanes), 1)
        row = rows[begin // lanes : begin // lanes + 1, :]
        pieces.append(jnp.sum(jnp.where(diagonal, row, 0.0), axis=1, keepdims=True))
    return jnp.concatenate(pieces, axis=0)


def as_rows(column, lanes):
    count = column.shape[0]
    rows = []
    for begin in range(0, count, lanes):
        held = min(lanes, count - begin)
        at = lax.broadcasted_iota(jnp.int32, (held, lanes), 0)
        diagonal = at == lax.broadcasted_iota(jnp.int32, (held, lanes), 1)
        rows.append(
            jnp.sum(jnp.where(diagonal, column[begin : begin + held], 0.0), axis=0, keepdims=True)
        )
    return rows


def as_lanes(rows, count):
    lanes = rows.shape[1]
    return jnp.concatenate(
        [
            rows[begin // lanes : begin // lanes + 1, : min(lanes, count - begin)]
            for begin in range(0, count, lanes)
        ],
        axis=1,
    )


def softmax_part(scale, query_message, messages, causal):
    valid = [present for message, present in messages]
    messages = [message for message, present in messages]
    query = query_message[:-EXTRA]
    query_docs = as_column(query_message[-EXTRA:].astype(jnp.float32), query.shape[0])
    block = (messages[0].shape[0] - EXTRA) // 2
    keys = jnp.concatenate([message[:block] for message in messages], axis=0)
    values = jnp.concatenate([message[block : 2 * block] for message in messages], axis=0)
    key_docs = jnp.concatenate(
        [
            jnp.where(present, as_lanes(message[2 * block :].astype(jnp.float32), block), 0.0)
            for message, present in zip(messages, valid)
        ],
        axis=1,
    )
    visible = query_docs == key_docs
    if causal:
        shape = (query.shape[0], keys.shape[0])
        query_places = lax.broadcasted_iota(jnp.int32, shape, 0)
        key_places = lax.broadcasted_iota(jnp.int32, shape, 1)
        visible &= (key_places <= query_places) | (key_places >= block)
    scores = lax.dot_general(
        query, keys, (((1,), (1,)), ((), ())), preferred_element_type=jnp.float32
    )
    masked = jnp.where(visible, scores, LOW)
    top = jnp.max(masked, axis=1, keepdims=True)
    exponentials = jnp.exp2((masked - top) * (scale * LOG2_E))
    total = jnp.sum(exponentials, axis=1, keepdims=True)
    summed = jnp.dot(exponentials.astype(jnp.bfloat16), values, preferred_element_type=jnp.float32)
    return summed / total, jnp.where(top > LOW / 2, top * scale + jnp.log(total), LOW)


def as_message(output, logs, size):
    along = jnp.concatenate(as_rows(logs, size), axis=0)
    high = along.astype(jnp.bfloat16).astype(jnp.float32)
    middle = (along - high).astype(jnp.bfloat16).astype(jnp.float32)
    pieces = [output, high, middle, along - high - middle]
    pieces.append(jnp.zeros((EXTRA - 3 * along.shape[0], size), jnp.float32))
    return jnp.concatenate(pieces, axis=0).astype(jnp.bfloat16)


def logs_of(message, rows):
    tile = message[rows:].astype(jnp.float32)
    groups = pl.cdiv(rows, tile.shape[1])
    return as_column(sum(tile[k * groups : (k + 1) * groups] for k in range(3)), rows)


def parted(row, value):
    rows = value.shape[0] // 2
    first = row == 0
    return (
        jnp.where(first, value[:rows], value[rows:]),
        jnp.where(first, value[rows:], value[:rows]),
    )


def joined(first, second):
    (output, logs), (other, other_logs) = first, second
    top = jnp.maximum(logs, other_logs)
    weight, other_weight = jnp.exp(logs - top), jnp.exp(other_logs - top)
    total = weight + other_weight
    return (output * weight + other * other_weight) / total, top + jnp.log(total)


def own_block_kernel(scale, place_ref, chunk_one, chunk_two, out_ref, logs_ref):
    for index, (queries, keys) in enumerate(((chunk_one, chunk_two), (chunk_two, chunk_one))):
        height = keys.shape[0] - out_ref.shape[1] - EXTRA
        out_ref[index], logs_ref[index] = softmax_part(
            scale, queries[height:, :], [(keys[:height, :], True)], True
        )


def guest_kernel(
    scale, place_ref, two_away, swapped, neighbour, chunk_one, chunk_two, unused_ref, out_ref
):
    height, size = neighbour.shape
    begin = (height - EXTRA) // 2

    def attend(index, query, messages):
        output, logs = softmax_part(scale, query, [(m, True) for m in messages], False)
        out_ref[index] = as_message(output, logs, size)

    @pl.when(place_ref[0] == 0)
    def one_up():
        attend(1, neighbour[begin:, :], [chunk_one[:height, :]])

    @pl.when(place_ref[0] == 1)
    def down():
        keys = [neighbour[...], chunk_two[:height, :]]
        attend(1, two_away[begin:, :], keys)
        attend(0, swapped[begin:, :], keys)

    @pl.when(place_ref[0] == 2)
    def three_up():
        attend(0, neighbour[begin:, :], [two_away[...], swapped[...], chunk_one[:height, :]])


def own_rest_kernel(
    scale, place_ref, own_out, own_logs, chunk_one, chunk_two, two_away, swapped, neighbour,
    unused_ref, out_ref, logs_ref,
):
    tok = place_ref[0]
    height = neighbour.shape[0]
    out_ref[...] = own_out[...]
    logs_ref[...] = own_logs[...]

    def add(index, query, messages):
        part = softmax_part(scale, query, [(m, True) for m in messages], False)
        out_ref[index], logs_ref[index] = joined((own_out[index], own_logs[index]), part)

    @pl.when((tok == 1) | (tok == 3))
    def down():
        add(0, chunk_one[height:, :], [neighbour[...]])

    @pl.when(tok == 2)
    def up():
        add(1, chunk_two[height:, :], [swapped[...], two_away[...]])


def merge_kernel(
    place_ref, out_ref, logs_ref, first_ref, below_ref, mine_ref, theirs_ref
):
    block, size = out_ref.shape[1:]
    tok, row = place_ref[0], place_ref[1]

    def with_guest(index, message, present):
        guest = jnp.where(present, message[:block].astype(jnp.float32), 0.0)
        guest_logs = jnp.where(present, logs_of(message, block), LOW)
        output, logs = joined((out_ref[index], logs_ref[index]), (guest, guest_logs))
        return output.astype(jnp.bfloat16)

    down = with_guest(0, jnp.where(tok == 2, below_ref[...], first_ref[...]), tok >= 2)
    up = with_guest(1, jnp.where(tok == 1, first_ref[...], below_ref[...]), (tok == 1) | (tok == 3))
    for index, output in enumerate((down, up)):
        columns = slice(index * size, (index + 1) * size)
        mine_ref[:, columns], theirs_ref[:, columns] = parted(row, output)


def attend_gathered(query, keys, values, places, starts, scale):
    heads, count, size = query.shape
    chunk = math.gcd(keys.shape[1], 1024)
    rounds = keys.shape[1] // chunk
    stacked = (
        keys.reshape(heads, rounds, chunk, size).transpose(1, 0, 2, 3),
        values.reshape(heads, rounds, chunk, size).transpose(1, 0, 2, 3),
        jnp.arange(rounds * chunk, dtype=jnp.int32).reshape(rounds, chunk),
    )

    def advance(state, blocks):
        running, totals, summed = state
        block_keys, block_values, key_places = blocks
        scores = (
            jnp.einsum("hqd,hkd->hqk", query, block_keys, preferred_element_type=jnp.float32) * scale
        )
        visible = (key_places[None, None, :] <= places[None, :, None]) & (
            key_places[None, None, :] >= starts[None, :, None]
        )
        masked = jnp.where(visible, scores, -jnp.inf)
        newest = jnp.maximum(running, jnp.max(masked, axis=2))
        factor = jnp.exp(running - newest)
        exponentials = jnp.where(visible, jnp.exp(masked - newest[:, :, None]), 0.0)
        totals = totals * factor + jnp.sum(exponentials, axis=2)
        summed = summed * factor[:, :, None] + jnp.einsum(
            "hqk,hkd->hqd", exponentials.astype(jnp.bfloat16), block_values,
            preferred_element_type=jnp.float32,
        )
        return (newest, totals, summed), None

    initial = (
        jnp.full((heads, count), -1e30, jnp.float32),
        jnp.zeros((heads, count), jnp.float32),
        jnp.zeros((heads, count, size), jnp.float32),
    )
    (running, totals, summed), unused = lax.scan(advance, initial, stacked)
    attended = (summed / totals[:, :, None]).astype(jnp.bfloat16)
    return attended.transpose(1, 0, 2).reshape(count, heads * size)


def in_vmem(count):
    return [pl.BlockSpec(memory_space=pltpu.VMEM)] * count


def per_device(activations, norm_gain, qkv_weight, doc_ids):
    rows, width = activations.shape
    span, local_heads, triple = qkv_weight.shape
    size = triple // 3
    pair = local_heads // 2
    block = 2 * rows
    toks = lax.axis_size("tok")
    tok, row, col = lax.axis_index("tok"), lax.axis_index("row"), lax.axis_index("col")
    chip, core = col >> 1, col & 1
    grid = [(r, c) for r in range(2) for c in range(4)]

    def by_col(value, flip):
        return lax.ppermute(value, "col", [(c, c ^ flip) for c in range(4)])

    def by_row(value):
        return lax.ppermute(value, "row", [(0, 1), (1, 0)])

    def ordered(index, own, other):
        first = index == 0
        return jnp.concatenate([jnp.where(first, own, other), jnp.where(first, other, own)])

    near = lax.ppermute(
        activations,
        ("row", "col"),
        [(r * 4 + c, (c // 2) * 4 + 2 * r + c % 2) for r, c in grid],
    )
    far = lax.ppermute(
        activations,
        ("row", "col"),
        [(r * 4 + c, (c // 2) * 4 + 2 * (1 - r) + c % 2) for r, c in grid],
    )
    widened = activations.astype(jnp.float32)
    squares = jnp.sum(widened * widened, axis=1)
    gain = norm_gain.astype(jnp.float32)
    message = jnp.concatenate([squares, gain])
    message, qkv_weight = lax.optimization_barrier((message, qkv_weight))
    flat_weight = qkv_weight.reshape(span, local_heads * triple)
    got = by_col(message, 1)
    squares = squares + got[:rows]
    gain = ordered(core, gain, got[rows:])
    by_chip = by_col(jnp.concatenate([squares, gain]), 2)
    near, far, by_chip, flat_weight = lax.optimization_barrier((near, far, by_chip, flat_weight))
    near_other, far_other = by_col(near, 1), by_col(far, 1)
    squares = squares + by_chip[:rows]
    gain = jnp.where(chip == row, gain, by_chip[rows:]).reshape(2, 1, width)
    codes = doc_ids.astype(jnp.float32) + 1.0
    got = by_row(jnp.concatenate([squares, codes]))
    squares = ordered(row, squares, got[:rows]).reshape(block, 1)
    codes = ordered(row, codes, got[rows:])
    doc_rows = jnp.pad(codes, (0, EXTRA * size - block)).reshape(EXTRA, size)
    places = tok * block + jnp.arange(block, dtype=jnp.int32)
    cosine, sine = rotary_tables(places, size, near[0, : size // 2].astype(jnp.float32) < 1e30)

    taller = 3 * block + 2 * EXTRA
    break_at = 2 * block + EXTRA

    partial_sums = jax.ShapeDtypeStruct((taller, size), jnp.float32)
    no_cost = pl.CostEstimate(flops=0, bytes_accessed=0, transcendentals=0)
    *away, normed, own_weight = pl.pallas_call(
        normalise_project_kernel,
        out_shape=(
            partial_sums,
            partial_sums,
            jax.ShapeDtypeStruct((2, block, width), jnp.bfloat16),
            pltpu.HBM((span, pair * triple), jnp.bfloat16),
        ),
        in_specs=[pl.BlockSpec(memory_space=pltpu.SMEM)] + in_vmem(9),
        out_specs=tuple(in_vmem(3)) + (pl.BlockSpec(memory_space=pltpu.HBM),),
        scratch_shapes=[pltpu.SemaphoreType.DMA(())],
        compiler_params=pltpu.CompilerParams(vmem_limit_bytes=12 * MIB),
        cost_estimate=no_cost,
    )(
        jnp.stack([core, chip, (1 - row) * (pair * triple), row * (pair * triple)]),
        near, far, near_other, far_other, squares, gain, cosine, sine, flat_weight,
    )
    arrived = [by_row(chunk.astype(jnp.float16)) for chunk in away]
    own = pl.pallas_call(
        project_kernel,
        out_shape=(partial_sums, partial_sums),
        in_specs=in_vmem(4) + [pl.BlockSpec(memory_space=pltpu.HBM)],
        out_specs=tuple(in_vmem(2)),
        scratch_shapes=[
            pltpu.VMEM((span, pair * triple), jnp.bfloat16),
            pltpu.SemaphoreType.DMA(()),
        ],
        compiler_params=pltpu.CompilerParams(vmem_limit_bytes=8 * MIB),
        cost_estimate=no_cost,
    )(
        normed, doc_rows, cosine, sine, pltpu.with_memory_space_constraint(own_weight, pltpu.HBM)
    )
    scale = 1.0 / math.sqrt(size)

    def summed(chunk):
        return (own[chunk] + arrived[chunk].astype(jnp.float32)).astype(jnp.bfloat16)

    def gathered_attention():
        chunks = [summed(0), summed(1)]
        keys = jnp.stack([chunks[1][: 2 * block], chunks[0][: 2 * block]])
        everything = lax.all_gather(keys, "tok", axis=0, tiled=False).transpose(1, 0, 2, 3)
        all_codes = lax.all_gather(codes, "tok", axis=0, tiled=True)
        starts = jnp.sum((all_codes[None, :] < codes[:, None]).astype(jnp.int32), axis=1)
        together = attend_gathered(
            jnp.stack([chunk[break_at : break_at + block] for chunk in chunks]),
            everything[:, :, :block].reshape(pair, toks * block, size),
            everything[:, :, block:].reshape(pair, toks * block, size),
            places, starts, scale,
        )
        return parted(row, together)

    if toks == 4:
        places = jnp.stack([tok, row])

        def along_tok(value, pairs):
            return lax.ppermute(value, "tok", pairs)

        def keys_or_query(chunk, is_query):
            begin = jnp.where(is_query, taller - break_at, 0)
            return lax.dynamic_slice_in_dim(chunk, begin.astype(jnp.uint32), break_at, 0)

        def on_place(kernel, out_shape, ins, unused=0):
            return pl.pallas_call(
                kernel,
                out_shape=out_shape,
                in_specs=[pl.BlockSpec(memory_space=pltpu.SMEM)]
                + in_vmem(ins - unused)
                + [pl.BlockSpec(memory_space=pl.ANY)] * unused,
                out_specs=jax.tree.map(lambda unused: in_vmem(1)[0], out_shape),
                compiler_params=pltpu.CompilerParams(vmem_limit_bytes=16 * MIB),
                cost_estimate=pl.CostEstimate(flops=0, bytes_accessed=0, transcendentals=0),
            )

        chunk_one = summed(0)
        two_away = along_tok(keys_or_query(chunk_one, tok == 3), [(0, 2), (3, 1), (1, 0), (2, 3)])
        swapped = along_tok(keys_or_query(chunk_one, tok == 2), [(1, 2), (2, 1), (0, 0), (3, 3)])
        across = by_col(chunk_one[:EXTRA], 2)
        arrived[1] = jnp.where(
            tok < toks,
            arrived[1].astype(jnp.float32),
            jnp.broadcast_to(across[:1].astype(jnp.float32), arrived[1].shape),
        )
        chunk_two = summed(1)
        neighbour = along_tok(
            keys_or_query(chunk_two, (tok & 1) == 1), [(0, 1), (1, 0), (2, 3), (3, 2)]
        )
        part_shapes = (
            jax.ShapeDtypeStruct((2, block, size), jnp.float32),
            jax.ShapeDtypeStruct((2, block, 1), jnp.float32),
        )
        own_out, own_logs = on_place(
            lambda *refs: own_block_kernel(scale, *refs), part_shapes, 2
        )(places, chunk_one, chunk_two)
        guests = on_place(
            lambda *refs: guest_kernel(scale, *refs),
            jax.ShapeDtypeStruct((2, block + EXTRA, size), jnp.bfloat16),
            6,
            1,
        )(places, two_away, swapped, neighbour, chunk_one, chunk_two, own_logs)
        from_first = along_tok(guests[1], [(0, 1), (1, 3), (2, 0), (3, 2)])
        from_below = along_tok(guests[0], [(1, 2), (2, 3)])
        output, logs = on_place(
            lambda *refs: own_rest_kernel(scale, *refs), part_shapes, 8, 1
        )(places, own_out, own_logs, chunk_one, chunk_two, two_away, swapped, neighbour, guests)
        half = jax.ShapeDtypeStruct((rows, pair * size), jnp.bfloat16)
        mine, theirs = on_place(merge_kernel, (half, half), 4)(
            places, output, logs, from_first, from_below
        )
    else:
        mine, theirs = gathered_attention()
    theirs = by_row(theirs)
    return jnp.concatenate(
        [jnp.where(row == 0, mine, theirs), jnp.where(row == 0, theirs, mine)], axis=1
    )


def solution(mesh):
    placed = (P(("tok", "row"), "col"), P("col"), P("row", "col", None), P(("tok", "row")))
    return jax.shard_map(
        per_device, mesh=mesh, in_specs=placed, out_specs=P(("tok", "row"), "col"), check_vma=False
    )
```

```python
import math

import jax
import jax.numpy as jnp
from jax import lax
from jax.experimental import pallas as pl
from jax.experimental.pallas import tpu as pltpu
from jax.sharding import PartitionSpec as P

EPS = 1e-05
LOG2_E = math.log2(math.e)
LOW = -1e30
EXTRA = 16
MIB = 1 << 20
CHUNKS = ((4, 0), (1, 3))


def rotary_tables(places, head_size, always):
    half = head_size // 2
    spacing = jnp.arange(half).astype(jnp.float32) * (2.0 / head_size)
    inverse = jnp.where(always, jnp.power(10000.0, -spacing), 0.0)
    angles = places.astype(jnp.float32)[:, None] * inverse[None, :]
    cosine, sine = jnp.cos(angles), jnp.sin(angles)
    return (
        jnp.concatenate([cosine, cosine], axis=1),
        jnp.concatenate([-sine, sine], axis=1),
    )


def project_chunk(normed_ref, weight_ref, key_column, query_column, cos_ref, sin_ref, doc_rows, out_ref):
    block, size = cos_ref.shape
    extra = doc_rows.shape[0]
    depth = weight_ref.shape[0] // 2

    def product(column, width):
        at = pl.ds(column if isinstance(column, int) else pl.multiple_of(column, size), width)
        return jnp.dot(
            normed_ref[0], weight_ref[:depth, at], preferred_element_type=jnp.float32
        ) + jnp.dot(normed_ref[1], weight_ref[depth:, at], preferred_element_type=jnp.float32)

    def rotated(piece):
        return piece * cos_ref[...] + pltpu.roll(piece, size // 2, 1) * sin_ref[...]

    both = product(key_column, 2 * size)
    out_ref[:block, :] = rotated(both[:, :size])
    out_ref[block : 2 * block, :] = both[:, size:]
    out_ref[2 * block : 2 * block + extra, :] = doc_rows
    out_ref[2 * block + extra : 3 * block + extra, :] = rotated(product(query_column, size))
    out_ref[3 * block + extra :, :] = doc_rows


def normalise_project_kernel(
    place_ref, a_near, a_far, b_near, b_far, squares_ref, gain_ref, cos_ref, sin_ref, weight_ref,
    one_ref, two_ref, normed_ref, own_hbm, semaphore,
):
    rows, size = a_near.shape[0], cos_ref.shape[1]
    features = 2 * gain_ref.shape[0] * gain_ref.shape[2]
    core, near_row, away, own = place_ref[0], place_ref[1], place_ref[2], place_ref[3]
    copy = pltpu.make_async_copy(
        weight_ref.at[:, pl.ds(pl.multiple_of(own, size), 6 * size)], own_hbm, semaphore
    )
    copy.start()
    for shards, half in (((a_near, a_far), core), ((b_near, b_far), 1 - core)):
        gain = gain_ref[half]
        for shard, row in zip(shards, (near_row, 1 - near_row)):
            at = pl.ds(pl.multiple_of(row * rows, 16), rows)
            factor = lax.rsqrt(squares_ref[at, :] / features + EPS)
            normed_ref[half, at, :] = (shard[...].astype(jnp.float32) * factor * gain).astype(
                jnp.bfloat16
            )
    nothing = jnp.zeros((EXTRA, size), jnp.float32)
    for chunk, (keys, query) in enumerate(CHUNKS):
        project_chunk(
            normed_ref, weight_ref, away + keys * size, away + query * size, cos_ref, sin_ref, nothing,
            (one_ref, two_ref)[chunk],
        )
    copy.wait()


def project_kernel(
    normed_ref, docs_ref, cos_ref, sin_ref, own_hbm, one_ref, two_ref, weight_buffer, semaphore
):
    copy = pltpu.make_async_copy(own_hbm, weight_buffer, semaphore)
    copy.start()
    copy.wait()
    size = cos_ref.shape[1]
    for chunk, (keys, query) in enumerate(CHUNKS):
        project_chunk(
            normed_ref, weight_buffer, keys * size, query * size, cos_ref, sin_ref, docs_ref[...],
            (one_ref, two_ref)[chunk],
        )


def as_column(rows, count):
    lanes = rows.shape[1]
    pieces = []
    for begin in range(0, count, lanes):
        held = min(lanes, count - begin)
        at = lax.broadcasted_iota(jnp.int32, (held, lanes), 0)
        diagonal = at == lax.broadcasted_iota(jnp.int32, (held, lanes), 1)
        row = rows[begin // lanes : begin // lanes + 1, :]
        pieces.append(jnp.sum(jnp.where(diagonal, row, 0.0), axis=1, keepdims=True))
    return jnp.concatenate(pieces, axis=0)


def as_rows(column, lanes):
    count = column.shape[0]
    rows = []
    for begin in range(0, count, lanes):
        held = min(lanes, count - begin)
        at = lax.broadcasted_iota(jnp.int32, (held, lanes), 0)
        diagonal = at == lax.broadcasted_iota(jnp.int32, (held, lanes), 1)
        rows.append(
            jnp.sum(jnp.where(diagonal, column[begin : begin + held], 0.0), axis=0, keepdims=True)
        )
    return rows


def as_lanes(rows, count):
    lanes = rows.shape[1]
    return jnp.concatenate(
        [
            rows[begin // lanes : begin // lanes + 1, : min(lanes, count - begin)]
            for begin in range(0, count, lanes)
        ],
        axis=1,
    )


def softmax_part(scale, query_message, messages, causal):
    valid = [present for message, present in messages]
    messages = [message for message, present in messages]
    query = query_message[:-EXTRA]
    query_docs = as_column(query_message[-EXTRA:].astype(jnp.float32), query.shape[0])
    block = (messages[0].shape[0] - EXTRA) // 2
    keys = jnp.concatenate([message[:block] for message in messages], axis=0)
    values = jnp.concatenate([message[block : 2 * block] for message in messages], axis=0)
    key_docs = jnp.concatenate(
        [
            jnp.where(present, as_lanes(message[2 * block :].astype(jnp.float32), block), 0.0)
            for message, present in zip(messages, valid)
        ],
        axis=1,
    )
    visible = query_docs == key_docs
    if causal:
        shape = (query.shape[0], keys.shape[0])
        query_places = lax.broadcasted_iota(jnp.int32, shape, 0)
        key_places = lax.broadcasted_iota(jnp.int32, shape, 1)
        visible &= (key_places <= query_places) | (key_places >= block)
    scores = lax.dot_general(
        query, keys, (((1,), (1,)), ((), ())), preferred_element_type=jnp.float32
    )
    masked = jnp.where(visible, scores, LOW)
    top = jnp.max(masked, axis=1, keepdims=True)
    exponentials = jnp.exp2((masked - top) * (scale * LOG2_E))
    total = jnp.sum(exponentials, axis=1, keepdims=True)
    summed = jnp.dot(exponentials.astype(jnp.bfloat16), values, preferred_element_type=jnp.float32)
    return summed / total, jnp.where(top > LOW / 2, top * scale + jnp.log(total), LOW)


def as_message(output, logs, size):
    along = jnp.concatenate(as_rows(logs, size), axis=0)
    high = along.astype(jnp.bfloat16).astype(jnp.float32)
    middle = (along - high).astype(jnp.bfloat16).astype(jnp.float32)
    pieces = [output, high, middle, along - high - middle]
    pieces.append(jnp.zeros((EXTRA - 3 * along.shape[0], size), jnp.float32))
    return jnp.concatenate(pieces, axis=0).astype(jnp.bfloat16)


def logs_of(message, rows):
    tile = message[rows:].astype(jnp.float32)
    groups = pl.cdiv(rows, tile.shape[1])
    return as_column(sum(tile[k * groups : (k + 1) * groups] for k in range(3)), rows)


def parted(row, value):
    rows = value.shape[0] // 2
    first = row == 0
    return (
        jnp.where(first, value[:rows], value[rows:]),
        jnp.where(first, value[rows:], value[:rows]),
    )


def joined(first, second):
    (output, logs), (other, other_logs) = first, second
    top = jnp.maximum(logs, other_logs)
    weight, other_weight = jnp.exp(logs - top), jnp.exp(other_logs - top)
    total = weight + other_weight
    return (output * weight + other * other_weight) / total, top + jnp.log(total)


def own_block_kernel(scale, place_ref, chunk_one, chunk_two, out_ref, logs_ref):
    for index, (queries, keys) in enumerate(((chunk_one, chunk_two), (chunk_two, chunk_one))):
        height = keys.shape[0] - out_ref.shape[1] - EXTRA
        out_ref[index], logs_ref[index] = softmax_part(
            scale, queries[height:, :], [(keys[:height, :], True)], True
        )


def guest_kernel(
    scale, place_ref, two_away, swapped, neighbour, chunk_one, chunk_two, unused_ref, out_ref
):
    height, size = neighbour.shape
    begin = (height - EXTRA) // 2

    def attend(index, query, messages):
        output, logs = softmax_part(scale, query, [(m, True) for m in messages], False)
        out_ref[index] = as_message(output, logs, size)

    @pl.when(place_ref[0] == 0)
    def one_up():
        attend(1, neighbour[begin:, :], [chunk_one[:height, :]])

    @pl.when(place_ref[0] == 1)
    def down():
        keys = [neighbour[...], chunk_two[:height, :]]
        attend(1, two_away[begin:, :], keys)
        attend(0, swapped[begin:, :], keys)

    @pl.when(place_ref[0] == 2)
    def three_up():
        attend(0, neighbour[begin:, :], [two_away[...], swapped[...], chunk_one[:height, :]])


def own_rest_kernel(
    scale, place_ref, own_out, own_logs, chunk_one, chunk_two, two_away, swapped, neighbour,
    unused_ref, out_ref, logs_ref,
):
    tok = place_ref[0]
    height = neighbour.shape[0]
    out_ref[...] = own_out[...]
    logs_ref[...] = own_logs[...]

    def add(index, query, messages):
        part = softmax_part(scale, query, [(m, True) for m in messages], False)
        out_ref[index], logs_ref[index] = joined((own_out[index], own_logs[index]), part)

    @pl.when((tok == 1) | (tok == 3))
    def down():
        add(0, chunk_one[height:, :], [neighbour[...]])

    @pl.when(tok == 2)
    def up():
        add(1, chunk_two[height:, :], [swapped[...], two_away[...]])


def merge_kernel(
    place_ref, out_ref, logs_ref, first_ref, below_ref, mine_ref, theirs_ref
):
    block, size = out_ref.shape[1:]
    tok, row = place_ref[0], place_ref[1]

    def with_guest(index, message, present):
        guest = jnp.where(present, message[:block].astype(jnp.float32), 0.0)
        guest_logs = jnp.where(present, logs_of(message, block), LOW)
        output, logs = joined((out_ref[index], logs_ref[index]), (guest, guest_logs))
        return output.astype(jnp.bfloat16)

    down = with_guest(0, jnp.where(tok == 2, below_ref[...], first_ref[...]), tok >= 2)
    up = with_guest(1, jnp.where(tok == 1, first_ref[...], below_ref[...]), (tok == 1) | (tok == 3))
    for index, output in enumerate((down, up)):
        columns = slice(index * size, (index + 1) * size)
        mine_ref[:, columns], theirs_ref[:, columns] = parted(row, output)


def attend_gathered(query, keys, values, places, starts, scale):
    heads, count, size = query.shape
    chunk = math.gcd(keys.shape[1], 1024)
    rounds = keys.shape[1] // chunk
    stacked = (
        keys.reshape(heads, rounds, chunk, size).transpose(1, 0, 2, 3),
        values.reshape(heads, rounds, chunk, size).transpose(1, 0, 2, 3),
        jnp.arange(rounds * chunk, dtype=jnp.int32).reshape(rounds, chunk),
    )

    def advance(state, blocks):
        running, totals, summed = state
        block_keys, block_values, key_places = blocks
        scores = (
            jnp.einsum("hqd,hkd->hqk", query, block_keys, preferred_element_type=jnp.float32) * scale
        )
        visible = (key_places[None, None, :] <= places[None, :, None]) & (
            key_places[None, None, :] >= starts[None, :, None]
        )
        masked = jnp.where(visible, scores, -jnp.inf)
        newest = jnp.maximum(running, jnp.max(masked, axis=2))
        factor = jnp.exp(running - newest)
        exponentials = jnp.where(visible, jnp.exp(masked - newest[:, :, None]), 0.0)
        totals = totals * factor + jnp.sum(exponentials, axis=2)
        summed = summed * factor[:, :, None] + jnp.einsum(
            "hqk,hkd->hqd", exponentials.astype(jnp.bfloat16), block_values,
            preferred_element_type=jnp.float32,
        )
        return (newest, totals, summed), None

    initial = (
        jnp.full((heads, count), -1e30, jnp.float32),
        jnp.zeros((heads, count), jnp.float32),
        jnp.zeros((heads, count, size), jnp.float32),
    )
    (running, totals, summed), unused = lax.scan(advance, initial, stacked)
    attended = (summed / totals[:, :, None]).astype(jnp.bfloat16)
    return attended.transpose(1, 0, 2).reshape(count, heads * size)


def in_vmem(count):
    return [pl.BlockSpec(memory_space=pltpu.VMEM)] * count


def per_device(activations, norm_gain, qkv_weight, doc_ids):
    rows, width = activations.shape
    span, local_heads, triple = qkv_weight.shape
    size = triple // 3
    pair = local_heads // 2
    block = 2 * rows
    toks = lax.axis_size("tok")
    tok, row, col = lax.axis_index("tok"), lax.axis_index("row"), lax.axis_index("col")
    chip, core = col >> 1, col & 1
    grid = [(r, c) for r in range(2) for c in range(4)]

    def by_col(value, flip):
        return lax.ppermute(value, "col", [(c, c ^ flip) for c in range(4)])

    def by_row(value):
        return lax.ppermute(value, "row", [(0, 1), (1, 0)])

    def ordered(index, own, other):
        first = index == 0
        return jnp.concatenate([jnp.where(first, own, other), jnp.where(first, other, own)])

    near = lax.ppermute(
        activations,
        ("row", "col"),
        [(r * 4 + c, (c // 2) * 4 + 2 * r + c % 2) for r, c in grid],
    )
    far = lax.ppermute(
        activations,
        ("row", "col"),
        [(r * 4 + c, (c // 2) * 4 + 2 * (1 - r) + c % 2) for r, c in grid],
    )
    widened = activations.astype(jnp.float32)
    squares = jnp.sum(widened * widened, axis=1)
    gain = norm_gain.astype(jnp.float32)
    message = jnp.concatenate([squares, gain])
    message, qkv_weight = lax.optimization_barrier((message, qkv_weight))
    flat_weight = qkv_weight.reshape(span, local_heads * triple)
    got = by_col(message, 1)
    squares = squares + got[:rows]
    gain = ordered(core, gain, got[rows:])
    by_chip = by_col(jnp.concatenate([squares, gain]), 2)
    near, far, by_chip, flat_weight = lax.optimization_barrier((near, far, by_chip, flat_weight))
    near_other, far_other = by_col(near, 1), by_col(far, 1)
    squares = squares + by_chip[:rows]
    gain = jnp.where(chip == row, gain, by_chip[rows:]).reshape(2, 1, width)
    codes = doc_ids.astype(jnp.float32) + 1.0
    got = by_row(jnp.concatenate([squares, codes]))
    squares = ordered(row, squares, got[:rows]).reshape(block, 1)
    codes = ordered(row, codes, got[rows:])
    doc_rows = jnp.pad(codes, (0, EXTRA * size - block)).reshape(EXTRA, size)
    places = tok * block + jnp.arange(block, dtype=jnp.int32)
    cosine, sine = rotary_tables(places, size, near[0, : size // 2].astype(jnp.float32) < 1e30)

    taller = 3 * block + 2 * EXTRA
    break_at = 2 * block + EXTRA

    partial_sums = jax.ShapeDtypeStruct((taller, size), jnp.float32)
    no_cost = pl.CostEstimate(flops=0, bytes_accessed=0, transcendentals=0)
    *away, normed, own_weight = pl.pallas_call(
        normalise_project_kernel,
        out_shape=(
            partial_sums,
            partial_sums,
            jax.ShapeDtypeStruct((2, block, width), jnp.bfloat16),
            pltpu.HBM((span, pair * triple), jnp.bfloat16),
        ),
        in_specs=[pl.BlockSpec(memory_space=pltpu.SMEM)] + in_vmem(9),
        out_specs=tuple(in_vmem(3)) + (pl.BlockSpec(memory_space=pltpu.HBM),),
        scratch_shapes=[pltpu.SemaphoreType.DMA(())],
        compiler_params=pltpu.CompilerParams(vmem_limit_bytes=12 * MIB),
        cost_estimate=no_cost,
    )(
        jnp.stack([core, chip, (1 - row) * (pair * triple), row * (pair * triple)]),
        near, far, near_other, far_other, squares, gain, cosine, sine, flat_weight,
    )
    arrived = [by_row(chunk.astype(jnp.float16)) for chunk in away]
    own = pl.pallas_call(
        project_kernel,
        out_shape=(partial_sums, partial_sums),
        in_specs=in_vmem(4) + [pl.BlockSpec(memory_space=pltpu.HBM)],
        out_specs=tuple(in_vmem(2)),
        scratch_shapes=[
            pltpu.VMEM((span, pair * triple), jnp.bfloat16),
            pltpu.SemaphoreType.DMA(()),
        ],
        compiler_params=pltpu.CompilerParams(vmem_limit_bytes=8 * MIB),
        cost_estimate=no_cost,
    )(
        normed, doc_rows, cosine, sine, pltpu.with_memory_space_constraint(own_weight, pltpu.HBM)
    )
    scale = 1.0 / math.sqrt(size)

    def summed(chunk):
        return (own[chunk] + arrived[chunk].astype(jnp.float32)).astype(jnp.bfloat16)

    def gathered_attention():
        chunks = [summed(0), summed(1)]
        keys = jnp.stack([chunks[1][: 2 * block], chunks[0][: 2 * block]])
        everything = lax.all_gather(keys, "tok", axis=0, tiled=False).transpose(1, 0, 2, 3)
        all_codes = lax.all_gather(codes, "tok", axis=0, tiled=True)
        starts = jnp.sum((all_codes[None, :] < codes[:, None]).astype(jnp.int32), axis=1)
        together = attend_gathered(
            jnp.stack([chunk[break_at : break_at + block] for chunk in chunks]),
            everything[:, :, :block].reshape(pair, toks * block, size),
            everything[:, :, block:].reshape(pair, toks * block, size),
            places, starts, scale,
        )
        return parted(row, together)

    if toks == 4:
        places = jnp.stack([tok, row])

        def along_tok(value, pairs):
            return lax.ppermute(value, "tok", pairs)

        def keys_or_query(chunk, is_query):
            begin = jnp.where(is_query, taller - break_at, 0)
            return lax.dynamic_slice_in_dim(chunk, begin.astype(jnp.uint32), break_at, 0)

        def on_place(kernel, out_shape, ins, unused=0):
            return pl.pallas_call(
                kernel,
                out_shape=out_shape,
                in_specs=[pl.BlockSpec(memory_space=pltpu.SMEM)]
                + in_vmem(ins - unused)
                + [pl.BlockSpec(memory_space=pl.ANY)] * unused,
                out_specs=jax.tree.map(lambda unused: in_vmem(1)[0], out_shape),
                compiler_params=pltpu.CompilerParams(vmem_limit_bytes=16 * MIB),
                cost_estimate=pl.CostEstimate(flops=0, bytes_accessed=0, transcendentals=0),
            )

        chunk_one = summed(0)
        two_away = along_tok(keys_or_query(chunk_one, tok == 3), [(0, 2), (3, 1), (1, 0), (2, 3)])
        swapped = along_tok(keys_or_query(chunk_one, tok == 2), [(1, 2), (2, 1), (0, 0), (3, 3)])
        across = lax.ppermute(chunk_one[:EXTRA], ("tok", "row", "col"), [(2, 3)])
        arrived[1] = jnp.where(
            tok < toks,
            arrived[1].astype(jnp.float32),
            jnp.broadcast_to(across[:1].astype(jnp.float32), arrived[1].shape),
        )
        chunk_two = summed(1)
        neighbour = along_tok(
            keys_or_query(chunk_two, (tok & 1) == 1), [(0, 1), (1, 0), (2, 3), (3, 2)]
        )
        part_shapes = (
            jax.ShapeDtypeStruct((2, block, size), jnp.float32),
            jax.ShapeDtypeStruct((2, block, 1), jnp.float32),
        )
        own_out, own_logs = on_place(
            lambda *refs: own_block_kernel(scale, *refs), part_shapes, 2
        )(places, chunk_one, chunk_two)
        guests = on_place(
            lambda *refs: guest_kernel(scale, *refs),
            jax.ShapeDtypeStruct((2, block + EXTRA, size), jnp.bfloat16),
            6,
            1,
        )(places, two_away, swapped, neighbour, chunk_one, chunk_two, own_logs)
        from_first = along_tok(guests[1], [(0, 1), (1, 3), (2, 0), (3, 2)])
        from_below = along_tok(guests[0], [(1, 2), (2, 3)])
        output, logs = on_place(
            lambda *refs: own_rest_kernel(scale, *refs), part_shapes, 8, 1
        )(places, own_out, own_logs, chunk_one, chunk_two, two_away, swapped, neighbour, guests)
        half = jax.ShapeDtypeStruct((rows, pair * size), jnp.bfloat16)
        mine, theirs = on_place(merge_kernel, (half, half), 4)(
            places, output, logs, from_first, from_below
        )
    else:
        mine, theirs = gathered_attention()
    theirs = by_row(theirs)
    return jnp.concatenate(
        [jnp.where(row == 0, mine, theirs), jnp.where(row == 0, theirs, mine)], axis=1
    )


def solution(mesh):
    placed = (P(("tok", "row"), "col"), P("col"), P("row", "col", None), P(("tok", "row")))
    return jax.shard_map(
        per_device, mesh=mesh, in_specs=placed, out_specs=P(("tok", "row"), "col"), check_vma=False
    )
```

```python
import math

import jax
import jax.numpy as jnp
from jax import lax
from jax.experimental import pallas as pl
from jax.experimental.pallas import tpu as pltpu
from jax.sharding import PartitionSpec as P

EPS = 1e-05
LOG2_E = math.log2(math.e)
LOW = -1e30
EXTRA = 16
MIB = 1 << 20
CHUNKS = ((4, 0), (1, 3))


def rotary_tables(places, head_size, always):
    half = head_size // 2
    spacing = jnp.arange(half).astype(jnp.float32) * (2.0 / head_size)
    inverse = jnp.where(always, jnp.power(10000.0, -spacing), 0.0)
    angles = places.astype(jnp.float32)[:, None] * inverse[None, :]
    cosine, sine = jnp.cos(angles), jnp.sin(angles)
    return (
        jnp.concatenate([cosine, cosine], axis=1),
        jnp.concatenate([-sine, sine], axis=1),
    )


def project_chunk(
    normed, place, weight_ref, key_column, query_column, cos_ref, sin_ref, doc_rows, out_ref
):
    core, near_row = place
    block, size = cos_ref.shape
    rows, extra = block // 2, doc_rows.shape[0]
    depth = weight_ref.shape[0] // 2

    def product(column, width):
        at = pl.ds(column if isinstance(column, int) else pl.multiple_of(column, size), width)
        return sum(
            jnp.dot(
                normed[index],
                weight_ref[pl.ds(pl.multiple_of(half * depth, depth), depth), at],
                preferred_element_type=jnp.float32,
            )
            for index, half in enumerate((core, 1 - core))
        )

    def store(begin, piece, rotating):
        for index, row in enumerate((near_row, 1 - near_row)):
            part = piece[index * rows : (index + 1) * rows]
            if rotating:
                at = pl.ds(pl.multiple_of(row * rows, 8), rows)
                part = part * cos_ref[at, :] + pltpu.roll(part, size // 2, 1) * sin_ref[at, :]
            out_ref[pl.ds(pl.multiple_of(row * rows + begin, 8), rows), :] = part

    both = product(key_column, 2 * size)
    query = product(query_column, size)
    store(0, both[:, :size], True)
    store(block, both[:, size:], False)
    store(2 * block + extra, query, True)
    out_ref[2 * block : 2 * block + extra, :] = doc_rows
    out_ref[3 * block + extra :, :] = doc_rows


def normalise_project_kernel(
    place_ref, a_near, a_far, b_near, b_far, squares_ref, gain_ref, cos_ref, sin_ref, weight_ref,
    one_ref, two_ref, normed_ref, own_hbm, semaphore,
):
    rows, size = a_near.shape[0], cos_ref.shape[1]
    features = 2 * gain_ref.shape[0] * gain_ref.shape[2]
    core, near_row, away, own = place_ref[0], place_ref[1], place_ref[2], place_ref[3]
    copy = pltpu.make_async_copy(
        weight_ref.at[:, pl.ds(pl.multiple_of(own, size), 6 * size)], own_hbm, semaphore
    )
    copy.start()
    factors = [
        lax.rsqrt(squares_ref[pl.ds(pl.multiple_of(row * rows, 8), rows), :] / features + EPS)
        for row in (near_row, 1 - near_row)
    ]
    normed = []
    for shards, half in (((a_near, a_far), core), ((b_near, b_far), 1 - core)):
        gain = gain_ref[half]
        normed.append(
            jnp.concatenate(
                [
                    (shard[...].astype(jnp.float32) * factor * gain).astype(jnp.bfloat16)
                    for shard, factor in zip(shards, factors)
                ],
                axis=0,
            )
        )
    for index in range(2):
        normed_ref[index] = normed[index]
    nothing = jnp.zeros((EXTRA, size), jnp.float32)
    for chunk, (keys, query) in enumerate(CHUNKS):
        project_chunk(
            normed, (core, near_row), weight_ref, away + keys * size, away + query * size, cos_ref,
            sin_ref, nothing, (one_ref, two_ref)[chunk],
        )
    copy.wait()


def project_kernel(
    place_ref, normed_ref, docs_ref, cos_ref, sin_ref, own_hbm, one_ref, two_ref, weight_buffer,
    semaphore,
):
    copy = pltpu.make_async_copy(own_hbm, weight_buffer, semaphore)
    copy.start()
    copy.wait()
    size = cos_ref.shape[1]
    for chunk, (keys, query) in enumerate(CHUNKS):
        project_chunk(
            normed_ref, (place_ref[0], place_ref[1]), weight_buffer, keys * size, query * size, cos_ref,
            sin_ref, docs_ref[...], (one_ref, two_ref)[chunk],
        )


def as_column(rows, count):
    lanes = rows.shape[1]
    pieces = []
    for begin in range(0, count, lanes):
        held = min(lanes, count - begin)
        at = lax.broadcasted_iota(jnp.int32, (held, lanes), 0)
        diagonal = at == lax.broadcasted_iota(jnp.int32, (held, lanes), 1)
        row = rows[begin // lanes : begin // lanes + 1, :]
        pieces.append(jnp.sum(jnp.where(diagonal, row, 0.0), axis=1, keepdims=True))
    return jnp.concatenate(pieces, axis=0)


def as_rows(column, lanes):
    count = column.shape[0]
    rows = []
    for begin in range(0, count, lanes):
        held = min(lanes, count - begin)
        at = lax.broadcasted_iota(jnp.int32, (held, lanes), 0)
        diagonal = at == lax.broadcasted_iota(jnp.int32, (held, lanes), 1)
        rows.append(
            jnp.sum(jnp.where(diagonal, column[begin : begin + held], 0.0), axis=0, keepdims=True)
        )
    return rows


def as_lanes(rows, count):
    lanes = rows.shape[1]
    return jnp.concatenate(
        [
            rows[begin // lanes : begin // lanes + 1, : min(lanes, count - begin)]
            for begin in range(0, count, lanes)
        ],
        axis=1,
    )


def softmax_part(scale, query_message, messages, causal):
    valid = [present for message, present in messages]
    messages = [message for message, present in messages]
    query = query_message[:-EXTRA]
    query_docs = as_column(query_message[-EXTRA:].astype(jnp.float32), query.shape[0])
    block = (messages[0].shape[0] - EXTRA) // 2
    keys = jnp.concatenate([message[:block] for message in messages], axis=0)
    values = jnp.concatenate([message[block : 2 * block] for message in messages], axis=0)
    key_docs = jnp.concatenate(
        [
            jnp.where(present, as_lanes(message[2 * block :].astype(jnp.float32), block), 0.0)
            for message, present in zip(messages, valid)
        ],
        axis=1,
    )
    visible = query_docs == key_docs
    if causal:
        shape = (query.shape[0], keys.shape[0])
        query_places = lax.broadcasted_iota(jnp.int32, shape, 0)
        key_places = lax.broadcasted_iota(jnp.int32, shape, 1)
        visible &= (key_places <= query_places) | (key_places >= block)
    scores = lax.dot_general(
        query, keys, (((1,), (1,)), ((), ())), preferred_element_type=jnp.float32
    )
    masked = jnp.where(visible, scores, LOW)
    top = jnp.max(masked, axis=1, keepdims=True)
    exponentials = jnp.exp2((masked - top) * (scale * LOG2_E))
    total = jnp.sum(exponentials, axis=1, keepdims=True)
    summed = jnp.dot(exponentials.astype(jnp.bfloat16), values, preferred_element_type=jnp.float32)
    return summed / total, jnp.where(top > LOW / 2, top * scale + jnp.log(total), LOW)


def as_message(output, logs, size):
    along = jnp.concatenate(as_rows(logs, size), axis=0)
    high = along.astype(jnp.bfloat16).astype(jnp.float32)
    middle = (along - high).astype(jnp.bfloat16).astype(jnp.float32)
    pieces = [output, high, middle, along - high - middle]
    pieces.append(jnp.zeros((EXTRA - 3 * along.shape[0], size), jnp.float32))
    return jnp.concatenate(pieces, axis=0).astype(jnp.bfloat16)


def logs_of(message, rows):
    tile = message[rows:].astype(jnp.float32)
    groups = pl.cdiv(rows, tile.shape[1])
    return as_column(sum(tile[k * groups : (k + 1) * groups] for k in range(3)), rows)


def parted(row, value):
    rows = value.shape[0] // 2
    first = row == 0
    return (
        jnp.where(first, value[:rows], value[rows:]),
        jnp.where(first, value[rows:], value[:rows]),
    )


def joined(first, second):
    (output, logs), (other, other_logs) = first, second
    top = jnp.maximum(logs, other_logs)
    weight, other_weight = jnp.exp(logs - top), jnp.exp(other_logs - top)
    total = weight + other_weight
    return (output * weight + other * other_weight) / total, top + jnp.log(total)


def own_block_kernel(scale, place_ref, chunk_one, chunk_two, out_ref, logs_ref):
    for index, (queries, keys) in enumerate(((chunk_one, chunk_two), (chunk_two, chunk_one))):
        height = keys.shape[0] - out_ref.shape[1] - EXTRA
        out_ref[index], logs_ref[index] = softmax_part(
            scale, queries[height:, :], [(keys[:height, :], True)], True
        )


def guest_kernel(
    scale, place_ref, two_away, swapped, neighbour, chunk_one, chunk_two, unused_ref, out_ref
):
    height, size = neighbour.shape
    begin = (height - EXTRA) // 2

    def attend(index, query, messages):
        output, logs = softmax_part(scale, query, [(m, True) for m in messages], False)
        out_ref[index] = as_message(output, logs, size)

    @pl.when(place_ref[0] == 0)
    def one_up():
        attend(1, neighbour[begin:, :], [chunk_one[:height, :]])

    @pl.when(place_ref[0] == 1)
    def down():
        keys = [neighbour[...], chunk_two[:height, :]]
        attend(1, two_away[begin:, :], keys)
        attend(0, swapped[begin:, :], keys)

    @pl.when(place_ref[0] == 2)
    def three_up():
        attend(0, neighbour[begin:, :], [two_away[...], swapped[...], chunk_one[:height, :]])


def own_rest_kernel(
    scale, place_ref, own_out, own_logs, chunk_one, chunk_two, two_away, swapped, neighbour,
    unused_ref, out_ref, logs_ref,
):
    tok = place_ref[0]
    height = neighbour.shape[0]
    out_ref[...] = own_out[...]
    logs_ref[...] = own_logs[...]

    def add(index, query, messages):
        part = softmax_part(scale, query, [(m, True) for m in messages], False)
        out_ref[index], logs_ref[index] = joined((own_out[index], own_logs[index]), part)

    @pl.when((tok == 1) | (tok == 3))
    def down():
        add(0, chunk_one[height:, :], [neighbour[...]])

    @pl.when(tok == 2)
    def up():
        add(1, chunk_two[height:, :], [swapped[...], two_away[...]])


def merge_kernel(
    place_ref, out_ref, logs_ref, first_ref, below_ref, mine_ref, theirs_ref
):
    block, size = out_ref.shape[1:]
    tok, row = place_ref[0], place_ref[1]

    def with_guest(index, message, present):
        guest = jnp.where(present, message[:block].astype(jnp.float32), 0.0)
        guest_logs = jnp.where(present, logs_of(message, block), LOW)
        output, logs = joined((out_ref[index], logs_ref[index]), (guest, guest_logs))
        return output.astype(jnp.bfloat16)

    down = with_guest(0, jnp.where(tok == 2, below_ref[...], first_ref[...]), tok >= 2)
    up = with_guest(1, jnp.where(tok == 1, first_ref[...], below_ref[...]), (tok == 1) | (tok == 3))
    for index, output in enumerate((down, up)):
        columns = slice(index * size, (index + 1) * size)
        mine_ref[:, columns], theirs_ref[:, columns] = parted(row, output)


def attend_gathered(query, keys, values, places, starts, scale):
    heads, count, size = query.shape
    chunk = math.gcd(keys.shape[1], 1024)
    rounds = keys.shape[1] // chunk
    stacked = (
        keys.reshape(heads, rounds, chunk, size).transpose(1, 0, 2, 3),
        values.reshape(heads, rounds, chunk, size).transpose(1, 0, 2, 3),
        jnp.arange(rounds * chunk, dtype=jnp.int32).reshape(rounds, chunk),
    )

    def advance(state, blocks):
        running, totals, summed = state
        block_keys, block_values, key_places = blocks
        scores = (
            jnp.einsum("hqd,hkd->hqk", query, block_keys, preferred_element_type=jnp.float32) * scale
        )
        visible = (key_places[None, None, :] <= places[None, :, None]) & (
            key_places[None, None, :] >= starts[None, :, None]
        )
        masked = jnp.where(visible, scores, -jnp.inf)
        newest = jnp.maximum(running, jnp.max(masked, axis=2))
        factor = jnp.exp(running - newest)
        exponentials = jnp.where(visible, jnp.exp(masked - newest[:, :, None]), 0.0)
        totals = totals * factor + jnp.sum(exponentials, axis=2)
        summed = summed * factor[:, :, None] + jnp.einsum(
            "hqk,hkd->hqd", exponentials.astype(jnp.bfloat16), block_values,
            preferred_element_type=jnp.float32,
        )
        return (newest, totals, summed), None

    initial = (
        jnp.full((heads, count), -1e30, jnp.float32),
        jnp.zeros((heads, count), jnp.float32),
        jnp.zeros((heads, count, size), jnp.float32),
    )
    (running, totals, summed), unused = lax.scan(advance, initial, stacked)
    attended = (summed / totals[:, :, None]).astype(jnp.bfloat16)
    return attended.transpose(1, 0, 2).reshape(count, heads * size)


def in_vmem(count):
    return [pl.BlockSpec(memory_space=pltpu.VMEM)] * count


def per_device(activations, norm_gain, qkv_weight, doc_ids):
    rows, width = activations.shape
    span, local_heads, triple = qkv_weight.shape
    size = triple // 3
    pair = local_heads // 2
    block = 2 * rows
    toks = lax.axis_size("tok")
    tok, row, col = lax.axis_index("tok"), lax.axis_index("row"), lax.axis_index("col")
    chip, core = col >> 1, col & 1
    grid = [(r, c) for r in range(2) for c in range(4)]

    def by_col(value, flip):
        return lax.ppermute(value, "col", [(c, c ^ flip) for c in range(4)])

    def by_row(value):
        return lax.ppermute(value, "row", [(0, 1), (1, 0)])

    def ordered(index, own, other):
        first = index == 0
        return jnp.concatenate([jnp.where(first, own, other), jnp.where(first, other, own)])

    near = lax.ppermute(
        activations,
        ("row", "col"),
        [(r * 4 + c, (c // 2) * 4 + 2 * r + c % 2) for r, c in grid],
    )
    far = lax.ppermute(
        activations,
        ("row", "col"),
        [(r * 4 + c, (c // 2) * 4 + 2 * (1 - r) + c % 2) for r, c in grid],
    )
    widened = activations.astype(jnp.float32)
    squares = jnp.sum(widened * widened, axis=1)
    gain = norm_gain.astype(jnp.float32)
    message = jnp.concatenate([squares, gain])
    message, qkv_weight = lax.optimization_barrier((message, qkv_weight))
    flat_weight = qkv_weight.reshape(span, local_heads * triple)
    got = by_col(message, 1)
    squares = squares + got[:rows]
    gain = ordered(core, gain, got[rows:])
    by_chip = by_col(jnp.concatenate([squares, gain]), 2)
    near, far, by_chip, flat_weight = lax.optimization_barrier((near, far, by_chip, flat_weight))
    near_other, far_other = by_col(near, 1), by_col(far, 1)
    squares = squares + by_chip[:rows]
    gain = jnp.where(chip == row, gain, by_chip[rows:]).reshape(2, 1, width)
    codes = doc_ids.astype(jnp.float32) + 1.0
    got = by_row(jnp.concatenate([squares, codes]))
    squares = ordered(row, squares, got[:rows]).reshape(block, 1)
    codes = ordered(row, codes, got[rows:])
    doc_rows = jnp.pad(codes, (0, EXTRA * size - block)).reshape(EXTRA, size)
    places = tok * block + jnp.arange(block, dtype=jnp.int32)
    cosine, sine = rotary_tables(places, size, near[0, : size // 2].astype(jnp.float32) < 1e30)

    taller = 3 * block + 2 * EXTRA
    break_at = 2 * block + EXTRA

    partial_sums = jax.ShapeDtypeStruct((taller, size), jnp.float32)
    no_cost = pl.CostEstimate(flops=0, bytes_accessed=0, transcendentals=0)
    *away, normed, own_weight = pl.pallas_call(
        normalise_project_kernel,
        out_shape=(
            partial_sums,
            partial_sums,
            jax.ShapeDtypeStruct((2, block, width), jnp.bfloat16),
            pltpu.HBM((span, pair * triple), jnp.bfloat16),
        ),
        in_specs=[pl.BlockSpec(memory_space=pltpu.SMEM)] + in_vmem(9),
        out_specs=tuple(in_vmem(3)) + (pl.BlockSpec(memory_space=pltpu.HBM),),
        scratch_shapes=[pltpu.SemaphoreType.DMA(())],
        compiler_params=pltpu.CompilerParams(vmem_limit_bytes=12 * MIB),
        cost_estimate=no_cost,
    )(
        jnp.stack([core, chip, (1 - row) * (pair * triple), row * (pair * triple)]),
        near, far, near_other, far_other, squares, gain, cosine, sine, flat_weight,
    )
    arrived = [by_row(chunk.astype(jnp.float16)) for chunk in away]
    own = pl.pallas_call(
        project_kernel,
        out_shape=(partial_sums, partial_sums),
        in_specs=[pl.BlockSpec(memory_space=pltpu.SMEM)]
        + in_vmem(4)
        + [pl.BlockSpec(memory_space=pltpu.HBM)],
        out_specs=tuple(in_vmem(2)),
        scratch_shapes=[
            pltpu.VMEM((span, pair * triple), jnp.bfloat16),
            pltpu.SemaphoreType.DMA(()),
        ],
        compiler_params=pltpu.CompilerParams(vmem_limit_bytes=8 * MIB),
        cost_estimate=no_cost,
    )(
        jnp.stack([core, chip]), normed, doc_rows, cosine, sine,
        pltpu.with_memory_space_constraint(own_weight, pltpu.HBM),
    )
    scale = 1.0 / math.sqrt(size)

    def summed(chunk):
        return (own[chunk] + arrived[chunk].astype(jnp.float32)).astype(jnp.bfloat16)

    def gathered_attention():
        chunks = [summed(0), summed(1)]
        keys = jnp.stack([chunks[1][: 2 * block], chunks[0][: 2 * block]])
        everything = lax.all_gather(keys, "tok", axis=0, tiled=False).transpose(1, 0, 2, 3)
        all_codes = lax.all_gather(codes, "tok", axis=0, tiled=True)
        starts = jnp.sum((all_codes[None, :] < codes[:, None]).astype(jnp.int32), axis=1)
        together = attend_gathered(
            jnp.stack([chunk[break_at : break_at + block] for chunk in chunks]),
            everything[:, :, :block].reshape(pair, toks * block, size),
            everything[:, :, block:].reshape(pair, toks * block, size),
            places, starts, scale,
        )
        return parted(row, together)

    if toks == 4:
        places = jnp.stack([tok, row])

        def along_tok(value, pairs):
            return lax.ppermute(value, "tok", pairs)

        def keys_or_query(chunk, is_query):
            begin = jnp.where(is_query, taller - break_at, 0)
            return lax.dynamic_slice_in_dim(chunk, begin.astype(jnp.uint32), break_at, 0)

        def on_place(kernel, out_shape, ins, unused=0):
            return pl.pallas_call(
                kernel,
                out_shape=out_shape,
                in_specs=[pl.BlockSpec(memory_space=pltpu.SMEM)]
                + in_vmem(ins - unused)
                + [pl.BlockSpec(memory_space=pl.ANY)] * unused,
                out_specs=jax.tree.map(lambda unused: in_vmem(1)[0], out_shape),
                compiler_params=pltpu.CompilerParams(vmem_limit_bytes=16 * MIB),
                cost_estimate=pl.CostEstimate(flops=0, bytes_accessed=0, transcendentals=0),
            )

        chunk_one = summed(0)
        two_away = along_tok(keys_or_query(chunk_one, tok == 3), [(0, 2), (3, 1), (1, 0), (2, 3)])
        swapped = along_tok(keys_or_query(chunk_one, tok == 2), [(1, 2), (2, 1), (0, 0), (3, 3)])
        across = lax.ppermute(chunk_one[:EXTRA], ("tok", "row", "col"), [(2, 3)])
        arrived[1] = jnp.where(
            tok < toks,
            arrived[1].astype(jnp.float32),
            jnp.broadcast_to(across[:1].astype(jnp.float32), arrived[1].shape),
        )
        chunk_two = summed(1)
        neighbour = along_tok(
            keys_or_query(chunk_two, (tok & 1) == 1), [(0, 1), (1, 0), (2, 3), (3, 2)]
        )
        part_shapes = (
            jax.ShapeDtypeStruct((2, block, size), jnp.float32),
            jax.ShapeDtypeStruct((2, block, 1), jnp.float32),
        )
        own_out, own_logs = on_place(
            lambda *refs: own_block_kernel(scale, *refs), part_shapes, 2
        )(places, chunk_one, chunk_two)
        guests = on_place(
            lambda *refs: guest_kernel(scale, *refs),
            jax.ShapeDtypeStruct((2, block + EXTRA, size), jnp.bfloat16),
            6,
            1,
        )(places, two_away, swapped, neighbour, chunk_one, chunk_two, own_logs)
        from_first = along_tok(guests[1], [(0, 1), (1, 3), (2, 0), (3, 2)])
        from_below = along_tok(guests[0], [(1, 2), (2, 3)])
        output, logs = on_place(
            lambda *refs: own_rest_kernel(scale, *refs), part_shapes, 8, 1
        )(places, own_out, own_logs, chunk_one, chunk_two, two_away, swapped, neighbour, guests)
        half = jax.ShapeDtypeStruct((rows, pair * size), jnp.bfloat16)
        mine, theirs = on_place(merge_kernel, (half, half), 4)(
            places, output, logs, from_first, from_below
        )
    else:
        mine, theirs = gathered_attention()
    theirs = by_row(theirs)
    return jnp.concatenate(
        [jnp.where(row == 0, mine, theirs), jnp.where(row == 0, theirs, mine)], axis=1
    )


def solution(mesh):
    placed = (P(("tok", "row"), "col"), P("col"), P("row", "col", None), P(("tok", "row")))
    return jax.shard_map(
        per_device, mesh=mesh, in_specs=placed, out_specs=P(("tok", "row"), "col"), check_vma=False
    )
```

```python
import math

import jax
import jax.numpy as jnp
from jax import lax
from jax.experimental import pallas as pl
from jax.experimental.pallas import tpu as pltpu
from jax.sharding import PartitionSpec as P

EPS = 1e-05
LOG2_E = math.log2(math.e)
LOW = -1e30
EXTRA = 16
MIB = 1 << 20
CHUNKS = ((4, 0), (1, 3))


def rotary_tables(places, head_size, always):
    half = head_size // 2
    spacing = jnp.arange(half).astype(jnp.float32) * (2.0 / head_size)
    inverse = jnp.where(always, jnp.power(10000.0, -spacing), 0.0)
    angles = places.astype(jnp.float32)[:, None] * inverse[None, :]
    cosine, sine = jnp.cos(angles), jnp.sin(angles)
    return (
        jnp.concatenate([cosine, cosine], axis=1),
        jnp.concatenate([-sine, sine], axis=1),
    )


def project_chunk(normed_ref, weight_ref, key_column, query_column, cos_ref, sin_ref, doc_rows, out_ref):
    block, size = cos_ref.shape
    extra = doc_rows.shape[0]
    depth = weight_ref.shape[0] // 2

    def product(column, width):
        at = pl.ds(column if isinstance(column, int) else pl.multiple_of(column, size), width)
        return jnp.dot(
            normed_ref[0], weight_ref[:depth, at], preferred_element_type=jnp.float32
        ) + jnp.dot(normed_ref[1], weight_ref[depth:, at], preferred_element_type=jnp.float32)

    def rotated(piece):
        return piece * cos_ref[...] + pltpu.roll(piece, size // 2, 1) * sin_ref[...]

    both = product(key_column, 2 * size)
    out_ref[:block, :] = rotated(both[:, :size])
    out_ref[block : 2 * block, :] = both[:, size:]
    out_ref[2 * block : 2 * block + extra, :] = doc_rows
    out_ref[2 * block + extra : 3 * block + extra, :] = rotated(product(query_column, size))
    out_ref[3 * block + extra :, :] = doc_rows


def normalise_project_kernel(
    place_ref, a_near, a_far, b_near, b_far, squares_ref, gain_ref, cos_ref, sin_ref, weight_ref,
    out_ref, normed_ref,
):
    rows, size = a_near.shape[0], cos_ref.shape[1]
    features = 2 * gain_ref.shape[0] * gain_ref.shape[2]
    core, near_row, away = place_ref[0], place_ref[1], place_ref[2]
    for shards, half in (((a_near, a_far), core), ((b_near, b_far), 1 - core)):
        gain = gain_ref[half]
        for shard, row in zip(shards, (near_row, 1 - near_row)):
            at = pl.ds(pl.multiple_of(row * rows, 16), rows)
            factor = lax.rsqrt(squares_ref[at, :] / features + EPS)
            normed_ref[half, at, :] = (shard[...].astype(jnp.float32) * factor * gain).astype(
                jnp.bfloat16
            )
    keys, query = CHUNKS[0]
    project_chunk(
        normed_ref, weight_ref, away + keys * size, away + query * size, cos_ref, sin_ref,
        jnp.zeros((EXTRA, size), jnp.float32), out_ref,
    )


def second_kernel(
    place_ref, normed_ref, cos_ref, sin_ref, weight_ref, out_ref, own_hbm, semaphore
):
    size = cos_ref.shape[1]
    away, own = place_ref[2], place_ref[3]
    copy = pltpu.make_async_copy(
        weight_ref.at[:, pl.ds(pl.multiple_of(own, size), 6 * size)], own_hbm, semaphore
    )
    copy.start()
    keys, query = CHUNKS[1]
    project_chunk(
        normed_ref, weight_ref, away + keys * size, away + query * size, cos_ref, sin_ref,
        jnp.zeros((EXTRA, size), jnp.float32), out_ref,
    )
    copy.wait()


def project_kernel(
    normed_ref, docs_ref, cos_ref, sin_ref, own_hbm, one_ref, two_ref, weight_buffer, semaphore
):
    copy = pltpu.make_async_copy(own_hbm, weight_buffer, semaphore)
    copy.start()
    copy.wait()
    size = cos_ref.shape[1]
    for chunk, (keys, query) in enumerate(CHUNKS):
        project_chunk(
            normed_ref, weight_buffer, keys * size, query * size, cos_ref, sin_ref, docs_ref[...],
            (one_ref, two_ref)[chunk],
        )


def as_column(rows, count):
    lanes = rows.shape[1]
    pieces = []
    for begin in range(0, count, lanes):
        held = min(lanes, count - begin)
        at = lax.broadcasted_iota(jnp.int32, (held, lanes), 0)
        diagonal = at == lax.broadcasted_iota(jnp.int32, (held, lanes), 1)
        row = rows[begin // lanes : begin // lanes + 1, :]
        pieces.append(jnp.sum(jnp.where(diagonal, row, 0.0), axis=1, keepdims=True))
    return jnp.concatenate(pieces, axis=0)


def as_rows(column, lanes):
    count = column.shape[0]
    rows = []
    for begin in range(0, count, lanes):
        held = min(lanes, count - begin)
        at = lax.broadcasted_iota(jnp.int32, (held, lanes), 0)
        diagonal = at == lax.broadcasted_iota(jnp.int32, (held, lanes), 1)
        rows.append(
            jnp.sum(jnp.where(diagonal, column[begin : begin + held], 0.0), axis=0, keepdims=True)
        )
    return rows


def as_lanes(rows, count):
    lanes = rows.shape[1]
    return jnp.concatenate(
        [
            rows[begin // lanes : begin // lanes + 1, : min(lanes, count - begin)]
            for begin in range(0, count, lanes)
        ],
        axis=1,
    )


def softmax_part(scale, query_message, messages, causal):
    valid = [present for message, present in messages]
    messages = [message for message, present in messages]
    query = query_message[:-EXTRA]
    query_docs = as_column(query_message[-EXTRA:].astype(jnp.float32), query.shape[0])
    block = (messages[0].shape[0] - EXTRA) // 2
    keys = jnp.concatenate([message[:block] for message in messages], axis=0)
    values = jnp.concatenate([message[block : 2 * block] for message in messages], axis=0)
    key_docs = jnp.concatenate(
        [
            jnp.where(present, as_lanes(message[2 * block :].astype(jnp.float32), block), 0.0)
            for message, present in zip(messages, valid)
        ],
        axis=1,
    )
    visible = query_docs == key_docs
    if causal:
        shape = (query.shape[0], keys.shape[0])
        query_places = lax.broadcasted_iota(jnp.int32, shape, 0)
        key_places = lax.broadcasted_iota(jnp.int32, shape, 1)
        visible &= (key_places <= query_places) | (key_places >= block)
    scores = lax.dot_general(
        query, keys, (((1,), (1,)), ((), ())), preferred_element_type=jnp.float32
    )
    masked = jnp.where(visible, scores, LOW)
    top = jnp.max(masked, axis=1, keepdims=True)
    exponentials = jnp.exp2((masked - top) * (scale * LOG2_E))
    total = jnp.sum(exponentials, axis=1, keepdims=True)
    summed = jnp.dot(exponentials.astype(jnp.bfloat16), values, preferred_element_type=jnp.float32)
    return summed / total, jnp.where(top > LOW / 2, top * scale + jnp.log(total), LOW)


def as_message(output, logs, size):
    along = jnp.concatenate(as_rows(logs, size), axis=0)
    high = along.astype(jnp.bfloat16).astype(jnp.float32)
    middle = (along - high).astype(jnp.bfloat16).astype(jnp.float32)
    pieces = [output, high, middle, along - high - middle]
    pieces.append(jnp.zeros((EXTRA - 3 * along.shape[0], size), jnp.float32))
    return jnp.concatenate(pieces, axis=0).astype(jnp.bfloat16)


def logs_of(message, rows):
    tile = message[rows:].astype(jnp.float32)
    groups = pl.cdiv(rows, tile.shape[1])
    return as_column(sum(tile[k * groups : (k + 1) * groups] for k in range(3)), rows)


def parted(row, value):
    rows = value.shape[0] // 2
    first = row == 0
    return (
        jnp.where(first, value[:rows], value[rows:]),
        jnp.where(first, value[rows:], value[:rows]),
    )


def joined(first, second):
    (output, logs), (other, other_logs) = first, second
    top = jnp.maximum(logs, other_logs)
    weight, other_weight = jnp.exp(logs - top), jnp.exp(other_logs - top)
    total = weight + other_weight
    return (output * weight + other * other_weight) / total, top + jnp.log(total)


def own_block_kernel(scale, place_ref, chunk_one, chunk_two, out_ref, logs_ref):
    for index, (queries, keys) in enumerate(((chunk_one, chunk_two), (chunk_two, chunk_one))):
        height = keys.shape[0] - out_ref.shape[1] - EXTRA
        out_ref[index], logs_ref[index] = softmax_part(
            scale, queries[height:, :], [(keys[:height, :], True)], True
        )


def guest_kernel(
    scale, place_ref, two_away, swapped, neighbour, chunk_one, chunk_two, unused_ref, out_ref
):
    height, size = neighbour.shape
    begin = (height - EXTRA) // 2

    def attend(index, query, messages):
        output, logs = softmax_part(scale, query, [(m, True) for m in messages], False)
        out_ref[index] = as_message(output, logs, size)

    @pl.when(place_ref[0] == 0)
    def one_up():
        attend(1, neighbour[begin:, :], [chunk_one[:height, :]])

    @pl.when(place_ref[0] == 1)
    def down():
        keys = [neighbour[...], chunk_two[:height, :]]
        attend(1, two_away[begin:, :], keys)
        attend(0, swapped[begin:, :], keys)

    @pl.when(place_ref[0] == 2)
    def three_up():
        attend(0, neighbour[begin:, :], [two_away[...], swapped[...], chunk_one[:height, :]])


def own_rest_kernel(
    scale, place_ref, own_out, own_logs, chunk_one, chunk_two, two_away, swapped, neighbour,
    unused_ref, out_ref, logs_ref,
):
    tok = place_ref[0]
    height = neighbour.shape[0]
    out_ref[...] = own_out[...]
    logs_ref[...] = own_logs[...]

    def add(index, query, messages):
        part = softmax_part(scale, query, [(m, True) for m in messages], False)
        out_ref[index], logs_ref[index] = joined((own_out[index], own_logs[index]), part)

    @pl.when((tok == 1) | (tok == 3))
    def down():
        add(0, chunk_one[height:, :], [neighbour[...]])

    @pl.when(tok == 2)
    def up():
        add(1, chunk_two[height:, :], [swapped[...], two_away[...]])


def merge_kernel(
    place_ref, out_ref, logs_ref, first_ref, below_ref, mine_ref, theirs_ref
):
    block, size = out_ref.shape[1:]
    tok, row = place_ref[0], place_ref[1]

    def with_guest(index, message, present):
        guest = jnp.where(present, message[:block].astype(jnp.float32), 0.0)
        guest_logs = jnp.where(present, logs_of(message, block), LOW)
        output, logs = joined((out_ref[index], logs_ref[index]), (guest, guest_logs))
        return output.astype(jnp.bfloat16)

    down = with_guest(0, jnp.where(tok == 2, below_ref[...], first_ref[...]), tok >= 2)
    up = with_guest(1, jnp.where(tok == 1, first_ref[...], below_ref[...]), (tok == 1) | (tok == 3))
    for index, output in enumerate((down, up)):
        columns = slice(index * size, (index + 1) * size)
        mine_ref[:, columns], theirs_ref[:, columns] = parted(row, output)


def attend_gathered(query, keys, values, places, starts, scale):
    heads, count, size = query.shape
    chunk = math.gcd(keys.shape[1], 1024)
    rounds = keys.shape[1] // chunk
    stacked = (
        keys.reshape(heads, rounds, chunk, size).transpose(1, 0, 2, 3),
        values.reshape(heads, rounds, chunk, size).transpose(1, 0, 2, 3),
        jnp.arange(rounds * chunk, dtype=jnp.int32).reshape(rounds, chunk),
    )

    def advance(state, blocks):
        running, totals, summed = state
        block_keys, block_values, key_places = blocks
        scores = (
            jnp.einsum("hqd,hkd->hqk", query, block_keys, preferred_element_type=jnp.float32) * scale
        )
        visible = (key_places[None, None, :] <= places[None, :, None]) & (
            key_places[None, None, :] >= starts[None, :, None]
        )
        masked = jnp.where(visible, scores, -jnp.inf)
        newest = jnp.maximum(running, jnp.max(masked, axis=2))
        factor = jnp.exp(running - newest)
        exponentials = jnp.where(visible, jnp.exp(masked - newest[:, :, None]), 0.0)
        totals = totals * factor + jnp.sum(exponentials, axis=2)
        summed = summed * factor[:, :, None] + jnp.einsum(
            "hqk,hkd->hqd", exponentials.astype(jnp.bfloat16), block_values,
            preferred_element_type=jnp.float32,
        )
        return (newest, totals, summed), None

    initial = (
        jnp.full((heads, count), -1e30, jnp.float32),
        jnp.zeros((heads, count), jnp.float32),
        jnp.zeros((heads, count, size), jnp.float32),
    )
    (running, totals, summed), unused = lax.scan(advance, initial, stacked)
    attended = (summed / totals[:, :, None]).astype(jnp.bfloat16)
    return attended.transpose(1, 0, 2).reshape(count, heads * size)


def in_vmem(count):
    return [pl.BlockSpec(memory_space=pltpu.VMEM)] * count


def per_device(activations, norm_gain, qkv_weight, doc_ids):
    rows, width = activations.shape
    span, local_heads, triple = qkv_weight.shape
    size = triple // 3
    pair = local_heads // 2
    block = 2 * rows
    toks = lax.axis_size("tok")
    tok, row, col = lax.axis_index("tok"), lax.axis_index("row"), lax.axis_index("col")
    chip, core = col >> 1, col & 1
    grid = [(r, c) for r in range(2) for c in range(4)]

    def by_col(value, flip):
        return lax.ppermute(value, "col", [(c, c ^ flip) for c in range(4)])

    def by_row(value):
        return lax.ppermute(value, "row", [(0, 1), (1, 0)])

    def ordered(index, own, other):
        first = index == 0
        return jnp.concatenate([jnp.where(first, own, other), jnp.where(first, other, own)])

    near = lax.ppermute(
        activations,
        ("row", "col"),
        [(r * 4 + c, (c // 2) * 4 + 2 * r + c % 2) for r, c in grid],
    )
    far = lax.ppermute(
        activations,
        ("row", "col"),
        [(r * 4 + c, (c // 2) * 4 + 2 * (1 - r) + c % 2) for r, c in grid],
    )
    widened = activations.astype(jnp.float32)
    squares = jnp.sum(widened * widened, axis=1)
    gain = norm_gain.astype(jnp.float32)
    message = jnp.concatenate([squares, gain])
    message, qkv_weight = lax.optimization_barrier((message, qkv_weight))
    flat_weight = qkv_weight.reshape(span, local_heads * triple)
    got = by_col(message, 1)
    squares = squares + got[:rows]
    gain = ordered(core, gain, got[rows:])
    by_chip = by_col(jnp.concatenate([squares, gain]), 2)
    near, far, by_chip, flat_weight = lax.optimization_barrier((near, far, by_chip, flat_weight))
    near_other, far_other = by_col(near, 1), by_col(far, 1)
    squares = squares + by_chip[:rows]
    gain = jnp.where(chip == row, gain, by_chip[rows:]).reshape(2, 1, width)
    codes = doc_ids.astype(jnp.float32) + 1.0
    got = by_row(jnp.concatenate([squares, codes]))
    squares = ordered(row, squares, got[:rows]).reshape(block, 1)
    codes = ordered(row, codes, got[rows:])
    doc_rows = jnp.pad(codes, (0, EXTRA * size - block)).reshape(EXTRA, size)
    places = tok * block + jnp.arange(block, dtype=jnp.int32)
    cosine, sine = rotary_tables(places, size, near[0, : size // 2].astype(jnp.float32) < 1e30)

    taller = 3 * block + 2 * EXTRA
    break_at = 2 * block + EXTRA

    partial_sums = jax.ShapeDtypeStruct((taller, size), jnp.float32)
    no_cost = pl.CostEstimate(flops=0, bytes_accessed=0, transcendentals=0)
    columns = jnp.stack([core, chip, (1 - row) * (pair * triple), row * (pair * triple)])
    first, normed = pl.pallas_call(
        normalise_project_kernel,
        out_shape=(partial_sums, jax.ShapeDtypeStruct((2, block, width), jnp.bfloat16)),
        in_specs=[pl.BlockSpec(memory_space=pltpu.SMEM)] + in_vmem(9),
        out_specs=tuple(in_vmem(2)),
        compiler_params=pltpu.CompilerParams(vmem_limit_bytes=12 * MIB),
        cost_estimate=no_cost,
    )(
        columns, near, far, near_other, far_other, squares, gain, cosine, sine, flat_weight,
    )
    second, own_weight = pl.pallas_call(
        second_kernel,
        out_shape=(partial_sums, pltpu.HBM((span, pair * triple), jnp.bfloat16)),
        in_specs=[pl.BlockSpec(memory_space=pltpu.SMEM)] + in_vmem(4),
        out_specs=(in_vmem(1)[0], pl.BlockSpec(memory_space=pltpu.HBM)),
        scratch_shapes=[pltpu.SemaphoreType.DMA(())],
        compiler_params=pltpu.CompilerParams(vmem_limit_bytes=12 * MIB),
        cost_estimate=no_cost,
    )(columns, normed, cosine, sine, flat_weight)
    arrived = [by_row(chunk.astype(jnp.float16)) for chunk in (first, second)]
    own = pl.pallas_call(
        project_kernel,
        out_shape=(partial_sums, partial_sums),
        in_specs=in_vmem(4) + [pl.BlockSpec(memory_space=pltpu.HBM)],
        out_specs=tuple(in_vmem(2)),
        scratch_shapes=[
            pltpu.VMEM((span, pair * triple), jnp.bfloat16),
            pltpu.SemaphoreType.DMA(()),
        ],
        compiler_params=pltpu.CompilerParams(vmem_limit_bytes=8 * MIB),
        cost_estimate=no_cost,
    )(
        normed, doc_rows, cosine, sine, pltpu.with_memory_space_constraint(own_weight, pltpu.HBM)
    )
    scale = 1.0 / math.sqrt(size)

    def summed(chunk):
        return (own[chunk] + arrived[chunk].astype(jnp.float32)).astype(jnp.bfloat16)

    def gathered_attention():
        chunks = [summed(0), summed(1)]
        keys = jnp.stack([chunks[1][: 2 * block], chunks[0][: 2 * block]])
        everything = lax.all_gather(keys, "tok", axis=0, tiled=False).transpose(1, 0, 2, 3)
        all_codes = lax.all_gather(codes, "tok", axis=0, tiled=True)
        starts = jnp.sum((all_codes[None, :] < codes[:, None]).astype(jnp.int32), axis=1)
        together = attend_gathered(
            jnp.stack([chunk[break_at : break_at + block] for chunk in chunks]),
            everything[:, :, :block].reshape(pair, toks * block, size),
            everything[:, :, block:].reshape(pair, toks * block, size),
            places, starts, scale,
        )
        return parted(row, together)

    if toks == 4:
        places = jnp.stack([tok, row])

        def along_tok(value, pairs):
            return lax.ppermute(value, "tok", pairs)

        def keys_or_query(chunk, is_query):
            begin = jnp.where(is_query, taller - break_at, 0)
            return lax.dynamic_slice_in_dim(chunk, begin.astype(jnp.uint32), break_at, 0)

        def on_place(kernel, out_shape, ins, unused=0):
            return pl.pallas_call(
                kernel,
                out_shape=out_shape,
                in_specs=[pl.BlockSpec(memory_space=pltpu.SMEM)]
                + in_vmem(ins - unused)
                + [pl.BlockSpec(memory_space=pl.ANY)] * unused,
                out_specs=jax.tree.map(lambda unused: in_vmem(1)[0], out_shape),
                compiler_params=pltpu.CompilerParams(vmem_limit_bytes=16 * MIB),
                cost_estimate=pl.CostEstimate(flops=0, bytes_accessed=0, transcendentals=0),
            )

        chunk_one = summed(0)
        two_away = along_tok(keys_or_query(chunk_one, tok == 3), [(0, 2), (3, 1), (1, 0), (2, 3)])
        swapped = along_tok(keys_or_query(chunk_one, tok == 2), [(1, 2), (2, 1), (0, 0), (3, 3)])
        across = lax.ppermute(chunk_one[:EXTRA], ("tok", "row", "col"), [(2, 3)])
        arrived[1] = jnp.where(
            tok < toks,
            arrived[1].astype(jnp.float32),
            jnp.broadcast_to(across[:1].astype(jnp.float32), arrived[1].shape),
        )
        chunk_two = summed(1)
        neighbour = along_tok(
            keys_or_query(chunk_two, (tok & 1) == 1), [(0, 1), (1, 0), (2, 3), (3, 2)]
        )
        part_shapes = (
            jax.ShapeDtypeStruct((2, block, size), jnp.float32),
            jax.ShapeDtypeStruct((2, block, 1), jnp.float32),
        )
        own_out, own_logs = on_place(
            lambda *refs: own_block_kernel(scale, *refs), part_shapes, 2
        )(places, chunk_one, chunk_two)
        guests = on_place(
            lambda *refs: guest_kernel(scale, *refs),
            jax.ShapeDtypeStruct((2, block + EXTRA, size), jnp.bfloat16),
            6,
            1,
        )(places, two_away, swapped, neighbour, chunk_one, chunk_two, own_logs)
        from_first = along_tok(guests[1], [(0, 1), (1, 3), (2, 0), (3, 2)])
        from_below = along_tok(guests[0], [(1, 2), (2, 3)])
        output, logs = on_place(
            lambda *refs: own_rest_kernel(scale, *refs), part_shapes, 8, 1
        )(places, own_out, own_logs, chunk_one, chunk_two, two_away, swapped, neighbour, guests)
        half = jax.ShapeDtypeStruct((rows, pair * size), jnp.bfloat16)
        mine, theirs = on_place(merge_kernel, (half, half), 4)(
            places, output, logs, from_first, from_below
        )
    else:
        mine, theirs = gathered_attention()
    theirs = by_row(theirs)
    return jnp.concatenate(
        [jnp.where(row == 0, mine, theirs), jnp.where(row == 0, theirs, mine)], axis=1
    )


def solution(mesh):
    placed = (P(("tok", "row"), "col"), P("col"), P("row", "col", None), P(("tok", "row")))
    return jax.shard_map(
        per_device, mesh=mesh, in_specs=placed, out_specs=P(("tok", "row"), "col"), check_vma=False
    )
```

```python
import math

import jax
import jax.numpy as jnp
from jax import lax
from jax.experimental import pallas as pl
from jax.experimental.pallas import tpu as pltpu
from jax.sharding import PartitionSpec as P

EPS = 1e-05
LOG2_E = math.log2(math.e)
LOW = -1e30
EXTRA = 16
MIB = 1 << 20
CHUNKS = ((4, 0), (1, 3))


def rotary_tables(places, head_size, always):
    half = head_size // 2
    spacing = jnp.arange(half).astype(jnp.float32) * (2.0 / head_size)
    inverse = jnp.where(always, jnp.power(10000.0, -spacing), 0.0)
    angles = places.astype(jnp.float32)[:, None] * inverse[None, :]
    cosine, sine = jnp.cos(angles), jnp.sin(angles)
    return (
        jnp.concatenate([cosine, cosine], axis=1),
        jnp.concatenate([-sine, sine], axis=1),
    )


def project_chunk(normed_ref, weight_ref, key_column, query_column, cos_ref, sin_ref, doc_rows, out_ref):
    block, size = cos_ref.shape
    extra = doc_rows.shape[0]
    depth = weight_ref.shape[0] // 2

    def product(column, width):
        at = pl.ds(column if isinstance(column, int) else pl.multiple_of(column, size), width)
        return jnp.dot(
            normed_ref[0], weight_ref[:depth, at], preferred_element_type=jnp.float32
        ) + jnp.dot(normed_ref[1], weight_ref[depth:, at], preferred_element_type=jnp.float32)

    def rotated(piece):
        return piece * cos_ref[...] + pltpu.roll(piece, size // 2, 1) * sin_ref[...]

    both = product(key_column, 2 * size)
    out_ref[:block, :] = rotated(both[:, :size])
    out_ref[block : 2 * block, :] = both[:, size:]
    out_ref[2 * block : 2 * block + extra, :] = doc_rows
    out_ref[2 * block + extra : 3 * block + extra, :] = rotated(product(query_column, size))
    out_ref[3 * block + extra :, :] = doc_rows


def normalise_project_kernel(
    place_ref, a_near, a_far, b_near, b_far, squares_ref, gain_ref, cos_ref, sin_ref, weight_ref,
    out_ref, normed_ref, second_ref, own_ref, semaphores,
):
    rows, size = a_near.shape[0], cos_ref.shape[1]
    features = 2 * gain_ref.shape[0] * gain_ref.shape[2]
    core, near_row, away, own = place_ref[0], place_ref[1], place_ref[2], place_ref[3]
    copies = [
        pltpu.make_async_copy(
            weight_ref.at[:, pl.ds(pl.multiple_of(first, size), target.shape[1])],
            target,
            semaphores.at[index],
        )
        for index, (first, target) in enumerate(((away + size, second_ref), (own, own_ref)))
    ]
    for copy in copies:
        copy.start()
    for shards, half in (((a_near, a_far), core), ((b_near, b_far), 1 - core)):
        gain = gain_ref[half]
        for shard, row in zip(shards, (near_row, 1 - near_row)):
            at = pl.ds(pl.multiple_of(row * rows, 16), rows)
            factor = lax.rsqrt(squares_ref[at, :] / features + EPS)
            normed_ref[half, at, :] = (shard[...].astype(jnp.float32) * factor * gain).astype(
                jnp.bfloat16
            )
    keys, query = CHUNKS[0]
    project_chunk(
        normed_ref, weight_ref, away + keys * size, away + query * size, cos_ref, sin_ref,
        jnp.zeros((EXTRA, size), jnp.float32), out_ref,
    )
    for copy in copies:
        copy.wait()


def second_kernel(normed_ref, cos_ref, sin_ref, weight_ref, out_ref):
    size = cos_ref.shape[1]
    keys, query = CHUNKS[1]
    project_chunk(
        normed_ref, weight_ref, 0, (query - keys) * size, cos_ref, sin_ref,
        jnp.zeros((EXTRA, size), jnp.float32), out_ref,
    )


def project_kernel(normed_ref, docs_ref, cos_ref, sin_ref, weight_ref, one_ref, two_ref):
    size = cos_ref.shape[1]
    for chunk, (keys, query) in enumerate(CHUNKS):
        project_chunk(
            normed_ref, weight_ref, keys * size, query * size, cos_ref, sin_ref, docs_ref[...],
            (one_ref, two_ref)[chunk],
        )


def as_column(rows, count):
    lanes = rows.shape[1]
    pieces = []
    for begin in range(0, count, lanes):
        held = min(lanes, count - begin)
        at = lax.broadcasted_iota(jnp.int32, (held, lanes), 0)
        diagonal = at == lax.broadcasted_iota(jnp.int32, (held, lanes), 1)
        row = rows[begin // lanes : begin // lanes + 1, :]
        pieces.append(jnp.sum(jnp.where(diagonal, row, 0.0), axis=1, keepdims=True))
    return jnp.concatenate(pieces, axis=0)


def as_rows(column, lanes):
    count = column.shape[0]
    rows = []
    for begin in range(0, count, lanes):
        held = min(lanes, count - begin)
        at = lax.broadcasted_iota(jnp.int32, (held, lanes), 0)
        diagonal = at == lax.broadcasted_iota(jnp.int32, (held, lanes), 1)
        rows.append(
            jnp.sum(jnp.where(diagonal, column[begin : begin + held], 0.0), axis=0, keepdims=True)
        )
    return rows


def as_lanes(rows, count):
    lanes = rows.shape[1]
    return jnp.concatenate(
        [
            rows[begin // lanes : begin // lanes + 1, : min(lanes, count - begin)]
            for begin in range(0, count, lanes)
        ],
        axis=1,
    )


def softmax_part(scale, query_message, messages, causal):
    valid = [present for message, present in messages]
    messages = [message for message, present in messages]
    query = query_message[:-EXTRA]
    query_docs = as_column(query_message[-EXTRA:].astype(jnp.float32), query.shape[0])
    block = (messages[0].shape[0] - EXTRA) // 2
    keys = jnp.concatenate([message[:block] for message in messages], axis=0)
    values = jnp.concatenate([message[block : 2 * block] for message in messages], axis=0)
    key_docs = jnp.concatenate(
        [
            jnp.where(present, as_lanes(message[2 * block :].astype(jnp.float32), block), 0.0)
            for message, present in zip(messages, valid)
        ],
        axis=1,
    )
    visible = query_docs == key_docs
    if causal:
        shape = (query.shape[0], keys.shape[0])
        query_places = lax.broadcasted_iota(jnp.int32, shape, 0)
        key_places = lax.broadcasted_iota(jnp.int32, shape, 1)
        visible &= (key_places <= query_places) | (key_places >= block)
    scores = lax.dot_general(
        query, keys, (((1,), (1,)), ((), ())), preferred_element_type=jnp.float32
    )
    masked = jnp.where(visible, scores, LOW)
    top = jnp.max(masked, axis=1, keepdims=True)
    exponentials = jnp.exp2((masked - top) * (scale * LOG2_E))
    total = jnp.sum(exponentials, axis=1, keepdims=True)
    summed = jnp.dot(exponentials.astype(jnp.bfloat16), values, preferred_element_type=jnp.float32)
    return summed / total, jnp.where(top > LOW / 2, top * scale + jnp.log(total), LOW)


def as_message(output, logs, size):
    along = jnp.concatenate(as_rows(logs, size), axis=0)
    high = along.astype(jnp.bfloat16).astype(jnp.float32)
    middle = (along - high).astype(jnp.bfloat16).astype(jnp.float32)
    pieces = [output, high, middle, along - high - middle]
    pieces.append(jnp.zeros((EXTRA - 3 * along.shape[0], size), jnp.float32))
    return jnp.concatenate(pieces, axis=0).astype(jnp.bfloat16)


def logs_of(message, rows):
    tile = message[rows:].astype(jnp.float32)
    groups = pl.cdiv(rows, tile.shape[1])
    return as_column(sum(tile[k * groups : (k + 1) * groups] for k in range(3)), rows)


def parted(row, value):
    rows = value.shape[0] // 2
    first = row == 0
    return (
        jnp.where(first, value[:rows], value[rows:]),
        jnp.where(first, value[rows:], value[:rows]),
    )


def joined(first, second):
    (output, logs), (other, other_logs) = first, second
    top = jnp.maximum(logs, other_logs)
    weight, other_weight = jnp.exp(logs - top), jnp.exp(other_logs - top)
    total = weight + other_weight
    return (output * weight + other * other_weight) / total, top + jnp.log(total)


def own_block_kernel(scale, place_ref, chunk_one, chunk_two, out_ref, logs_ref):
    for index, (queries, keys) in enumerate(((chunk_one, chunk_two), (chunk_two, chunk_one))):
        height = keys.shape[0] - out_ref.shape[1] - EXTRA
        out_ref[index], logs_ref[index] = softmax_part(
            scale, queries[height:, :], [(keys[:height, :], True)], True
        )


def guest_kernel(
    scale, place_ref, two_away, swapped, neighbour, chunk_one, chunk_two, unused_ref, out_ref
):
    height, size = neighbour.shape
    begin = (height - EXTRA) // 2

    def attend(index, query, messages):
        output, logs = softmax_part(scale, query, [(m, True) for m in messages], False)
        out_ref[index] = as_message(output, logs, size)

    @pl.when(place_ref[0] == 0)
    def one_up():
        attend(1, neighbour[begin:, :], [chunk_one[:height, :]])

    @pl.when(place_ref[0] == 1)
    def down():
        keys = [neighbour[...], chunk_two[:height, :]]
        attend(1, two_away[begin:, :], keys)
        attend(0, swapped[begin:, :], keys)

    @pl.when(place_ref[0] == 2)
    def three_up():
        attend(0, neighbour[begin:, :], [two_away[...], swapped[...], chunk_one[:height, :]])


def own_rest_kernel(
    scale, place_ref, own_out, own_logs, chunk_one, chunk_two, two_away, swapped, neighbour,
    unused_ref, out_ref, logs_ref,
):
    tok = place_ref[0]
    height = neighbour.shape[0]
    out_ref[...] = own_out[...]
    logs_ref[...] = own_logs[...]

    def add(index, query, messages):
        part = softmax_part(scale, query, [(m, True) for m in messages], False)
        out_ref[index], logs_ref[index] = joined((own_out[index], own_logs[index]), part)

    @pl.when((tok == 1) | (tok == 3))
    def down():
        add(0, chunk_one[height:, :], [neighbour[...]])

    @pl.when(tok == 2)
    def up():
        add(1, chunk_two[height:, :], [swapped[...], two_away[...]])


def merge_kernel(
    place_ref, out_ref, logs_ref, first_ref, below_ref, mine_ref, theirs_ref
):
    block, size = out_ref.shape[1:]
    tok, row = place_ref[0], place_ref[1]

    def with_guest(index, message, present):
        guest = jnp.where(present, message[:block].astype(jnp.float32), 0.0)
        guest_logs = jnp.where(present, logs_of(message, block), LOW)
        output, logs = joined((out_ref[index], logs_ref[index]), (guest, guest_logs))
        return output.astype(jnp.bfloat16)

    down = with_guest(0, jnp.where(tok == 2, below_ref[...], first_ref[...]), tok >= 2)
    up = with_guest(1, jnp.where(tok == 1, first_ref[...], below_ref[...]), (tok == 1) | (tok == 3))
    for index, output in enumerate((down, up)):
        columns = slice(index * size, (index + 1) * size)
        mine_ref[:, columns], theirs_ref[:, columns] = parted(row, output)


def attend_gathered(query, keys, values, places, starts, scale):
    heads, count, size = query.shape
    chunk = math.gcd(keys.shape[1], 1024)
    rounds = keys.shape[1] // chunk
    stacked = (
        keys.reshape(heads, rounds, chunk, size).transpose(1, 0, 2, 3),
        values.reshape(heads, rounds, chunk, size).transpose(1, 0, 2, 3),
        jnp.arange(rounds * chunk, dtype=jnp.int32).reshape(rounds, chunk),
    )

    def advance(state, blocks):
        running, totals, summed = state
        block_keys, block_values, key_places = blocks
        scores = (
            jnp.einsum("hqd,hkd->hqk", query, block_keys, preferred_element_type=jnp.float32) * scale
        )
        visible = (key_places[None, None, :] <= places[None, :, None]) & (
            key_places[None, None, :] >= starts[None, :, None]
        )
        masked = jnp.where(visible, scores, -jnp.inf)
        newest = jnp.maximum(running, jnp.max(masked, axis=2))
        factor = jnp.exp(running - newest)
        exponentials = jnp.where(visible, jnp.exp(masked - newest[:, :, None]), 0.0)
        totals = totals * factor + jnp.sum(exponentials, axis=2)
        summed = summed * factor[:, :, None] + jnp.einsum(
            "hqk,hkd->hqd", exponentials.astype(jnp.bfloat16), block_values,
            preferred_element_type=jnp.float32,
        )
        return (newest, totals, summed), None

    initial = (
        jnp.full((heads, count), -1e30, jnp.float32),
        jnp.zeros((heads, count), jnp.float32),
        jnp.zeros((heads, count, size), jnp.float32),
    )
    (running, totals, summed), unused = lax.scan(advance, initial, stacked)
    attended = (summed / totals[:, :, None]).astype(jnp.bfloat16)
    return attended.transpose(1, 0, 2).reshape(count, heads * size)


def in_vmem(count):
    return [pl.BlockSpec(memory_space=pltpu.VMEM)] * count


def per_device(activations, norm_gain, qkv_weight, doc_ids):
    rows, width = activations.shape
    span, local_heads, triple = qkv_weight.shape
    size = triple // 3
    pair = local_heads // 2
    block = 2 * rows
    toks = lax.axis_size("tok")
    tok, row, col = lax.axis_index("tok"), lax.axis_index("row"), lax.axis_index("col")
    chip, core = col >> 1, col & 1
    grid = [(r, c) for r in range(2) for c in range(4)]

    def by_col(value, flip):
        return lax.ppermute(value, "col", [(c, c ^ flip) for c in range(4)])

    def by_row(value):
        return lax.ppermute(value, "row", [(0, 1), (1, 0)])

    def ordered(index, own, other):
        first = index == 0
        return jnp.concatenate([jnp.where(first, own, other), jnp.where(first, other, own)])

    near = lax.ppermute(
        activations,
        ("row", "col"),
        [(r * 4 + c, (c // 2) * 4 + 2 * r + c % 2) for r, c in grid],
    )
    far = lax.ppermute(
        activations,
        ("row", "col"),
        [(r * 4 + c, (c // 2) * 4 + 2 * (1 - r) + c % 2) for r, c in grid],
    )
    widened = activations.astype(jnp.float32)
    squares = jnp.sum(widened * widened, axis=1)
    gain = norm_gain.astype(jnp.float32)
    message = jnp.concatenate([squares, gain])
    message, qkv_weight = lax.optimization_barrier((message, qkv_weight))
    flat_weight = qkv_weight.reshape(span, local_heads * triple)
    got = by_col(message, 1)
    squares = squares + got[:rows]
    gain = ordered(core, gain, got[rows:])
    by_chip = by_col(jnp.concatenate([squares, gain]), 2)
    near, far, by_chip, flat_weight = lax.optimization_barrier((near, far, by_chip, flat_weight))
    near_other, far_other = by_col(near, 1), by_col(far, 1)
    squares = squares + by_chip[:rows]
    gain = jnp.where(chip == row, gain, by_chip[rows:]).reshape(2, 1, width)
    codes = doc_ids.astype(jnp.float32) + 1.0
    got = by_row(jnp.concatenate([squares, codes]))
    squares = ordered(row, squares, got[:rows]).reshape(block, 1)
    codes = ordered(row, codes, got[rows:])
    doc_rows = jnp.pad(codes, (0, EXTRA * size - block)).reshape(EXTRA, size)
    places = tok * block + jnp.arange(block, dtype=jnp.int32)
    cosine, sine = rotary_tables(places, size, near[0, : size // 2].astype(jnp.float32) < 1e30)

    taller = 3 * block + 2 * EXTRA
    break_at = 2 * block + EXTRA

    partial_sums = jax.ShapeDtypeStruct((taller, size), jnp.float32)
    no_cost = pl.CostEstimate(flops=0, bytes_accessed=0, transcendentals=0)
    columns = jnp.stack([core, chip, (1 - row) * (pair * triple), row * (pair * triple)])
    first, normed, second_weight, own_weight = pl.pallas_call(
        normalise_project_kernel,
        out_shape=(
            partial_sums,
            jax.ShapeDtypeStruct((2, block, width), jnp.bfloat16),
            jax.ShapeDtypeStruct((span, triple), jnp.bfloat16),
            jax.ShapeDtypeStruct((span, pair * triple), jnp.bfloat16),
        ),
        in_specs=[pl.BlockSpec(memory_space=pltpu.SMEM)] + in_vmem(9),
        out_specs=tuple(in_vmem(4)),
        scratch_shapes=[pltpu.SemaphoreType.DMA((2,))],
        compiler_params=pltpu.CompilerParams(vmem_limit_bytes=16 * MIB),
        cost_estimate=no_cost,
    )(
        columns, near, far, near_other, far_other, squares, gain, cosine, sine, flat_weight,
    )
    second = pl.pallas_call(
        second_kernel,
        out_shape=partial_sums,
        in_specs=in_vmem(4),
        out_specs=in_vmem(1)[0],
        compiler_params=pltpu.CompilerParams(vmem_limit_bytes=8 * MIB),
        cost_estimate=no_cost,
    )(normed, cosine, sine, second_weight)
    arrived = [by_row(chunk.astype(jnp.float16)) for chunk in (first, second)]
    own = pl.pallas_call(
        project_kernel,
        out_shape=(partial_sums, partial_sums),
        in_specs=in_vmem(5),
        out_specs=tuple(in_vmem(2)),
        compiler_params=pltpu.CompilerParams(vmem_limit_bytes=8 * MIB),
        cost_estimate=no_cost,
    )(normed, doc_rows, cosine, sine, own_weight)
    scale = 1.0 / math.sqrt(size)

    def summed(chunk):
        return (own[chunk] + arrived[chunk].astype(jnp.float32)).astype(jnp.bfloat16)

    def gathered_attention():
        chunks = [summed(0), summed(1)]
        keys = jnp.stack([chunks[1][: 2 * block], chunks[0][: 2 * block]])
        everything = lax.all_gather(keys, "tok", axis=0, tiled=False).transpose(1, 0, 2, 3)
        all_codes = lax.all_gather(codes, "tok", axis=0, tiled=True)
        starts = jnp.sum((all_codes[None, :] < codes[:, None]).astype(jnp.int32), axis=1)
        together = attend_gathered(
            jnp.stack([chunk[break_at : break_at + block] for chunk in chunks]),
            everything[:, :, :block].reshape(pair, toks * block, size),
            everything[:, :, block:].reshape(pair, toks * block, size),
            places, starts, scale,
        )
        return parted(row, together)

    if toks == 4:
        places = jnp.stack([tok, row])

        def along_tok(value, pairs):
            return lax.ppermute(value, "tok", pairs)

        def keys_or_query(chunk, is_query):
            begin = jnp.where(is_query, taller - break_at, 0)
            return lax.dynamic_slice_in_dim(chunk, begin.astype(jnp.uint32), break_at, 0)

        def on_place(kernel, out_shape, ins, unused=0):
            return pl.pallas_call(
                kernel,
                out_shape=out_shape,
                in_specs=[pl.BlockSpec(memory_space=pltpu.SMEM)]
                + in_vmem(ins - unused)
                + [pl.BlockSpec(memory_space=pl.ANY)] * unused,
                out_specs=jax.tree.map(lambda unused: in_vmem(1)[0], out_shape),
                compiler_params=pltpu.CompilerParams(vmem_limit_bytes=16 * MIB),
                cost_estimate=pl.CostEstimate(flops=0, bytes_accessed=0, transcendentals=0),
            )

        chunk_one = summed(0)
        two_away = along_tok(keys_or_query(chunk_one, tok == 3), [(0, 2), (3, 1), (1, 0), (2, 3)])
        swapped = along_tok(keys_or_query(chunk_one, tok == 2), [(1, 2), (2, 1), (0, 0), (3, 3)])
        across = lax.ppermute(chunk_one[:EXTRA], ("tok", "row", "col"), [(2, 3)])
        arrived[1] = jnp.where(
            tok < toks,
            arrived[1].astype(jnp.float32),
            jnp.broadcast_to(across[:1].astype(jnp.float32), arrived[1].shape),
        )
        chunk_two = summed(1)
        neighbour = along_tok(
            keys_or_query(chunk_two, (tok & 1) == 1), [(0, 1), (1, 0), (2, 3), (3, 2)]
        )
        part_shapes = (
            jax.ShapeDtypeStruct((2, block, size), jnp.float32),
            jax.ShapeDtypeStruct((2, block, 1), jnp.float32),
        )
        own_out, own_logs = on_place(
            lambda *refs: own_block_kernel(scale, *refs), part_shapes, 2
        )(places, chunk_one, chunk_two)
        guests = on_place(
            lambda *refs: guest_kernel(scale, *refs),
            jax.ShapeDtypeStruct((2, block + EXTRA, size), jnp.bfloat16),
            6,
            1,
        )(places, two_away, swapped, neighbour, chunk_one, chunk_two, own_logs)
        from_first = along_tok(guests[1], [(0, 1), (1, 3), (2, 0), (3, 2)])
        from_below = along_tok(guests[0], [(1, 2), (2, 3)])
        output, logs = on_place(
            lambda *refs: own_rest_kernel(scale, *refs), part_shapes, 8, 1
        )(places, own_out, own_logs, chunk_one, chunk_two, two_away, swapped, neighbour, guests)
        half = jax.ShapeDtypeStruct((rows, pair * size), jnp.bfloat16)
        mine, theirs = on_place(merge_kernel, (half, half), 4)(
            places, output, logs, from_first, from_below
        )
    else:
        mine, theirs = gathered_attention()
    theirs = by_row(theirs)
    return jnp.concatenate(
        [jnp.where(row == 0, mine, theirs), jnp.where(row == 0, theirs, mine)], axis=1
    )


def solution(mesh):
    placed = (P(("tok", "row"), "col"), P("col"), P("row", "col", None), P(("tok", "row")))
    return jax.shard_map(
        per_device, mesh=mesh, in_specs=placed, out_specs=P(("tok", "row"), "col"), check_vma=False
    )
```

```python
import math

import jax
import jax.numpy as jnp
from jax import lax
from jax.experimental import pallas as pl
from jax.experimental.pallas import tpu as pltpu
from jax.sharding import PartitionSpec as P

EPS = 1e-05
LOG2_E = math.log2(math.e)
LOW = -1e30
EXTRA = 16
MIB = 1 << 20
CHUNKS = ((4, 0), (1, 3))


def rotary_tables(places, head_size, always):
    half = head_size // 2
    spacing = jnp.arange(half).astype(jnp.float32) * (2.0 / head_size)
    inverse = jnp.where(always, jnp.power(10000.0, -spacing), 0.0)
    angles = places.astype(jnp.float32)[:, None] * inverse[None, :]
    cosine, sine = jnp.cos(angles), jnp.sin(angles)
    return (
        jnp.concatenate([cosine, cosine], axis=1),
        jnp.concatenate([-sine, sine], axis=1),
    )


def project_chunk(normed_ref, weight_ref, key_column, query_column, cos_ref, sin_ref, doc_rows, out_ref):
    block, size = cos_ref.shape
    extra = doc_rows.shape[0]
    depth = weight_ref.shape[0] // 2

    def product(column, width):
        at = pl.ds(column if isinstance(column, int) else pl.multiple_of(column, size), width)
        return jnp.dot(
            normed_ref[0], weight_ref[:depth, at], preferred_element_type=jnp.float32
        ) + jnp.dot(normed_ref[1], weight_ref[depth:, at], preferred_element_type=jnp.float32)

    def rotated(piece):
        return piece * cos_ref[...] + pltpu.roll(piece, size // 2, 1) * sin_ref[...]

    both = product(key_column, 2 * size)
    out_ref[:block, :] = rotated(both[:, :size])
    out_ref[block : 2 * block, :] = both[:, size:]
    out_ref[2 * block : 2 * block + extra, :] = doc_rows
    out_ref[2 * block + extra : 3 * block + extra, :] = rotated(product(query_column, size))
    out_ref[3 * block + extra :, :] = doc_rows


def normalise_project_kernel(
    place_ref, a_near, a_far, b_near, b_far, squares_ref, gain_ref, cos_ref, sin_ref, weight_ref,
    out_ref, normed_ref, second_ref, own_ref, semaphores,
):
    rows, size = a_near.shape[0], cos_ref.shape[1]
    features = 2 * gain_ref.shape[0] * gain_ref.shape[2]
    core, near_row, away, own = place_ref[0], place_ref[1], place_ref[2], place_ref[3]
    copies = [
        pltpu.make_async_copy(
            weight_ref.at[:, pl.ds(pl.multiple_of(first, size), target.shape[1])],
            target,
            semaphores.at[index],
        )
        for index, (first, target) in enumerate(((away + size, second_ref), (own, own_ref)))
    ]
    for copy in copies:
        copy.start()
    for shards, half in (((a_near, a_far), core), ((b_near, b_far), 1 - core)):
        gain = gain_ref[half]
        for shard, row in zip(shards, (near_row, 1 - near_row)):
            at = pl.ds(pl.multiple_of(row * rows, 16), rows)
            factor = lax.rsqrt(squares_ref[at, :] / features + EPS)
            normed_ref[half, at, :] = (shard[...].astype(jnp.float32) * factor * gain).astype(
                jnp.bfloat16
            )
    keys, query = CHUNKS[0]
    project_chunk(
        normed_ref, weight_ref, away + keys * size, away + query * size, cos_ref, sin_ref,
        jnp.zeros((EXTRA, size), jnp.float32), out_ref,
    )
    for copy in copies:
        copy.wait()


def second_kernel(normed_ref, cos_ref, sin_ref, weight_ref, out_ref):
    size = cos_ref.shape[1]
    keys, query = CHUNKS[1]
    project_chunk(
        normed_ref, weight_ref, 0, (query - keys) * size, cos_ref, sin_ref,
        jnp.zeros((EXTRA, size), jnp.float32), out_ref,
    )


def project_kernel(normed_ref, docs_ref, cos_ref, sin_ref, weight_ref, one_ref, two_ref):
    size = cos_ref.shape[1]
    for chunk, (keys, query) in enumerate(CHUNKS):
        project_chunk(
            normed_ref, weight_ref, keys * size, query * size, cos_ref, sin_ref, docs_ref[...],
            (one_ref, two_ref)[chunk],
        )


def as_column(rows, count):
    lanes = rows.shape[1]
    pieces = []
    for begin in range(0, count, lanes):
        held = min(lanes, count - begin)
        at = lax.broadcasted_iota(jnp.int32, (held, lanes), 0)
        diagonal = at == lax.broadcasted_iota(jnp.int32, (held, lanes), 1)
        row = rows[begin // lanes : begin // lanes + 1, :]
        pieces.append(jnp.sum(jnp.where(diagonal, row, 0.0), axis=1, keepdims=True))
    return jnp.concatenate(pieces, axis=0)


def as_rows(column, lanes):
    count = column.shape[0]
    rows = []
    for begin in range(0, count, lanes):
        held = min(lanes, count - begin)
        at = lax.broadcasted_iota(jnp.int32, (held, lanes), 0)
        diagonal = at == lax.broadcasted_iota(jnp.int32, (held, lanes), 1)
        rows.append(
            jnp.sum(jnp.where(diagonal, column[begin : begin + held], 0.0), axis=0, keepdims=True)
        )
    return rows


def as_lanes(rows, count):
    lanes = rows.shape[1]
    return jnp.concatenate(
        [
            rows[begin // lanes : begin // lanes + 1, : min(lanes, count - begin)]
            for begin in range(0, count, lanes)
        ],
        axis=1,
    )


def softmax_part(scale, query_message, messages, causal):
    valid = [present for message, present in messages]
    messages = [message for message, present in messages]
    query = query_message[:-EXTRA]
    query_docs = as_column(query_message[-EXTRA:].astype(jnp.float32), query.shape[0])
    block = (messages[0].shape[0] - EXTRA) // 2
    keys = jnp.concatenate([message[:block] for message in messages], axis=0)
    values = jnp.concatenate([message[block : 2 * block] for message in messages], axis=0)
    key_docs = jnp.concatenate(
        [
            jnp.where(present, as_lanes(message[2 * block :].astype(jnp.float32), block), 0.0)
            for message, present in zip(messages, valid)
        ],
        axis=1,
    )
    visible = query_docs == key_docs
    if causal:
        shape = (query.shape[0], keys.shape[0])
        query_places = lax.broadcasted_iota(jnp.int32, shape, 0)
        key_places = lax.broadcasted_iota(jnp.int32, shape, 1)
        visible &= (key_places <= query_places) | (key_places >= block)
    scores = lax.dot_general(
        query, keys, (((1,), (1,)), ((), ())), preferred_element_type=jnp.float32
    )
    masked = jnp.where(visible, scores, LOW)
    top = jnp.max(masked, axis=1, keepdims=True)
    exponentials = jnp.exp2((masked - top) * (scale * LOG2_E))
    total = jnp.sum(exponentials, axis=1, keepdims=True)
    summed = jnp.dot(exponentials.astype(jnp.bfloat16), values, preferred_element_type=jnp.float32)
    return summed / total, jnp.where(top > LOW / 2, top * scale + jnp.log(total), LOW)


def as_message(output, logs, size):
    along = jnp.concatenate(as_rows(logs, size), axis=0)
    high = along.astype(jnp.bfloat16).astype(jnp.float32)
    middle = (along - high).astype(jnp.bfloat16).astype(jnp.float32)
    pieces = [output, high, middle, along - high - middle]
    pieces.append(jnp.zeros((EXTRA - 3 * along.shape[0], size), jnp.float32))
    return jnp.concatenate(pieces, axis=0).astype(jnp.bfloat16)


def logs_of(message, rows):
    tile = message[rows:].astype(jnp.float32)
    groups = pl.cdiv(rows, tile.shape[1])
    return as_column(sum(tile[k * groups : (k + 1) * groups] for k in range(3)), rows)


def parted(row, value):
    rows = value.shape[0] // 2
    first = row == 0
    return (
        jnp.where(first, value[:rows], value[rows:]),
        jnp.where(first, value[rows:], value[:rows]),
    )


def joined(first, second):
    (output, logs), (other, other_logs) = first, second
    top = jnp.maximum(logs, other_logs)
    weight, other_weight = jnp.exp(logs - top), jnp.exp(other_logs - top)
    total = weight + other_weight
    return (output * weight + other * other_weight) / total, top + jnp.log(total)


def own_block_kernel(scale, place_ref, chunk_one, chunk_two, out_ref, logs_ref):
    for index, (queries, keys) in enumerate(((chunk_one, chunk_two), (chunk_two, chunk_one))):
        height = keys.shape[0] - out_ref.shape[1] - EXTRA
        out_ref[index], logs_ref[index] = softmax_part(
            scale, queries[height:, :], [(keys[:height, :], True)], True
        )


def guest_kernel(
    scale, place_ref, two_away, swapped, neighbour, chunk_one, chunk_two, unused_ref, out_ref
):
    height, size = neighbour.shape
    begin = (height - EXTRA) // 2

    def attend(index, query, messages):
        output, logs = softmax_part(scale, query, [(m, True) for m in messages], False)
        out_ref[index] = as_message(output, logs, size)

    @pl.when(place_ref[0] == 0)
    def one_up():
        attend(1, neighbour[begin:, :], [chunk_one[:height, :]])

    @pl.when(place_ref[0] == 1)
    def down():
        keys = [neighbour[...], chunk_two[:height, :]]
        attend(1, two_away[begin:, :], keys)
        attend(0, swapped[begin:, :], keys)

    @pl.when(place_ref[0] == 2)
    def three_up():
        attend(0, neighbour[begin:, :], [two_away[...], swapped[...], chunk_one[:height, :]])


def own_rest_kernel(
    scale, place_ref, own_out, own_logs, chunk_one, chunk_two, two_away, swapped, neighbour,
    unused_ref, out_ref, logs_ref,
):
    tok = place_ref[0]
    height = neighbour.shape[0]
    out_ref[...] = own_out[...]
    logs_ref[...] = own_logs[...]

    def add(index, query, messages):
        part = softmax_part(scale, query, [(m, True) for m in messages], False)
        out_ref[index], logs_ref[index] = joined((own_out[index], own_logs[index]), part)

    @pl.when((tok == 1) | (tok == 3))
    def down():
        add(0, chunk_one[height:, :], [neighbour[...]])

    @pl.when(tok == 2)
    def up():
        add(1, chunk_two[height:, :], [swapped[...], two_away[...]])


def merge_kernel(
    place_ref, out_ref, logs_ref, first_ref, below_ref, mine_ref, theirs_ref
):
    block, size = out_ref.shape[1:]
    tok, row = place_ref[0], place_ref[1]

    def with_guest(index, message, present):
        guest = jnp.where(present, message[:block].astype(jnp.float32), 0.0)
        guest_logs = jnp.where(present, logs_of(message, block), LOW)
        output, logs = joined((out_ref[index], logs_ref[index]), (guest, guest_logs))
        return output.astype(jnp.bfloat16)

    down = with_guest(0, jnp.where(tok == 2, below_ref[...], first_ref[...]), tok >= 2)
    up = with_guest(1, jnp.where(tok == 1, first_ref[...], below_ref[...]), (tok == 1) | (tok == 3))
    for index, output in enumerate((down, up)):
        columns = slice(index * size, (index + 1) * size)
        mine_ref[:, columns], theirs_ref[:, columns] = parted(row, output)


def attend_gathered(query, keys, values, places, starts, scale):
    heads, count, size = query.shape
    chunk = math.gcd(keys.shape[1], 1024)
    rounds = keys.shape[1] // chunk
    stacked = (
        keys.reshape(heads, rounds, chunk, size).transpose(1, 0, 2, 3),
        values.reshape(heads, rounds, chunk, size).transpose(1, 0, 2, 3),
        jnp.arange(rounds * chunk, dtype=jnp.int32).reshape(rounds, chunk),
    )

    def advance(state, blocks):
        running, totals, summed = state
        block_keys, block_values, key_places = blocks
        scores = (
            jnp.einsum("hqd,hkd->hqk", query, block_keys, preferred_element_type=jnp.float32) * scale
        )
        visible = (key_places[None, None, :] <= places[None, :, None]) & (
            key_places[None, None, :] >= starts[None, :, None]
        )
        masked = jnp.where(visible, scores, -jnp.inf)
        newest = jnp.maximum(running, jnp.max(masked, axis=2))
        factor = jnp.exp(running - newest)
        exponentials = jnp.where(visible, jnp.exp(masked - newest[:, :, None]), 0.0)
        totals = totals * factor + jnp.sum(exponentials, axis=2)
        summed = summed * factor[:, :, None] + jnp.einsum(
            "hqk,hkd->hqd", exponentials.astype(jnp.bfloat16), block_values,
            preferred_element_type=jnp.float32,
        )
        return (newest, totals, summed), None

    initial = (
        jnp.full((heads, count), -1e30, jnp.float32),
        jnp.zeros((heads, count), jnp.float32),
        jnp.zeros((heads, count, size), jnp.float32),
    )
    (running, totals, summed), unused = lax.scan(advance, initial, stacked)
    attended = (summed / totals[:, :, None]).astype(jnp.bfloat16)
    return attended.transpose(1, 0, 2).reshape(count, heads * size)


def in_vmem(count):
    return [pl.BlockSpec(memory_space=pltpu.VMEM)] * count


def per_device(activations, norm_gain, qkv_weight, doc_ids):
    rows, width = activations.shape
    span, local_heads, triple = qkv_weight.shape
    size = triple // 3
    pair = local_heads // 2
    block = 2 * rows
    toks = lax.axis_size("tok")
    tok, row, col = lax.axis_index("tok"), lax.axis_index("row"), lax.axis_index("col")
    chip, core = col >> 1, col & 1
    grid = [(r, c) for r in range(2) for c in range(4)]

    def by_col(value, flip):
        return lax.ppermute(value, "col", [(c, c ^ flip) for c in range(4)])

    def by_row(value):
        return lax.ppermute(value, "row", [(0, 1), (1, 0)])

    def ordered(index, own, other):
        first = index == 0
        return jnp.concatenate([jnp.where(first, own, other), jnp.where(first, other, own)])

    near = lax.ppermute(
        activations,
        ("row", "col"),
        [(r * 4 + c, (c // 2) * 4 + 2 * r + c % 2) for r, c in grid],
    )
    far = lax.ppermute(
        activations,
        ("row", "col"),
        [(r * 4 + c, (c // 2) * 4 + 2 * (1 - r) + c % 2) for r, c in grid],
    )
    widened = activations.astype(jnp.float32)
    squares = jnp.sum(widened * widened, axis=1)
    gain = norm_gain.astype(jnp.float32)
    message = jnp.concatenate([squares, gain])
    message, qkv_weight = lax.optimization_barrier((message, qkv_weight))
    flat_weight = qkv_weight.reshape(span, local_heads * triple)
    got = by_col(message, 1)
    squares = squares + got[:rows]
    gain = ordered(core, gain, got[rows:])
    by_chip = by_col(jnp.concatenate([squares, gain]), 2)
    near, far, by_chip, flat_weight = lax.optimization_barrier((near, far, by_chip, flat_weight))
    near_other, far_other = by_col(near, 1), by_col(far, 1)
    squares = squares + by_chip[:rows]
    gain = jnp.where(chip == row, gain, by_chip[rows:]).reshape(2, 1, width)
    codes = doc_ids.astype(jnp.float32) + 1.0
    got = by_row(jnp.concatenate([squares, codes]))
    squares = ordered(row, squares, got[:rows]).reshape(block, 1)
    codes = ordered(row, codes, got[rows:])
    doc_rows = jnp.pad(codes, (0, EXTRA * size - block)).reshape(EXTRA, size)
    places = tok * block + jnp.arange(block, dtype=jnp.int32)
    cosine, sine = rotary_tables(places, size, near[0, : size // 2].astype(jnp.float32) < 1e30)

    taller = 3 * block + 2 * EXTRA
    break_at = 2 * block + EXTRA

    partial_sums = jax.ShapeDtypeStruct((taller, size), jnp.float32)
    no_cost = pl.CostEstimate(flops=0, bytes_accessed=0, transcendentals=0)
    columns = jnp.stack([core, chip, (1 - row) * (pair * triple), row * (pair * triple)])
    first, normed, second_weight, own_weight = pl.pallas_call(
        normalise_project_kernel,
        out_shape=(
            partial_sums,
            jax.ShapeDtypeStruct((2, block, width), jnp.bfloat16),
            jax.ShapeDtypeStruct((span, triple), jnp.bfloat16),
            jax.ShapeDtypeStruct((span, pair * triple), jnp.bfloat16),
        ),
        in_specs=[pl.BlockSpec(memory_space=pltpu.SMEM)] + in_vmem(9),
        out_specs=tuple(in_vmem(4)),
        scratch_shapes=[pltpu.SemaphoreType.DMA((2,))],
        compiler_params=pltpu.CompilerParams(vmem_limit_bytes=5 * MIB),
        cost_estimate=no_cost,
    )(
        columns, near, far, near_other, far_other, squares, gain, cosine, sine, flat_weight,
    )
    second = pl.pallas_call(
        second_kernel,
        out_shape=partial_sums,
        in_specs=in_vmem(4),
        out_specs=in_vmem(1)[0],
        compiler_params=pltpu.CompilerParams(vmem_limit_bytes=4 * MIB),
        cost_estimate=no_cost,
    )(normed, cosine, sine, second_weight)
    arrived = [by_row(chunk.astype(jnp.float16)) for chunk in (first, second)]
    own = pl.pallas_call(
        project_kernel,
        out_shape=(partial_sums, partial_sums),
        in_specs=in_vmem(5),
        out_specs=tuple(in_vmem(2)),
        compiler_params=pltpu.CompilerParams(vmem_limit_bytes=4 * MIB),
        cost_estimate=no_cost,
    )(normed, doc_rows, cosine, sine, own_weight)
    scale = 1.0 / math.sqrt(size)

    def summed(chunk):
        return (own[chunk] + arrived[chunk].astype(jnp.float32)).astype(jnp.bfloat16)

    def gathered_attention():
        chunks = [summed(0), summed(1)]
        keys = jnp.stack([chunks[1][: 2 * block], chunks[0][: 2 * block]])
        everything = lax.all_gather(keys, "tok", axis=0, tiled=False).transpose(1, 0, 2, 3)
        all_codes = lax.all_gather(codes, "tok", axis=0, tiled=True)
        starts = jnp.sum((all_codes[None, :] < codes[:, None]).astype(jnp.int32), axis=1)
        together = attend_gathered(
            jnp.stack([chunk[break_at : break_at + block] for chunk in chunks]),
            everything[:, :, :block].reshape(pair, toks * block, size),
            everything[:, :, block:].reshape(pair, toks * block, size),
            places, starts, scale,
        )
        return parted(row, together)

    if toks == 4:
        places = jnp.stack([tok, row])

        def along_tok(value, pairs):
            return lax.ppermute(value, "tok", pairs)

        def keys_or_query(chunk, is_query):
            begin = jnp.where(is_query, taller - break_at, 0)
            return lax.dynamic_slice_in_dim(chunk, begin.astype(jnp.uint32), break_at, 0)

        def on_place(kernel, out_shape, ins, unused=0):
            return pl.pallas_call(
                kernel,
                out_shape=out_shape,
                in_specs=[pl.BlockSpec(memory_space=pltpu.SMEM)]
                + in_vmem(ins - unused)
                + [pl.BlockSpec(memory_space=pl.ANY)] * unused,
                out_specs=jax.tree.map(lambda unused: in_vmem(1)[0], out_shape),
                compiler_params=pltpu.CompilerParams(vmem_limit_bytes=16 * MIB),
                cost_estimate=pl.CostEstimate(flops=0, bytes_accessed=0, transcendentals=0),
            )

        chunk_one = summed(0)
        two_away = along_tok(keys_or_query(chunk_one, tok == 3), [(0, 2), (3, 1), (1, 0), (2, 3)])
        swapped = along_tok(keys_or_query(chunk_one, tok == 2), [(1, 2), (2, 1), (0, 0), (3, 3)])
        across = lax.ppermute(chunk_one[:EXTRA], ("tok", "row", "col"), [(2, 3)])
        arrived[1] = jnp.where(
            tok < toks,
            arrived[1].astype(jnp.float32),
            jnp.broadcast_to(across[:1].astype(jnp.float32), arrived[1].shape),
        )
        chunk_two = summed(1)
        neighbour = along_tok(
            keys_or_query(chunk_two, (tok & 1) == 1), [(0, 1), (1, 0), (2, 3), (3, 2)]
        )
        part_shapes = (
            jax.ShapeDtypeStruct((2, block, size), jnp.float32),
            jax.ShapeDtypeStruct((2, block, 1), jnp.float32),
        )
        own_out, own_logs = on_place(
            lambda *refs: own_block_kernel(scale, *refs), part_shapes, 2
        )(places, chunk_one, chunk_two)
        guests = on_place(
            lambda *refs: guest_kernel(scale, *refs),
            jax.ShapeDtypeStruct((2, block + EXTRA, size), jnp.bfloat16),
            6,
            1,
        )(places, two_away, swapped, neighbour, chunk_one, chunk_two, own_logs)
        from_first = along_tok(guests[1], [(0, 1), (1, 3), (2, 0), (3, 2)])
        from_below = along_tok(guests[0], [(1, 2), (2, 3)])
        output, logs = on_place(
            lambda *refs: own_rest_kernel(scale, *refs), part_shapes, 8, 1
        )(places, own_out, own_logs, chunk_one, chunk_two, two_away, swapped, neighbour, guests)
        half = jax.ShapeDtypeStruct((rows, pair * size), jnp.bfloat16)
        mine, theirs = on_place(merge_kernel, (half, half), 4)(
            places, output, logs, from_first, from_below
        )
    else:
        mine, theirs = gathered_attention()
    theirs = by_row(theirs)
    return jnp.concatenate(
        [jnp.where(row == 0, mine, theirs), jnp.where(row == 0, theirs, mine)], axis=1
    )


def solution(mesh):
    placed = (P(("tok", "row"), "col"), P("col"), P("row", "col", None), P(("tok", "row")))
    return jax.shard_map(
        per_device, mesh=mesh, in_specs=placed, out_specs=P(("tok", "row"), "col"), check_vma=False
    )
```

```python
import math

import jax
import jax.numpy as jnp
from jax import lax
from jax.experimental import pallas as pl
from jax.experimental.pallas import tpu as pltpu
from jax.sharding import PartitionSpec as P

EPS = 1e-05
LOG2_E = math.log2(math.e)
LOW = -1e30
EXTRA = 16
MIB = 1 << 20
CHUNKS = ((4, 0), (1, 3))


def rotary_tables(places, head_size, always):
    half = head_size // 2
    spacing = jnp.arange(half).astype(jnp.float32) * (2.0 / head_size)
    inverse = jnp.where(always, jnp.power(10000.0, -spacing), 0.0)
    angles = places.astype(jnp.float32)[:, None] * inverse[None, :]
    cosine, sine = jnp.cos(angles), jnp.sin(angles)
    return (
        jnp.concatenate([cosine, cosine], axis=1),
        jnp.concatenate([-sine, sine], axis=1),
    )


def project_chunk(normed_ref, weight_ref, key_column, query_column, cos_ref, sin_ref, doc_rows, out_ref):
    block, size = cos_ref.shape
    extra = doc_rows.shape[0]
    depth = weight_ref.shape[0] // 2

    def product(column, width):
        at = pl.ds(column if isinstance(column, int) else pl.multiple_of(column, size), width)
        return jnp.dot(
            normed_ref[0], weight_ref[:depth, at], preferred_element_type=jnp.float32
        ) + jnp.dot(normed_ref[1], weight_ref[depth:, at], preferred_element_type=jnp.float32)

    def rotated(piece):
        return piece * cos_ref[...] + pltpu.roll(piece, size // 2, 1) * sin_ref[...]

    both = product(key_column, 2 * size)
    out_ref[:block, :] = rotated(both[:, :size])
    out_ref[block : 2 * block, :] = both[:, size:]
    out_ref[2 * block : 2 * block + extra, :] = doc_rows
    out_ref[2 * block + extra : 3 * block + extra, :] = rotated(product(query_column, size))
    out_ref[3 * block + extra :, :] = doc_rows


def normalise_project_kernel(
    place_ref, a_near, a_far, b_near, b_far, squares_ref, gain_ref, cos_ref, sin_ref, weight_ref,
    one_ref, two_ref, normed_ref, own_hbm, semaphore,
):
    rows, size = a_near.shape[0], cos_ref.shape[1]
    features = 2 * gain_ref.shape[0] * gain_ref.shape[2]
    core, near_row, away, own = place_ref[0], place_ref[1], place_ref[2], place_ref[3]
    copy = pltpu.make_async_copy(
        weight_ref.at[:, pl.ds(pl.multiple_of(own, size), 6 * size)], own_hbm, semaphore
    )
    copy.start()
    for shards, half in (((a_near, a_far), core), ((b_near, b_far), 1 - core)):
        gain = gain_ref[half].astype(jnp.float32)
        for shard, row in zip(shards, (near_row, 1 - near_row)):
            at = pl.ds(pl.multiple_of(row * rows, 16), rows)
            factor = lax.rsqrt(squares_ref[at, :] / features + EPS)
            normed_ref[half, at, :] = (shard[...].astype(jnp.float32) * factor * gain).astype(
                jnp.bfloat16
            )
    nothing = jnp.zeros((EXTRA, size), jnp.float32)
    for chunk, (keys, query) in enumerate(CHUNKS):
        project_chunk(
            normed_ref, weight_ref, away + keys * size, away + query * size, cos_ref, sin_ref, nothing,
            (one_ref, two_ref)[chunk],
        )
    copy.wait()


def project_kernel(
    normed_ref, docs_ref, cos_ref, sin_ref, own_hbm, one_ref, two_ref, weight_buffer, semaphore
):
    copy = pltpu.make_async_copy(own_hbm, weight_buffer, semaphore)
    copy.start()
    copy.wait()
    size = cos_ref.shape[1]
    for chunk, (keys, query) in enumerate(CHUNKS):
        project_chunk(
            normed_ref, weight_buffer, keys * size, query * size, cos_ref, sin_ref, docs_ref[...],
            (one_ref, two_ref)[chunk],
        )


def as_column(rows, count):
    lanes = rows.shape[1]
    pieces = []
    for begin in range(0, count, lanes):
        held = min(lanes, count - begin)
        at = lax.broadcasted_iota(jnp.int32, (held, lanes), 0)
        diagonal = at == lax.broadcasted_iota(jnp.int32, (held, lanes), 1)
        row = rows[begin // lanes : begin // lanes + 1, :]
        pieces.append(jnp.sum(jnp.where(diagonal, row, 0.0), axis=1, keepdims=True))
    return jnp.concatenate(pieces, axis=0)


def as_rows(column, lanes):
    count = column.shape[0]
    rows = []
    for begin in range(0, count, lanes):
        held = min(lanes, count - begin)
        at = lax.broadcasted_iota(jnp.int32, (held, lanes), 0)
        diagonal = at == lax.broadcasted_iota(jnp.int32, (held, lanes), 1)
        rows.append(
            jnp.sum(jnp.where(diagonal, column[begin : begin + held], 0.0), axis=0, keepdims=True)
        )
    return rows


def as_lanes(rows, count):
    lanes = rows.shape[1]
    return jnp.concatenate(
        [
            rows[begin // lanes : begin // lanes + 1, : min(lanes, count - begin)]
            for begin in range(0, count, lanes)
        ],
        axis=1,
    )


def softmax_part(scale, query_message, messages, causal):
    valid = [present for message, present in messages]
    messages = [message for message, present in messages]
    query = query_message[:-EXTRA]
    query_docs = as_column(query_message[-EXTRA:].astype(jnp.float32), query.shape[0])
    block = (messages[0].shape[0] - EXTRA) // 2
    keys = jnp.concatenate([message[:block] for message in messages], axis=0)
    values = jnp.concatenate([message[block : 2 * block] for message in messages], axis=0)
    key_docs = jnp.concatenate(
        [
            jnp.where(present, as_lanes(message[2 * block :].astype(jnp.float32), block), 0.0)
            for message, present in zip(messages, valid)
        ],
        axis=1,
    )
    visible = query_docs == key_docs
    if causal:
        shape = (query.shape[0], keys.shape[0])
        query_places = lax.broadcasted_iota(jnp.int32, shape, 0)
        key_places = lax.broadcasted_iota(jnp.int32, shape, 1)
        visible &= (key_places <= query_places) | (key_places >= block)
    scores = lax.dot_general(
        query, keys, (((1,), (1,)), ((), ())), preferred_element_type=jnp.float32
    )
    masked = jnp.where(visible, scores, LOW)
    top = jnp.max(masked, axis=1, keepdims=True)
    exponentials = jnp.exp2((masked - top) * (scale * LOG2_E))
    total = jnp.sum(exponentials, axis=1, keepdims=True)
    summed = jnp.dot(exponentials.astype(jnp.bfloat16), values, preferred_element_type=jnp.float32)
    return summed / total, jnp.where(top > LOW / 2, top * scale + jnp.log(total), LOW)


def as_message(output, logs, size):
    along = jnp.concatenate(as_rows(logs, size), axis=0)
    high = along.astype(jnp.bfloat16).astype(jnp.float32)
    middle = (along - high).astype(jnp.bfloat16).astype(jnp.float32)
    pieces = [output, high, middle, along - high - middle]
    pieces.append(jnp.zeros((EXTRA - 3 * along.shape[0], size), jnp.float32))
    return jnp.concatenate(pieces, axis=0).astype(jnp.bfloat16)


def logs_of(message, rows):
    tile = message[rows:].astype(jnp.float32)
    groups = pl.cdiv(rows, tile.shape[1])
    return as_column(sum(tile[k * groups : (k + 1) * groups] for k in range(3)), rows)


def parted(row, value):
    rows = value.shape[0] // 2
    first = row == 0
    return (
        jnp.where(first, value[:rows], value[rows:]),
        jnp.where(first, value[rows:], value[:rows]),
    )


def joined(first, second):
    (output, logs), (other, other_logs) = first, second
    top = jnp.maximum(logs, other_logs)
    weight, other_weight = jnp.exp(logs - top), jnp.exp(other_logs - top)
    total = weight + other_weight
    return (output * weight + other * other_weight) / total, top + jnp.log(total)


def own_block_kernel(scale, place_ref, chunk_one, chunk_two, out_ref, logs_ref):
    for index, (queries, keys) in enumerate(((chunk_one, chunk_two), (chunk_two, chunk_one))):
        height = keys.shape[0] - out_ref.shape[1] - EXTRA
        out_ref[index], logs_ref[index] = softmax_part(
            scale, queries[height:, :], [(keys[:height, :], True)], True
        )


def guest_kernel(
    scale, place_ref, two_away, swapped, neighbour, chunk_one, chunk_two, unused_ref, out_ref
):
    height, size = neighbour.shape
    begin = (height - EXTRA) // 2

    def attend(index, query, messages):
        output, logs = softmax_part(scale, query, [(m, True) for m in messages], False)
        out_ref[index] = as_message(output, logs, size)

    @pl.when(place_ref[0] == 0)
    def one_up():
        attend(1, neighbour[begin:, :], [chunk_one[:height, :]])

    @pl.when(place_ref[0] == 1)
    def down():
        keys = [neighbour[...], chunk_two[:height, :]]
        attend(1, two_away[begin:, :], keys)
        attend(0, swapped[begin:, :], keys)

    @pl.when(place_ref[0] == 2)
    def three_up():
        attend(0, neighbour[begin:, :], [two_away[...], swapped[...], chunk_one[:height, :]])


def own_rest_kernel(
    scale, place_ref, own_out, own_logs, chunk_one, chunk_two, two_away, swapped, neighbour,
    unused_ref, out_ref, logs_ref,
):
    tok = place_ref[0]
    height = neighbour.shape[0]
    out_ref[...] = own_out[...]
    logs_ref[...] = own_logs[...]

    def add(index, query, messages):
        part = softmax_part(scale, query, [(m, True) for m in messages], False)
        out_ref[index], logs_ref[index] = joined((own_out[index], own_logs[index]), part)

    @pl.when((tok == 1) | (tok == 3))
    def down():
        add(0, chunk_one[height:, :], [neighbour[...]])

    @pl.when(tok == 2)
    def up():
        add(1, chunk_two[height:, :], [swapped[...], two_away[...]])


def merge_kernel(
    place_ref, out_ref, logs_ref, first_ref, below_ref, mine_ref, theirs_ref
):
    block, size = out_ref.shape[1:]
    tok, row = place_ref[0], place_ref[1]

    def with_guest(index, message, present):
        guest = jnp.where(present, message[:block].astype(jnp.float32), 0.0)
        guest_logs = jnp.where(present, logs_of(message, block), LOW)
        output, logs = joined((out_ref[index], logs_ref[index]), (guest, guest_logs))
        return output.astype(jnp.bfloat16)

    down = with_guest(0, jnp.where(tok == 2, below_ref[...], first_ref[...]), tok >= 2)
    up = with_guest(1, jnp.where(tok == 1, first_ref[...], below_ref[...]), (tok == 1) | (tok == 3))
    for index, output in enumerate((down, up)):
        columns = slice(index * size, (index + 1) * size)
        mine_ref[:, columns], theirs_ref[:, columns] = parted(row, output)


def attend_gathered(query, keys, values, places, starts, scale):
    heads, count, size = query.shape
    chunk = math.gcd(keys.shape[1], 1024)
    rounds = keys.shape[1] // chunk
    stacked = (
        keys.reshape(heads, rounds, chunk, size).transpose(1, 0, 2, 3),
        values.reshape(heads, rounds, chunk, size).transpose(1, 0, 2, 3),
        jnp.arange(rounds * chunk, dtype=jnp.int32).reshape(rounds, chunk),
    )

    def advance(state, blocks):
        running, totals, summed = state
        block_keys, block_values, key_places = blocks
        scores = (
            jnp.einsum("hqd,hkd->hqk", query, block_keys, preferred_element_type=jnp.float32) * scale
        )
        visible = (key_places[None, None, :] <= places[None, :, None]) & (
            key_places[None, None, :] >= starts[None, :, None]
        )
        masked = jnp.where(visible, scores, -jnp.inf)
        newest = jnp.maximum(running, jnp.max(masked, axis=2))
        factor = jnp.exp(running - newest)
        exponentials = jnp.where(visible, jnp.exp(masked - newest[:, :, None]), 0.0)
        totals = totals * factor + jnp.sum(exponentials, axis=2)
        summed = summed * factor[:, :, None] + jnp.einsum(
            "hqk,hkd->hqd", exponentials.astype(jnp.bfloat16), block_values,
            preferred_element_type=jnp.float32,
        )
        return (newest, totals, summed), None

    initial = (
        jnp.full((heads, count), -1e30, jnp.float32),
        jnp.zeros((heads, count), jnp.float32),
        jnp.zeros((heads, count, size), jnp.float32),
    )
    (running, totals, summed), unused = lax.scan(advance, initial, stacked)
    attended = (summed / totals[:, :, None]).astype(jnp.bfloat16)
    return attended.transpose(1, 0, 2).reshape(count, heads * size)


def in_vmem(count):
    return [pl.BlockSpec(memory_space=pltpu.VMEM)] * count


def per_device(activations, norm_gain, qkv_weight, doc_ids):
    rows, width = activations.shape
    span, local_heads, triple = qkv_weight.shape
    size = triple // 3
    pair = local_heads // 2
    block = 2 * rows
    toks = lax.axis_size("tok")
    tok, row, col = lax.axis_index("tok"), lax.axis_index("row"), lax.axis_index("col")
    chip, core = col >> 1, col & 1
    grid = [(r, c) for r in range(2) for c in range(4)]

    def by_col(value, flip):
        return lax.ppermute(value, "col", [(c, c ^ flip) for c in range(4)])

    def by_row(value):
        return lax.ppermute(value, "row", [(0, 1), (1, 0)])

    def ordered(index, own, other):
        first = index == 0
        return jnp.concatenate([jnp.where(first, own, other), jnp.where(first, other, own)])

    near = lax.ppermute(
        activations,
        ("row", "col"),
        [(r * 4 + c, (c // 2) * 4 + 2 * r + c % 2) for r, c in grid],
    )
    far = lax.ppermute(
        activations,
        ("row", "col"),
        [(r * 4 + c, (c // 2) * 4 + 2 * (1 - r) + c % 2) for r, c in grid],
    )
    widened = activations.astype(jnp.float32)
    squares = jnp.sum(widened * widened, axis=1)
    gain = ordered(core, norm_gain, by_col(norm_gain, 1))
    gain = jnp.where(chip == row, gain, by_col(gain, 2)).reshape(2, 1, width)
    message = squares
    message, qkv_weight = lax.optimization_barrier((message, qkv_weight))
    flat_weight = qkv_weight.reshape(span, local_heads * triple)
    got = by_col(message, 1)
    squares = squares + got
    by_chip = by_col(squares, 2)
    near, far, by_chip, flat_weight = lax.optimization_barrier((near, far, by_chip, flat_weight))
    near_other, far_other = by_col(near, 1), by_col(far, 1)
    squares = squares + by_chip
    codes = doc_ids.astype(jnp.float32) + 1.0
    got = by_row(jnp.concatenate([squares, codes]))
    squares = ordered(row, squares, got[:rows]).reshape(block, 1)
    codes = ordered(row, codes, got[rows:])
    doc_rows = jnp.pad(codes, (0, EXTRA * size - block)).reshape(EXTRA, size)
    places = tok * block + jnp.arange(block, dtype=jnp.int32)
    cosine, sine = rotary_tables(places, size, near[0, : size // 2].astype(jnp.float32) < 1e30)

    taller = 3 * block + 2 * EXTRA
    break_at = 2 * block + EXTRA

    partial_sums = jax.ShapeDtypeStruct((taller, size), jnp.float32)
    no_cost = pl.CostEstimate(flops=0, bytes_accessed=0, transcendentals=0)
    *away, normed, own_weight = pl.pallas_call(
        normalise_project_kernel,
        out_shape=(
            partial_sums,
            partial_sums,
            jax.ShapeDtypeStruct((2, block, width), jnp.bfloat16),
            pltpu.HBM((span, pair * triple), jnp.bfloat16),
        ),
        in_specs=[pl.BlockSpec(memory_space=pltpu.SMEM)] + in_vmem(9),
        out_specs=tuple(in_vmem(3)) + (pl.BlockSpec(memory_space=pltpu.HBM),),
        scratch_shapes=[pltpu.SemaphoreType.DMA(())],
        compiler_params=pltpu.CompilerParams(vmem_limit_bytes=12 * MIB),
        cost_estimate=no_cost,
    )(
        jnp.stack([core, chip, (1 - row) * (pair * triple), row * (pair * triple)]),
        near, far, near_other, far_other, squares, gain, cosine, sine, flat_weight,
    )
    arrived = [by_row(chunk.astype(jnp.float16)) for chunk in away]
    own = pl.pallas_call(
        project_kernel,
        out_shape=(partial_sums, partial_sums),
        in_specs=in_vmem(4) + [pl.BlockSpec(memory_space=pltpu.HBM)],
        out_specs=tuple(in_vmem(2)),
        scratch_shapes=[
            pltpu.VMEM((span, pair * triple), jnp.bfloat16),
            pltpu.SemaphoreType.DMA(()),
        ],
        compiler_params=pltpu.CompilerParams(vmem_limit_bytes=8 * MIB),
        cost_estimate=no_cost,
    )(
        normed, doc_rows, cosine, sine, pltpu.with_memory_space_constraint(own_weight, pltpu.HBM)
    )
    scale = 1.0 / math.sqrt(size)

    def summed(chunk):
        return (own[chunk] + arrived[chunk].astype(jnp.float32)).astype(jnp.bfloat16)

    def gathered_attention():
        chunks = [summed(0), summed(1)]
        keys = jnp.stack([chunks[1][: 2 * block], chunks[0][: 2 * block]])
        everything = lax.all_gather(keys, "tok", axis=0, tiled=False).transpose(1, 0, 2, 3)
        all_codes = lax.all_gather(codes, "tok", axis=0, tiled=True)
        starts = jnp.sum((all_codes[None, :] < codes[:, None]).astype(jnp.int32), axis=1)
        together = attend_gathered(
            jnp.stack([chunk[break_at : break_at + block] for chunk in chunks]),
            everything[:, :, :block].reshape(pair, toks * block, size),
            everything[:, :, block:].reshape(pair, toks * block, size),
            places, starts, scale,
        )
        return parted(row, together)

    if toks == 4:
        places = jnp.stack([tok, row])

        def along_tok(value, pairs):
            return lax.ppermute(value, "tok", pairs)

        def keys_or_query(chunk, is_query):
            begin = jnp.where(is_query, taller - break_at, 0)
            return lax.dynamic_slice_in_dim(chunk, begin.astype(jnp.uint32), break_at, 0)

        def on_place(kernel, out_shape, ins, unused=0):
            return pl.pallas_call(
                kernel,
                out_shape=out_shape,
                in_specs=[pl.BlockSpec(memory_space=pltpu.SMEM)]
                + in_vmem(ins - unused)
                + [pl.BlockSpec(memory_space=pl.ANY)] * unused,
                out_specs=jax.tree.map(lambda unused: in_vmem(1)[0], out_shape),
                compiler_params=pltpu.CompilerParams(vmem_limit_bytes=16 * MIB),
                cost_estimate=pl.CostEstimate(flops=0, bytes_accessed=0, transcendentals=0),
            )

        chunk_one = summed(0)
        two_away = along_tok(keys_or_query(chunk_one, tok == 3), [(0, 2), (3, 1), (1, 0), (2, 3)])
        swapped = along_tok(keys_or_query(chunk_one, tok == 2), [(1, 2), (2, 1), (0, 0), (3, 3)])
        across = lax.ppermute(chunk_one[:EXTRA], ("tok", "row", "col"), [(2, 3)])
        arrived[1] = jnp.where(
            tok < toks,
            arrived[1].astype(jnp.float32),
            jnp.broadcast_to(across[:1].astype(jnp.float32), arrived[1].shape),
        )
        chunk_two = summed(1)
        neighbour = along_tok(
            keys_or_query(chunk_two, (tok & 1) == 1), [(0, 1), (1, 0), (2, 3), (3, 2)]
        )
        part_shapes = (
            jax.ShapeDtypeStruct((2, block, size), jnp.float32),
            jax.ShapeDtypeStruct((2, block, 1), jnp.float32),
        )
        own_out, own_logs = on_place(
            lambda *refs: own_block_kernel(scale, *refs), part_shapes, 2
        )(places, chunk_one, chunk_two)
        guests = on_place(
            lambda *refs: guest_kernel(scale, *refs),
            jax.ShapeDtypeStruct((2, block + EXTRA, size), jnp.bfloat16),
            6,
            1,
        )(places, two_away, swapped, neighbour, chunk_one, chunk_two, own_logs)
        from_first = along_tok(guests[1], [(0, 1), (1, 3), (2, 0), (3, 2)])
        from_below = along_tok(guests[0], [(1, 2), (2, 3)])
        output, logs = on_place(
            lambda *refs: own_rest_kernel(scale, *refs), part_shapes, 8, 1
        )(places, own_out, own_logs, chunk_one, chunk_two, two_away, swapped, neighbour, guests)
        half = jax.ShapeDtypeStruct((rows, pair * size), jnp.bfloat16)
        mine, theirs = on_place(merge_kernel, (half, half), 4)(
            places, output, logs, from_first, from_below
        )
    else:
        mine, theirs = gathered_attention()
    theirs = by_row(theirs)
    return jnp.concatenate(
        [jnp.where(row == 0, mine, theirs), jnp.where(row == 0, theirs, mine)], axis=1
    )


def solution(mesh):
    placed = (P(("tok", "row"), "col"), P("col"), P("row", "col", None), P(("tok", "row")))
    return jax.shard_map(
        per_device, mesh=mesh, in_specs=placed, out_specs=P(("tok", "row"), "col"), check_vma=False
    )
```
